256 devices in a mesh: gx: 8 (over z), gy: 32 (over y, x, core).
Axes of the slice: x: 4, y: 4, z: 8, core: 2. Of those that a mesh axis runs over, the one named last changes fastest.
Arguments:
- source: float32 [2, 256, 1024, 256], P(None, 'gx', 'gy'), may hold values from -4 to 4
- wavenumber_sq: float32 [256, 1024, 256], P('gx', 'gy'), may hold values from 0.1 to 0.8
Outputs:
- fine_iterate: float32 [2, 256, 1024, 256], P(None, 'gx', 'gy')
- second_iterate: float32 [2, 128, 512, 128], P(None, 'gx', 'gy')
- third_iterate: float32 [2, 64, 256, 64], P(None, 'gx', 'gy')
- coarse_iterate: float32 [2, 32, 128, 32], P(None, 'gx', 'gy')
The draws below stay inside these ranges and needn't reach their ends.
All inputs are finite; a program needn't handle non-finite values.
Results may differ from the reference program's by a relative error of at most 0.0001.
Values sent between devices are 32-bit elements; how exact they have to be, the bound alone decides.
No kernel may reach another device: no remote copies, remote signals or barrier semaphores. Data moves between devices by JAX's collectives and lax.ppermute only.
A program may use at most 192 MiB of HBM per device.

```python
import math
import jax
import jax.numpy as jnp
from jax import lax

LEVELS = 3
COARSE_SWEEPS = 4
NX = 256
NY = 1024
NZ = 256


def draw_source(key, part):
    key = jax.random.fold_in(key, 7)
    return jnp.clip(jax.random.normal(key, (2, NX, NY, NZ), jnp.float32), -4.0, 4.0)


def shard_levels(own_key, shape, pieces, smallest, top_value):
    loudness, own = 1.0, jax.random.fold_in(own_key, 6)
    for position, blocks in pieces:
        heights = jnp.exp(jax.random.uniform(jax.random.fold_in(own, position), (blocks,), jnp.float32, smallest / len(pieces), top_value / len(pieces)))
        loudness = loudness * jnp.repeat(heights, shape[position] // blocks).reshape([-1 if axis == position else 1 for axis in range(len(shape))])
    return loudness


def setup_inputs(seed: int = 0) -> dict:
    splits = jax.random.split(jax.random.key(seed), 3)
    source = draw_source(jax.random.fold_in(splits[2], 71), 0)
    wavenumber_sq = jnp.clip(jnp.exp(math.log(0.8) - 2.0794415 * jax.random.uniform(splits[1], (NX, NY, NZ), jnp.float32) ** shard_levels(splits[1], (NX, NY, NZ), ((0, 8), (1, 32)), -0.2, 0.2)), 0.1, 0.8)
    return dict(source=source, wavenumber_sq=wavenumber_sq)


DAMPING = 0.8
SHIFT_IMAG = 0.5


def beside_all(padded):
    zpadded = jnp.pad(padded, ((0, 0), (0, 0), (0, 0), (1, 1)))
    middle = zpadded[:, 1:-1, 1:-1, :]
    sides = padded[:, 2:, 1:-1, :] + padded[:, :-2, 1:-1, :] + padded[:, 1:-1, 2:, :] + padded[:, 1:-1, :-2, :]
    return sides + middle[..., 2:] + middle[..., :-2]


def combine(field, neighbours, wavenum, spacing):
    real_part = (6.0 * field[0] - neighbours[0]) / spacing - wavenum * (field[0] + SHIFT_IMAG * field[1])
    imag_part = (6.0 * field[1] - neighbours[1]) / spacing - wavenum * (field[1] - SHIFT_IMAG * field[0])
    return jnp.stack([real_part, imag_part])


def divide(resid, wavenum, spacing):
    diag_real = 6.0 / spacing - wavenum
    diag_imag = SHIFT_IMAG * wavenum
    modulus = diag_real * diag_real + diag_imag * diag_imag
    return jnp.stack([(resid[0] * diag_real + resid[1] * diag_imag) / modulus,
                      (resid[1] * diag_real - resid[0] * diag_imag) / modulus])


def apply_local(field, wavenum, spacing):
    padded = jnp.pad(field, ((0, 0), (1, 1), (1, 1), (0, 0)))
    return combine(field, beside_all(padded), wavenum, spacing)


def halves(padded, axis):
    length = padded.shape[axis] - 2
    parts = [lax.slice_in_dim(padded, start, start + length - 1, 2, axis) for start in range(4)]
    return (parts[0] + 3.0 * parts[1] + 3.0 * parts[2] + parts[3]) / 8.0


def restrict_padded(padded):
    padded = jnp.pad(padded, ((0, 0), (0, 0), (0, 0), (1, 1)))
    return halves(halves(halves(padded, 1), 2), 3)


def coarsen(wavenum):
    xsize, ysize, zsize = wavenum.shape
    return wavenum.reshape(xsize // 2, 2, ysize // 2, 2, zsize // 2, 2).mean(axis=(1, 3, 5))


def reference(source, wavenumber_sq):
    rhs_level = source
    wavenum = wavenumber_sq
    results = []
    for level_index in range(LEVELS):
        spacing = 4.0 ** level_index
        field = DAMPING * divide(rhs_level, wavenum, spacing)
        field = field + DAMPING * divide(rhs_level - apply_local(field, wavenum, spacing), wavenum, spacing)
        residual = rhs_level - apply_local(field, wavenum, spacing)
        results.append(field)
        rhs_level = restrict_padded(jnp.pad(residual, ((0, 0), (1, 1), (1, 1), (0, 0))))
        wavenum = coarsen(wavenum)
    spacing = 4.0 ** LEVELS
    field = DAMPING * divide(rhs_level, wavenum, spacing)
    for sweep_index in range(COARSE_SWEEPS - 1):
        field = field + DAMPING * divide(rhs_level - apply_local(field, wavenum, spacing), wavenum, spacing)
    return results[0], results[1], results[2], field
```

```python
import functools
import jax
import jax.numpy as jnp
import numpy as np
from jax import lax
from jax.experimental import pallas as pl
from jax.experimental.pallas import tpu as pltpu
from jax.sharding import PartitionSpec as P

DAMPING = 0.8
SHIFT_IMAG = 0.5
VMEM = pl.BlockSpec(memory_space=pltpu.VMEM)
SMEM = pl.BlockSpec(memory_space=pltpu.SMEM)


def params():
    return pltpu.CompilerParams(vmem_limit_bytes=40 * 1024 * 1024)


def around(ref, k, x, full_lanes):
    mid = ref[k, x]
    rows, lanes = mid.shape
    up = pltpu.roll(mid, 1, 1)
    down = pltpu.roll(mid, lanes - 1, 1)
    if full_lanes:
        lane = lax.broadcasted_iota(jnp.int32, mid.shape, 1)
        up = jnp.where(lane == 0, 0.0, up)
        down = jnp.where(lane == lanes - 1, 0.0, down)
    sides = pltpu.roll(mid, 1, 0) + pltpu.roll(mid, rows - 1, 0)
    return (ref[k, x - 1] + ref[k, x + 1]) + sides + (up + down)


def inside(shape, x, x0, xsize, y0, ysize, zsize):
    row = lax.broadcasted_iota(jnp.int32, shape, 0) + y0
    ok = (row >= 0) & (row < ysize)
    if zsize < shape[1]:
        ok = ok & (lax.broadcasted_iota(jnp.int32, shape, 1) < zsize)
    gx = x + x0
    return ok & ((gx >= 0) & (gx < xsize))


def first_pass(f, c, ga, gb, u, scale, count, where):
    def step(x, carry):
        cc = c(x)
        a = 6.0 / scale - cc
        b = SHIFT_IMAG * cc
        g = jnp.where(where(x, cc.shape), DAMPING / (a * a + b * b), 0.0)
        a = g * a
        b = g * b
        re, im = f(0, x), f(1, x)
        ga[x] = a
        gb[x] = b
        u[0, x] = re * a + im * b
        u[1, x] = im * a - re * b
        return carry

    lax.fori_loop(0, count, step, 0)


def turned(ga, gb, x, s_re, s_im, scale):
    a, b = ga[x], gb[x]
    if scale != 1.0:
        a, b = a * (1.0 / scale), b * (1.0 / scale)
    return s_re * a + s_im * b, s_im * a - s_re * b


def smooth(f, ga, gb, u, e, r, scale, count, full_lanes, where, put):
    def second(x, carry):
        d_re, d_im = turned(ga, gb, x, around(u, 0, x, full_lanes), around(u, 1, x, full_lanes), scale)
        for k, d in ((0, d_re), (1, d_im)):
            first = u[k, x]
            e[k, x] = 0.4 * first + d
            put(k, x, 1.2 * first + d)
        return carry

    lax.fori_loop(1, count - 1, second, 0)

    def third(x, carry):
        for k in (0, 1):
            s = around(e, k, x, full_lanes)
            val = 0.04 * f(k, x) + (s if scale == 1.0 else s * (1.0 / scale))
            r[k, x] = jnp.where(where(x, val.shape), val, 0.0)
        return carry

    lax.fori_loop(2, count - 2, third, 0)


def restrict_xy(r, c, t, out, planes, rows, plane0, row0):
    halves = t.shape[1]

    def step(i, carry):
        p = plane0 + 2 * i
        for k in range(3):
            if k < 2:
                val = (r[k, p] + r[k, p + 3]) + 3.0 * (r[k, p + 1] + r[k, p + 2])
            else:
                val = c(p + 1) + c(p + 2)
            for half in range(halves):
                lanes = slice(128 * half, 128 * half + 128)
                t[k, half] = val[:, lanes]
                part = [t[k, half, pl.ds(row0 + j, rows, 2), :] for j in range(4)]
                inner = part[1] + part[2]
                out[k, i, pl.ds(0, rows), lanes] = inner if k == 2 else (part[0] + part[3]) + 3.0 * inner
        return carry

    lax.fori_loop(0, planes, step, 0)


def weights(zsize, lanes_in, lanes_out):
    full = np.zeros((lanes_in, lanes_out), np.float32)
    mean = np.zeros((lanes_in, lanes_out), np.float32)
    for i in range(zsize // 2):
        for j, w in enumerate((1.0, 3.0, 3.0, 1.0)):
            z = 2 * i - 1 + j
            if 0 <= z < zsize:
                full[z, i] = w / 512.0
        mean[2 * i, i] = mean[2 * i + 1, i] = 0.125
    return jnp.asarray(full, jnp.bfloat16), jnp.asarray(mean, jnp.bfloat16)


def exact_dot(x, w):
    hi = x.astype(jnp.bfloat16)
    rest = x - hi.astype(jnp.float32)
    mid = rest.astype(jnp.bfloat16)
    low = (rest - mid.astype(jnp.float32)).astype(jnp.bfloat16)
    dot = functools.partial(jnp.dot, preferred_element_type=jnp.float32)
    return dot(hi, w) + (dot(mid, w) + dot(low, w))


def restrict_z(t, w_full, w_mean, k):
    planes, rows, lanes = t.shape[1:]
    flat = t[k].reshape(planes * rows, lanes)
    w = w_mean[...] if k == 2 else w_full[...]
    return exact_dot(flat, w).reshape(planes, rows, w.shape[1])


def pack_kernel(h, f_lo, f_hi, c_lo, c_hi, lo, hi):
    for k in range(3):
        for j in range(h):
            lo[k, j] = f_lo[k, :, j, :] if k < 2 else c_lo[:, j, :]
            hi[k, j] = f_hi[k, :, 8 - h + j, :] if k < 2 else c_hi[:, 8 - h + j, :]


def fine_kernel(h, xsize, ysize, place, f_own, c_own, xlo, xhi, ylo, yhi, w_full, w_mean, u_out, fc_out, fc, ga, gb, u, e, t, part):
    n, rows, lanes = c_own.shape
    count = n + 2 * h
    for k in range(3):
        fc[k, pl.ds(h, n), pl.ds(8, rows), :] = f_own[k] if k < 2 else c_own[...]
        for base, side in ((0, xlo), (n + h, xhi)):
            fc[k, pl.ds(base, h), pl.ds(8, rows), :] = side[k, :, pl.ds(0, rows), :]
            fc[k, pl.ds(base, h), pl.ds(8 - h, h), :] = side[k, :, pl.ds(rows, h), :]
            fc[k, pl.ds(base, h), pl.ds(8 + rows, h), :] = side[k, :, pl.ds(rows + h, h), :]
        for j in range(h):
            fc[k, pl.ds(h, n), 8 - h + j, :] = ylo[k, j]
            fc[k, pl.ds(h, n), 8 + rows + j, :] = yhi[k, j]
    x0, y0 = place[0] * n - h, place[1] * rows - 8

    def where(x, shape):
        return inside(shape, x, x0, xsize, y0, ysize, lanes)

    def put(k, x, val):
        @pl.when((x >= h) & (x < n + h))
        def _():
            u_out[k, x - h] = val[8 : 8 + rows]

    f = lambda k, x: fc[k, x]
    c = lambda x: fc[2, x]
    first_pass(f, c, ga, gb, u, 1.0, count, where)
    smooth(f, ga, gb, u, e, u, 1.0, count, True, where, put)
    restrict_xy(u, c, t, part, n // 2, rows // 2, h - 1, 7)
    for k in range(3):
        fc_out[k] = restrict_z(part, w_full, w_mean, k)


def middle_kernel(h, over, xsize, ysize, place, fc_own, xlo, xhi, ylo, yhi, w_full, w_mean, u_out, fc_out, fc, ga, gb, u, e, t, part):
    n, rows, lanes = fc_own.shape[1:]
    count = n + 2 * h
    for k in range(3):
        fc[k, pl.ds(h, n), pl.ds(8, rows), :] = fc_own[k]
        fc[k, pl.ds(0, h), pl.ds(8, rows), :] = xlo[k]
        fc[k, pl.ds(n + h, h), pl.ds(8, rows), :] = xhi[k]
        fc[k, :, pl.ds(0, 8), :] = ylo[k]
        fc[k, :, pl.ds(8 + rows, 8), :] = yhi[k]
    x0, y0 = place[0] * n - h, place[1] * rows - 8

    def where(x, shape):
        return inside(shape, x, x0, xsize, y0, ysize, lanes)

    def put(k, x, val):
        @pl.when((x >= h) & (x < n + h))
        def _():
            u_out[k, x - h] = val[8 : 8 + rows]

    f = lambda k, x: fc[k, x]
    c = lambda x: fc[2, x]
    first_pass(f, c, ga, gb, u, 4.0, count, where)
    smooth(f, ga, gb, u, e, u, 4.0, count, True, where, put)
    planes, width = n // 2 + 2 * over, rows // 2 + 2 * over
    restrict_xy(u, c, t, part, planes, width, h - 1 - 2 * over, 7 - 2 * over)
    for k in range(3):
        fc_out[k] = restrict_z(part, w_full, w_mean, k)[:, :width]


def coarse_kernel(n, sweeps, xsize, ysize, zsize, place, fc_own, xlo, xhi, ylo, yhi, w_full, w_mean, u_out, v_out, fc, ga, gb, u, e, t, part, fd, gc, gd, v, w):
    lanes = fc_own.shape[3]
    count = n + 18
    for k in range(3):
        fc[k, pl.ds(8, n + 2), pl.ds(8, n + 2), :] = fc_own[k]
        fc[k, pl.ds(0, 8), pl.ds(8, n + 2), :] = xlo[k]
        fc[k, pl.ds(n + 10, 8), pl.ds(8, n + 2), :] = xhi[k]
        fc[k, :, pl.ds(0, 8), :] = ylo[k]
        fc[k, :, pl.ds(n + 10, 8), :] = yhi[k]
    x0, y0 = place[0] * n - 9, place[1] * n - 9

    def where(x, shape):
        return inside(shape, x, x0, xsize, y0, ysize, zsize)

    def put(k, x, val):
        @pl.when((x >= 9) & (x < n + 9))
        def _():
            u_out[k, x - 9] = val[9 : 9 + n, :zsize]

    f = lambda k, x: fc[k, x]
    c = lambda x: fc[2, x]
    first_pass(f, c, ga, gb, u, 16.0, count, where)
    smooth(f, ga, gb, u, e, u, 16.0, count, False, where, put)
    m = n // 2
    width = m + 6
    restrict_xy(u, c, t, part, width, width, 2, 2)
    for k in range(3):
        fd[k] = restrict_z(part, w_full, w_mean, k)
    x1, y1 = place[0] * m - 3, place[1] * m - 3

    def where_c(x, shape):
        return inside(shape, x, x1, xsize // 2, y1, ysize // 2, zsize // 2)

    first_pass(lambda k, x: fd[k, x], lambda x: fd[2, x], gc, gd, v, 64.0, width, where_c)
    old, new = v, w
    for sweep in range(sweeps - 1):
        for x in range(1 + sweep, width - 1 - sweep):
            d = turned(gc, gd, x, around(old, 0, x, False), around(old, 1, x, False), 64.0)
            for k in (0, 1):
                val = (v[k, x] if sweep == 0 else 0.2 * old[k, x] + v[k, x]) + d[k]
                if sweep == 0:
                    val = 0.2 * v[k, x] + val
                if sweep == sweeps - 2:
                    v_out[k, x - 3] = val[3 : 3 + m, : zsize // 2]
                else:
                    new[sweep % 2, k, x] = val
        old = _Half(w, sweep % 2)


class _Half:
    def __init__(self, ref, half):
        self.ref, self.half = ref, half

    def __getitem__(self, index):
        return self.ref[(self.half,) + tuple(index)]


def body(source, wavenumber_sq):
    f32 = jnp.float32
    xdev, ydev = lax.axis_size("gx"), lax.axis_size("gy")
    place = jnp.stack([lax.axis_index("gx"), lax.axis_index("gy")]).astype(jnp.int32)

    def swap(axis, devices, first, last):
        before = lax.ppermute(last, axis, [(i, (i + 1) % devices) for i in range(devices)])
        after = lax.ppermute(first, axis, [((i + 1) % devices, i) for i in range(devices)])
        return before, after

    _, n, rows, lanes = source.shape
    xsize, ysize = n * xdev, rows * ydev
    S = lambda *shape: jax.ShapeDtypeStruct(shape, f32)
    V = lambda *shape: pltpu.VMEM(shape, f32)

    h = 3
    fblock = lambda j: pl.BlockSpec((2, n, 8, lanes), lambda i, j=j: (0, 0, j, 0))
    cblock = lambda j: pl.BlockSpec((n, 8, lanes), lambda i, j=j: (0, j, 0))
    last = rows // 8 - 1
    side = pl.BlockSpec((3, h, n, lanes), lambda i: (0, 0, 0, 0))
    first_rows, last_rows = pl.pallas_call(
        functools.partial(pack_kernel, h),
        grid=(1,),
        in_specs=[fblock(0), fblock(last), cblock(0), cblock(last)],
        out_specs=[side, side],
        out_shape=[S(3, h, n, lanes)] * 2,
        compiler_params=params(),
        name="pack_rows",
    )(source, source, wavenumber_sq, wavenumber_sq)
    ylo, yhi = swap("gy", ydev, first_rows, last_rows)

    def planes(start):
        own = jnp.concatenate([source[:, start : start + h], wavenumber_sq[None, start : start + h]], 0)
        lo = ylo[:, :, start : start + h].transpose(0, 2, 1, 3)
        hi = yhi[:, :, start : start + h].transpose(0, 2, 1, 3)
        return jnp.concatenate([own, lo, hi, jnp.zeros((3, h, 8 - 2 * h, lanes), f32)], 2)

    xlo, xhi = swap("gx", xdev, planes(0), planes(n - h))
    zsize = lanes
    w_full, w_mean = weights(zsize, lanes, lanes // 2)
    full = (n + 2 * h, rows + 16, lanes)
    fine, fc = pl.pallas_call(
        functools.partial(fine_kernel, h, xsize, ysize),
        in_specs=[SMEM] + [VMEM] * 8,
        out_specs=[VMEM] * 2,
        out_shape=[S(2, n, rows, lanes), S(3, n // 2, rows // 2, lanes // 2)],
        scratch_shapes=[V(3, *full), V(*full), V(*full), V(2, *full), V(2, *full), V(3, lanes // 128, full[1], 128), V(3, n // 2, rows // 2, lanes)],
        compiler_params=params(),
        name="fine_level",
    )(place, source, wavenumber_sq, xlo, xhi, ylo, yhi, w_full, w_mean)

    n, rows, lanes, xsize, ysize, zsize = n // 2, rows // 2, lanes // 2, xsize // 2, ysize // 2, zsize // 2
    h, over = 5, 1
    xlo, xhi = swap("gx", xdev, fc[:, :h], fc[:, n - h :])
    first_rows, last_rows = [jnp.concatenate([a[:, :, s : s + 8] for a in (xlo, fc, xhi)], 1) for s in (0, rows - 8)]
    ylo, yhi = swap("gy", ydev, first_rows, last_rows)
    w_full, w_mean = weights(zsize, lanes, lanes)
    full = (n + 2 * h, rows + 16, lanes)
    width = n // 2 + 2 * over
    second, fc = pl.pallas_call(
        functools.partial(middle_kernel, h, over, xsize, ysize),
        in_specs=[SMEM] + [VMEM] * 7,
        out_specs=[VMEM] * 2,
        out_shape=[S(2, n, rows, lanes), S(3, width, width, lanes)],
        scratch_shapes=[V(3, *full), V(*full), V(*full), V(2, *full), V(2, *full), V(3, lanes // 128, full[1], 128), V(3, width, 16, lanes)],
        compiler_params=params(),
        name="second_level",
    )(place, fc, xlo, xhi, ylo, yhi, w_full, w_mean)

    n, xsize, ysize, zsize = n // 2, xsize // 2, ysize // 2, zsize // 2
    xlo, xhi = swap("gx", xdev, fc[:, 2:], fc[:, :n])
    first_rows, last_rows = [jnp.concatenate([a[:, :, s : s + 8] for a in (xlo, fc, xhi)], 1) for s in (2, 0)]
    ylo, yhi = swap("gy", ydev, first_rows, last_rows)
    w_full, w_mean = weights(zsize, lanes, lanes)
    full = (n + 18, 32, lanes)
    m = n // 2
    small = (m + 6, 16, lanes)
    third, coarse = pl.pallas_call(
        functools.partial(coarse_kernel, n, 4, xsize, ysize, zsize),
        in_specs=[SMEM] + [VMEM] * 7,
        out_specs=[VMEM] * 2,
        out_shape=[S(2, n, n, zsize), S(2, m, m, zsize // 2)],
        scratch_shapes=[V(3, *full), V(*full), V(*full), V(2, *full), V(2, *full), V(3, lanes // 128, full[1], 128), V(3, *small)]
        + [V(3, *small), V(*small), V(*small), V(2, *small), V(2, 2, *small)],
        compiler_params=params(),
        name="coarse_levels",
    )(place, fc, xlo, xhi, ylo, yhi, w_full, w_mean)
    return fine, second, third, coarse


def solution(mesh):
    placed = (P(None, "gx", "gy", None), P("gx", "gy", None))
    return jax.shard_map(body, mesh=mesh, in_specs=placed, out_specs=(P(None, "gx", "gy", None),) * 4, check_vma=False)
```

```python
import functools
import jax
import jax.numpy as jnp
import numpy as np
from jax import lax
from jax.experimental import pallas as pl
from jax.experimental.pallas import tpu as pltpu
from jax.sharding import PartitionSpec as P

DAMPING = 0.8
SHIFT_IMAG = 0.5
LANES = 128
VMEM = pl.BlockSpec(memory_space=pltpu.VMEM)
SMEM = pl.BlockSpec(memory_space=pltpu.SMEM)


def params(mib):
    return pltpu.CompilerParams(vmem_limit_bytes=mib * 1024 * 1024)


def around(ref, k, x, row, rows, full):
    halves = ref.shape[2]
    mid = [ref[k, x, h, pl.ds(row, rows), :] for h in range(halves)]
    up = [pltpu.roll(m, 1, 1) for m in mid]
    down = [pltpu.roll(m, LANES - 1, 1) for m in mid]
    if full:
        lane = lax.broadcasted_iota(jnp.int32, mid[0].shape, 1)
        first, last = lane == 0, lane == LANES - 1
        up = [jnp.where(first, up[h - 1] if h else 0.0, up[h]) for h in range(halves)]
        down = [jnp.where(last, down[h + 1] if h < halves - 1 else 0.0, down[h]) for h in range(halves)]
    sums = []
    for h in range(halves):
        planes = ref[k, x - 1, h, pl.ds(row, rows), :] + ref[k, x + 1, h, pl.ds(row, rows), :]
        sides = ref[k, x, h, pl.ds(row - 1, rows), :] + ref[k, x, h, pl.ds(row + 1, rows), :]
        sums.append((planes + sides) + (up[h] + down[h]))
    return sums


def inverse(c, scale, ok):
    a = 6.0 / scale - c
    b = SHIFT_IMAG * c
    g = DAMPING / (a * a + b * b)
    if ok is not None:
        g = jnp.where(ok, g, 0.0)
    return g * a, g * b


def divided(re, im, a, b):
    return re * a + im * b, im * a - re * b


def point(re, im, c, scale, ok, u, ga, gb, x, h, row):
    a, b = inverse(c, scale, ok)
    at = pl.ds(row, c.shape[0])
    ga[x, h, at, :], gb[x, h, at, :] = a, b
    u[0, x, h, at, :], u[1, x, h, at, :] = divided(re, im, a, b)


def second(u, ga, gb, e, x, row, rows, scale, full):
    s_re, s_im = around(u, 0, x, row, rows, full), around(u, 1, x, row, rows, full)
    at = pl.ds(row, rows)
    for h in range(u.shape[2]):
        a, b = ga[x, h, at, :], gb[x, h, at, :]
        if scale != 1.0:
            a, b = a * (1.0 / scale), b * (1.0 / scale)
        d = divided(s_re[h], s_im[h], a, b)
        for k in (0, 1):
            e[k, x, h, at, :] = 0.4 * u[k, x, h, at, :] + d[k]


def rows_inside(shape, y0, ysize):
    row = lax.broadcasted_iota(jnp.int32, shape, 0) + y0
    return (row >= 0) & (row < ysize)


def restrict_xy(r, t, out, i, plane, row, rows, k):
    for h in range(r.shape[2]):
        val = (r[k, plane, h] + r[k, plane + 3, h]) + 3.0 * (r[k, plane + 1, h] + r[k, plane + 2, h])
        t[k, h] = val
        part = [t[k, h, pl.ds(row + j, rows, 2), :] for j in range(4)]
        out[k, i, pl.ds(0, rows), pl.ds(LANES * h, LANES)] = (part[0] + part[3]) + 3.0 * (part[1] + part[2])


def add_pairs(c0, c1, t, h, out, i, row, rows):
    t[0, h, pl.ds(0, c0.shape[0]), :] = c0 + c1
    val = t[0, h, pl.ds(row, rows, 2), :] + t[0, h, pl.ds(row + 1, rows, 2), :]
    out[i, pl.ds(0, rows), pl.ds(LANES * h, LANES)] = val


def weights(zsize, lanes_in, lanes_out):
    full = np.zeros((lanes_in, lanes_out), np.float32)
    mean = np.zeros((lanes_in, lanes_out), np.float32)
    for i in range(zsize // 2):
        for j, w in enumerate((1.0, 3.0, 3.0, 1.0)):
            z = 2 * i - 1 + j
            if 0 <= z < zsize:
                full[z, i] = w / 512.0
        mean[2 * i, i] = mean[2 * i + 1, i] = 0.125
    return jnp.asarray(full, jnp.bfloat16), jnp.asarray(mean, jnp.bfloat16)


def exact_dot(part, w):
    planes, rows, lanes = part.shape
    x = part.reshape(planes * rows, lanes)
    hi = x.astype(jnp.bfloat16)
    rest = x - hi.astype(jnp.float32)
    mid = rest.astype(jnp.bfloat16)
    low = (rest - mid.astype(jnp.float32)).astype(jnp.bfloat16)
    dot = functools.partial(jnp.dot, preferred_element_type=jnp.float32)
    return (dot(hi, w) + (dot(mid, w) + dot(low, w))).reshape(planes, rows, w.shape[1])


PX, PY = 3, 8


def inner_kernel(f, c, w_mean, u, e, r, ga, gb, c_out, t, part):
    n, rows, lanes = c.shape
    halves = lanes // LANES
    at = pl.ds(PY, rows)
    cut = [pl.ds(LANES * h, LANES) for h in range(halves)]

    def first(x, carry):
        for h in range(halves):
            point(f[0, x, :, cut[h]], f[1, x, :, cut[h]], c[x, :, cut[h]], 1.0, None, u, ga, gb, x + PX, h, PY)
        return carry

    lax.fori_loop(0, n, first, 0, unroll=2)

    def middle(x, carry):
        second(u, ga, gb, e, x + PX, PY, rows, 1.0, True)
        return carry

    lax.fori_loop(1, n - 1, middle, 0, unroll=2)
    row = lax.broadcasted_iota(jnp.int32, (rows, LANES), 0)
    full = (row >= 2) & (row < rows - 2)

    def last(x, carry):
        for k in (0, 1):
            s = around(e, k, x + PX, PY, rows, True)
            for h in range(halves):
                r[k, x + PX, h, at, :] = 0.04 * f[k, x, :, cut[h]] + jnp.where(full, s[h], 0.0)
        return carry

    lax.fori_loop(2, n - 2, last, 0, unroll=2)
    for x in (0, 1, n - 2, n - 1):
        for k in (0, 1):
            for h in range(halves):
                r[k, x + PX, h, at, :] = 0.04 * f[k, x, :, cut[h]]

    def pairs(i, carry):
        for h in range(halves):
            add_pairs(c[2 * i, :, cut[h]], c[2 * i + 1, :, cut[h]], t, h, part, i, 0, rows // 2)
        return carry

    lax.fori_loop(0, n // 2, pairs, 0, unroll=2)
    c_out[...] = exact_dot(part[...], w_mean[...])


def outer_kernel(xsize, ysize, place, u_in, e_in, r_in, ga_in, gb_in, xlo, xhi, ylo, yhi, clo, chi, c_own, w_full, u, e, r, ga, gb, fc_out, t, part):
    n, rows, lanes = ylo.shape[1], xlo.shape[2], xlo.shape[3]
    halves = lanes // LANES
    cut = [pl.ds(LANES * h, LANES) for h in range(halves)]
    x0, y0 = place[0] * n - PX, place[1] * rows - PY
    del u_in, e_in, r_in, ga_in, gb_in

    def ok(x, row, count):
        gx = x + x0
        return rows_inside((count, LANES), y0 + row, ysize) & ((gx >= 0) & (gx < xsize))

    def halo(src, i, x, row):
        for h in range(halves):
            re, im, c = [src[k, i, :, cut[h]] for k in range(3)]
            good = ok(x, row, c.shape[0])
            point(re, im, c, 1.0, good, u, ga, gb, x, h, row)
            at = pl.ds(row, c.shape[0])
            for k, val in ((0, re), (1, im)):
                r[k, x, h, at, :] = jnp.where(good, 0.04 * val, 0.0)

    for i in range(PX):
        for side, x in ((xlo, i), (xhi, n + PX + i)):
            halo(side, i, x, PY)
            j = i if side is xlo else PX + i
            halo(clo, j, x, PY - 4)
            halo(chi, j, x, PY + rows)

    def strips(x, carry):
        halo(ylo, x, x + PX, PY - 4)
        halo(yhi, x, x + PX, PY + rows)
        return carry

    lax.fori_loop(0, n, strips, 0, unroll=2)
    low, high = PY - 4, PY + rows - 4

    for x in (PX - 2, PX - 1, PX, n + PX - 1, n + PX, n + PX + 1):
        second(u, ga, gb, e, x, low, rows + 8, 1.0, True)

    def middle(x, carry):
        for row in (low, high):
            second(u, ga, gb, e, x, row, 8, 1.0, True)
        return carry

    lax.fori_loop(PX + 1, n + PX - 1, middle, 0, unroll=2)

    def finish(x, row, count, good):
        for k in (0, 1):
            s = around(e, k, x, row, count, True)
            for h in range(halves):
                at = pl.ds(row, count)
                r[k, x, h, at, :] = r[k, x, h, at, :] + jnp.where(good, s[h], 0.0)

    for x in (PX - 1, PX, PX + 1, n + PX - 2, n + PX - 1, n + PX):
        finish(x, low, rows + 8, ok(x, low, rows + 8))
    row = lax.broadcasted_iota(jnp.int32, (8, LANES), 0)
    good_low = rows_inside((8, LANES), y0 + low, ysize) & (row < 6)
    good_high = rows_inside((8, LANES), y0 + high, ysize) & (row >= 2)

    def last(x, carry):
        finish(x, low, 8, good_low)
        finish(x, high, 8, good_high)
        return carry

    lax.fori_loop(PX + 2, n + PX - 2, last, 0, unroll=2)

    def coarse(i, carry):
        for k in (0, 1):
            restrict_xy(r, t, part, i, 2 * i + PX - 1, PY - 1, rows // 2, k)
        return carry

    lax.fori_loop(0, n // 2, coarse, 0, unroll=2)
    for k in (0, 1):
        fc_out[k] = exact_dot(part[k], w_full[...])
    fc_out[2] = c_own[...]


def iterate_kernel(u, e, out):
    n, rows = out.shape[1:3]
    at = pl.ds(PY, rows)

    def step(x, carry):
        for k in (0, 1):
            for h in range(u.shape[2]):
                out[k, x, :, pl.ds(LANES * h, LANES)] = e[k, x + PX, h, at, :] + 0.8 * u[k, x + PX, h, at, :]
        return carry

    lax.fori_loop(0, n, step, 0, unroll=2)


def whole_level(fc, u, e, r, ga, gb, planes, used, row, rows, scale, full, ok, u_put):
    first, count = used
    for x in range(planes):
        cells = [fc[k, x, 0, pl.ds(first, count), :] for k in range(3)]
        point(*cells, scale, ok(x, first, count), u, ga, gb, x, 0, first)
    at = pl.ds(row, rows)
    for x in range(1, planes - 1):
        second(u, ga, gb, e, x, row, rows, scale, full)
        u_put(x)
    for x in range(2, planes - 2):
        good = ok(x, row, rows)
        for k in (0, 1):
            s = around(e, k, x, row, rows, full)[0] * (1.0 / scale)
            r[k, x, 0, at, :] = jnp.where(good, 0.04 * fc[k, x, 0, at, :] + s, 0.0)


def middle_kernel(halo, over, xsize, ysize, place, fc_own, xlo, xhi, ylo, yhi, w_full, w_mean, u_out, fc_out, fc, ga, gb, u, e, r, t, part, part_c):
    n, rows = fc_own.shape[1:3]
    planes = n + 2 * halo
    for k in range(3):
        for src, x, count in ((xlo, 0, halo), (fc_own, halo, n), (xhi, n + halo, halo)):
            fc[k, pl.ds(x, count), 0, pl.ds(8, rows), :] = src[k]
        fc[k, :, 0, pl.ds(0, 8), :] = ylo[k]
        fc[k, :, 0, pl.ds(8 + rows, 8), :] = yhi[k]
    x0, y0 = place[0] * n - halo, place[1] * rows - 8

    def ok(x, row, count):
        gx = x + x0
        return rows_inside((count, LANES), y0 + row, ysize) & ((gx >= 0) & (gx < xsize))

    def u_put(x):
        if halo <= x < n + halo:
            at = pl.ds(8, rows)
            for k in (0, 1):
                u_out[k, x - halo] = e[k, x, 0, at, :] + 0.8 * u[k, x, 0, at, :]

    whole_level(fc, u, e, r, ga, gb, planes, (0, rows + 16), 4, rows + 8, 4.0, True, ok, u_put)
    width = n // 2 + 2 * over
    for i in range(width):
        x, row = 2 * i + halo - 1 - 2 * over, 7 - 2 * over
        for k in (0, 1):
            restrict_xy(r, t, part, i, x, row, width, k)
        add_pairs(fc[2, x + 1, 0], fc[2, x + 2, 0], t, 0, part_c, i, row + 1, width)
    for k in (0, 1):
        fc_out[k] = exact_dot(part[k], w_full[...])[:, :width]
    fc_out[2] = exact_dot(part_c[...], w_mean[...])[:, :width]


def coarse_kernel(n, sweeps, xsize, ysize, zsize, place, fc_own, xlo, xhi, ylo, yhi, w_full, w_mean, u_out, v_out, fc, ga, gb, u, e, r, t, part, part_c, gc, gd, v, w):
    m = n // 2
    for k in range(3):
        for src, x, count in ((xlo, 0, 8), (fc_own, 8, n + 2), (xhi, n + 10, 8)):
            fc[k, pl.ds(x, count), 0, pl.ds(15, n + 2), :] = src[k]
        fc[k, :, 0, pl.ds(7, 8), :] = ylo[k]
        fc[k, :, 0, pl.ds(n + 17, 8), :] = yhi[k]
    lane = lax.broadcasted_iota(jnp.int32, (1, LANES), 1)

    def inside(x0, y0, xs, ys, zs):
        def ok(x, row, count):
            gx = x + x0
            here = rows_inside((count, LANES), y0 + row, ys) & (lane < zs)
            return here & ((gx >= 0) & (gx < xs))

        return ok

    def u_put(x):
        if 9 <= x < n + 9:
            at = pl.ds(16, n)
            for k in (0, 1):
                u_out[k, x - 9] = (e[k, x, 0, at, :] + 0.8 * u[k, x, 0, at, :])[:, :zsize]

    ok = inside(place[0] * n - 9, place[1] * n - 16, xsize, ysize, zsize)
    whole_level(fc, u, e, r, ga, gb, n + 18, (7, n + 18), 8, n + 16, 16.0, False, ok, u_put)
    width = m + 6
    for i in range(width):
        for k in (0, 1):
            restrict_xy(r, t, part, i, 2 * i + 2, 9, width, k)
        add_pairs(fc[2, 2 * i + 3, 0], fc[2, 2 * i + 4, 0], t, 0, part_c, i, 10, width)
    f = [exact_dot(part[k], w_full[...]) for k in (0, 1)] + [exact_dot(part_c[...], w_mean[...])]
    ok = inside(place[0] * m - 3, place[1] * m - 3, xsize // 2, ysize // 2, zsize // 2)
    for x in range(width):
        point(f[0][x], f[1][x], f[2][x], 64.0, ok(x, 0, 16), v, gc, gd, x, 0, 0)
    old = v
    for sweep in range(1, sweeps):
        new = w.at[sweep % 2]
        for x in range(sweep, width - sweep):
            at = pl.ds(1, m + 4)
            s = [around(old, k, x, 1, m + 4, False)[0] for k in (0, 1)]
            d = divided(*s, gc[x, 0, at, :] * (1.0 / 64.0), gd[x, 0, at, :] * (1.0 / 64.0))
            for k in (0, 1):
                val = 0.2 * old[k, x, 0, at, :] + v[k, x, 0, at, :] + d[k]
                if sweep < sweeps - 1:
                    new[k, x, 0, at, :] = val
                else:
                    v_out[k, x - 3] = val[2 : 2 + m, : zsize // 2]
        old = new


def body(source, wavenumber_sq):
    f32 = jnp.float32
    xdev, ydev = lax.axis_size("gx"), lax.axis_size("gy")
    place = jnp.stack([lax.axis_index("gx"), lax.axis_index("gy")]).astype(jnp.int32)

    def swap(axis, devices, first, last):
        before = lax.ppermute(last, axis, [(i, (i + 1) % devices) for i in range(devices)])
        after = lax.ppermute(first, axis, [((i + 1) % devices, i) for i in range(devices)])
        return before, after

    _, n, rows, lanes = source.shape
    xsize, ysize = n * xdev, rows * ydev
    S = lambda *shape: jax.ShapeDtypeStruct(shape, f32)
    V = lambda *shape: pltpu.VMEM(shape, f32)

    def both(*cut):
        return jnp.concatenate([source[(slice(None),) + cut], wavenumber_sq[cut][None]], 0)

    whole = slice(None)
    xlo, xhi = swap("gx", xdev, both(slice(0, PX)), both(slice(n - PX, n)))
    ylo, yhi = swap("gy", ydev, both(whole, slice(0, 4)), both(whole, slice(rows - 4, rows)))
    corners = jnp.concatenate([xlo, xhi], 1)
    clo, chi = swap("gy", ydev, corners[:, :, :4], corners[:, :, rows - 4 :])
    halves = lanes // LANES
    w_full, w_mean = weights(lanes, lanes, lanes // 2)
    state = (n + 2 * PX, halves, rows + 2 * PY, LANES)
    part = (n // 2, rows // 2, lanes)
    u, e, r, ga, gb, c_next = pl.pallas_call(
        inner_kernel,
        in_specs=[VMEM] * 3,
        out_specs=[VMEM] * 6,
        out_shape=[S(2, *state)] * 3 + [S(*state)] * 2 + [S(n // 2, rows // 2, lanes // 2)],
        scratch_shapes=[V(1, halves, rows, LANES), V(*part)],
        compiler_params=params(24),
        cost_estimate=pl.CostEstimate(flops=100_000_000, bytes_accessed=16_000_000, transcendentals=0),
        name="inner_cells",
    )(source, wavenumber_sq, w_mean)
    u, e, _, _, _, fc = pl.pallas_call(
        functools.partial(outer_kernel, xsize, ysize),
        in_specs=[SMEM] + [VMEM] * 13,
        out_specs=[VMEM] * 6,
        out_shape=[S(2, *state)] * 3 + [S(*state)] * 2 + [S(3, n // 2, rows // 2, lanes // 2)],
        input_output_aliases={1: 0, 2: 1, 3: 2, 4: 3, 5: 4},
        scratch_shapes=[V(2, halves, rows + 2 * PY, LANES), V(2, *part)],
        compiler_params=params(24),
        name="outer_cells",
    )(place, u, e, r, ga, gb, xlo, xhi, ylo, yhi, clo, chi, c_next, w_full)
    fine = pl.pallas_call(
        iterate_kernel,
        in_specs=[VMEM] * 2,
        out_specs=VMEM,
        out_shape=S(2, n, rows, lanes),
        compiler_params=params(24),
        cost_estimate=pl.CostEstimate(flops=1_000_000, bytes_accessed=8_000_000, transcendentals=0),
        name="fine_iterate",
    )(u, e)

    n, rows, lanes, xsize, ysize, zsize = n // 2, rows // 2, lanes // 2, xsize // 2, ysize // 2, lanes // 2
    h, over = 5, 1
    xlo, xhi = swap("gx", xdev, fc[:, :h], fc[:, n - h :])
    first_rows, last_rows = [jnp.concatenate([a[:, :, s : s + 8] for a in (xlo, fc, xhi)], 1) for s in (0, rows - 8)]
    ylo, yhi = swap("gy", ydev, first_rows, last_rows)
    w_full, w_mean = weights(zsize, lanes, lanes)
    state = (n + 2 * h, 1, rows + 16, LANES)
    scratch = lambda s, width: [V(3, *s), V(*s), V(*s), V(2, *s), V(2, *s), V(2, *s), V(2, 1, *s[2:]), V(2, width, 16, LANES), V(width, 16, LANES)]
    width = n // 2 + 2 * over
    second_u, fc = pl.pallas_call(
        functools.partial(middle_kernel, h, over, xsize, ysize),
        in_specs=[SMEM] + [VMEM] * 7,
        out_specs=[VMEM] * 2,
        out_shape=[S(2, n, rows, lanes), S(3, width, width, lanes)],
        scratch_shapes=scratch(state, width),
        compiler_params=params(24),
        name="second_level",
    )(place, fc, xlo, xhi, ylo, yhi, w_full, w_mean)

    n, xsize, ysize, zsize = n // 2, xsize // 2, ysize // 2, zsize // 2
    xlo, xhi = swap("gx", xdev, fc[:, 2:], fc[:, :n])
    first_rows, last_rows = [jnp.concatenate([a[:, :, s : s + 8] for a in (xlo, fc, xhi)], 1) for s in (2, 0)]
    ylo, yhi = swap("gy", ydev, first_rows, last_rows)
    w_full, w_mean = weights(zsize, lanes, lanes)
    state = (n + 18, 1, 40, LANES)
    m = n // 2
    small = (m + 6, 1, 16, LANES)
    third, coarse = pl.pallas_call(
        functools.partial(coarse_kernel, n, 4, xsize, ysize, zsize),
        in_specs=[SMEM] + [VMEM] * 7,
        out_specs=[VMEM] * 2,
        out_shape=[S(2, n, n, zsize), S(2, m, m, zsize // 2)],
        scratch_shapes=scratch(state, m + 6) + [V(*small), V(*small), V(2, *small), V(2, 2, *small)],
        compiler_params=params(24),
        name="coarse_levels",
    )(place, fc, xlo, xhi, ylo, yhi, w_full, w_mean)
    return fine, second_u, third, coarse


def solution(mesh):
    placed = (P(None, "gx", "gy", None), P("gx", "gy", None))
    return jax.shard_map(body, mesh=mesh, in_specs=placed, out_specs=(P(None, "gx", "gy", None),) * 4, check_vma=False)
```

```python
import functools
import jax
import jax.numpy as jnp
import numpy as np
from jax import lax
from jax.experimental import pallas as pl
from jax.experimental.pallas import tpu as pltpu
from jax.sharding import PartitionSpec as P

DAMPING = 0.8
SHIFT_IMAG = 0.5
LANES = 128
VMEM = pl.BlockSpec(memory_space=pltpu.VMEM)
SMEM = pl.BlockSpec(memory_space=pltpu.SMEM)


def params(mib):
    return pltpu.CompilerParams(vmem_limit_bytes=mib * 1024 * 1024)


def around(ref, k, x, row, rows, full):
    halves = ref.shape[2]
    mid = [ref[k, x, h, pl.ds(row, rows), :] for h in range(halves)]
    up = [pltpu.roll(m, 1, 1) for m in mid]
    down = [pltpu.roll(m, LANES - 1, 1) for m in mid]
    if full:
        lane = lax.broadcasted_iota(jnp.int32, mid[0].shape, 1)
        first, last = lane == 0, lane == LANES - 1
        up = [jnp.where(first, up[h - 1] if h else 0.0, up[h]) for h in range(halves)]
        down = [jnp.where(last, down[h + 1] if h < halves - 1 else 0.0, down[h]) for h in range(halves)]
    sums = []
    for h in range(halves):
        planes = ref[k, x - 1, h, pl.ds(row, rows), :] + ref[k, x + 1, h, pl.ds(row, rows), :]
        sides = ref[k, x, h, pl.ds(row - 1, rows), :] + ref[k, x, h, pl.ds(row + 1, rows), :]
        sums.append((planes + sides) + (up[h] + down[h]))
    return sums


def inverse(c, scale, ok):
    a = 6.0 / scale - c
    b = SHIFT_IMAG * c
    g = DAMPING / (a * a + b * b)
    if ok is not None:
        g = jnp.where(ok, g, 0.0)
    return g * a, g * b


def divided(re, im, a, b):
    return re * a + im * b, im * a - re * b


def point(re, im, c, scale, ok, u, ga, gb, x, h, row):
    a, b = inverse(c, scale, ok)
    at = pl.ds(row, c.shape[0])
    ga[x, h, at, :], gb[x, h, at, :] = a, b
    u[0, x, h, at, :], u[1, x, h, at, :] = divided(re, im, a, b)


def second(u, ga, gb, e, x, row, rows, scale, full):
    s_re, s_im = around(u, 0, x, row, rows, full), around(u, 1, x, row, rows, full)
    at = pl.ds(row, rows)
    for h in range(u.shape[2]):
        a, b = ga[x, h, at, :], gb[x, h, at, :]
        if scale != 1.0:
            a, b = a * (1.0 / scale), b * (1.0 / scale)
        d = divided(s_re[h], s_im[h], a, b)
        for k in (0, 1):
            e[k, x, h, at, :] = 0.4 * u[k, x, h, at, :] + d[k]


def rows_inside(shape, y0, ysize):
    row = lax.broadcasted_iota(jnp.int32, shape, 0) + y0
    return (row >= 0) & (row < ysize)


def restrict_xy(r, t, out, to, plane, row, rows, k, window):
    at = pl.ds(*window)
    for h in range(r.shape[2]):
        val = (r[k, plane, h, at, :] + r[k, plane + 3, h, at, :]) + 3.0 * (r[k, plane + 1, h, at, :] + r[k, plane + 2, h, at, :])
        t[k, h, at, :] = val
        part = [t[k, h, pl.ds(row + j, rows, 2), :] for j in range(4)]
        out[k, to, pl.ds(0, rows), pl.ds(LANES * h, LANES)] = (part[0] + part[3]) + 3.0 * (part[1] + part[2])


def add_pairs(c0, c1, t, h, out, i, row, rows):
    t[0, h, pl.ds(0, c0.shape[0]), :] = c0 + c1
    val = t[0, h, pl.ds(row, rows, 2), :] + t[0, h, pl.ds(row + 1, rows, 2), :]
    out[i, pl.ds(0, rows), pl.ds(LANES * h, LANES)] = val


def weights(zsize, lanes_in, lanes_out):
    full = np.zeros((lanes_in, lanes_out), np.float32)
    mean = np.zeros((lanes_in, lanes_out), np.float32)
    for i in range(zsize // 2):
        for j, w in enumerate((1.0, 3.0, 3.0, 1.0)):
            z = 2 * i - 1 + j
            if 0 <= z < zsize:
                full[z, i] = w / 512.0
        mean[2 * i, i] = mean[2 * i + 1, i] = 0.125
    return jnp.asarray(full, jnp.bfloat16), jnp.asarray(mean, jnp.bfloat16)


def exact_dot(part, w):
    planes, rows, lanes = part.shape
    x = part.reshape(planes * rows, lanes)
    hi = x.astype(jnp.bfloat16)
    rest = x - hi.astype(jnp.float32)
    mid = rest.astype(jnp.bfloat16)
    low = (rest - mid.astype(jnp.float32)).astype(jnp.bfloat16)
    dot = functools.partial(jnp.dot, preferred_element_type=jnp.float32)
    return (dot(hi, w) + (dot(mid, w) + dot(low, w))).reshape(planes, rows, w.shape[1])


PX, PY = 3, 8


def pack_kernel(f, c, f_out, c_out, x_first, x_last, y_first, y_last, sems):
    n, rows, lanes = c_out.shape
    cuts = [(0, PX), (n - PX, PX)]
    step = (n - 2 * PX + 3) // 4
    inner = [(x, min(step, n - PX - x)) for x in range(PX, n - PX, step)]
    copies = []
    for x, count in cuts + inner:
        at = pl.ds(x, count)
        copies += [(f.at[0, at], f_out.at[0, at]), (f.at[1, at], f_out.at[1, at]), (c.at[at], c_out.at[at])]
    copies = [pltpu.make_async_copy(src, dst, sems.at[i]) for i, (src, dst) in enumerate(copies)]
    for copy in copies:
        copy.start()
    for copy in copies[:6]:
        copy.wait()
    for out, first, c_first in ((x_first, 0, 0), (x_last, n - PX, n - 2)):
        for j in range(PX):
            x = first + j
            a, b = inverse(c_out[x], 1.0, None)
            out[j], out[PX + j] = divided(f_out[0, x], f_out[1, x], a, b)
        for j in range(2):
            out[2 * PX + j] = c_out[c_first + j]
    for copy in copies[6:]:
        copy.wait()
    row = lax.broadcasted_iota(jnp.int32, (8, lanes), 0)

    def strip(x, carry):
        for out, start, shifts in ((y_first, 0, (0, 3, 6)), (y_last, rows - 8, (3, 6, 0))):
            at = pl.ds(start, 8)
            cc = c_out[x, at, :]
            a, b = inverse(cc, 1.0, None)
            re, im = divided(f_out[0, x, at, :], f_out[1, x, at, :], a, b)
            re, im, cc = [pltpu.roll(v, shift, 0) if shift else v for v, shift in zip((re, im, cc), shifts)]
            out[x] = jnp.where(row < 3, re, jnp.where(row < 6, im, cc))
        return carry

    lax.fori_loop(0, n, strip, 0, unroll=4)


def inner_kernel(f, c, w_full, w_mean, u, e, r, ga, gb, fc_out, t, part):
    n, rows, lanes = c.shape
    halves = lanes // LANES
    at = pl.ds(PY, rows)
    cut = [pl.ds(LANES * h, LANES) for h in range(halves)]

    def first(x, carry):
        for h in range(halves):
            point(f[0, x, :, cut[h]], f[1, x, :, cut[h]], c[x, :, cut[h]], 1.0, None, u, ga, gb, x + PX, h, PY)
        return carry

    lax.fori_loop(0, n, first, 0, unroll=2)

    def middle(x, carry):
        second(u, ga, gb, e, x + PX, PY, rows, 1.0, True)
        return carry

    lax.fori_loop(1, n - 1, middle, 0, unroll=2)
    row = lax.broadcasted_iota(jnp.int32, (rows, LANES), 0)
    full = (row >= 2) & (row < rows - 2)

    def last(x, carry):
        for k in (0, 1):
            s = around(e, k, x + PX, PY, rows, True)
            for h in range(halves):
                r[k, x + PX, h, at, :] = 0.04 * f[k, x, :, cut[h]] + jnp.where(full, s[h], 0.0)
        return carry

    lax.fori_loop(2, n - 2, last, 0, unroll=2)
    for x in (0, 1, n - 2, n - 1):
        for k in (0, 1):
            for h in range(halves):
                r[k, x + PX, h, at, :] = 0.04 * f[k, x, :, cut[h]]

    def pairs(i, carry):
        for h in range(halves):
            add_pairs(c[2 * i, :, cut[h]], c[2 * i + 1, :, cut[h]], t, h, part.at[2], i, 0, rows // 2)
        return carry

    lax.fori_loop(0, n // 2, pairs, 0, unroll=2)

    def coarse(i, carry):
        for k in (0, 1):
            restrict_xy(r, t, part, i, 2 * i + PX - 1, PY - 1, rows // 2, k, (PY, rows))
        return carry

    lax.fori_loop(2, n // 2 - 2, coarse, 0, unroll=2)
    for k in (0, 1):
        fc_out[k, 2 : n // 2 - 2] = exact_dot(part[k, 2 : n // 2 - 2], w_full[...])
    fc_out[2] = exact_dot(part[2], w_mean[...])


def inside(place, n, rows, xsize, ysize):
    x0, y0 = place[0] * n - PX, place[1] * rows - PY

    def ok(x, row, count):
        gx = x + x0
        return rows_inside((count, LANES), y0 + row, ysize) & ((gx >= 0) & (gx < xsize))

    return ok


def halo(re, im, cc, good, u, ga, gb, r, x, h, row, c_here, r_here):
    at = pl.ds(row, re.shape[0])
    re, im = jnp.where(good, re, 0.0), jnp.where(good, im, 0.0)
    u[0, x, h, at, :], u[1, x, h, at, :] = re, im
    if c_here:
        a, b = inverse(cc, 1.0, good)
        ga[x, h, at, :], gb[x, h, at, :] = a, b
    if r_here:
        a, b = 0.05 * (6.0 - cc), (0.05 * SHIFT_IMAG) * cc
        r[0, x, h, at, :], r[1, x, h, at, :] = re * a - im * b, im * a + re * b


def finish(e, r, x, row, count, good):
    for k in (0, 1):
        s = around(e, k, x, row, count, True)
        for h in range(e.shape[2]):
            at = pl.ds(row, count)
            r[k, x, h, at, :] = r[k, x, h, at, :] + jnp.where(good, s[h], 0.0)


def plane_cells(side, low, i, h):
    cut = pl.ds(LANES * h, LANES)
    j = i - 1 if low else i
    c_here = 0 <= j < 2
    cc = side[2 * PX + j, :, cut] if c_here else None
    return side[i, :, cut], side[PX + i, :, cut], cc, c_here, i == (PX - 1 if low else 0)


def faces_kernel(xsize, ysize, place, u_in, e_in, r_in, ga_in, gb_in, fc_in, xlo, xhi, ylo, yhi, w_full, u, e, r, ga, gb, fc_out, part, q):
    n, (rows, lanes) = ylo.shape[0], xlo.shape[1:]
    halves = lanes // LANES
    cut = [pl.ds(LANES * h, LANES) for h in range(halves)]
    ok = inside(place, n, rows, xsize, ysize)
    del u_in, e_in, r_in, ga_in, gb_in, fc_in
    for side, low, base in ((xlo, True, 0), (xhi, False, n + PX)):
        for i in range(PX):
            good = ok(base + i, PY, rows)
            for h in range(halves):
                re, im, cc, c_here, r_here = plane_cells(side, low, i, h)
                halo(re, im, cc, good, u, ga, gb, r, base + i, h, PY, c_here, r_here)
    low, high = PY - 4, PY + rows - 4
    good_lo, good_hi = ok(PX, 0, 8), ok(PX, PY + rows, 8)

    def strips(x, carry):
        for side, good, row, shifts in ((ylo, good_lo, 0, (5, 2, 0)), (yhi, good_hi, PY + rows, (0, 5, 2))):
            for h in range(halves):
                tile = side[x, :, cut[h]]
                re, im, cc = [pltpu.roll(tile, shift, 0) if shift else tile for shift in shifts]
                halo(re, im, cc, good, u, ga, gb, r, x + PX, h, row, True, True)
        return carry

    lax.fori_loop(0, n, strips, 0, unroll=4)
    for x in (PX - 2, PX - 1, PX, n + PX - 1, n + PX, n + PX + 1):
        second(u, ga, gb, e, x, PY, rows, 1.0, True)

    def middle(x, carry):
        for row in (low, high):
            second(u, ga, gb, e, x, row, 8, 1.0, True)
        return carry

    lax.fori_loop(PX + 1, n + PX - 1, middle, 0, unroll=3)
    for x in (PX - 1, PX, PX + 1, n + PX - 2, n + PX - 1, n + PX):
        finish(e, r, x, PY + 4, rows - 8, ok(x, PY + 4, rows - 8))
    row = lax.broadcasted_iota(jnp.int32, (8, LANES), 0)
    good_low, good_high = ok(PX, low, 8) & (row < 6), ok(PX, high, 8) & (row >= 2)

    def last(x, carry):
        finish(e, r, x, low, 8, good_low)
        finish(e, r, x, high, 8, good_high)
        return carry

    lax.fori_loop(PX + 2, n + PX - 2, last, 0, unroll=4)
    m = n // 2 - 4

    def coarse(i, carry):
        x = 2 * i + PX + 3
        for k in (0, 1):
            for h in range(halves):
                for j, row in ((0, PY - 1), (8, PY + rows - 7)):
                    at = pl.ds(row, 8)
                    part[k, i, pl.ds(j, 8), cut[h]] = (r[k, x, h, at, :] + r[k, x + 3, h, at, :]) + 3.0 * (
                        r[k, x + 1, h, at, :] + r[k, x + 2, h, at, :]
                    )
        return carry

    lax.fori_loop(0, m, coarse, 0, unroll=4)
    for k in (0, 1):
        q[k] = exact_dot(part[k], w_full[...])
        for row, start in ((0, 0), (rows // 2 - 2, 10)):
            four = [q[k, :, pl.ds(start + j, 2, 2), :] for j in range(4)]
            fc_out[k, pl.ds(2, m), pl.ds(row, 2), :] = (four[0] + four[3]) + 3.0 * (four[1] + four[2])


def corners_kernel(xsize, ysize, n, rows, place, u_in, e_in, r_in, ga_in, gb_in, fc_in, clo, chi, w_full, u, e, r, ga, gb, fc_out, t, part):
    halves = clo.shape[2] // LANES
    ok = inside(place, n, rows, xsize, ysize)
    del u_in, e_in, r_in, ga_in, gb_in, fc_in
    low, high = PY - 4, PY + rows - 4
    for side, row in ((clo, PY - 4), (chi, PY + rows)):
        for planes, is_low, base in ((side.at[pl.ds(0, 8)], True, 0), (side.at[pl.ds(8, 8)], False, n + PX)):
            for i in range(PX):
                good = ok(base + i, row, 4)
                for h in range(halves):
                    re, im, cc, c_here, r_here = plane_cells(planes, is_low, i, h)
                    halo(re, im, cc, good, u, ga, gb, r, base + i, h, row, c_here, r_here)
    for x in (PX - 2, PX - 1, PX, n + PX - 1, n + PX, n + PX + 1):
        for row in (low, high):
            second(u, ga, gb, e, x, row, 8, 1.0, True)
    for x in (PX - 1, PX, PX + 1, n + PX - 2, n + PX - 1, n + PX):
        for row in (low, high):
            finish(e, r, x, row, 8, ok(x, row, 8))
    planes = (0, 1, n // 2 - 2, n // 2 - 1)
    for k in (0, 1):
        for j, i in enumerate(planes):
            restrict_xy(r, t, part, j, 2 * i + PX - 1, PY - 1, rows // 2, k, (low, rows + 8))
        val = exact_dot(part[k], w_full[...])
        for j, i in enumerate(planes):
            fc_out[k, i] = val[j]


def iterate_kernel(u, e, out):
    n, rows = out.shape[1:3]
    at = pl.ds(PY, rows)

    def step(x, carry):
        for k in (0, 1):
            for h in range(u.shape[2]):
                out[k, x, :, pl.ds(LANES * h, LANES)] = e[k, x + PX, h, at, :] + 0.8 * u[k, x + PX, h, at, :]
        return carry

    lax.fori_loop(0, n, step, 0, unroll=2)


def whole_level(cells, u, e, r, ga, gb, planes, used, row, rows, scale, full, ok, u_put):
    first, count = used
    for x in range(planes):
        at = pl.ds(first, count)
        point(cells(0, x, at), cells(1, x, at), cells(2, x, at), scale, ok(x, first, count), u, ga, gb, x, 0, first)
    at = pl.ds(row, rows)
    for x in range(1, planes - 1):
        second(u, ga, gb, e, x, row, rows, scale, full)
        u_put(x)
    for x in range(2, planes - 2):
        good = ok(x, row, rows)
        for k in (0, 1):
            s = around(e, k, x, row, rows, full)[0] * (1.0 / scale)
            r[k, x, 0, at, :] = jnp.where(good, 0.04 * cells(k, x, at) + s, 0.0)


def rows_kernel(xlo, fc, xhi, first, last):
    halo, n, rows = xlo.shape[1], fc.shape[1], fc.shape[2]
    row = lax.broadcasted_iota(jnp.int32, (8, LANES), 0)
    for src, base, count in ((xlo, 0, halo), (fc, halo, n), (xhi, n + halo, halo)):
        for i in range(count):
            for out, start, own in ((first, 0, row < 5), (last, rows - 8, row >= 3)):
                re, im, cc = [src[k, i, pl.ds(start, 8), :] for k in range(3)]
                out[0, base + i] = jnp.where(own, re, pltpu.roll(cc, 5, 0))
                out[1, base + i] = jnp.where(own, im, pltpu.roll(cc, 2, 0))


def middle_kernel(halo, over, xsize, ysize, place, fc_own, xlo, xhi, ylo, yhi, w_full, w_mean, u_out, fc_out, fc, ga, gb, u, e, r, t, part, part_c):
    n, rows = fc_own.shape[1:3]
    planes = n + 2 * halo
    for k in range(3):
        for src, x, count in ((xlo, 0, halo), (fc_own, halo, n), (xhi, n + halo, halo)):
            fc[k, pl.ds(x, count), 0, pl.ds(8, rows), :] = src[k]
    row = lax.broadcasted_iota(jnp.int32, (8, LANES), 0)
    for side, start, split in ((ylo, 0, 6), (yhi, 8 + rows, 3)):
        at = pl.ds(start, 8)
        for x in range(planes):
            one, two = side[0, x], side[1, x]
            fc[0, x, 0, at, :], fc[1, x, 0, at, :] = one, two
            fc[2, x, 0, at, :] = jnp.where(row < split, pltpu.roll(one, 3, 0), pltpu.roll(two, 6, 0))
    x0, y0 = place[0] * n - halo, place[1] * rows - 8

    def ok(x, row, count):
        gx = x + x0
        return rows_inside((count, LANES), y0 + row, ysize) & ((gx >= 0) & (gx < xsize))

    def u_put(x):
        if halo <= x < n + halo:
            at = pl.ds(8, rows)
            for k in (0, 1):
                u_out[k, x - halo] = e[k, x, 0, at, :] + 0.8 * u[k, x, 0, at, :]

    def cells(k, x, at):
        return fc[k, x, 0, at, :]

    whole_level(cells, u, e, r, ga, gb, planes, (0, rows + 16), 4, rows + 8, 4.0, True, ok, u_put)
    width = n // 2 + 2 * over
    pairs = width // 2
    for i in range(width):
        x, row = 2 * i + halo - 1 - 2 * over, 7 - 2 * over
        for k in (0, 1):
            restrict_xy(r, t, part, i, x, row, width, k, (4, rows + 8))
        add_pairs(fc[2, x + 1, 0], fc[2, x + 2, 0], t, 0, part_c.at[i % 2], i // 2, row + 1, width)
    fc_out[pl.ds(0, width)] = (exact_dot(part[0], w_full[0]) + exact_dot(part[1], w_full[1]))[:, :width]
    fc_out[pl.ds(width, pairs)] = (exact_dot(part_c[0], w_mean[0]) + exact_dot(part_c[1], w_mean[1]))[:, :width]


def coarse_kernel(n, sweeps, xsize, ysize, zsize, place, fc_own, xlo, xhi, ylo, yhi, w_full, w_mean, u_out, v_out, fc, ga, gb, u, e, r, t, part, part_c, gc, gd, v, w):
    m = n // 2
    planes = n + 18
    for src, x, first, count in ((xlo, 0, 0, 8), (fc_own, 8, 0, n + 2), (xhi, n + 10, 0, 8), (xlo, planes, 8, 4), (fc_own, planes + 4, n + 2, m + 1), (xhi, planes + m + 5, 8, 4)):
        fc[pl.ds(x, count), 0, pl.ds(15, n + 2), :] = src[pl.ds(first, count)]
    fc[:, 0, pl.ds(7, 8), :] = ylo[...]
    fc[:, 0, pl.ds(n + 17, 8), :] = yhi[...]
    lane = lax.broadcasted_iota(jnp.int32, (1, LANES), 1)

    def cells(k, x, at):
        val = fc[planes + x // 2 if k == 2 else x, 0, at, :]
        return pltpu.roll(val, LANES - zsize, 1) if k == 1 or (k == 2 and x % 2) else val

    def inside(x0, y0, xs, ys, zs):
        def ok(x, row, count):
            gx = x + x0
            here = rows_inside((count, LANES), y0 + row, ys) & (lane < zs)
            return here & ((gx >= 0) & (gx < xs))

        return ok

    def u_put(x):
        if 9 <= x < n + 9:
            at = pl.ds(16, n)
            for k in (0, 1):
                u_out[k, x - 9] = (e[k, x, 0, at, :] + 0.8 * u[k, x, 0, at, :])[:, :zsize]

    ok = inside(place[0] * n - 9, place[1] * n - 16, xsize, ysize, zsize)
    whole_level(cells, u, e, r, ga, gb, planes, (7, n + 18), 8, n + 16, 16.0, False, ok, u_put)
    width = m + 6
    every = pl.ds(8, n + 16)
    for i in range(width):
        for k in (0, 1):
            restrict_xy(r, t, part, i, 2 * i + 2, 9, width, k, (8, n + 16))
        t[0, 0, every, :] = cells(2, 2 * i + 3, every) + cells(2, 2 * i + 4, every)
        part_c[i, pl.ds(0, width), :] = t[0, 0, pl.ds(10, width, 2), :] + t[0, 0, pl.ds(11, width, 2), :]
    f = [exact_dot(part[k], w_full[...]) for k in (0, 1)] + [exact_dot(part_c[...], w_mean[...])]
    ok = inside(place[0] * m - 3, place[1] * m - 3, xsize // 2, ysize // 2, zsize // 2)
    for x in range(width):
        point(f[0][x], f[1][x], f[2][x], 64.0, ok(x, 0, 16), v, gc, gd, x, 0, 0)
    old = v
    for sweep in range(1, sweeps):
        new = w.at[sweep % 2]
        for x in range(sweep, width - sweep):
            at = pl.ds(1, m + 4)
            s = [around(old, k, x, 1, m + 4, False)[0] for k in (0, 1)]
            d = divided(*s, gc[x, 0, at, :] * (1.0 / 64.0), gd[x, 0, at, :] * (1.0 / 64.0))
            for k in (0, 1):
                val = 0.2 * old[k, x, 0, at, :] + v[k, x, 0, at, :] + d[k]
                if sweep < sweeps - 1:
                    new[k, x, 0, at, :] = val
                else:
                    v_out[k, x - 3] = val[2 : 2 + m, : zsize // 2]
        old = new


def body(source, wavenumber_sq):
    f32 = jnp.float32
    xdev, ydev = lax.axis_size("gx"), lax.axis_size("gy")
    place = jnp.stack([lax.axis_index("gx"), lax.axis_index("gy")]).astype(jnp.int32)

    def swap(axis, devices, first, last):
        before = lax.ppermute(last, axis, [(i, (i + 1) % devices) for i in range(devices)])
        after = lax.ppermute(first, axis, [((i + 1) % devices, i) for i in range(devices)])
        return before, after

    _, n, rows, lanes = source.shape
    xsize, ysize = n * xdev, rows * ydev
    S = lambda *shape: jax.ShapeDtypeStruct(shape, f32)
    V = lambda *shape: pltpu.VMEM(shape, f32)

    f, c, x_first, x_last, y_first, y_last = pl.pallas_call(
        pack_kernel,
        in_specs=[pl.BlockSpec(memory_space=pl.ANY)] * 2,
        out_specs=[VMEM] * 6,
        out_shape=[S(2, n, rows, lanes), S(n, rows, lanes)] + [S(8, rows, lanes)] * 2 + [S(n, 8, lanes)] * 2,
        scratch_shapes=[pltpu.SemaphoreType.DMA((18,))],
        compiler_params=params(48),
        name="pack_faces",
    )(source, wavenumber_sq)
    xlo, xhi = swap("gx", xdev, x_first, x_last)
    ylo, yhi = swap("gy", ydev, y_first, y_last)
    planes = jnp.concatenate([xlo, xhi], 0)
    clo, chi = swap("gy", ydev, planes[:, :4], planes[:, rows - 4 :])
    halves = lanes // LANES
    w_full, w_mean = weights(lanes, lanes, lanes // 2)
    state = (n + 2 * PX, halves, rows + 2 * PY, LANES)
    part = (n // 2, rows // 2, lanes)
    shapes = [S(2, *state)] * 3 + [S(*state)] * 2 + [S(3, n // 2, rows // 2, lanes // 2)]
    column = V(2, halves, rows + 2 * PY, LANES)
    held = pl.pallas_call(
        inner_kernel,
        in_specs=[VMEM] * 4,
        out_specs=[VMEM] * 6,
        out_shape=shapes,
        scratch_shapes=[column, V(3, *part)],
        compiler_params=params(24),
        cost_estimate=pl.CostEstimate(flops=100_000_000, bytes_accessed=16_000_000, transcendentals=0),
        name="inner_cells",
    )(f, c, w_full, w_mean)
    in_place = {i + 1: i for i in range(6)}
    held = pl.pallas_call(
        functools.partial(faces_kernel, xsize, ysize),
        in_specs=[SMEM] + [VMEM] * 11,
        out_specs=[VMEM] * 6,
        out_shape=shapes,
        input_output_aliases=in_place,
        scratch_shapes=[V(2, n // 2 - 4, 16, lanes), V(2, n // 2 - 4, 16, lanes // 2)],
        compiler_params=params(24),
        cost_estimate=pl.CostEstimate(flops=50_000_000, bytes_accessed=8_000_000, transcendentals=0),
        name="face_cells",
    )(place, *held, xlo, xhi, ylo, yhi, w_full)
    u, e, _, _, _, fc = pl.pallas_call(
        functools.partial(corners_kernel, xsize, ysize, n, rows),
        in_specs=[SMEM] + [VMEM] * 9,
        out_specs=[VMEM] * 6,
        out_shape=shapes,
        input_output_aliases=in_place,
        scratch_shapes=[column, V(2, 4, rows // 2, lanes)],
        compiler_params=params(24),
        name="corner_cells",
    )(place, *held, clo, chi, w_full)
    fine = pl.pallas_call(
        iterate_kernel,
        in_specs=[VMEM] * 2,
        out_specs=VMEM,
        out_shape=S(2, n, rows, lanes),
        compiler_params=params(24),
        cost_estimate=pl.CostEstimate(flops=1_000_000, bytes_accessed=8_000_000, transcendentals=0),
        name="fine_iterate",
    )(u, e)

    n, rows, lanes, xsize, ysize, zsize = n // 2, rows // 2, lanes // 2, xsize // 2, ysize // 2, lanes // 2
    h, over = 5, 1
    xlo, xhi = swap("gx", xdev, fc[:, :h], fc[:, n - h :])
    first_rows, last_rows = pl.pallas_call(
        rows_kernel,
        in_specs=[VMEM] * 3,
        out_specs=[VMEM] * 2,
        out_shape=[S(2, n + 2 * h, 8, lanes)] * 2,
        compiler_params=params(24),
        name="second_rows",
    )(xlo, fc, xhi)
    ylo, yhi = swap("gy", ydev, first_rows, last_rows)
    both = [jnp.stack([w, jnp.roll(w, lanes // 2, 1)]) for w in weights(zsize, lanes, lanes)]
    state = (n + 2 * h, 1, rows + 16, LANES)
    work = lambda s: [V(*s), V(*s), V(2, *s), V(2, *s), V(2, *s), V(2, 1, *s[2:])]
    width = n // 2 + 2 * over
    second_u, fc = pl.pallas_call(
        functools.partial(middle_kernel, h, over, xsize, ysize),
        in_specs=[SMEM] + [VMEM] * 7,
        out_specs=[VMEM] * 2,
        out_shape=[S(2, n, rows, lanes), S(width + width // 2, width, lanes)],
        scratch_shapes=[V(3, *state)] + work(state) + [V(2, width, 16, LANES), V(2, width // 2, 16, LANES)],
        compiler_params=params(24),
        name="second_level",
    )(place, fc, xlo, xhi, ylo, yhi, *both)

    n, xsize, ysize, zsize = n // 2, xsize // 2, ysize // 2, zsize // 2
    m = n // 2

    def joined(lo, own, hi, cells):
        f = (lo[:n], own[: n + 2], hi[:n])
        c = (lo[n:], own[n + 2 :], hi[n:])
        return jnp.concatenate([a[:, cells] for a in f + c], 0)

    pick = lambda i, j: jnp.concatenate([fc[i : i + n], fc[n + 2 + j : n + 2 + j + m]], 0)
    xlo, xhi = swap("gx", xdev, pick(2, 1), pick(0, 0))
    ylo, yhi = swap("gy", ydev, joined(xlo, fc, xhi, slice(2, n + 2)), joined(xlo, fc, xhi, slice(0, n)))
    state = (n + 18, 1, 40, LANES)
    small = (m + 6, 1, 16, LANES)
    third, coarse = pl.pallas_call(
        functools.partial(coarse_kernel, n, 4, xsize, ysize, zsize),
        in_specs=[SMEM] + [VMEM] * 7,
        out_specs=[VMEM] * 2,
        out_shape=[S(2, n, n, zsize), S(2, m, m, zsize // 2)],
        scratch_shapes=[V(n + 18 + m + 9, 1, 40, LANES)] + work(state) + [V(2, m + 6, 16, LANES), V(m + 6, 16, LANES)]
        + [V(*small), V(*small), V(2, *small), V(2, 2, *small)],
        compiler_params=params(24),
        name="coarse_levels",
    )(place, fc, xlo, xhi, ylo, yhi, *weights(zsize, lanes, lanes))
    return fine, second_u, third, coarse


def solution(mesh):
    placed = (P(None, "gx", "gy", None), P("gx", "gy", None))
    return jax.shard_map(body, mesh=mesh, in_specs=placed, out_specs=(P(None, "gx", "gy", None),) * 4, check_vma=False)
```

```python
import functools
import jax
import jax.numpy as jnp
from jax import lax
from jax.experimental import pallas as pl
from jax.experimental.pallas import tpu as pltpu
from jax.sharding import PartitionSpec as P

DAMPING = 0.8
SHIFT_IMAG = 0.5
LANES = 128
VMEM = pl.BlockSpec(memory_space=pltpu.VMEM)
SMEM = pl.BlockSpec(memory_space=pltpu.SMEM)


def params(mib):
    return pltpu.CompilerParams(vmem_limit_bytes=mib * 1024 * 1024)


def around(ref, k, x, row, rows, full):
    halves = ref.shape[2]
    mid = [ref[k, x, h, pl.ds(row, rows), :] for h in range(halves)]
    up = [pltpu.roll(m, 1, 1) for m in mid]
    down = [pltpu.roll(m, LANES - 1, 1) for m in mid]
    if full:
        lane = lax.broadcasted_iota(jnp.int32, mid[0].shape, 1)
        first, last = lane == 0, lane == LANES - 1
        up = [jnp.where(first, up[h - 1] if h else 0.0, up[h]) for h in range(halves)]
        down = [jnp.where(last, down[h + 1] if h < halves - 1 else 0.0, down[h]) for h in range(halves)]
    sums = []
    for h in range(halves):
        planes = ref[k, x - 1, h, pl.ds(row, rows), :] + ref[k, x + 1, h, pl.ds(row, rows), :]
        sides = ref[k, x, h, pl.ds(row - 1, rows), :] + ref[k, x, h, pl.ds(row + 1, rows), :]
        sums.append((planes + sides) + (up[h] + down[h]))
    return sums


def inverse(c, scale, ok):
    a = 6.0 / scale - c
    b = SHIFT_IMAG * c
    g = DAMPING / (a * a + b * b)
    if ok is not None:
        g = jnp.where(ok, g, 0.0)
    return g * a, g * b


def divided(re, im, a, b):
    return re * a + im * b, im * a - re * b


def point(re, im, c, scale, ok, u, ga, gb, x, h, row):
    a, b = inverse(c, scale, ok)
    at = pl.ds(row, c.shape[0])
    ga[x, h, at, :], gb[x, h, at, :] = a, b
    u[0, x, h, at, :], u[1, x, h, at, :] = divided(re, im, a, b)


def second(u, ga, gb, e, x, row, rows, scale, full):
    s_re, s_im = around(u, 0, x, row, rows, full), around(u, 1, x, row, rows, full)
    at = pl.ds(row, rows)
    for h in range(u.shape[2]):
        a, b = ga[x, h, at, :], gb[x, h, at, :]
        if scale != 1.0:
            a, b = a * (1.0 / scale), b * (1.0 / scale)
        d = divided(s_re[h], s_im[h], a, b)
        for k in (0, 1):
            e[k, x, h, at, :] = 0.4 * u[k, x, h, at, :] + d[k]


def rows_inside(shape, y0, ysize):
    row = lax.broadcasted_iota(jnp.int32, shape, 0) + y0
    return (row >= 0) & (row < ysize)


def restrict_xy(r, t, out, to, plane, row, rows, k, window):
    at = pl.ds(*window)
    for h in range(r.shape[2]):
        val = (r[k, plane, h, at, :] + r[k, plane + 3, h, at, :]) + 3.0 * (r[k, plane + 1, h, at, :] + r[k, plane + 2, h, at, :])
        t[k, h, at, :] = val
        part = [t[k, h, pl.ds(row + j, rows, 2), :] for j in range(4)]
        out[k, to, pl.ds(0, rows), pl.ds(LANES * h, LANES)] = (part[0] + part[3]) + 3.0 * (part[1] + part[2])


def add_pairs(c0, c1, t, h, out, i, row, rows):
    t[0, h, pl.ds(0, c0.shape[0]), :] = c0 + c1
    val = t[0, h, pl.ds(row, rows, 2), :] + t[0, h, pl.ds(row + 1, rows, 2), :]
    out[i, pl.ds(0, rows), pl.ds(LANES * h, LANES)] = val


def weights(lanes, zsize, mean=False, shift=0):
    z = lax.broadcasted_iota(jnp.int32, (lanes, LANES), 0)
    i = lax.broadcasted_iota(jnp.int32, (lanes, LANES), 1) - shift
    d = z - 2 * i
    inner = (d == 0) | (d == 1)
    if mean:
        w = jnp.where(inner, 0.125, 0.0)
    else:
        w = jnp.where(inner, 3.0 / 512.0, jnp.where((d == -1) | (d == 2), 1.0 / 512.0, 0.0))
    return jnp.where((z < zsize) & (i >= 0) & (i < zsize // 2), w, 0.0).astype(jnp.bfloat16)


def exact_dot(part, w):
    planes, rows, lanes = part.shape
    x = part.reshape(planes * rows, lanes)
    hi = x.astype(jnp.bfloat16)
    rest = x - hi.astype(jnp.float32)
    mid = rest.astype(jnp.bfloat16)
    low = (rest - mid.astype(jnp.float32)).astype(jnp.bfloat16)
    dot = functools.partial(jnp.dot, preferred_element_type=jnp.float32)
    return (dot(hi, w) + (dot(mid, w) + dot(low, w))).reshape(planes, rows, w.shape[1])


PX, PY = 3, 8


def pack_kernel(f, c, x_first, x_last, y_first, y_last, planes, strips, sems):
    n, rows = c.shape[:2]
    edges = (0, n - PX)
    tiles = (0, rows - 8)
    middle = pl.ds(PX, n - 2 * PX)
    copies = []
    for side, x in enumerate(edges):
        at = pl.ds(x, PX)
        copies += [(f.at[0, at], planes.at[side, 0]), (f.at[1, at], planes.at[side, 1]), (c.at[at], planes.at[side, 2])]
    for side, row in enumerate(tiles):
        at = pl.ds(row, 8)
        into = [strips.at[side, k, middle] for k in range(3)]
        copies += [(f.at[0, middle, at], into[0]), (f.at[1, middle, at], into[1]), (c.at[middle, at], into[2])]
    copies = [pltpu.make_async_copy(src, dst, sems.at[i]) for i, (src, dst) in enumerate(copies)]
    for copy in copies:
        copy.start()
    for copy in copies[:6]:
        copy.wait()
    for side, out in enumerate((x_first, x_last)):
        for j in range(PX):
            a, b = inverse(planes[side, 2, j], 1.0, None)
            out[j], out[PX + j] = divided(planes[side, 0, j], planes[side, 1, j], a, b)
        for j in range(2):
            out[2 * PX + j] = planes[side, 2, j + side]
        for end, row in enumerate(tiles):
            strips[end, :, pl.ds(edges[side], PX)] = planes[side, :, :, pl.ds(row, 8), :]
    for copy in copies[6:]:
        copy.wait()
    row = lax.broadcasted_iota(jnp.int32, (8, c.shape[2]), 0)

    def strip(x, carry):
        for side, out, shifts in ((0, y_first, (0, 3, 6)), (1, y_last, (3, 6, 0))):
            cc = strips[side, 2, x]
            a, b = inverse(cc, 1.0, None)
            re, im = divided(strips[side, 0, x], strips[side, 1, x], a, b)
            re, im, cc = [pltpu.roll(v, shift, 0) if shift else v for v, shift in zip((re, im, cc), shifts)]
            out[x] = jnp.where(row < 3, re, jnp.where(row < 6, im, cc))
        return carry

    lax.fori_loop(0, n, strip, 0, unroll=4)


def inner_kernel(f, c, u, e, r, ga, gb, fc_out, t, part):
    n, rows, lanes = c.shape
    halves = lanes // LANES
    at = pl.ds(PY, rows)
    cut = [pl.ds(LANES * h, LANES) for h in range(halves)]

    def first(x, carry):
        for h in range(halves):
            point(f[0, x, :, cut[h]], f[1, x, :, cut[h]], c[x, :, cut[h]], 1.0, None, u, ga, gb, x + PX, h, PY)
        return carry

    lax.fori_loop(0, n, first, 0, unroll=2)

    def middle(x, carry):
        second(u, ga, gb, e, x + PX, PY, rows, 1.0, True)
        return carry

    lax.fori_loop(1, n - 1, middle, 0, unroll=2)
    row = lax.broadcasted_iota(jnp.int32, (rows, LANES), 0)
    full = (row >= 2) & (row < rows - 2)

    def last(x, carry):
        for k in (0, 1):
            s = around(e, k, x + PX, PY, rows, True)
            for h in range(halves):
                r[k, x + PX, h, at, :] = 0.04 * f[k, x, :, cut[h]] + jnp.where(full, s[h], 0.0)
        return carry

    lax.fori_loop(2, n - 2, last, 0, unroll=2)
    for x in (0, 1, n - 2, n - 1):
        for k in (0, 1):
            for h in range(halves):
                r[k, x + PX, h, at, :] = 0.04 * f[k, x, :, cut[h]]

    def pairs(i, carry):
        for h in range(halves):
            add_pairs(c[2 * i, :, cut[h]], c[2 * i + 1, :, cut[h]], t, h, part.at[2], i, 0, rows // 2)
        return carry

    lax.fori_loop(0, n // 2, pairs, 0, unroll=2)

    def coarse(i, carry):
        for k in (0, 1):
            restrict_xy(r, t, part, i, 2 * i + PX - 1, PY - 1, rows // 2, k, (PY, rows))
        return carry

    lax.fori_loop(2, n // 2 - 2, coarse, 0, unroll=2)
    w = weights(lanes, lanes)
    for k in (0, 1):
        fc_out[k, 2 : n // 2 - 2] = exact_dot(part[k, 2 : n // 2 - 2], w)
    fc_out[2] = exact_dot(part[2], weights(lanes, lanes, mean=True))


def inside(place, n, rows, xsize, ysize):
    x0, y0 = place[0] * n - PX, place[1] * rows - PY

    def ok(x, row, count):
        gx = x + x0
        return rows_inside((count, LANES), y0 + row, ysize) & ((gx >= 0) & (gx < xsize))

    return ok


def halo(re, im, cc, good, u, ga, gb, r, x, h, row, c_here, r_here):
    at = pl.ds(row, re.shape[0])
    re, im = jnp.where(good, re, 0.0), jnp.where(good, im, 0.0)
    u[0, x, h, at, :], u[1, x, h, at, :] = re, im
    if c_here:
        a, b = inverse(cc, 1.0, good)
        ga[x, h, at, :], gb[x, h, at, :] = a, b
    if r_here:
        a, b = 0.05 * (6.0 - cc), (0.05 * SHIFT_IMAG) * cc
        r[0, x, h, at, :], r[1, x, h, at, :] = re * a - im * b, im * a + re * b


def finish(e, r, x, row, count, good):
    for k in (0, 1):
        s = around(e, k, x, row, count, True)
        for h in range(e.shape[2]):
            at = pl.ds(row, count)
            r[k, x, h, at, :] = r[k, x, h, at, :] + jnp.where(good, s[h], 0.0)


def plane_cells(side, low, i, h):
    cut = pl.ds(LANES * h, LANES)
    j = i - 1 if low else i
    c_here = 0 <= j < 2
    cc = side[2 * PX + j, :, cut] if c_here else None
    return side[i, :, cut], side[PX + i, :, cut], cc, c_here, i == (PX - 1 if low else 0)


def faces_kernel(xsize, ysize, place, u_in, e_in, r_in, ga_in, gb_in, fc_in, xlo, xhi, ylo, yhi, u, e, r, ga, gb, fc_out, part, q):
    n, (rows, lanes) = ylo.shape[0], xlo.shape[1:]
    halves = lanes // LANES
    cut = [pl.ds(LANES * h, LANES) for h in range(halves)]
    ok = inside(place, n, rows, xsize, ysize)
    del u_in, e_in, r_in, ga_in, gb_in, fc_in
    for side, low, base in ((xlo, True, 0), (xhi, False, n + PX)):
        for i in range(PX):
            good = ok(base + i, PY, rows)
            for h in range(halves):
                re, im, cc, c_here, r_here = plane_cells(side, low, i, h)
                halo(re, im, cc, good, u, ga, gb, r, base + i, h, PY, c_here, r_here)
    low, high = PY - 4, PY + rows - 4
    good_lo, good_hi = ok(PX, 0, 8), ok(PX, PY + rows, 8)

    def strips(x, carry):
        for side, good, row, shifts in ((ylo, good_lo, 0, (5, 2, 0)), (yhi, good_hi, PY + rows, (0, 5, 2))):
            for h in range(halves):
                tile = side[x, :, cut[h]]
                re, im, cc = [pltpu.roll(tile, shift, 0) if shift else tile for shift in shifts]
                halo(re, im, cc, good, u, ga, gb, r, x + PX, h, row, True, True)
        return carry

    lax.fori_loop(0, n, strips, 0, unroll=4)
    for x in (PX - 2, PX - 1, PX, n + PX - 1, n + PX, n + PX + 1):
        second(u, ga, gb, e, x, PY, rows, 1.0, True)

    def middle(x, carry):
        for row in (low, high):
            second(u, ga, gb, e, x, row, 8, 1.0, True)
        return carry

    lax.fori_loop(PX + 1, n + PX - 1, middle, 0, unroll=3)
    for x in (PX - 1, PX, PX + 1, n + PX - 2, n + PX - 1, n + PX):
        finish(e, r, x, PY + 4, rows - 8, ok(x, PY + 4, rows - 8))
    row = lax.broadcasted_iota(jnp.int32, (8, LANES), 0)
    good_low, good_high = ok(PX, low, 8) & (row < 6), ok(PX, high, 8) & (row >= 2)

    def last(x, carry):
        finish(e, r, x, low, 8, good_low)
        finish(e, r, x, high, 8, good_high)
        return carry

    lax.fori_loop(PX + 2, n + PX - 2, last, 0, unroll=4)
    m = n // 2 - 4

    def coarse(i, carry):
        x = 2 * i + PX + 3
        for k in (0, 1):
            for h in range(halves):
                for j, row in ((0, PY - 1), (8, PY + rows - 7)):
                    at = pl.ds(row, 8)
                    part[k, i, pl.ds(j, 8), cut[h]] = (r[k, x, h, at, :] + r[k, x + 3, h, at, :]) + 3.0 * (
                        r[k, x + 1, h, at, :] + r[k, x + 2, h, at, :]
                    )
        return carry

    lax.fori_loop(0, m, coarse, 0, unroll=4)
    w = weights(lanes, lanes)
    for k in (0, 1):
        q[k] = exact_dot(part[k], w)
        for row, start in ((0, 0), (rows // 2 - 2, 10)):
            four = [q[k, :, pl.ds(start + j, 2, 2), :] for j in range(4)]
            fc_out[k, pl.ds(2, m), pl.ds(row, 2), :] = (four[0] + four[3]) + 3.0 * (four[1] + four[2])


def corners_kernel(xsize, ysize, n, rows, place, u_in, e_in, r_in, ga_in, gb_in, fc_in, clo, chi, u, e, r, ga, gb, fc_out, t, part):
    halves = clo.shape[2] // LANES
    ok = inside(place, n, rows, xsize, ysize)
    del u_in, e_in, r_in, ga_in, gb_in, fc_in
    low, high = PY - 4, PY + rows - 4
    for side, row in ((clo, PY - 4), (chi, PY + rows)):
        for planes, is_low, base in ((side.at[pl.ds(0, 8)], True, 0), (side.at[pl.ds(8, 8)], False, n + PX)):
            for i in range(PX):
                good = ok(base + i, row, 4)
                for h in range(halves):
                    re, im, cc, c_here, r_here = plane_cells(planes, is_low, i, h)
                    halo(re, im, cc, good, u, ga, gb, r, base + i, h, row, c_here, r_here)
    for x in (PX - 2, PX - 1, PX, n + PX - 1, n + PX, n + PX + 1):
        for row in (low, high):
            second(u, ga, gb, e, x, row, 8, 1.0, True)
    for x in (PX - 1, PX, PX + 1, n + PX - 2, n + PX - 1, n + PX):
        for row in (low, high):
            finish(e, r, x, row, 8, ok(x, row, 8))
    planes = (0, 1, n // 2 - 2, n // 2 - 1)
    w = weights(part.shape[3], part.shape[3])
    for k in (0, 1):
        for j, i in enumerate(planes):
            restrict_xy(r, t, part, j, 2 * i + PX - 1, PY - 1, rows // 2, k, (low, rows + 8))
        val = exact_dot(part[k], w)
        for j, i in enumerate(planes):
            fc_out[k, i] = val[j]


def iterate_kernel(u, e, out):
    n, rows = out.shape[1:3]
    at = pl.ds(PY, rows)

    def step(x, carry):
        for k in (0, 1):
            for h in range(u.shape[2]):
                out[k, x, :, pl.ds(LANES * h, LANES)] = e[k, x + PX, h, at, :] + 0.8 * u[k, x + PX, h, at, :]
        return carry

    lax.fori_loop(0, n, step, 0, unroll=2)


def whole_level(cells, u, e, r, ga, gb, planes, used, row, rows, scale, full, ok, u_put):
    first, count = used
    for x in range(planes):
        at = pl.ds(first, count)
        point(cells(0, x, at), cells(1, x, at), cells(2, x, at), scale, ok(x, first, count), u, ga, gb, x, 0, first)
    at = pl.ds(row, rows)
    for x in range(1, planes - 1):
        second(u, ga, gb, e, x, row, rows, scale, full)
        u_put(x)
    for x in range(2, planes - 2):
        good = ok(x, row, rows)
        for k in (0, 1):
            s = around(e, k, x, row, rows, full)[0] * (1.0 / scale)
            r[k, x, 0, at, :] = jnp.where(good, 0.04 * cells(k, x, at) + s, 0.0)


def rows_kernel(xlo, fc, xhi, first, last):
    halo, n, rows = xlo.shape[1], fc.shape[1], fc.shape[2]
    row = lax.broadcasted_iota(jnp.int32, (8, LANES), 0)
    for src, base, count in ((xlo, 0, halo), (fc, halo, n), (xhi, n + halo, halo)):
        for i in range(count):
            for out, start, own in ((first, 0, row < 5), (last, rows - 8, row >= 3)):
                re, im, cc = [src[k, i, pl.ds(start, 8), :] for k in range(3)]
                out[0, base + i] = jnp.where(own, re, pltpu.roll(cc, 5, 0))
                out[1, base + i] = jnp.where(own, im, pltpu.roll(cc, 2, 0))


def middle_kernel(halo, over, xsize, ysize, place, fc_own, xlo, xhi, ylo, yhi, u_out, fc_out, fc, ga, gb, u, e, r, t, part, part_c):
    n, rows = fc_own.shape[1:3]
    planes = n + 2 * halo
    for k in range(3):
        for src, x, count in ((xlo, 0, halo), (fc_own, halo, n), (xhi, n + halo, halo)):
            fc[k, pl.ds(x, count), 0, pl.ds(8, rows), :] = src[k]
    row = lax.broadcasted_iota(jnp.int32, (8, LANES), 0)
    for side, start, split in ((ylo, 0, 6), (yhi, 8 + rows, 3)):
        at = pl.ds(start, 8)
        for x in range(planes):
            one, two = side[0, x], side[1, x]
            fc[0, x, 0, at, :], fc[1, x, 0, at, :] = one, two
            fc[2, x, 0, at, :] = jnp.where(row < split, pltpu.roll(one, 3, 0), pltpu.roll(two, 6, 0))
    x0, y0 = place[0] * n - halo, place[1] * rows - 8

    def ok(x, row, count):
        gx = x + x0
        return rows_inside((count, LANES), y0 + row, ysize) & ((gx >= 0) & (gx < xsize))

    def u_put(x):
        if halo <= x < n + halo:
            at = pl.ds(8, rows)
            for k in (0, 1):
                u_out[k, x - halo] = e[k, x, 0, at, :] + 0.8 * u[k, x, 0, at, :]

    def cells(k, x, at):
        return fc[k, x, 0, at, :]

    whole_level(cells, u, e, r, ga, gb, planes, (0, rows + 16), 4, rows + 8, 4.0, True, ok, u_put)
    width = n // 2 + 2 * over
    pairs = width // 2
    for i in range(width):
        x, row = 2 * i + halo - 1 - 2 * over, 7 - 2 * over
        for k in (0, 1):
            restrict_xy(r, t, part, i, x, row, width, k, (4, rows + 8))
        add_pairs(fc[2, x + 1, 0], fc[2, x + 2, 0], t, 0, part_c.at[i % 2], i // 2, row + 1, width)
    two = [(part.at[k], part_c.at[k], LANES // 2 * k) for k in (0, 1)]
    fc_out[pl.ds(0, width)] = sum(exact_dot(p[...], weights(LANES, LANES, shift=s)) for p, _, s in two)[:, :width]
    fc_out[pl.ds(width, pairs)] = sum(exact_dot(p[...], weights(LANES, LANES, True, s)) for _, p, s in two)[:, :width]


def coarse_kernel(n, sweeps, xsize, ysize, zsize, place, fc_own, xlo, xhi, ylo, yhi, u_out, v_out, fc, ga, gb, u, e, r, t, part, part_c, gc, gd, v, w):
    m = n // 2
    planes = n + 18
    for src, x, first, count in ((xlo, 0, 0, 8), (fc_own, 8, 0, n + 2), (xhi, n + 10, 0, 8), (xlo, planes, 8, 4), (fc_own, planes + 4, n + 2, m + 1), (xhi, planes + m + 5, 8, 4)):
        fc[pl.ds(x, count), 0, pl.ds(15, n + 2), :] = src[pl.ds(first, count)]
    fc[:, 0, pl.ds(7, 8), :] = ylo[...]
    fc[:, 0, pl.ds(n + 17, 8), :] = yhi[...]
    lane = lax.broadcasted_iota(jnp.int32, (1, LANES), 1)

    def cells(k, x, at):
        val = fc[planes + x // 2 if k == 2 else x, 0, at, :]
        return pltpu.roll(val, LANES - zsize, 1) if k == 1 or (k == 2 and x % 2) else val

    def inside(x0, y0, xs, ys, zs):
        def ok(x, row, count):
            gx = x + x0
            here = rows_inside((count, LANES), y0 + row, ys) & (lane < zs)
            return here & ((gx >= 0) & (gx < xs))

        return ok

    def u_put(x):
        if 9 <= x < n + 9:
            at = pl.ds(16, n)
            for k in (0, 1):
                u_out[k, x - 9] = (e[k, x, 0, at, :] + 0.8 * u[k, x, 0, at, :])[:, :zsize]

    ok = inside(place[0] * n - 9, place[1] * n - 16, xsize, ysize, zsize)
    whole_level(cells, u, e, r, ga, gb, planes, (7, n + 18), 8, n + 16, 16.0, False, ok, u_put)
    width = m + 6
    every = pl.ds(8, n + 16)
    for i in range(width):
        for k in (0, 1):
            restrict_xy(r, t, part, i, 2 * i + 2, 9, width, k, (8, n + 16))
        t[0, 0, every, :] = cells(2, 2 * i + 3, every) + cells(2, 2 * i + 4, every)
        part_c[i, pl.ds(0, width), :] = t[0, 0, pl.ds(10, width, 2), :] + t[0, 0, pl.ds(11, width, 2), :]
    w_full = weights(LANES, zsize)
    f = [exact_dot(part[k], w_full) for k in (0, 1)] + [exact_dot(part_c[...], weights(LANES, zsize, True))]
    ok = inside(place[0] * m - 3, place[1] * m - 3, xsize // 2, ysize // 2, zsize // 2)
    for x in range(width):
        point(f[0][x], f[1][x], f[2][x], 64.0, ok(x, 0, 16), v, gc, gd, x, 0, 0)
    old = v
    for sweep in range(1, sweeps):
        new = w.at[sweep % 2]
        for x in range(sweep, width - sweep):
            at = pl.ds(1, m + 4)
            s = [around(old, k, x, 1, m + 4, False)[0] for k in (0, 1)]
            d = divided(*s, gc[x, 0, at, :] * (1.0 / 64.0), gd[x, 0, at, :] * (1.0 / 64.0))
            for k in (0, 1):
                val = 0.2 * old[k, x, 0, at, :] + v[k, x, 0, at, :] + d[k]
                if sweep < sweeps - 1:
                    new[k, x, 0, at, :] = val
                else:
                    v_out[k, x - 3] = val[2 : 2 + m, : zsize // 2]
        old = new


def body(source, wavenumber_sq):
    f32 = jnp.float32
    xdev, ydev = lax.axis_size("gx"), lax.axis_size("gy")
    place = jnp.stack([lax.axis_index("gx"), lax.axis_index("gy")]).astype(jnp.int32)

    def swap(axis, devices, first, last):
        before = lax.ppermute(last, axis, [(i, (i + 1) % devices) for i in range(devices)])
        after = lax.ppermute(first, axis, [((i + 1) % devices, i) for i in range(devices)])
        return before, after

    _, n, rows, lanes = source.shape
    xsize, ysize = n * xdev, rows * ydev
    S = lambda *shape: jax.ShapeDtypeStruct(shape, f32)
    V = lambda *shape: pltpu.VMEM(shape, f32)

    x_first, x_last, y_first, y_last = pl.pallas_call(
        pack_kernel,
        in_specs=[pl.BlockSpec(memory_space=pltpu.HBM)] * 2,
        out_specs=[VMEM] * 4,
        out_shape=[S(8, rows, lanes)] * 2 + [S(n, 8, lanes)] * 2,
        scratch_shapes=[V(2, 3, PX, rows, lanes), V(2, 3, n, 8, lanes), pltpu.SemaphoreType.DMA((12,))],
        compiler_params=params(60),
        name="pack_faces",
    )(source, wavenumber_sq)
    xlo, xhi = swap("gx", xdev, x_first, x_last)
    ylo, yhi = swap("gy", ydev, y_first, y_last)
    halves = lanes // LANES
    state = (n + 2 * PX, halves, rows + 2 * PY, LANES)
    part = (n // 2, rows // 2, lanes)
    shapes = [S(2, *state)] * 3 + [S(*state)] * 2 + [S(3, n // 2, rows // 2, lanes // 2)]
    column = V(2, halves, rows + 2 * PY, LANES)
    held = pl.pallas_call(
        inner_kernel,
        in_specs=[VMEM] * 2,
        out_specs=[VMEM] * 6,
        out_shape=shapes,
        scratch_shapes=[column, V(3, *part)],
        compiler_params=params(24),
        cost_estimate=pl.CostEstimate(flops=100_000_000, bytes_accessed=16_000_000, transcendentals=0),
        name="inner_cells",
    )(source, wavenumber_sq)
    xlo, xhi, held = lax.optimization_barrier((xlo, xhi, held))
    planes = jnp.concatenate([xlo, xhi], 0)
    clo, chi = swap("gy", ydev, planes[:, :4], planes[:, rows - 4 :])
    in_place = {i + 1: i for i in range(6)}
    held = pl.pallas_call(
        functools.partial(faces_kernel, xsize, ysize),
        in_specs=[SMEM] + [VMEM] * 10,
        out_specs=[VMEM] * 6,
        out_shape=shapes,
        input_output_aliases=in_place,
        scratch_shapes=[V(2, n // 2 - 4, 16, lanes), V(2, n // 2 - 4, 16, lanes // 2)],
        compiler_params=params(24),
        cost_estimate=pl.CostEstimate(flops=50_000_000, bytes_accessed=8_000_000, transcendentals=0),
        name="face_cells",
    )(place, *held, xlo, xhi, ylo, yhi)
    u, e, _, _, _, fc = pl.pallas_call(
        functools.partial(corners_kernel, xsize, ysize, n, rows),
        in_specs=[SMEM] + [VMEM] * 8,
        out_specs=[VMEM] * 6,
        out_shape=shapes,
        input_output_aliases=in_place,
        scratch_shapes=[column, V(2, 4, rows // 2, lanes)],
        compiler_params=params(24),
        name="corner_cells",
    )(place, *held, clo, chi)
    fine = pl.pallas_call(
        iterate_kernel,
        in_specs=[VMEM] * 2,
        out_specs=VMEM,
        out_shape=S(2, n, rows, lanes),
        compiler_params=params(24),
        cost_estimate=pl.CostEstimate(flops=1_000_000, bytes_accessed=8_000_000, transcendentals=0),
        name="fine_iterate",
    )(u, e)

    n, rows, lanes, xsize, ysize, zsize = n // 2, rows // 2, lanes // 2, xsize // 2, ysize // 2, lanes // 2
    h, over = 5, 1
    xlo, xhi = swap("gx", xdev, fc[:, :h], fc[:, n - h :])
    first_rows, last_rows = pl.pallas_call(
        rows_kernel,
        in_specs=[VMEM] * 3,
        out_specs=[VMEM] * 2,
        out_shape=[S(2, n + 2 * h, 8, lanes)] * 2,
        compiler_params=params(24),
        name="second_rows",
    )(xlo, fc, xhi)
    ylo, yhi = swap("gy", ydev, first_rows, last_rows)
    state = (n + 2 * h, 1, rows + 16, LANES)
    work = lambda s: [V(*s), V(*s), V(2, *s), V(2, *s), V(2, *s), V(2, 1, *s[2:])]
    width = n // 2 + 2 * over
    second_u, fc = pl.pallas_call(
        functools.partial(middle_kernel, h, over, xsize, ysize),
        in_specs=[SMEM] + [VMEM] * 5,
        out_specs=[VMEM] * 2,
        out_shape=[S(2, n, rows, lanes), S(width + width // 2, width, lanes)],
        scratch_shapes=[V(3, *state)] + work(state) + [V(2, width, 16, LANES), V(2, width // 2, 16, LANES)],
        compiler_params=params(24),
        name="second_level",
    )(place, fc, xlo, xhi, ylo, yhi)

    n, xsize, ysize, zsize = n // 2, xsize // 2, ysize // 2, zsize // 2
    m = n // 2

    def joined(lo, own, hi, cells):
        f = (lo[:n], own[: n + 2], hi[:n])
        c = (lo[n:], own[n + 2 :], hi[n:])
        return jnp.concatenate([a[:, cells] for a in f + c], 0)

    pick = lambda i, j: jnp.concatenate([fc[i : i + n], fc[n + 2 + j : n + 2 + j + m]], 0)
    xlo, xhi = swap("gx", xdev, pick(2, 1), pick(0, 0))
    ylo, yhi = swap("gy", ydev, joined(xlo, fc, xhi, slice(2, n + 2)), joined(xlo, fc, xhi, slice(0, n)))
    state = (n + 18, 1, 40, LANES)
    small = (m + 6, 1, 16, LANES)
    third, coarse = pl.pallas_call(
        functools.partial(coarse_kernel, n, 4, xsize, ysize, zsize),
        in_specs=[SMEM] + [VMEM] * 5,
        out_specs=[VMEM] * 2,
        out_shape=[S(2, n, n, zsize), S(2, m, m, zsize // 2)],
        scratch_shapes=[V(n + 18 + m + 9, 1, 40, LANES)] + work(state) + [V(2, m + 6, 16, LANES), V(m + 6, 16, LANES)]
        + [V(*small), V(*small), V(2, *small), V(2, 2, *small)],
        compiler_params=params(24),
        name="coarse_levels",
    )(place, fc, xlo, xhi, ylo, yhi)
    return fine, second_u, third, coarse


def solution(mesh):
    placed = (P(None, "gx", "gy", None), P("gx", "gy", None))
    return jax.shard_map(body, mesh=mesh, in_specs=placed, out_specs=(P(None, "gx", "gy", None),) * 4, check_vma=False)
```

```python
import functools
import jax
import jax.numpy as jnp
from jax import lax
from jax.experimental import pallas as pl
from jax.experimental.pallas import tpu as pltpu
from jax.sharding import PartitionSpec as P

DAMPING = 0.8
SHIFT_IMAG = 0.5
LANES = 128
VMEM = pl.BlockSpec(memory_space=pltpu.VMEM)
SMEM = pl.BlockSpec(memory_space=pltpu.SMEM)


def params(mib):
    return pltpu.CompilerParams(vmem_limit_bytes=mib * 1024 * 1024)


def around(ref, k, x, row, rows, full):
    halves = ref.shape[2]
    mid = [ref[k, x, h, pl.ds(row, rows), :] for h in range(halves)]
    up = [pltpu.roll(m, 1, 1) for m in mid]
    down = [pltpu.roll(m, LANES - 1, 1) for m in mid]
    if full:
        lane = lax.broadcasted_iota(jnp.int32, mid[0].shape, 1)
        first, last = lane == 0, lane == LANES - 1
        up = [jnp.where(first, up[h - 1] if h else 0.0, up[h]) for h in range(halves)]
        down = [jnp.where(last, down[h + 1] if h < halves - 1 else 0.0, down[h]) for h in range(halves)]
    sums = []
    for h in range(halves):
        planes = ref[k, x - 1, h, pl.ds(row, rows), :] + ref[k, x + 1, h, pl.ds(row, rows), :]
        sides = ref[k, x, h, pl.ds(row - 1, rows), :] + ref[k, x, h, pl.ds(row + 1, rows), :]
        sums.append((planes + sides) + (up[h] + down[h]))
    return sums


def inverse(c, scale, ok):
    a = 6.0 / scale - c
    b = SHIFT_IMAG * c
    g = DAMPING / (a * a + b * b)
    if ok is not None:
        g = jnp.where(ok, g, 0.0)
    return g * a, g * b


def divided(re, im, a, b):
    return re * a + im * b, im * a - re * b


def point(re, im, c, scale, ok, u, ga, gb, x, h, row):
    a, b = inverse(c, scale, ok)
    at = pl.ds(row, c.shape[0])
    ga[x, h, at, :], gb[x, h, at, :] = a, b
    u[0, x, h, at, :], u[1, x, h, at, :] = divided(re, im, a, b)


def second(u, ga, gb, e, x, row, rows, scale, full):
    s_re, s_im = around(u, 0, x, row, rows, full), around(u, 1, x, row, rows, full)
    at = pl.ds(row, rows)
    for h in range(u.shape[2]):
        a, b = ga[x, h, at, :], gb[x, h, at, :]
        if scale != 1.0:
            a, b = a * (1.0 / scale), b * (1.0 / scale)
        d = divided(s_re[h], s_im[h], a, b)
        for k in (0, 1):
            e[k, x, h, at, :] = 0.4 * u[k, x, h, at, :] + d[k]


def is_even(place, shape):
    return jnp.full(shape, lax.rem(place[1], 2)) == 0


def rows_inside(shape, y0, ysize):
    row = lax.broadcasted_iota(jnp.int32, shape, 0) + y0
    return (row >= 0) & (row < ysize)


def restrict_xy(r, t, out, to, plane, row, rows, k, window):
    at = pl.ds(*window)
    for h in range(r.shape[2]):
        val = (r[k, plane, h, at, :] + r[k, plane + 3, h, at, :]) + 3.0 * (r[k, plane + 1, h, at, :] + r[k, plane + 2, h, at, :])
        t[k, h, at, :] = val
        part = [t[k, h, pl.ds(row + j, rows, 2), :] for j in range(4)]
        out[k, to, pl.ds(0, rows), pl.ds(LANES * h, LANES)] = (part[0] + part[3]) + 3.0 * (part[1] + part[2])


def add_pairs(c0, c1, t, h, out, i, row, rows):
    t[0, h, pl.ds(0, c0.shape[0]), :] = c0 + c1
    val = t[0, h, pl.ds(row, rows, 2), :] + t[0, h, pl.ds(row + 1, rows, 2), :]
    out[i, pl.ds(0, rows), pl.ds(LANES * h, LANES)] = val


def weights(lanes, zsize, mean=False, shift=0):
    z = lax.broadcasted_iota(jnp.int32, (lanes, LANES), 0)
    i = lax.broadcasted_iota(jnp.int32, (lanes, LANES), 1) - shift
    d = z - 2 * i
    inner = (d == 0) | (d == 1)
    if mean:
        w = jnp.where(inner, 0.125, 0.0)
    else:
        w = jnp.where(inner, 3.0 / 512.0, jnp.where((d == -1) | (d == 2), 1.0 / 512.0, 0.0))
    return jnp.where((z < zsize) & (i >= 0) & (i < zsize // 2), w, 0.0).astype(jnp.bfloat16)


def exact_dot(part, w):
    planes, rows, lanes = part.shape
    x = part.reshape(planes * rows, lanes)
    hi = x.astype(jnp.bfloat16)
    rest = x - hi.astype(jnp.float32)
    mid = rest.astype(jnp.bfloat16)
    low = (rest - mid.astype(jnp.float32)).astype(jnp.bfloat16)
    dot = functools.partial(jnp.dot, preferred_element_type=jnp.float32)
    return (dot(hi, w) + (dot(mid, w) + dot(low, w))).reshape(planes, rows, w.shape[1])


PX, PY = 3, 8


def pack_kernel(place, f, c, x_first, x_last, y_chip, y_next, planes, strips, sems):
    n, rows = c.shape[:2]
    edges = (0, n - PX)
    tiles = (0, rows - 8)
    middle = pl.ds(PX, n - 2 * PX)
    copies = []
    for side, x in enumerate(edges):
        at = pl.ds(x, PX)
        copies += [(f.at[0, at], planes.at[side, 0]), (f.at[1, at], planes.at[side, 1]), (c.at[at], planes.at[side, 2])]
    for side, row in enumerate(tiles):
        at = pl.ds(row, 8)
        into = [strips.at[side, k, middle] for k in range(3)]
        copies += [(f.at[0, middle, at], into[0]), (f.at[1, middle, at], into[1]), (c.at[middle, at], into[2])]
    copies = [pltpu.make_async_copy(src, dst, sems.at[i]) for i, (src, dst) in enumerate(copies)]
    for copy in copies:
        copy.start()
    for copy in copies[:6]:
        copy.wait()
    for side, out in enumerate((x_first, x_last)):
        for j in range(PX):
            a, b = inverse(planes[side, 2, j], 1.0, None)
            out[j], out[PX + j] = divided(planes[side, 0, j], planes[side, 1, j], a, b)
        for j in range(2):
            out[2 * PX + j] = planes[side, 2, j + side]
        for end, row in enumerate(tiles):
            strips[end, :, pl.ds(edges[side], PX)] = planes[side, :, :, pl.ds(row, 8), :]
    for copy in copies[6:]:
        copy.wait()
    shape = (8, c.shape[2])
    row = lax.broadcasted_iota(jnp.int32, shape, 0)
    even = is_even(place, shape)

    def strip(x, carry):
        made = []
        for side, shifts in ((0, (0, 3, 6)), (1, (3, 6, 0))):
            cc = strips[side, 2, x]
            a, b = inverse(cc, 1.0, None)
            re, im = divided(strips[side, 0, x], strips[side, 1, x], a, b)
            re, im, cc = [pltpu.roll(v, shift, 0) if shift else v for v, shift in zip((re, im, cc), shifts)]
            made.append(jnp.where(row < 3, re, jnp.where(row < 6, im, cc)))
        y_chip[x], y_next[x] = jnp.where(even, made[1], made[0]), jnp.where(even, made[0], made[1])
        return carry

    lax.fori_loop(0, n, strip, 0, unroll=4)


def inner_kernel(f, c, u, e, r, ga, gb, fc_out, t, part):
    n, rows, lanes = c.shape
    halves = lanes // LANES
    at = pl.ds(PY, rows)
    cut = [pl.ds(LANES * h, LANES) for h in range(halves)]

    def first(x, carry):
        for h in range(halves):
            point(f[0, x, :, cut[h]], f[1, x, :, cut[h]], c[x, :, cut[h]], 1.0, None, u, ga, gb, x + PX, h, PY)
        return carry

    lax.fori_loop(0, n, first, 0, unroll=2)

    def middle(x, carry):
        second(u, ga, gb, e, x + PX, PY, rows, 1.0, True)
        return carry

    lax.fori_loop(1, n - 1, middle, 0, unroll=2)
    row = lax.broadcasted_iota(jnp.int32, (rows, LANES), 0)
    full = (row >= 2) & (row < rows - 2)

    def last(x, carry):
        for k in (0, 1):
            s = around(e, k, x + PX, PY, rows, True)
            for h in range(halves):
                r[k, x + PX, h, at, :] = 0.04 * f[k, x, :, cut[h]] + jnp.where(full, s[h], 0.0)
        return carry

    lax.fori_loop(2, n - 2, last, 0, unroll=2)
    for x in (0, 1, n - 2, n - 1):
        for k in (0, 1):
            for h in range(halves):
                r[k, x + PX, h, at, :] = 0.04 * f[k, x, :, cut[h]]

    def pairs(i, carry):
        for h in range(halves):
            add_pairs(c[2 * i, :, cut[h]], c[2 * i + 1, :, cut[h]], t, h, part.at[2], i, 0, rows // 2)
        return carry

    lax.fori_loop(0, n // 2, pairs, 0, unroll=2)

    def coarse(i, carry):
        for k in (0, 1):
            restrict_xy(r, t, part, i, 2 * i + PX - 1, PY - 1, rows // 2, k, (PY, rows))
        return carry

    lax.fori_loop(2, n // 2 - 2, coarse, 0, unroll=2)
    w = weights(lanes, lanes)
    for k in (0, 1):
        fc_out[k, 2 : n // 2 - 2] = exact_dot(part[k, 2 : n // 2 - 2], w)
    fc_out[2] = exact_dot(part[2], weights(lanes, lanes, mean=True))


def inside(place, n, rows, xsize, ysize):
    x0, y0 = place[0] * n - PX, place[1] * rows - PY

    def ok(x, row, count):
        gx = x + x0
        return rows_inside((count, LANES), y0 + row, ysize) & ((gx >= 0) & (gx < xsize))

    return ok


def halo(re, im, cc, good, u, ga, gb, r, x, h, row, c_here, r_here):
    at = pl.ds(row, re.shape[0])
    re, im = jnp.where(good, re, 0.0), jnp.where(good, im, 0.0)
    u[0, x, h, at, :], u[1, x, h, at, :] = re, im
    if c_here:
        a, b = inverse(cc, 1.0, good)
        ga[x, h, at, :], gb[x, h, at, :] = a, b
    if r_here:
        a, b = 0.05 * (6.0 - cc), (0.05 * SHIFT_IMAG) * cc
        r[0, x, h, at, :], r[1, x, h, at, :] = re * a - im * b, im * a + re * b


def finish(e, r, x, row, count, good):
    for k in (0, 1):
        s = around(e, k, x, row, count, True)
        for h in range(e.shape[2]):
            at = pl.ds(row, count)
            r[k, x, h, at, :] = r[k, x, h, at, :] + jnp.where(good, s[h], 0.0)


def plane_cells(side, low, i, h):
    cut = pl.ds(LANES * h, LANES)
    j = i - 1 if low else i
    c_here = 0 <= j < 2
    cc = side[2 * PX + j, :, cut] if c_here else None
    return side[i, :, cut], side[PX + i, :, cut], cc, c_here, i == (PX - 1 if low else 0)


def faces_kernel(xsize, ysize, place, u_in, e_in, r_in, ga_in, gb_in, fc_in, xlo, xhi, y_chip, y_next, u, e, r, ga, gb, fc_out, part, q):
    n, (rows, lanes) = y_chip.shape[0], xlo.shape[1:]
    halves = lanes // LANES
    cut = [pl.ds(LANES * h, LANES) for h in range(halves)]
    ok = inside(place, n, rows, xsize, ysize)
    del u_in, e_in, r_in, ga_in, gb_in, fc_in
    for side, low, base in ((xlo, True, 0), (xhi, False, n + PX)):
        for i in range(PX):
            good = ok(base + i, PY, rows)
            for h in range(halves):
                re, im, cc, c_here, r_here = plane_cells(side, low, i, h)
                halo(re, im, cc, good, u, ga, gb, r, base + i, h, PY, c_here, r_here)
    low, high = PY - 4, PY + rows - 4
    good_lo, good_hi = ok(PX, 0, 8), ok(PX, PY + rows, 8)
    even = is_even(place, (8, LANES))

    def strips(x, carry):
        for h in range(halves):
            chip, other = y_chip[x, :, cut[h]], y_next[x, :, cut[h]]
            lo, hi = jnp.where(even, other, chip), jnp.where(even, chip, other)
            for tile, good, row, shifts in ((lo, good_lo, 0, (5, 2, 0)), (hi, good_hi, PY + rows, (0, 5, 2))):
                re, im, cc = [pltpu.roll(tile, shift, 0) if shift else tile for shift in shifts]
                halo(re, im, cc, good, u, ga, gb, r, x + PX, h, row, True, True)
        return carry

    lax.fori_loop(0, n, strips, 0, unroll=4)
    for x in (PX - 2, PX - 1, PX, n + PX - 1, n + PX, n + PX + 1):
        second(u, ga, gb, e, x, PY, rows, 1.0, True)

    def middle(x, carry):
        for row in (low, high):
            second(u, ga, gb, e, x, row, 8, 1.0, True)
        return carry

    lax.fori_loop(PX + 1, n + PX - 1, middle, 0, unroll=3)
    for x in (PX - 1, PX, PX + 1, n + PX - 2, n + PX - 1, n + PX):
        finish(e, r, x, PY + 4, rows - 8, ok(x, PY + 4, rows - 8))
    row = lax.broadcasted_iota(jnp.int32, (8, LANES), 0)
    good_low, good_high = ok(PX, low, 8) & (row < 6), ok(PX, high, 8) & (row >= 2)

    def last(x, carry):
        finish(e, r, x, low, 8, good_low)
        finish(e, r, x, high, 8, good_high)
        return carry

    lax.fori_loop(PX + 2, n + PX - 2, last, 0, unroll=4)
    m = n // 2 - 4

    def coarse(i, carry):
        x = 2 * i + PX + 3
        for k in (0, 1):
            for h in range(halves):
                for j, row in ((0, PY - 1), (8, PY + rows - 7)):
                    at = pl.ds(row, 8)
                    part[k, i, pl.ds(j, 8), cut[h]] = (r[k, x, h, at, :] + r[k, x + 3, h, at, :]) + 3.0 * (
                        r[k, x + 1, h, at, :] + r[k, x + 2, h, at, :]
                    )
        return carry

    lax.fori_loop(0, m, coarse, 0, unroll=4)
    w = weights(lanes, lanes)
    for k in (0, 1):
        q[k] = exact_dot(part[k], w)
        for row, start in ((0, 0), (rows // 2 - 2, 10)):
            four = [q[k, :, pl.ds(start + j, 2, 2), :] for j in range(4)]
            fc_out[k, pl.ds(2, m), pl.ds(row, 2), :] = (four[0] + four[3]) + 3.0 * (four[1] + four[2])


def pack_corners_kernel(place, xlo, xhi, chip, other):
    rows = xlo.shape[1]
    even = is_even(place, (4, xlo.shape[2]))
    for side, base in ((xlo, 0), (xhi, 8)):
        for j in range(8):
            first, last = side[j, pl.ds(0, 4), :], side[j, pl.ds(rows - 4, 4), :]
            chip[base + j], other[base + j] = jnp.where(even, last, first), jnp.where(even, first, last)


def corners_kernel(xsize, ysize, n, rows, place, u_in, e_in, r_in, ga_in, gb_in, fc_in, c_chip, c_next, u, e, r, ga, gb, fc_out, t, part):
    halves = c_chip.shape[2] // LANES
    even = is_even(place, (4, LANES))
    ok = inside(place, n, rows, xsize, ysize)
    del u_in, e_in, r_in, ga_in, gb_in, fc_in
    low, high = PY - 4, PY + rows - 4
    for first, low_planes, base in ((0, True, 0), (8, False, n + PX)):
        chip, other = c_chip.at[pl.ds(first, 8)], c_next.at[pl.ds(first, 8)]
        for i in range(PX):
            for h in range(halves):
                one, two = plane_cells(chip, low_planes, i, h), plane_cells(other, low_planes, i, h)
                for row, (p, q) in ((PY - 4, (two, one)), (PY + rows, (one, two))):
                    re, im, cc = [None if v is None else jnp.where(even, v, w) for v, w in zip(p[:3], q[:3])]
                    halo(re, im, cc, ok(base + i, row, 4), u, ga, gb, r, base + i, h, row, *one[3:])
    for x in (PX - 2, PX - 1, PX, n + PX - 1, n + PX, n + PX + 1):
        for row in (low, high):
            second(u, ga, gb, e, x, row, 8, 1.0, True)
    for x in (PX - 1, PX, PX + 1, n + PX - 2, n + PX - 1, n + PX):
        for row in (low, high):
            finish(e, r, x, row, 8, ok(x, row, 8))
    planes = (0, 1, n // 2 - 2, n // 2 - 1)
    w = weights(part.shape[3], part.shape[3])
    for k in (0, 1):
        for j, i in enumerate(planes):
            restrict_xy(r, t, part, j, 2 * i + PX - 1, PY - 1, rows // 2, k, (low, rows + 8))
        val = exact_dot(part[k], w)
        for j, i in enumerate(planes):
            fc_out[k, i] = val[j]


def iterate_kernel(u, e, out):
    n, rows = out.shape[1:3]
    at = pl.ds(PY, rows)

    def step(x, carry):
        for k in (0, 1):
            for h in range(u.shape[2]):
                out[k, x, :, pl.ds(LANES * h, LANES)] = e[k, x + PX, h, at, :] + 0.8 * u[k, x + PX, h, at, :]
        return carry

    lax.fori_loop(0, n, step, 0, unroll=2)


def whole_level(cells, u, e, r, ga, gb, planes, used, row, rows, scale, full, ok, u_put):
    first, count = used
    for x in range(planes):
        at = pl.ds(first, count)
        point(cells(0, x, at), cells(1, x, at), cells(2, x, at), scale, ok(x, first, count), u, ga, gb, x, 0, first)
    at = pl.ds(row, rows)
    for x in range(1, planes - 1):
        second(u, ga, gb, e, x, row, rows, scale, full)
        u_put(x)
    for x in range(2, planes - 2):
        good = ok(x, row, rows)
        for k in (0, 1):
            s = around(e, k, x, row, rows, full)[0] * (1.0 / scale)
            r[k, x, 0, at, :] = jnp.where(good, 0.04 * cells(k, x, at) + s, 0.0)


def rows_kernel(place, xlo, fc, xhi, chip, other):
    halo, n, rows = xlo.shape[1], fc.shape[1], fc.shape[2]
    row = lax.broadcasted_iota(jnp.int32, (8, LANES), 0)
    even = is_even(place, (8, LANES))
    for src, base, count in ((xlo, 0, halo), (fc, halo, n), (xhi, n + halo, halo)):
        for i in range(count):
            made = []
            for start, own in ((0, row < 5), (rows - 8, row >= 3)):
                re, im, cc = [src[k, i, pl.ds(start, 8), :] for k in range(3)]
                made.append((jnp.where(own, re, pltpu.roll(cc, 5, 0)), jnp.where(own, im, pltpu.roll(cc, 2, 0))))
            for k, (first, last) in enumerate(zip(*made)):
                chip[k, base + i], other[k, base + i] = jnp.where(even, last, first), jnp.where(even, first, last)


def middle_kernel(halo, over, xsize, ysize, place, fc_own, xlo, xhi, y_chip, y_next, u_out, fc_out, fc, ga, gb, u, e, r, t, part, part_c):
    n, rows = fc_own.shape[1:3]
    planes = n + 2 * halo
    for k in range(3):
        for src, x, count in ((xlo, 0, halo), (fc_own, halo, n), (xhi, n + halo, halo)):
            fc[k, pl.ds(x, count), 0, pl.ds(8, rows), :] = src[k]
    row = lax.broadcasted_iota(jnp.int32, (8, LANES), 0)
    even = is_even(place, (8, LANES))
    for x in range(planes):
        chip, other = [y_chip[k, x] for k in (0, 1)], [y_next[k, x] for k in (0, 1)]
        for start, split, p, q in ((0, 6, other, chip), (8 + rows, 3, chip, other)):
            at = pl.ds(start, 8)
            one, two = [jnp.where(even, v, w) for v, w in zip(p, q)]
            fc[0, x, 0, at, :], fc[1, x, 0, at, :] = one, two
            fc[2, x, 0, at, :] = jnp.where(row < split, pltpu.roll(one, 3, 0), pltpu.roll(two, 6, 0))
    x0, y0 = place[0] * n - halo, place[1] * rows - 8

    def ok(x, row, count):
        gx = x + x0
        return rows_inside((count, LANES), y0 + row, ysize) & ((gx >= 0) & (gx < xsize))

    def u_put(x):
        if halo <= x < n + halo:
            at = pl.ds(8, rows)
            for k in (0, 1):
                u_out[k, x - halo] = e[k, x, 0, at, :] + 0.8 * u[k, x, 0, at, :]

    def cells(k, x, at):
        return fc[k, x, 0, at, :]

    whole_level(cells, u, e, r, ga, gb, planes, (0, rows + 16), 4, rows + 8, 4.0, True, ok, u_put)
    width = n // 2 + 2 * over
    pairs = width // 2
    for i in range(width):
        x, row = 2 * i + halo - 1 - 2 * over, 7 - 2 * over
        for k in (0, 1):
            restrict_xy(r, t, part, i, x, row, width, k, (4, rows + 8))
        add_pairs(fc[2, x + 1, 0], fc[2, x + 2, 0], t, 0, part_c.at[i % 2], i // 2, row + 1, width)
    two = [(part.at[k], part_c.at[k], LANES // 2 * k) for k in (0, 1)]
    fc_out[pl.ds(0, width)] = sum(exact_dot(p[...], weights(LANES, LANES, shift=s)) for p, _, s in two)[:, :width]
    fc_out[pl.ds(width, pairs)] = sum(exact_dot(p[...], weights(LANES, LANES, True, s)) for _, p, s in two)[:, :width]


def coarse_kernel(n, sweeps, xsize, ysize, zsize, place, fc_own, xlo, xhi, y_chip, y_next, u_out, v_out, fc, ga, gb, u, e, r, t, part, part_c, gc, gd, v, w):
    m = n // 2
    planes = n + 18
    for src, x, first, count in ((xlo, 0, 0, 8), (fc_own, 8, 0, n + 2), (xhi, n + 10, 0, 8), (xlo, planes, 8, 4), (fc_own, planes + 4, n + 2, m + 1), (xhi, planes + m + 5, 8, 4)):
        fc[pl.ds(x, count), 0, pl.ds(15, n + 2), :] = src[pl.ds(first, count)]
    even = is_even(place, (8, LANES))
    for x in range(fc.shape[0]):
        chip, other = y_chip[x], y_next[x]
        fc[x, 0, pl.ds(7, 8), :], fc[x, 0, pl.ds(n + 17, 8), :] = jnp.where(even, other, chip), jnp.where(even, chip, other)
    lane = lax.broadcasted_iota(jnp.int32, (1, LANES), 1)

    def cells(k, x, at):
        val = fc[planes + x // 2 if k == 2 else x, 0, at, :]
        return pltpu.roll(val, LANES - zsize, 1) if k == 1 or (k == 2 and x % 2) else val

    def inside(x0, y0, xs, ys, zs):
        def ok(x, row, count):
            gx = x + x0
            here = rows_inside((count, LANES), y0 + row, ys) & (lane < zs)
            return here & ((gx >= 0) & (gx < xs))

        return ok

    def u_put(x):
        if 9 <= x < n + 9:
            at = pl.ds(16, n)
            for k in (0, 1):
                u_out[k, x - 9] = (e[k, x, 0, at, :] + 0.8 * u[k, x, 0, at, :])[:, :zsize]

    ok = inside(place[0] * n - 9, place[1] * n - 16, xsize, ysize, zsize)
    whole_level(cells, u, e, r, ga, gb, planes, (7, n + 18), 8, n + 16, 16.0, False, ok, u_put)
    width = m + 6
    every = pl.ds(8, n + 16)
    for i in range(width):
        for k in (0, 1):
            restrict_xy(r, t, part, i, 2 * i + 2, 9, width, k, (8, n + 16))
        t[0, 0, every, :] = cells(2, 2 * i + 3, every) + cells(2, 2 * i + 4, every)
        part_c[i, pl.ds(0, width), :] = t[0, 0, pl.ds(10, width, 2), :] + t[0, 0, pl.ds(11, width, 2), :]
    w_full = weights(LANES, zsize)
    f = [exact_dot(part[k], w_full) for k in (0, 1)] + [exact_dot(part_c[...], weights(LANES, zsize, True))]
    ok = inside(place[0] * m - 3, place[1] * m - 3, xsize // 2, ysize // 2, zsize // 2)
    for x in range(width):
        point(f[0][x], f[1][x], f[2][x], 64.0, ok(x, 0, 16), v, gc, gd, x, 0, 0)
    old = v
    for sweep in range(1, sweeps):
        new = w.at[sweep % 2]
        for x in range(sweep, width - sweep):
            at = pl.ds(1, m + 4)
            s = [around(old, k, x, 1, m + 4, False)[0] for k in (0, 1)]
            d = divided(*s, gc[x, 0, at, :] * (1.0 / 64.0), gd[x, 0, at, :] * (1.0 / 64.0))
            for k in (0, 1):
                val = 0.2 * old[k, x, 0, at, :] + v[k, x, 0, at, :] + d[k]
                if sweep < sweeps - 1:
                    new[k, x, 0, at, :] = val
                else:
                    v_out[k, x - 3] = val[2 : 2 + m, : zsize // 2]
        old = new


def body(source, wavenumber_sq):
    f32 = jnp.float32
    xdev, ydev = lax.axis_size("gx"), lax.axis_size("gy")
    place = jnp.stack([lax.axis_index("gx"), lax.axis_index("gy")]).astype(jnp.int32)

    def planes_step(first, last):
        before = lax.ppermute(last, "gx", [(i, (i + 1) % xdev) for i in range(xdev)])
        after = lax.ppermute(first, "gx", [((i + 1) % xdev, i) for i in range(xdev)])
        return before, after

    every = [(i, j) for i in range(xdev) for j in range(ydev)]
    number = lambda i, j: i * ydev + j
    on_chip = [(number(i, j), number(i, j ^ 1)) for i, j in every]
    next_chip = [(number(i, j), number(i ^ 1, j) if j in (0, ydev - 1) else number(i, ((j - 1) ^ 1) + 1)) for i, j in every]

    def rows_step(chip, other):
        return lax.ppermute(chip, ("gx", "gy"), on_chip), lax.ppermute(other, ("gx", "gy"), next_chip)

    _, n, rows, lanes = source.shape
    xsize, ysize = n * xdev, rows * ydev
    S = lambda *shape: jax.ShapeDtypeStruct(shape, f32)
    V = lambda *shape: pltpu.VMEM(shape, f32)

    x_first, x_last, y_chip, y_next = pl.pallas_call(
        pack_kernel,
        in_specs=[SMEM] + [pl.BlockSpec(memory_space=pltpu.HBM)] * 2,
        out_specs=[VMEM] * 4,
        out_shape=[S(8, rows, lanes)] * 2 + [S(n, 8, lanes)] * 2,
        scratch_shapes=[V(2, 3, PX, rows, lanes), V(2, 3, n, 8, lanes), pltpu.SemaphoreType.DMA((12,))],
        compiler_params=params(60),
        name="pack_faces",
    )(place, source, wavenumber_sq)
    xlo, xhi = planes_step(x_first, x_last)
    y_chip, y_next = rows_step(y_chip, y_next)
    halves = lanes // LANES
    state = (n + 2 * PX, halves, rows + 2 * PY, LANES)
    part = (n // 2, rows // 2, lanes)
    shapes = [S(2, *state)] * 3 + [S(*state)] * 2 + [S(3, n // 2, rows // 2, lanes // 2)]
    column = V(2, halves, rows + 2 * PY, LANES)
    held = pl.pallas_call(
        inner_kernel,
        in_specs=[VMEM] * 2,
        out_specs=[VMEM] * 6,
        out_shape=shapes,
        scratch_shapes=[column, V(3, *part)],
        compiler_params=params(24),
        cost_estimate=pl.CostEstimate(flops=100_000_000, bytes_accessed=16_000_000, transcendentals=0),
        name="inner_cells",
    )(source, wavenumber_sq)
    xlo, xhi, held = lax.optimization_barrier((xlo, xhi, held))
    c_chip, c_next = rows_step(
        *pl.pallas_call(
            pack_corners_kernel,
            in_specs=[SMEM] + [VMEM] * 2,
            out_specs=[VMEM] * 2,
            out_shape=[S(16, 4, lanes)] * 2,
            compiler_params=params(24),
            name="pack_corners",
        )(place, xlo, xhi)
    )
    in_place = {i + 1: i for i in range(6)}
    held = pl.pallas_call(
        functools.partial(faces_kernel, xsize, ysize),
        in_specs=[SMEM] + [VMEM] * 10,
        out_specs=[VMEM] * 6,
        out_shape=shapes,
        input_output_aliases=in_place,
        scratch_shapes=[V(2, n // 2 - 4, 16, lanes), V(2, n // 2 - 4, 16, lanes // 2)],
        compiler_params=params(24),
        cost_estimate=pl.CostEstimate(flops=50_000_000, bytes_accessed=8_000_000, transcendentals=0),
        name="face_cells",
    )(place, *held, xlo, xhi, y_chip, y_next)
    u, e, _, _, _, fc = pl.pallas_call(
        functools.partial(corners_kernel, xsize, ysize, n, rows),
        in_specs=[SMEM] + [VMEM] * 8,
        out_specs=[VMEM] * 6,
        out_shape=shapes,
        input_output_aliases=in_place,
        scratch_shapes=[column, V(2, 4, rows // 2, lanes)],
        compiler_params=params(24),
        name="corner_cells",
    )(place, *held, c_chip, c_next)
    fine = pl.pallas_call(
        iterate_kernel,
        in_specs=[VMEM] * 2,
        out_specs=VMEM,
        out_shape=S(2, n, rows, lanes),
        compiler_params=params(24),
        cost_estimate=pl.CostEstimate(flops=1_000_000, bytes_accessed=8_000_000, transcendentals=0),
        name="fine_iterate",
    )(u, e)

    n, rows, lanes, xsize, ysize, zsize = n // 2, rows // 2, lanes // 2, xsize // 2, ysize // 2, lanes // 2
    h, over = 5, 1
    xlo, xhi = planes_step(fc[:, :h], fc[:, n - h :])
    chip, other = pl.pallas_call(
        rows_kernel,
        in_specs=[SMEM] + [VMEM] * 3,
        out_specs=[VMEM] * 2,
        out_shape=[S(2, n + 2 * h, 8, lanes)] * 2,
        compiler_params=params(24),
        name="second_rows",
    )(place, xlo, fc, xhi)
    chip, other = rows_step(chip, other)
    state = (n + 2 * h, 1, rows + 16, LANES)
    work = lambda s: [V(*s), V(*s), V(2, *s), V(2, *s), V(2, *s), V(2, 1, *s[2:])]
    width = n // 2 + 2 * over
    second_u, fc = pl.pallas_call(
        functools.partial(middle_kernel, h, over, xsize, ysize),
        in_specs=[SMEM] + [VMEM] * 5,
        out_specs=[VMEM] * 2,
        out_shape=[S(2, n, rows, lanes), S(width + width // 2, width, lanes)],
        scratch_shapes=[V(3, *state)] + work(state) + [V(2, width, 16, LANES), V(2, width // 2, 16, LANES)],
        compiler_params=params(24),
        name="second_level",
    )(place, fc, xlo, xhi, chip, other)

    n, xsize, ysize, zsize = n // 2, xsize // 2, ysize // 2, zsize // 2
    m = n // 2

    def joined(lo, own, hi, cells):
        f = (lo[:n], own[: n + 2], hi[:n])
        c = (lo[n:], own[n + 2 :], hi[n:])
        return jnp.concatenate([a[:, cells] for a in f + c], 0)

    pick = lambda i, j: jnp.concatenate([fc[i : i + n], fc[n + 2 + j : n + 2 + j + m]], 0)
    xlo, xhi = planes_step(pick(2, 1), pick(0, 0))
    first, last = joined(xlo, fc, xhi, slice(2, n + 2)), joined(xlo, fc, xhi, slice(0, n))
    even = place[1] % 2 == 0
    chip, other = rows_step(jnp.where(even, last, first), jnp.where(even, first, last))
    state = (n + 18, 1, 40, LANES)
    small = (m + 6, 1, 16, LANES)
    third, coarse = pl.pallas_call(
        functools.partial(coarse_kernel, n, 4, xsize, ysize, zsize),
        in_specs=[SMEM] + [VMEM] * 5,
        out_specs=[VMEM] * 2,
        out_shape=[S(2, n, n, zsize), S(2, m, m, zsize // 2)],
        scratch_shapes=[V(n + 18 + m + 9, 1, 40, LANES)] + work(state) + [V(2, m + 6, 16, LANES), V(m + 6, 16, LANES)]
        + [V(*small), V(*small), V(2, *small), V(2, 2, *small)],
        compiler_params=params(24),
        name="coarse_levels",
    )(place, fc, xlo, xhi, chip, other)
    return fine, second_u, third, coarse


def solution(mesh):
    placed = (P(None, "gx", "gy", None), P("gx", "gy", None))
    return jax.shard_map(body, mesh=mesh, in_specs=placed, out_specs=(P(None, "gx", "gy", None),) * 4, check_vma=False)
```

```python
import functools
import jax
import jax.numpy as jnp
from jax import lax
from jax.experimental import pallas as pl
from jax.experimental.pallas import tpu as pltpu
from jax.sharding import PartitionSpec as P

DAMPING = 0.8
SHIFT_IMAG = 0.5
LANES = 128
VMEM = pl.BlockSpec(memory_space=pltpu.VMEM)
SMEM = pl.BlockSpec(memory_space=pltpu.SMEM)


def params(mib):
    return pltpu.CompilerParams(vmem_limit_bytes=mib * 1024 * 1024)


def around(ref, k, x, row, rows, full):
    halves = ref.shape[2]
    mid = [ref[k, x, h, pl.ds(row, rows), :] for h in range(halves)]
    up = [pltpu.roll(m, 1, 1) for m in mid]
    down = [pltpu.roll(m, LANES - 1, 1) for m in mid]
    if full:
        lane = lax.broadcasted_iota(jnp.int32, mid[0].shape, 1)
        first, last = lane == 0, lane == LANES - 1
        up = [jnp.where(first, up[h - 1] if h else 0.0, up[h]) for h in range(halves)]
        down = [jnp.where(last, down[h + 1] if h < halves - 1 else 0.0, down[h]) for h in range(halves)]
    sums = []
    for h in range(halves):
        planes = ref[k, x - 1, h, pl.ds(row, rows), :] + ref[k, x + 1, h, pl.ds(row, rows), :]
        sides = ref[k, x, h, pl.ds(row - 1, rows), :] + ref[k, x, h, pl.ds(row + 1, rows), :]
        sums.append((planes + sides) + (up[h] + down[h]))
    return sums


def inverse(c, scale, ok):
    a = 6.0 / scale - c
    b = SHIFT_IMAG * c
    g = DAMPING / (a * a + b * b)
    if ok is not None:
        g = jnp.where(ok, g, 0.0)
    return g * a, g * b


def divided(re, im, a, b):
    return re * a + im * b, im * a - re * b


def point(re, im, c, scale, ok, u, ga, gb, x, h, row):
    a, b = inverse(c, scale, ok)
    at = pl.ds(row, c.shape[0])
    ga[x, h, at, :], gb[x, h, at, :] = a, b
    u[0, x, h, at, :], u[1, x, h, at, :] = divided(re, im, a, b)


def second(u, ga, gb, e, x, row, rows, scale, full):
    s_re, s_im = around(u, 0, x, row, rows, full), around(u, 1, x, row, rows, full)
    at = pl.ds(row, rows)
    for h in range(u.shape[2]):
        a, b = ga[x, h, at, :], gb[x, h, at, :]
        if scale != 1.0:
            a, b = a * (1.0 / scale), b * (1.0 / scale)
        d = divided(s_re[h], s_im[h], a, b)
        for k in (0, 1):
            e[k, x, h, at, :] = 0.4 * u[k, x, h, at, :] + d[k]


def is_even(place, shape):
    return jnp.full(shape, lax.rem(place[1], 2)) == 0


def rows_inside(shape, y0, ysize):
    row = lax.broadcasted_iota(jnp.int32, shape, 0) + y0
    return (row >= 0) & (row < ysize)


def restrict_xy(r, t, out, to, plane, row, rows, k, window):
    at = pl.ds(*window)
    for h in range(r.shape[2]):
        val = (r[k, plane, h, at, :] + r[k, plane + 3, h, at, :]) + 3.0 * (r[k, plane + 1, h, at, :] + r[k, plane + 2, h, at, :])
        t[k, h, at, :] = val
        part = [t[k, h, pl.ds(row + j, rows, 2), :] for j in range(4)]
        out[k, to, pl.ds(0, rows), pl.ds(LANES * h, LANES)] = (part[0] + part[3]) + 3.0 * (part[1] + part[2])


def add_pairs(c0, c1, t, h, out, i, row, rows):
    t[0, h, pl.ds(0, c0.shape[0]), :] = c0 + c1
    val = t[0, h, pl.ds(row, rows, 2), :] + t[0, h, pl.ds(row + 1, rows, 2), :]
    out[i, pl.ds(0, rows), pl.ds(LANES * h, LANES)] = val


def weights(lanes, zsize, mean=False, shift=0):
    z = lax.broadcasted_iota(jnp.int32, (lanes, LANES), 0)
    i = lax.broadcasted_iota(jnp.int32, (lanes, LANES), 1) - shift
    d = z - 2 * i
    inner = (d == 0) | (d == 1)
    if mean:
        w = jnp.where(inner, 0.125, 0.0)
    else:
        w = jnp.where(inner, 3.0 / 512.0, jnp.where((d == -1) | (d == 2), 1.0 / 512.0, 0.0))
    return jnp.where((z < zsize) & (i >= 0) & (i < zsize // 2), w, 0.0).astype(jnp.bfloat16)


def exact_dot(part, w):
    planes, rows, lanes = part.shape
    x = part.reshape(planes * rows, lanes)
    hi = x.astype(jnp.bfloat16)
    rest = x - hi.astype(jnp.float32)
    mid = rest.astype(jnp.bfloat16)
    low = (rest - mid.astype(jnp.float32)).astype(jnp.bfloat16)
    dot = functools.partial(jnp.dot, preferred_element_type=jnp.float32)
    return (dot(hi, w) + (dot(mid, w) + dot(low, w))).reshape(planes, rows, w.shape[1])


PX, PY = 3, 8


def planes_kernel(f, c, x_first, x_last, planes, sems):
    n = c.shape[0]
    copies = []
    for side, x in enumerate((0, n - PX)):
        at = pl.ds(x, PX)
        copies += [(c.at[at], planes.at[side, 2]), (f.at[0, at], planes.at[side, 0]), (f.at[1, at], planes.at[side, 1])]
    copies = [pltpu.make_async_copy(src, dst, sems.at[i]) for i, (src, dst) in enumerate(copies)]
    for copy in copies:
        copy.start()
    for side, out in enumerate((x_first, x_last)):
        for copy in copies[3 * side : 3 * side + 3]:
            copy.wait()
        for j in range(PX):
            a, b = inverse(planes[side, 2, j], 1.0, None)
            out[j], out[PX + j] = divided(planes[side, 0, j], planes[side, 1, j], a, b)
        for j in range(2):
            out[2 * PX + j] = planes[side, 2, j + side]


def first_kernel(place, f, c, u, ga, gb, y_chip, y_next):
    n, rows, lanes = c.shape
    cut = [pl.ds(LANES * h, LANES) for h in range(lanes // LANES)]
    row = lax.broadcasted_iota(jnp.int32, (8, LANES), 0)
    even = is_even(place, (8, LANES))

    def step(x, carry):
        for h, lane in enumerate(cut):
            point(f[0, x, :, lane], f[1, x, :, lane], c[x, :, lane], 1.0, None, u, ga, gb, x + PX, h, PY)
            made = []
            for start, shifts in ((0, (0, 3, 6)), (rows - 8, (3, 6, 0))):
                tiles = [u[k, x + PX, h, pl.ds(PY + start, 8), :] for k in (0, 1)] + [c[x, pl.ds(start, 8), lane]]
                re, im, cc = [pltpu.roll(v, shift, 0) if shift else v for v, shift in zip(tiles, shifts)]
                made.append(jnp.where(row < 3, re, jnp.where(row < 6, im, cc)))
            y_chip[x, :, lane], y_next[x, :, lane] = jnp.where(even, made[1], made[0]), jnp.where(even, made[0], made[1])
        return carry

    lax.fori_loop(0, n, step, 0, unroll=2)


def inner_kernel(f, c, u, ga, gb, e, r, fc_out, t, part):
    n, rows, lanes = c.shape
    halves = lanes // LANES
    at = pl.ds(PY, rows)
    cut = [pl.ds(LANES * h, LANES) for h in range(halves)]

    def middle(x, carry):
        second(u, ga, gb, e, x + PX, PY, rows, 1.0, True)
        return carry

    lax.fori_loop(1, n - 1, middle, 0, unroll=2)
    row = lax.broadcasted_iota(jnp.int32, (rows, LANES), 0)
    full = (row >= 2) & (row < rows - 2)

    def last(x, carry):
        for k in (0, 1):
            s = around(e, k, x + PX, PY, rows, True)
            for h in range(halves):
                r[k, x + PX, h, at, :] = 0.04 * f[k, x, :, cut[h]] + jnp.where(full, s[h], 0.0)
        return carry

    lax.fori_loop(2, n - 2, last, 0, unroll=2)
    for x in (0, 1, n - 2, n - 1):
        for k in (0, 1):
            for h in range(halves):
                r[k, x + PX, h, at, :] = 0.04 * f[k, x, :, cut[h]]

    def pairs(i, carry):
        for h in range(halves):
            add_pairs(c[2 * i, :, cut[h]], c[2 * i + 1, :, cut[h]], t, h, part.at[2], i, 0, rows // 2)
        return carry

    lax.fori_loop(0, n // 2, pairs, 0, unroll=2)

    def coarse(i, carry):
        for k in (0, 1):
            restrict_xy(r, t, part, i, 2 * i + PX - 1, PY - 1, rows // 2, k, (PY, rows))
        return carry

    lax.fori_loop(2, n // 2 - 2, coarse, 0, unroll=2)
    w = weights(lanes, lanes)
    for k in (0, 1):
        fc_out[k, 2 : n // 2 - 2] = exact_dot(part[k, 2 : n // 2 - 2], w)
    fc_out[2] = exact_dot(part[2], weights(lanes, lanes, mean=True))


def inside(place, n, rows, xsize, ysize):
    x0, y0 = place[0] * n - PX, place[1] * rows - PY

    def ok(x, row, count):
        gx = x + x0
        return rows_inside((count, LANES), y0 + row, ysize) & ((gx >= 0) & (gx < xsize))

    return ok


def halo(re, im, cc, good, u, ga, gb, r, x, h, row, c_here, r_here):
    at = pl.ds(row, re.shape[0])
    re, im = jnp.where(good, re, 0.0), jnp.where(good, im, 0.0)
    u[0, x, h, at, :], u[1, x, h, at, :] = re, im
    if c_here:
        a, b = inverse(cc, 1.0, good)
        ga[x, h, at, :], gb[x, h, at, :] = a, b
    if r_here:
        a, b = 0.05 * (6.0 - cc), (0.05 * SHIFT_IMAG) * cc
        r[0, x, h, at, :], r[1, x, h, at, :] = re * a - im * b, im * a + re * b


def finish(e, r, x, row, count, good):
    for k in (0, 1):
        s = around(e, k, x, row, count, True)
        for h in range(e.shape[2]):
            at = pl.ds(row, count)
            r[k, x, h, at, :] = r[k, x, h, at, :] + jnp.where(good, s[h], 0.0)


def plane_cells(side, low, i, h):
    cut = pl.ds(LANES * h, LANES)
    j = i - 1 if low else i
    c_here = 0 <= j < 2
    cc = side[2 * PX + j, :, cut] if c_here else None
    return side[i, :, cut], side[PX + i, :, cut], cc, c_here, i == (PX - 1 if low else 0)


def faces_kernel(xsize, ysize, place, u_in, e_in, r_in, ga_in, gb_in, fc_in, xlo, xhi, y_chip, y_next, u, e, r, ga, gb, fc_out, part, q):
    n, (rows, lanes) = y_chip.shape[0], xlo.shape[1:]
    halves = lanes // LANES
    cut = [pl.ds(LANES * h, LANES) for h in range(halves)]
    ok = inside(place, n, rows, xsize, ysize)
    del u_in, e_in, r_in, ga_in, gb_in, fc_in
    for side, low, base in ((xlo, True, 0), (xhi, False, n + PX)):
        for i in range(PX):
            good = ok(base + i, PY, rows)
            for h in range(halves):
                re, im, cc, c_here, r_here = plane_cells(side, low, i, h)
                halo(re, im, cc, good, u, ga, gb, r, base + i, h, PY, c_here, r_here)
    low, high = PY - 4, PY + rows - 4
    good_lo, good_hi = ok(PX, 0, 8), ok(PX, PY + rows, 8)
    even = is_even(place, (8, LANES))

    def strips(x, carry):
        for h in range(halves):
            chip, other = y_chip[x, :, cut[h]], y_next[x, :, cut[h]]
            lo, hi = jnp.where(even, other, chip), jnp.where(even, chip, other)
            for tile, good, row, shifts in ((lo, good_lo, 0, (5, 2, 0)), (hi, good_hi, PY + rows, (0, 5, 2))):
                re, im, cc = [pltpu.roll(tile, shift, 0) if shift else tile for shift in shifts]
                halo(re, im, cc, good, u, ga, gb, r, x + PX, h, row, True, True)
        return carry

    lax.fori_loop(0, n, strips, 0, unroll=4)
    for x in (PX - 2, PX - 1, PX, n + PX - 1, n + PX, n + PX + 1):
        second(u, ga, gb, e, x, PY, rows, 1.0, True)

    def middle(x, carry):
        for row in (low, high):
            second(u, ga, gb, e, x, row, 8, 1.0, True)
        return carry

    lax.fori_loop(PX + 1, n + PX - 1, middle, 0, unroll=3)
    for x in (PX - 1, PX, PX + 1, n + PX - 2, n + PX - 1, n + PX):
        finish(e, r, x, PY + 4, rows - 8, ok(x, PY + 4, rows - 8))
    row = lax.broadcasted_iota(jnp.int32, (8, LANES), 0)
    good_low, good_high = ok(PX, low, 8) & (row < 6), ok(PX, high, 8) & (row >= 2)

    def last(x, carry):
        finish(e, r, x, low, 8, good_low)
        finish(e, r, x, high, 8, good_high)
        return carry

    lax.fori_loop(PX + 2, n + PX - 2, last, 0, unroll=4)
    m = n // 2 - 4

    def coarse(i, carry):
        x = 2 * i + PX + 3
        for k in (0, 1):
            for h in range(halves):
                for j, row in ((0, PY - 1), (8, PY + rows - 7)):
                    at = pl.ds(row, 8)
                    part[k, i, pl.ds(j, 8), cut[h]] = (r[k, x, h, at, :] + r[k, x + 3, h, at, :]) + 3.0 * (
                        r[k, x + 1, h, at, :] + r[k, x + 2, h, at, :]
                    )
        return carry

    lax.fori_loop(0, m, coarse, 0, unroll=4)
    w = weights(lanes, lanes)
    for k in (0, 1):
        q[k] = exact_dot(part[k], w)
        for row, start in ((0, 0), (rows // 2 - 2, 10)):
            four = [q[k, :, pl.ds(start + j, 2, 2), :] for j in range(4)]
            fc_out[k, pl.ds(2, m), pl.ds(row, 2), :] = (four[0] + four[3]) + 3.0 * (four[1] + four[2])


def pack_corners_kernel(place, xlo, xhi, chip, other):
    rows = xlo.shape[1]
    even = is_even(place, (4, xlo.shape[2]))
    for side, base in ((xlo, 0), (xhi, 8)):
        for j in range(8):
            first, last = side[j, pl.ds(0, 4), :], side[j, pl.ds(rows - 4, 4), :]
            chip[base + j], other[base + j] = jnp.where(even, last, first), jnp.where(even, first, last)


def corners_kernel(xsize, ysize, n, rows, place, u_in, e_in, r_in, ga_in, gb_in, fc_in, c_chip, c_next, u, e, r, ga, gb, fc_out, t, part):
    halves = c_chip.shape[2] // LANES
    even = is_even(place, (4, LANES))
    ok = inside(place, n, rows, xsize, ysize)
    del u_in, e_in, r_in, ga_in, gb_in, fc_in
    low, high = PY - 4, PY + rows - 4
    for first, low_planes, base in ((0, True, 0), (8, False, n + PX)):
        chip, other = c_chip.at[pl.ds(first, 8)], c_next.at[pl.ds(first, 8)]
        for i in range(PX):
            for h in range(halves):
                one, two = plane_cells(chip, low_planes, i, h), plane_cells(other, low_planes, i, h)
                for row, (p, q) in ((PY - 4, (two, one)), (PY + rows, (one, two))):
                    re, im, cc = [None if v is None else jnp.where(even, v, w) for v, w in zip(p[:3], q[:3])]
                    halo(re, im, cc, ok(base + i, row, 4), u, ga, gb, r, base + i, h, row, *one[3:])
    for x in (PX - 2, PX - 1, PX, n + PX - 1, n + PX, n + PX + 1):
        for row in (low, high):
            second(u, ga, gb, e, x, row, 8, 1.0, True)
    for x in (PX - 1, PX, PX + 1, n + PX - 2, n + PX - 1, n + PX):
        for row in (low, high):
            finish(e, r, x, row, 8, ok(x, row, 8))
    planes = (0, 1, n // 2 - 2, n // 2 - 1)
    w = weights(part.shape[3], part.shape[3])
    for k in (0, 1):
        for j, i in enumerate(planes):
            restrict_xy(r, t, part, j, 2 * i + PX - 1, PY - 1, rows // 2, k, (low, rows + 8))
        val = exact_dot(part[k], w)
        for j, i in enumerate(planes):
            fc_out[k, i] = val[j]


def iterate_kernel(u, e, out):
    n, rows = out.shape[1:3]
    at = pl.ds(PY, rows)

    def step(x, carry):
        for k in (0, 1):
            for h in range(u.shape[2]):
                out[k, x, :, pl.ds(LANES * h, LANES)] = e[k, x + PX, h, at, :] + 0.8 * u[k, x + PX, h, at, :]
        return carry

    lax.fori_loop(0, n, step, 0, unroll=2)


def whole_level(cells, u, e, r, ga, gb, planes, used, row, rows, scale, full, ok, u_put):
    first, count = used
    for x in range(planes):
        at = pl.ds(first, count)
        point(cells(0, x, at), cells(1, x, at), cells(2, x, at), scale, ok(x, first, count), u, ga, gb, x, 0, first)
    at = pl.ds(row, rows)
    for x in range(1, planes - 1):
        second(u, ga, gb, e, x, row, rows, scale, full)
        u_put(x)
    for x in range(2, planes - 2):
        good = ok(x, row, rows)
        for k in (0, 1):
            s = around(e, k, x, row, rows, full)[0] * (1.0 / scale)
            r[k, x, 0, at, :] = jnp.where(good, 0.04 * cells(k, x, at) + s, 0.0)


def rows_kernel(place, xlo, fc, xhi, chip, other):
    halo, n, rows = xlo.shape[1], fc.shape[1], fc.shape[2]
    row = lax.broadcasted_iota(jnp.int32, (8, LANES), 0)
    even = is_even(place, (8, LANES))
    for src, base, count in ((xlo, 0, halo), (fc, halo, n), (xhi, n + halo, halo)):
        for i in range(count):
            made = []
            for start, own in ((0, row < 5), (rows - 8, row >= 3)):
                re, im, cc = [src[k, i, pl.ds(start, 8), :] for k in range(3)]
                made.append((jnp.where(own, re, pltpu.roll(cc, 5, 0)), jnp.where(own, im, pltpu.roll(cc, 2, 0))))
            for k, (first, last) in enumerate(zip(*made)):
                chip[k, base + i], other[k, base + i] = jnp.where(even, last, first), jnp.where(even, first, last)


def middle_kernel(halo, over, xsize, ysize, place, fc_own, xlo, xhi, y_chip, y_next, u_out, fc_out, fc, ga, gb, u, e, r, t, part, part_c):
    n, rows = fc_own.shape[1:3]
    planes = n + 2 * halo
    for k in range(3):
        for src, x, count in ((xlo, 0, halo), (fc_own, halo, n), (xhi, n + halo, halo)):
            fc[k, pl.ds(x, count), 0, pl.ds(8, rows), :] = src[k]
    row = lax.broadcasted_iota(jnp.int32, (8, LANES), 0)
    even = is_even(place, (8, LANES))
    for x in range(planes):
        chip, other = [y_chip[k, x] for k in (0, 1)], [y_next[k, x] for k in (0, 1)]
        for start, split, p, q in ((0, 6, other, chip), (8 + rows, 3, chip, other)):
            at = pl.ds(start, 8)
            one, two = [jnp.where(even, v, w) for v, w in zip(p, q)]
            fc[0, x, 0, at, :], fc[1, x, 0, at, :] = one, two
            fc[2, x, 0, at, :] = jnp.where(row < split, pltpu.roll(one, 3, 0), pltpu.roll(two, 6, 0))
    x0, y0 = place[0] * n - halo, place[1] * rows - 8

    def ok(x, row, count):
        gx = x + x0
        return rows_inside((count, LANES), y0 + row, ysize) & ((gx >= 0) & (gx < xsize))

    def u_put(x):
        if halo <= x < n + halo:
            at = pl.ds(8, rows)
            for k in (0, 1):
                u_out[k, x - halo] = e[k, x, 0, at, :] + 0.8 * u[k, x, 0, at, :]

    def cells(k, x, at):
        return fc[k, x, 0, at, :]

    whole_level(cells, u, e, r, ga, gb, planes, (0, rows + 16), 4, rows + 8, 4.0, True, ok, u_put)
    width = n // 2 + 2 * over
    pairs = width // 2
    for i in range(width):
        x, row = 2 * i + halo - 1 - 2 * over, 7 - 2 * over
        for k in (0, 1):
            restrict_xy(r, t, part, i, x, row, width, k, (4, rows + 8))
        add_pairs(fc[2, x + 1, 0], fc[2, x + 2, 0], t, 0, part_c.at[i % 2], i // 2, row + 1, width)
    two = [(part.at[k], part_c.at[k], LANES // 2 * k) for k in (0, 1)]
    fc_out[pl.ds(0, width)] = sum(exact_dot(p[...], weights(LANES, LANES, shift=s)) for p, _, s in two)[:, :width]
    fc_out[pl.ds(width, pairs)] = sum(exact_dot(p[...], weights(LANES, LANES, True, s)) for _, p, s in two)[:, :width]


def coarse_kernel(n, sweeps, xsize, ysize, zsize, place, fc_own, xlo, xhi, y_chip, y_next, u_out, v_out, fc, ga, gb, u, e, r, t, part, part_c, gc, gd, v, w):
    m = n // 2
    planes = n + 18
    for src, x, first, count in ((xlo, 0, 0, 8), (fc_own, 8, 0, n + 2), (xhi, n + 10, 0, 8), (xlo, planes, 8, 4), (fc_own, planes + 4, n + 2, m + 1), (xhi, planes + m + 5, 8, 4)):
        fc[pl.ds(x, count), 0, pl.ds(15, n + 2), :] = src[pl.ds(first, count)]
    even = is_even(place, (8, LANES))
    for x in range(fc.shape[0]):
        chip, other = y_chip[x], y_next[x]
        fc[x, 0, pl.ds(7, 8), :], fc[x, 0, pl.ds(n + 17, 8), :] = jnp.where(even, other, chip), jnp.where(even, chip, other)
    lane = lax.broadcasted_iota(jnp.int32, (1, LANES), 1)

    def cells(k, x, at):
        val = fc[planes + x // 2 if k == 2 else x, 0, at, :]
        return pltpu.roll(val, LANES - zsize, 1) if k == 1 or (k == 2 and x % 2) else val

    def inside(x0, y0, xs, ys, zs):
        def ok(x, row, count):
            gx = x + x0
            here = rows_inside((count, LANES), y0 + row, ys) & (lane < zs)
            return here & ((gx >= 0) & (gx < xs))

        return ok

    def u_put(x):
        if 9 <= x < n + 9:
            at = pl.ds(16, n)
            for k in (0, 1):
                u_out[k, x - 9] = (e[k, x, 0, at, :] + 0.8 * u[k, x, 0, at, :])[:, :zsize]

    ok = inside(place[0] * n - 9, place[1] * n - 16, xsize, ysize, zsize)
    whole_level(cells, u, e, r, ga, gb, planes, (7, n + 18), 8, n + 16, 16.0, False, ok, u_put)
    width = m + 6
    every = pl.ds(8, n + 16)
    for i in range(width):
        for k in (0, 1):
            restrict_xy(r, t, part, i, 2 * i + 2, 9, width, k, (8, n + 16))
        t[0, 0, every, :] = cells(2, 2 * i + 3, every) + cells(2, 2 * i + 4, every)
        part_c[i, pl.ds(0, width), :] = t[0, 0, pl.ds(10, width, 2), :] + t[0, 0, pl.ds(11, width, 2), :]
    w_full = weights(LANES, zsize)
    f = [exact_dot(part[k], w_full) for k in (0, 1)] + [exact_dot(part_c[...], weights(LANES, zsize, True))]
    ok = inside(place[0] * m - 3, place[1] * m - 3, xsize // 2, ysize // 2, zsize // 2)
    for x in range(width):
        point(f[0][x], f[1][x], f[2][x], 64.0, ok(x, 0, 16), v, gc, gd, x, 0, 0)
    old = v
    for sweep in range(1, sweeps):
        new = w.at[sweep % 2]
        for x in range(sweep, width - sweep):
            at = pl.ds(1, m + 4)
            s = [around(old, k, x, 1, m + 4, False)[0] for k in (0, 1)]
            d = divided(*s, gc[x, 0, at, :] * (1.0 / 64.0), gd[x, 0, at, :] * (1.0 / 64.0))
            for k in (0, 1):
                val = 0.2 * old[k, x, 0, at, :] + v[k, x, 0, at, :] + d[k]
                if sweep < sweeps - 1:
                    new[k, x, 0, at, :] = val
                else:
                    v_out[k, x - 3] = val[2 : 2 + m, : zsize // 2]
        old = new


def body(source, wavenumber_sq):
    f32 = jnp.float32
    xdev, ydev = lax.axis_size("gx"), lax.axis_size("gy")
    place = jnp.stack([lax.axis_index("gx"), lax.axis_index("gy")]).astype(jnp.int32)

    def planes_step(first, last):
        before = lax.ppermute(last, "gx", [(i, (i + 1) % xdev) for i in range(xdev)])
        after = lax.ppermute(first, "gx", [((i + 1) % xdev, i) for i in range(xdev)])
        return before, after

    every = [(i, j) for i in range(xdev) for j in range(ydev)]
    number = lambda i, j: i * ydev + j
    on_chip = [(number(i, j), number(i, j ^ 1)) for i, j in every]
    next_chip = [(number(i, j), number(i ^ 1, j) if j in (0, ydev - 1) else number(i, ((j - 1) ^ 1) + 1)) for i, j in every]

    def rows_step(chip, other):
        return lax.ppermute(chip, ("gx", "gy"), on_chip), lax.ppermute(other, ("gx", "gy"), next_chip)

    _, n, rows, lanes = source.shape
    xsize, ysize = n * xdev, rows * ydev
    S = lambda *shape: jax.ShapeDtypeStruct(shape, f32)
    V = lambda *shape: pltpu.VMEM(shape, f32)

    halves = lanes // LANES
    state = (n + 2 * PX, halves, rows + 2 * PY, LANES)
    part = (n // 2, rows // 2, lanes)
    two, one, coarser = S(2, *state), S(*state), S(3, n // 2, rows // 2, lanes // 2)
    column = V(2, halves, rows + 2 * PY, LANES)
    x_first, x_last = pl.pallas_call(
        planes_kernel,
        in_specs=[pl.BlockSpec(memory_space=pltpu.HBM)] * 2,
        out_specs=[VMEM] * 2,
        out_shape=[S(8, rows, lanes)] * 2,
        scratch_shapes=[V(2, 3, PX, rows, lanes), pltpu.SemaphoreType.DMA((6,))],
        compiler_params=params(60),
        name="pack_planes",
    )(source, wavenumber_sq)
    source, wavenumber_sq, x_first, x_last = lax.optimization_barrier((source, wavenumber_sq, x_first, x_last))
    xlo, xhi = planes_step(x_first, x_last)
    u, ga, gb, y_chip, y_next = pl.pallas_call(
        first_kernel,
        in_specs=[SMEM] + [VMEM] * 2,
        out_specs=[VMEM] * 5,
        out_shape=[two, one, one] + [S(n, 8, lanes)] * 2,
        compiler_params=params(24),
        cost_estimate=pl.CostEstimate(flops=30_000_000, bytes_accessed=8_000_000, transcendentals=0),
        name="first_iterate",
    )(place, source, wavenumber_sq)
    y_chip, y_next = rows_step(y_chip, y_next)
    e, r, fc = pl.pallas_call(
        inner_kernel,
        in_specs=[VMEM] * 5,
        out_specs=[VMEM] * 3,
        out_shape=[two, two, coarser],
        scratch_shapes=[column, V(3, *part)],
        compiler_params=params(24),
        cost_estimate=pl.CostEstimate(flops=70_000_000, bytes_accessed=16_000_000, transcendentals=0),
        name="inner_cells",
    )(source, wavenumber_sq, u, ga, gb)
    held = (u, e, r, ga, gb, fc)
    shapes = [two] * 3 + [one] * 2 + [coarser]
    xlo, xhi, held = lax.optimization_barrier((xlo, xhi, held))
    c_chip, c_next = rows_step(
        *pl.pallas_call(
            pack_corners_kernel,
            in_specs=[SMEM] + [VMEM] * 2,
            out_specs=[VMEM] * 2,
            out_shape=[S(16, 4, lanes)] * 2,
            compiler_params=params(24),
            name="pack_corners",
        )(place, xlo, xhi)
    )
    in_place = {i + 1: i for i in range(6)}
    held = pl.pallas_call(
        functools.partial(faces_kernel, xsize, ysize),
        in_specs=[SMEM] + [VMEM] * 10,
        out_specs=[VMEM] * 6,
        out_shape=shapes,
        input_output_aliases=in_place,
        scratch_shapes=[V(2, n // 2 - 4, 16, lanes), V(2, n // 2 - 4, 16, lanes // 2)],
        compiler_params=params(24),
        cost_estimate=pl.CostEstimate(flops=50_000_000, bytes_accessed=8_000_000, transcendentals=0),
        name="face_cells",
    )(place, *held, xlo, xhi, y_chip, y_next)
    u, e, _, _, _, fc = pl.pallas_call(
        functools.partial(corners_kernel, xsize, ysize, n, rows),
        in_specs=[SMEM] + [VMEM] * 8,
        out_specs=[VMEM] * 6,
        out_shape=shapes,
        input_output_aliases=in_place,
        scratch_shapes=[column, V(2, 4, rows // 2, lanes)],
        compiler_params=params(24),
        name="corner_cells",
    )(place, *held, c_chip, c_next)
    fine_shape = S(2, n, rows, lanes)
    n, rows, lanes, xsize, ysize, zsize = n // 2, rows // 2, lanes // 2, xsize // 2, ysize // 2, lanes // 2
    h, over = 5, 1
    xlo, xhi = planes_step(fc[:, :h], fc[:, n - h :])
    fine = pl.pallas_call(
        iterate_kernel,
        in_specs=[VMEM] * 2,
        out_specs=VMEM,
        out_shape=fine_shape,
        compiler_params=params(24),
        cost_estimate=pl.CostEstimate(flops=1_000_000, bytes_accessed=8_000_000, transcendentals=0),
        name="fine_iterate",
    )(u, e)
    xlo, xhi, fine = lax.optimization_barrier((xlo, xhi, fine))
    chip, other = pl.pallas_call(
        rows_kernel,
        in_specs=[SMEM] + [VMEM] * 3,
        out_specs=[VMEM] * 2,
        out_shape=[S(2, n + 2 * h, 8, lanes)] * 2,
        compiler_params=params(24),
        name="second_rows",
    )(place, xlo, fc, xhi)
    chip, other = rows_step(chip, other)
    state = (n + 2 * h, 1, rows + 16, LANES)
    work = lambda s: [V(*s), V(*s), V(2, *s), V(2, *s), V(2, *s), V(2, 1, *s[2:])]
    width = n // 2 + 2 * over
    second_u, fc = pl.pallas_call(
        functools.partial(middle_kernel, h, over, xsize, ysize),
        in_specs=[SMEM] + [VMEM] * 5,
        out_specs=[VMEM] * 2,
        out_shape=[S(2, n, rows, lanes), S(width + width // 2, width, lanes)],
        scratch_shapes=[V(3, *state)] + work(state) + [V(2, width, 16, LANES), V(2, width // 2, 16, LANES)],
        compiler_params=params(24),
        name="second_level",
    )(place, fc, xlo, xhi, chip, other)

    n, xsize, ysize, zsize = n // 2, xsize // 2, ysize // 2, zsize // 2
    m = n // 2

    def joined(lo, own, hi, cells):
        f = (lo[:n], own[: n + 2], hi[:n])
        c = (lo[n:], own[n + 2 :], hi[n:])
        return jnp.concatenate([a[:, cells] for a in f + c], 0)

    pick = lambda i, j: jnp.concatenate([fc[i : i + n], fc[n + 2 + j : n + 2 + j + m]], 0)
    xlo, xhi = planes_step(pick(2, 1), pick(0, 0))
    first, last = joined(xlo, fc, xhi, slice(2, n + 2)), joined(xlo, fc, xhi, slice(0, n))
    even = place[1] % 2 == 0
    chip, other = rows_step(jnp.where(even, last, first), jnp.where(even, first, last))
    state = (n + 18, 1, 40, LANES)
    small = (m + 6, 1, 16, LANES)
    third, coarse = pl.pallas_call(
        functools.partial(coarse_kernel, n, 4, xsize, ysize, zsize),
        in_specs=[SMEM] + [VMEM] * 5,
        out_specs=[VMEM] * 2,
        out_shape=[S(2, n, n, zsize), S(2, m, m, zsize // 2)],
        scratch_shapes=[V(n + 18 + m + 9, 1, 40, LANES)] + work(state) + [V(2, m + 6, 16, LANES), V(m + 6, 16, LANES)]
        + [V(*small), V(*small), V(2, *small), V(2, 2, *small)],
        compiler_params=params(24),
        name="coarse_levels",
    )(place, fc, xlo, xhi, chip, other)
    return fine, second_u, third, coarse


def solution(mesh):
    placed = (P(None, "gx", "gy", None), P("gx", "gy", None))
    return jax.shard_map(body, mesh=mesh, in_specs=placed, out_specs=(P(None, "gx", "gy", None),) * 4, check_vma=False)
```

```python
import functools
import jax
import jax.numpy as jnp
from jax import lax
from jax.experimental import pallas as pl
from jax.experimental.pallas import tpu as pltpu
from jax.sharding import PartitionSpec as P

DAMPING = 0.8
SHIFT_IMAG = 0.5
LANES = 128
VMEM = pl.BlockSpec(memory_space=pltpu.VMEM)
SMEM = pl.BlockSpec(memory_space=pltpu.SMEM)
ANY = pl.BlockSpec(memory_space=pl.ANY)


def params(mib):
    return pltpu.CompilerParams(vmem_limit_bytes=mib * 1024 * 1024)


def around(ref, k, x, row, rows, full):
    halves = ref.shape[2]
    mid = [ref[k, x, h, pl.ds(row, rows), :] for h in range(halves)]
    up = [pltpu.roll(m, 1, 1) for m in mid]
    down = [pltpu.roll(m, LANES - 1, 1) for m in mid]
    if full:
        lane = lax.broadcasted_iota(jnp.int32, mid[0].shape, 1)
        first, last = lane == 0, lane == LANES - 1
        up = [jnp.where(first, up[h - 1] if h else 0.0, up[h]) for h in range(halves)]
        down = [jnp.where(last, down[h + 1] if h < halves - 1 else 0.0, down[h]) for h in range(halves)]
    sums = []
    for h in range(halves):
        planes = ref[k, x - 1, h, pl.ds(row, rows), :] + ref[k, x + 1, h, pl.ds(row, rows), :]
        sides = ref[k, x, h, pl.ds(row - 1, rows), :] + ref[k, x, h, pl.ds(row + 1, rows), :]
        sums.append((planes + sides) + (up[h] + down[h]))
    return sums


def inverse(c, scale, ok):
    a = 6.0 / scale - c
    b = SHIFT_IMAG * c
    g = DAMPING / (a * a + b * b)
    if ok is not None:
        g = jnp.where(ok, g, 0.0)
    return g * a, g * b


def divided(re, im, a, b):
    return re * a + im * b, im * a - re * b


def point(re, im, c, scale, ok, u, ga, gb, x, h, row):
    a, b = inverse(c, scale, ok)
    at = pl.ds(row, c.shape[0])
    ga[x, h, at, :], gb[x, h, at, :] = a, b
    u[0, x, h, at, :], u[1, x, h, at, :] = divided(re, im, a, b)


def second(u, ga, gb, e, x, row, rows, scale, full):
    s_re, s_im = around(u, 0, x, row, rows, full), around(u, 1, x, row, rows, full)
    at = pl.ds(row, rows)
    for h in range(u.shape[2]):
        a, b = ga[x, h, at, :], gb[x, h, at, :]
        if scale != 1.0:
            a, b = a * (1.0 / scale), b * (1.0 / scale)
        d = divided(s_re[h], s_im[h], a, b)
        for k in (0, 1):
            e[k, x, h, at, :] = 0.4 * u[k, x, h, at, :] + d[k]


def is_even(place, shape):
    return jnp.full(shape, lax.rem(place[1], 2)) == 0


def rows_inside(shape, y0, ysize):
    row = lax.broadcasted_iota(jnp.int32, shape, 0) + y0
    return (row >= 0) & (row < ysize)


def restrict_xy(r, t, out, to, plane, row, rows, k, window):
    at = pl.ds(*window)
    for h in range(r.shape[2]):
        val = (r[k, plane, h, at, :] + r[k, plane + 3, h, at, :]) + 3.0 * (r[k, plane + 1, h, at, :] + r[k, plane + 2, h, at, :])
        t[k, h, at, :] = val
        part = [t[k, h, pl.ds(row + j, rows, 2), :] for j in range(4)]
        out[k, to, pl.ds(0, rows), pl.ds(LANES * h, LANES)] = (part[0] + part[3]) + 3.0 * (part[1] + part[2])


def add_pairs(c0, c1, t, h, out, i, row, rows):
    t[0, h, pl.ds(0, c0.shape[0]), :] = c0 + c1
    val = t[0, h, pl.ds(row, rows, 2), :] + t[0, h, pl.ds(row + 1, rows, 2), :]
    out[i, pl.ds(0, rows), pl.ds(LANES * h, LANES)] = val


def weights(lanes, zsize, mean=False, shift=0):
    z = lax.broadcasted_iota(jnp.int32, (lanes, LANES), 0)
    i = lax.broadcasted_iota(jnp.int32, (lanes, LANES), 1) - shift
    d = z - 2 * i
    inner = (d == 0) | (d == 1)
    if mean:
        w = jnp.where(inner, 0.125, 0.0)
    else:
        w = jnp.where(inner, 3.0 / 512.0, jnp.where((d == -1) | (d == 2), 1.0 / 512.0, 0.0))
    return jnp.where((z < zsize) & (i >= 0) & (i < zsize // 2), w, 0.0).astype(jnp.bfloat16)


def exact_dot(part, w):
    planes, rows, lanes = part.shape
    x = part.reshape(planes * rows, lanes)
    hi = x.astype(jnp.bfloat16)
    rest = x - hi.astype(jnp.float32)
    mid = rest.astype(jnp.bfloat16)
    low = (rest - mid.astype(jnp.float32)).astype(jnp.bfloat16)
    dot = functools.partial(jnp.dot, preferred_element_type=jnp.float32)
    return (dot(hi, w) + (dot(mid, w) + dot(low, w))).reshape(planes, rows, w.shape[1])


PX, PY = 3, 8


def planes_kernel(f, c, x_first, x_last, planes, sems):
    n = c.shape[0]
    copies = []
    for side, x in enumerate((0, n - PX)):
        at = pl.ds(x, PX)
        copies += [(c.at[at], planes.at[side, 2]), (f.at[0, at], planes.at[side, 0]), (f.at[1, at], planes.at[side, 1])]
    copies = [pltpu.make_async_copy(src, dst, sems.at[i]) for i, (src, dst) in enumerate(copies)]
    for copy in copies:
        copy.start()
    for side, out in enumerate((x_first, x_last)):
        for copy in copies[3 * side : 3 * side + 3]:
            copy.wait()
        for j in range(PX):
            a, b = inverse(planes[side, 2, j], 1.0, None)
            out[j], out[PX + j] = divided(planes[side, 0, j], planes[side, 1, j], a, b)
        for j in range(2):
            out[2 * PX + j] = planes[side, 2, j + side]


def first_kernel(place, f, c, u, ga, gb, y_chip, y_next):
    n, rows, lanes = c.shape
    cut = [pl.ds(LANES * h, LANES) for h in range(lanes // LANES)]
    row = lax.broadcasted_iota(jnp.int32, (8, LANES), 0)
    even = is_even(place, (8, LANES))

    def step(x, carry):
        for h, lane in enumerate(cut):
            point(f[0, x, :, lane], f[1, x, :, lane], c[x, :, lane], 1.0, None, u, ga, gb, x + PX, h, PY)
            made = []
            for start, shifts in ((0, (0, 3, 6)), (rows - 8, (3, 6, 0))):
                tiles = [u[k, x + PX, h, pl.ds(PY + start, 8), :] for k in (0, 1)] + [c[x, pl.ds(start, 8), lane]]
                re, im, cc = [pltpu.roll(v, shift, 0) if shift else v for v, shift in zip(tiles, shifts)]
                made.append(jnp.where(row < 3, re, jnp.where(row < 6, im, cc)))
            y_chip[x, :, lane], y_next[x, :, lane] = jnp.where(even, made[1], made[0]), jnp.where(even, made[0], made[1])
        return carry

    lax.fori_loop(0, n, step, 0, unroll=True)


def inner_kernel(f, c, u, ga, gb, e, r, fc_out, t, part):
    n, rows, lanes = c.shape
    halves = lanes // LANES
    at = pl.ds(PY, rows)
    cut = [pl.ds(LANES * h, LANES) for h in range(halves)]

    def middle(x, carry):
        second(u, ga, gb, e, x + PX, PY, rows, 1.0, True)
        return carry

    lax.fori_loop(1, n - 1, middle, 0, unroll=True)
    row = lax.broadcasted_iota(jnp.int32, (rows, LANES), 0)
    full = (row >= 2) & (row < rows - 2)

    def last(x, carry):
        for k in (0, 1):
            s = around(e, k, x + PX, PY, rows, True)
            for h in range(halves):
                r[k, x + PX, h, at, :] = 0.04 * f[k, x, :, cut[h]] + jnp.where(full, s[h], 0.0)
        return carry

    lax.fori_loop(2, n - 2, last, 0, unroll=True)
    for x in (0, 1, n - 2, n - 1):
        for k in (0, 1):
            for h in range(halves):
                r[k, x + PX, h, at, :] = 0.04 * f[k, x, :, cut[h]]

    def pairs(i, carry):
        for h in range(halves):
            add_pairs(c[2 * i, :, cut[h]], c[2 * i + 1, :, cut[h]], t, h, part.at[2], i, 0, rows // 2)
        return carry

    lax.fori_loop(0, n // 2, pairs, 0, unroll=True)

    def coarse(i, carry):
        for k in (0, 1):
            restrict_xy(r, t, part, i, 2 * i + PX - 1, PY - 1, rows // 2, k, (PY, rows))
        return carry

    lax.fori_loop(2, n // 2 - 2, coarse, 0, unroll=True)
    w = weights(lanes, lanes)
    for k in (0, 1):
        fc_out[k, 2 : n // 2 - 2] = exact_dot(part[k, 2 : n // 2 - 2], w)
    fc_out[2] = exact_dot(part[2], weights(lanes, lanes, mean=True))


def inside(place, n, rows, xsize, ysize):
    x0, y0 = place[0] * n - PX, place[1] * rows - PY

    def ok(x, row, count):
        gx = x + x0
        return rows_inside((count, LANES), y0 + row, ysize) & ((gx >= 0) & (gx < xsize))

    return ok


def halo(re, im, cc, good, u, ga, gb, r, x, h, row, c_here, r_here):
    at = pl.ds(row, re.shape[0])
    re, im = jnp.where(good, re, 0.0), jnp.where(good, im, 0.0)
    u[0, x, h, at, :], u[1, x, h, at, :] = re, im
    if c_here:
        a, b = inverse(cc, 1.0, good)
        ga[x, h, at, :], gb[x, h, at, :] = a, b
    if r_here:
        a, b = 0.05 * (6.0 - cc), (0.05 * SHIFT_IMAG) * cc
        r[0, x, h, at, :], r[1, x, h, at, :] = re * a - im * b, im * a + re * b


def finish(e, r, x, row, count, good):
    for k in (0, 1):
        s = around(e, k, x, row, count, True)
        for h in range(e.shape[2]):
            at = pl.ds(row, count)
            r[k, x, h, at, :] = r[k, x, h, at, :] + jnp.where(good, s[h], 0.0)


def plane_cells(side, low, i, h):
    cut = pl.ds(LANES * h, LANES)
    j = i - 1 if low else i
    c_here = 0 <= j < 2
    cc = side[2 * PX + j, :, cut] if c_here else None
    return side[i, :, cut], side[PX + i, :, cut], cc, c_here, i == (PX - 1 if low else 0)


def faces_kernel(xsize, ysize, place, u_in, e_in, r_in, ga_in, gb_in, fc_in, xlo, xhi, y_chip, y_next, u, e, r, ga, gb, fc_out, part, q, sides, sems):
    n, (rows, lanes) = y_chip.shape[0], xlo.shape[1:]
    halves = lanes // LANES
    cut = [pl.ds(LANES * h, LANES) for h in range(halves)]
    ok = inside(place, n, rows, xsize, ysize)
    del u_in, e_in, r_in, ga_in, gb_in, fc_in
    copies = [pltpu.make_async_copy(src, sides.at[i], sems.at[i]) for i, src in enumerate((xlo, xhi))]
    for copy in copies:
        copy.start()
    low, high = PY - 4, PY + rows - 4
    good_lo, good_hi = ok(PX, 0, 8), ok(PX, PY + rows, 8)
    even = is_even(place, (8, LANES))

    def strips(x, carry):
        for h in range(halves):
            chip, other = y_chip[x, :, cut[h]], y_next[x, :, cut[h]]
            lo, hi = jnp.where(even, other, chip), jnp.where(even, chip, other)
            for tile, good, row, shifts in ((lo, good_lo, 0, (5, 2, 0)), (hi, good_hi, PY + rows, (0, 5, 2))):
                re, im, cc = [pltpu.roll(tile, shift, 0) if shift else tile for shift in shifts]
                halo(re, im, cc, good, u, ga, gb, r, x + PX, h, row, True, True)
        return carry

    lax.fori_loop(0, n, strips, 0, unroll=True)
    for copy in copies:
        copy.wait()
    for side, is_low, base in ((sides.at[0], True, 0), (sides.at[1], False, n + PX)):
        for i in range(PX):
            good = ok(base + i, PY, rows)
            for h in range(halves):
                re, im, cc, c_here, r_here = plane_cells(side, is_low, i, h)
                halo(re, im, cc, good, u, ga, gb, r, base + i, h, PY, c_here, r_here)
    for x in (PX - 2, PX - 1, PX, n + PX - 1, n + PX, n + PX + 1):
        second(u, ga, gb, e, x, PY, rows, 1.0, True)

    def middle(x, carry):
        for row in (low, high):
            second(u, ga, gb, e, x, row, 8, 1.0, True)
        return carry

    lax.fori_loop(PX + 1, n + PX - 1, middle, 0, unroll=True)
    for x in (PX - 1, PX, PX + 1, n + PX - 2, n + PX - 1, n + PX):
        finish(e, r, x, PY + 4, rows - 8, ok(x, PY + 4, rows - 8))
    row = lax.broadcasted_iota(jnp.int32, (8, LANES), 0)
    good_low, good_high = ok(PX, low, 8) & (row < 6), ok(PX, high, 8) & (row >= 2)

    def last(x, carry):
        finish(e, r, x, low, 8, good_low)
        finish(e, r, x, high, 8, good_high)
        return carry

    lax.fori_loop(PX + 2, n + PX - 2, last, 0, unroll=True)
    m = n // 2 - 4

    def coarse(i, carry):
        x = 2 * i + PX + 3
        for k in (0, 1):
            for h in range(halves):
                for j, row in ((0, PY - 1), (8, PY + rows - 7)):
                    at = pl.ds(row, 8)
                    part[k, i, pl.ds(j, 8), cut[h]] = (r[k, x, h, at, :] + r[k, x + 3, h, at, :]) + 3.0 * (
                        r[k, x + 1, h, at, :] + r[k, x + 2, h, at, :]
                    )
        return carry

    lax.fori_loop(0, m, coarse, 0, unroll=True)
    w = weights(lanes, lanes)
    for k in (0, 1):
        q[k] = exact_dot(part[k], w)
        for row, start in ((0, 0), (rows // 2 - 2, 10)):
            four = [q[k, :, pl.ds(start + j, 2, 2), :] for j in range(4)]
            fc_out[k, pl.ds(2, m), pl.ds(row, 2), :] = (four[0] + four[3]) + 3.0 * (four[1] + four[2])


def pack_corners_kernel(place, xlo, xhi, chip, other, tiles, sems):
    rows = xlo.shape[1]
    copies = []
    for i, side in enumerate((xlo, xhi)):
        for j, row in enumerate((0, rows - 8)):
            copies.append(pltpu.make_async_copy(side.at[:, pl.ds(row, 8)], tiles.at[j, pl.ds(8 * i, 8)], sems.at[2 * i + j]))
    for copy in copies:
        copy.start()
    even = is_even(place, (4, xlo.shape[2]))
    for copy in copies:
        copy.wait()
    for j in range(16):
        first, last = tiles[0, j, pl.ds(0, 4), :], tiles[1, j, pl.ds(4, 4), :]
        chip[j], other[j] = jnp.where(even, last, first), jnp.where(even, first, last)


def corners_kernel(xsize, ysize, n, rows, place, u_in, e_in, r_in, ga_in, gb_in, fc_in, c_chip, c_next, u, e, r, ga, gb, fc_out, t, part):
    halves = c_chip.shape[2] // LANES
    even = is_even(place, (4, LANES))
    ok = inside(place, n, rows, xsize, ysize)
    del u_in, e_in, r_in, ga_in, gb_in, fc_in
    low, high = PY - 4, PY + rows - 4
    for first, low_planes, base in ((0, True, 0), (8, False, n + PX)):
        chip, other = c_chip.at[pl.ds(first, 8)], c_next.at[pl.ds(first, 8)]
        for i in range(PX):
            for h in range(halves):
                one, two = plane_cells(chip, low_planes, i, h), plane_cells(other, low_planes, i, h)
                for row, (p, q) in ((PY - 4, (two, one)), (PY + rows, (one, two))):
                    re, im, cc = [None if v is None else jnp.where(even, v, w) for v, w in zip(p[:3], q[:3])]
                    halo(re, im, cc, ok(base + i, row, 4), u, ga, gb, r, base + i, h, row, *one[3:])
    for x in (PX - 2, PX - 1, PX, n + PX - 1, n + PX, n + PX + 1):
        for row in (low, high):
            second(u, ga, gb, e, x, row, 8, 1.0, True)
    for x in (PX - 1, PX, PX + 1, n + PX - 2, n + PX - 1, n + PX):
        for row in (low, high):
            finish(e, r, x, row, 8, ok(x, row, 8))
    planes = (0, 1, n // 2 - 2, n // 2 - 1)
    w = weights(part.shape[3], part.shape[3])
    for k in (0, 1):
        for j, i in enumerate(planes):
            restrict_xy(r, t, part, j, 2 * i + PX - 1, PY - 1, rows // 2, k, (low, rows + 8))
        val = exact_dot(part[k], w)
        for j, i in enumerate(planes):
            fc_out[k, i] = val[j]


def iterate_kernel(u, e, out):
    n, rows = out.shape[1:3]
    at = pl.ds(PY, rows)

    def step(x, carry):
        for k in (0, 1):
            for h in range(u.shape[2]):
                out[k, x, :, pl.ds(LANES * h, LANES)] = e[k, x + PX, h, at, :] + 0.8 * u[k, x + PX, h, at, :]
        return carry

    lax.fori_loop(0, n, step, 0, unroll=2)


def whole_level(cells, u, e, r, ga, gb, planes, used, row, rows, scale, full, ok, u_put):
    first, count = used
    for x in range(planes):
        at = pl.ds(first, count)
        point(cells(0, x, at), cells(1, x, at), cells(2, x, at), scale, ok(x, first, count), u, ga, gb, x, 0, first)
    at = pl.ds(row, rows)
    for x in range(1, planes - 1):
        second(u, ga, gb, e, x, row, rows, scale, full)
        u_put(x)
    for x in range(2, planes - 2):
        good = ok(x, row, rows)
        for k in (0, 1):
            s = around(e, k, x, row, rows, full)[0] * (1.0 / scale)
            r[k, x, 0, at, :] = jnp.where(good, 0.04 * cells(k, x, at) + s, 0.0)


def rows_kernel(place, xlo, fc, xhi, chip, other):
    halo, n, rows = xlo.shape[1], fc.shape[1], fc.shape[2]
    row = lax.broadcasted_iota(jnp.int32, (8, LANES), 0)
    even = is_even(place, (8, LANES))
    for src, base, count in ((xlo, 0, halo), (fc, halo, n), (xhi, n + halo, halo)):
        for i in range(count):
            made = []
            for start, own in ((0, row < 5), (rows - 8, row >= 3)):
                re, im, cc = [src[k, i, pl.ds(start, 8), :] for k in range(3)]
                made.append((jnp.where(own, re, pltpu.roll(cc, 5, 0)), jnp.where(own, im, pltpu.roll(cc, 2, 0))))
            for k, (first, last) in enumerate(zip(*made)):
                chip[k, base + i], other[k, base + i] = jnp.where(even, last, first), jnp.where(even, first, last)


def middle_kernel(halo, over, xsize, ysize, place, fc_own, xlo, xhi, y_chip, y_next, u_out, fc_out, fc, ga, gb, u, e, r, t, part, part_c):
    n, rows = fc_own.shape[1:3]
    planes = n + 2 * halo
    for k in range(3):
        for src, x, count in ((xlo, 0, halo), (fc_own, halo, n), (xhi, n + halo, halo)):
            fc[k, pl.ds(x, count), 0, pl.ds(8, rows), :] = src[k]
    row = lax.broadcasted_iota(jnp.int32, (8, LANES), 0)
    even = is_even(place, (8, LANES))
    for x in range(planes):
        chip, other = [y_chip[k, x] for k in (0, 1)], [y_next[k, x] for k in (0, 1)]
        for start, split, p, q in ((0, 6, other, chip), (8 + rows, 3, chip, other)):
            at = pl.ds(start, 8)
            one, two = [jnp.where(even, v, w) for v, w in zip(p, q)]
            fc[0, x, 0, at, :], fc[1, x, 0, at, :] = one, two
            fc[2, x, 0, at, :] = jnp.where(row < split, pltpu.roll(one, 3, 0), pltpu.roll(two, 6, 0))
    x0, y0 = place[0] * n - halo, place[1] * rows - 8

    def ok(x, row, count):
        gx = x + x0
        return rows_inside((count, LANES), y0 + row, ysize) & ((gx >= 0) & (gx < xsize))

    def u_put(x):
        if halo <= x < n + halo:
            at = pl.ds(8, rows)
            for k in (0, 1):
                u_out[k, x - halo] = e[k, x, 0, at, :] + 0.8 * u[k, x, 0, at, :]

    def cells(k, x, at):
        return fc[k, x, 0, at, :]

    whole_level(cells, u, e, r, ga, gb, planes, (0, rows + 16), 4, rows + 8, 4.0, True, ok, u_put)
    width = n // 2 + 2 * over
    pairs = width // 2
    for i in range(width):
        x, row = 2 * i + halo - 1 - 2 * over, 7 - 2 * over
        for k in (0, 1):
            restrict_xy(r, t, part, i, x, row, width, k, (4, rows + 8))
        add_pairs(fc[2, x + 1, 0], fc[2, x + 2, 0], t, 0, part_c.at[i % 2], i // 2, row + 1, width)
    two = [(part.at[k], part_c.at[k], LANES // 2 * k) for k in (0, 1)]
    fc_out[pl.ds(0, width)] = sum(exact_dot(p[...], weights(LANES, LANES, shift=s)) for p, _, s in two)[:, :width]
    fc_out[pl.ds(width, pairs)] = sum(exact_dot(p[...], weights(LANES, LANES, True, s)) for _, p, s in two)[:, :width]


def coarse_kernel(n, sweeps, xsize, ysize, zsize, place, fc_own, xlo, xhi, y_chip, y_next, u_out, v_out, fc, ga, gb, u, e, r, t, part, part_c, gc, gd, v, w):
    m = n // 2
    planes = n + 18
    for src, x, first, count in ((xlo, 0, 0, 8), (fc_own, 8, 0, n + 2), (xhi, n + 10, 0, 8), (xlo, planes, 8, 4), (fc_own, planes + 4, n + 2, m + 1), (xhi, planes + m + 5, 8, 4)):
        fc[pl.ds(x, count), 0, pl.ds(15, n + 2), :] = src[pl.ds(first, count)]
    even = is_even(place, (8, LANES))
    for x in range(fc.shape[0]):
        chip, other = y_chip[x], y_next[x]
        fc[x, 0, pl.ds(7, 8), :], fc[x, 0, pl.ds(n + 17, 8), :] = jnp.where(even, other, chip), jnp.where(even, chip, other)
    lane = lax.broadcasted_iota(jnp.int32, (1, LANES), 1)

    def cells(k, x, at):
        val = fc[planes + x // 2 if k == 2 else x, 0, at, :]
        return pltpu.roll(val, LANES - zsize, 1) if k == 1 or (k == 2 and x % 2) else val

    def inside(x0, y0, xs, ys, zs):
        def ok(x, row, count):
            gx = x + x0
            here = rows_inside((count, LANES), y0 + row, ys) & (lane < zs)
            return here & ((gx >= 0) & (gx < xs))

        return ok

    def u_put(x):
        if 9 <= x < n + 9:
            at = pl.ds(16, n)
            for k in (0, 1):
                u_out[k, x - 9] = (e[k, x, 0, at, :] + 0.8 * u[k, x, 0, at, :])[:, :zsize]

    ok = inside(place[0] * n - 9, place[1] * n - 16, xsize, ysize, zsize)
    whole_level(cells, u, e, r, ga, gb, planes, (7, n + 18), 8, n + 16, 16.0, False, ok, u_put)
    width = m + 6
    every = pl.ds(8, n + 16)
    for i in range(width):
        for k in (0, 1):
            restrict_xy(r, t, part, i, 2 * i + 2, 9, width, k, (8, n + 16))
        t[0, 0, every, :] = cells(2, 2 * i + 3, every) + cells(2, 2 * i + 4, every)
        part_c[i, pl.ds(0, width), :] = t[0, 0, pl.ds(10, width, 2), :] + t[0, 0, pl.ds(11, width, 2), :]
    w_full = weights(LANES, zsize)
    f = [exact_dot(part[k], w_full) for k in (0, 1)] + [exact_dot(part_c[...], weights(LANES, zsize, True))]
    ok = inside(place[0] * m - 3, place[1] * m - 3, xsize // 2, ysize // 2, zsize // 2)
    for x in range(width):
        point(f[0][x], f[1][x], f[2][x], 64.0, ok(x, 0, 16), v, gc, gd, x, 0, 0)
    old = v
    for sweep in range(1, sweeps):
        new = w.at[sweep % 2]
        for x in range(sweep, width - sweep):
            at = pl.ds(1, m + 4)
            s = [around(old, k, x, 1, m + 4, False)[0] for k in (0, 1)]
            d = divided(*s, gc[x, 0, at, :] * (1.0 / 64.0), gd[x, 0, at, :] * (1.0 / 64.0))
            for k in (0, 1):
                val = 0.2 * old[k, x, 0, at, :] + v[k, x, 0, at, :] + d[k]
                if sweep < sweeps - 1:
                    new[k, x, 0, at, :] = val
                else:
                    v_out[k, x - 3] = val[2 : 2 + m, : zsize // 2]
        old = new


def body(source, wavenumber_sq):
    f32 = jnp.float32
    xdev, ydev = lax.axis_size("gx"), lax.axis_size("gy")
    place = jnp.stack([lax.axis_index("gx"), lax.axis_index("gy")]).astype(jnp.int32)

    def planes_step(first, last):
        before = lax.ppermute(last, "gx", [(i, (i + 1) % xdev) for i in range(xdev)])
        after = lax.ppermute(first, "gx", [((i + 1) % xdev, i) for i in range(xdev)])
        return before, after

    every = [(i, j) for i in range(xdev) for j in range(ydev)]
    number = lambda i, j: i * ydev + j
    on_chip = [(number(i, j), number(i, j ^ 1)) for i, j in every]
    next_chip = [(number(i, j), number(i ^ 1, j) if j in (0, ydev - 1) else number(i, ((j - 1) ^ 1) + 1)) for i, j in every]

    def rows_step(chip, other):
        return lax.ppermute(chip, ("gx", "gy"), on_chip), lax.ppermute(other, ("gx", "gy"), next_chip)

    _, n, rows, lanes = source.shape
    xsize, ysize = n * xdev, rows * ydev
    S = lambda *shape: jax.ShapeDtypeStruct(shape, f32)
    V = lambda *shape: pltpu.VMEM(shape, f32)

    halves = lanes // LANES
    state = (n + 2 * PX, halves, rows + 2 * PY, LANES)
    part = (n // 2, rows // 2, lanes)
    two, one, coarser = S(2, *state), S(*state), S(3, n // 2, rows // 2, lanes // 2)
    column = V(2, halves, rows + 2 * PY, LANES)
    x_first, x_last = pl.pallas_call(
        planes_kernel,
        in_specs=[pl.BlockSpec(memory_space=pltpu.HBM)] * 2,
        out_specs=[VMEM] * 2,
        out_shape=[S(8, rows, lanes)] * 2,
        scratch_shapes=[V(2, 3, PX, rows, lanes), pltpu.SemaphoreType.DMA((6,))],
        compiler_params=params(24),
        name="pack_planes",
    )(*[pltpu.with_memory_space_constraint(x, pltpu.HBM) for x in (source, wavenumber_sq)])
    source, wavenumber_sq, x_first, x_last = lax.optimization_barrier((source, wavenumber_sq, x_first, x_last))
    xlo, xhi = planes_step(x_first, x_last)
    u, ga, gb, y_chip, y_next = pl.pallas_call(
        first_kernel,
        in_specs=[SMEM] + [VMEM] * 2,
        out_specs=[VMEM] * 5,
        out_shape=[two, one, one] + [S(n, 8, lanes)] * 2,
        compiler_params=params(24),
        cost_estimate=pl.CostEstimate(flops=30_000_000, bytes_accessed=8_000_000, transcendentals=0),
        name="first_iterate",
    )(place, source, wavenumber_sq)
    y_chip, y_next = rows_step(y_chip, y_next)
    e, r, fc = pl.pallas_call(
        inner_kernel,
        in_specs=[VMEM] * 5,
        out_specs=[VMEM] * 3,
        out_shape=[two, two, coarser],
        scratch_shapes=[column, V(3, *part)],
        compiler_params=params(24),
        cost_estimate=pl.CostEstimate(flops=70_000_000, bytes_accessed=16_000_000, transcendentals=0),
        name="inner_cells",
    )(source, wavenumber_sq, u, ga, gb)
    held = (u, e, r, ga, gb, fc)
    shapes = [two] * 3 + [one] * 2 + [coarser]
    xlo, xhi, held = lax.optimization_barrier((xlo, xhi, held))
    c_chip, c_next = rows_step(
        *pl.pallas_call(
            pack_corners_kernel,
            in_specs=[SMEM] + [ANY] * 2,
            out_specs=[VMEM] * 2,
            out_shape=[S(16, 4, lanes)] * 2,
            scratch_shapes=[V(2, 16, 8, lanes), pltpu.SemaphoreType.DMA((4,))],
            compiler_params=params(24),
            name="pack_corners",
        )(place, xlo, xhi)
    )
    in_place = {i + 1: i for i in range(6)}
    held = pl.pallas_call(
        functools.partial(faces_kernel, xsize, ysize),
        in_specs=[SMEM] + [VMEM] * 6 + [ANY] * 2 + [VMEM] * 2,
        out_specs=[VMEM] * 6,
        out_shape=shapes,
        input_output_aliases=in_place,
        scratch_shapes=[V(2, n // 2 - 4, 16, lanes), V(2, n // 2 - 4, 16, lanes // 2), V(2, 8, rows, lanes), pltpu.SemaphoreType.DMA((2,))],
        compiler_params=params(24),
        cost_estimate=pl.CostEstimate(flops=50_000_000, bytes_accessed=8_000_000, transcendentals=0),
        name="face_cells",
    )(place, *held, xlo, xhi, y_chip, y_next)
    u, e, _, _, _, fc = pl.pallas_call(
        functools.partial(corners_kernel, xsize, ysize, n, rows),
        in_specs=[SMEM] + [VMEM] * 8,
        out_specs=[VMEM] * 6,
        out_shape=shapes,
        input_output_aliases=in_place,
        scratch_shapes=[column, V(2, 4, rows // 2, lanes)],
        compiler_params=params(24),
        name="corner_cells",
    )(place, *held, c_chip, c_next)
    fine_shape = S(2, n, rows, lanes)
    n, rows, lanes, xsize, ysize, zsize = n // 2, rows // 2, lanes // 2, xsize // 2, ysize // 2, lanes // 2
    h, over = 5, 1
    xlo, xhi = planes_step(fc[:, :h], fc[:, n - h :])
    fine = pl.pallas_call(
        iterate_kernel,
        in_specs=[VMEM] * 2,
        out_specs=VMEM,
        out_shape=fine_shape,
        compiler_params=params(24),
        cost_estimate=pl.CostEstimate(flops=1_000_000, bytes_accessed=8_000_000, transcendentals=0),
        name="fine_iterate",
    )(u, e)
    xlo, xhi, fine = lax.optimization_barrier((xlo, xhi, fine))
    chip, other = pl.pallas_call(
        rows_kernel,
        in_specs=[SMEM] + [VMEM] * 3,
        out_specs=[VMEM] * 2,
        out_shape=[S(2, n + 2 * h, 8, lanes)] * 2,
        compiler_params=params(24),
        name="second_rows",
    )(place, xlo, fc, xhi)
    chip, other = rows_step(chip, other)
    state = (n + 2 * h, 1, rows + 16, LANES)
    work = lambda s: [V(*s), V(*s), V(2, *s), V(2, *s), V(2, *s), V(2, 1, *s[2:])]
    width = n // 2 + 2 * over
    second_u, fc = pl.pallas_call(
        functools.partial(middle_kernel, h, over, xsize, ysize),
        in_specs=[SMEM] + [VMEM] * 5,
        out_specs=[VMEM] * 2,
        out_shape=[S(2, n, rows, lanes), S(width + width // 2, width, lanes)],
        scratch_shapes=[V(3, *state)] + work(state) + [V(2, width, 16, LANES), V(2, width // 2, 16, LANES)],
        compiler_params=params(24),
        name="second_level",
    )(place, fc, xlo, xhi, chip, other)

    n, xsize, ysize, zsize = n // 2, xsize // 2, ysize // 2, zsize // 2
    m = n // 2

    def joined(lo, own, hi, cells):
        f = (lo[:n], own[: n + 2], hi[:n])
        c = (lo[n:], own[n + 2 :], hi[n:])
        return jnp.concatenate([a[:, cells] for a in f + c], 0)

    pick = lambda i, j: jnp.concatenate([fc[i : i + n], fc[n + 2 + j : n + 2 + j + m]], 0)
    xlo, xhi = planes_step(pick(2, 1), pick(0, 0))
    first, last = joined(xlo, fc, xhi, slice(2, n + 2)), joined(xlo, fc, xhi, slice(0, n))
    even = place[1] % 2 == 0
    chip, other = rows_step(jnp.where(even, last, first), jnp.where(even, first, last))
    state = (n + 18, 1, 40, LANES)
    small = (m + 6, 1, 16, LANES)
    third, coarse = pl.pallas_call(
        functools.partial(coarse_kernel, n, 4, xsize, ysize, zsize),
        in_specs=[SMEM] + [VMEM] * 5,
        out_specs=[VMEM] * 2,
        out_shape=[S(2, n, n, zsize), S(2, m, m, zsize // 2)],
        scratch_shapes=[V(n + 18 + m + 9, 1, 40, LANES)] + work(state) + [V(2, m + 6, 16, LANES), V(m + 6, 16, LANES)]
        + [V(*small), V(*small), V(2, *small), V(2, 2, *small)],
        compiler_params=params(24),
        name="coarse_levels",
    )(place, fc, xlo, xhi, chip, other)
    return fine, second_u, third, coarse


def solution(mesh):
    placed = (P(None, "gx", "gy", None), P("gx", "gy", None))
    return jax.shard_map(body, mesh=mesh, in_specs=placed, out_specs=(P(None, "gx", "gy", None),) * 4, check_vma=False)
```

```python
import functools
import jax
import jax.numpy as jnp
from jax import lax
from jax.experimental import pallas as pl
from jax.experimental.pallas import tpu as pltpu
from jax.sharding import PartitionSpec as P

DAMPING = 0.8
SHIFT_IMAG = 0.5
LANES = 128
VMEM = pl.BlockSpec(memory_space=pltpu.VMEM)
SMEM = pl.BlockSpec(memory_space=pltpu.SMEM)
ANY = pl.BlockSpec(memory_space=pl.ANY)


def params(mib):
    return pltpu.CompilerParams(vmem_limit_bytes=mib * 1024 * 1024)


def around(ref, k, x, row, rows, full):
    halves = ref.shape[2]
    mid = [ref[k, x, h, pl.ds(row, rows), :] for h in range(halves)]
    up = [pltpu.roll(m, 1, 1) for m in mid]
    down = [pltpu.roll(m, LANES - 1, 1) for m in mid]
    if full:
        lane = lax.broadcasted_iota(jnp.int32, mid[0].shape, 1)
        first, last = lane == 0, lane == LANES - 1
        up = [jnp.where(first, up[h - 1] if h else 0.0, up[h]) for h in range(halves)]
        down = [jnp.where(last, down[h + 1] if h < halves - 1 else 0.0, down[h]) for h in range(halves)]
    sums = []
    for h in range(halves):
        planes = ref[k, x - 1, h, pl.ds(row, rows), :] + ref[k, x + 1, h, pl.ds(row, rows), :]
        sides = ref[k, x, h, pl.ds(row - 1, rows), :] + ref[k, x, h, pl.ds(row + 1, rows), :]
        sums.append((planes + sides) + (up[h] + down[h]))
    return sums


def inverse(c, scale, ok):
    a = 6.0 / scale - c
    b = SHIFT_IMAG * c
    g = DAMPING / (a * a + b * b)
    if ok is not None:
        g = jnp.where(ok, g, 0.0)
    return g * a, g * b


def divided(re, im, a, b):
    return re * a + im * b, im * a - re * b


def point(re, im, c, scale, ok, u, ga, gb, x, h, row):
    a, b = inverse(c, scale, ok)
    at = pl.ds(row, c.shape[0])
    ga[x, h, at, :], gb[x, h, at, :] = a, b
    u[0, x, h, at, :], u[1, x, h, at, :] = divided(re, im, a, b)


def second(u, ga, gb, e, x, row, rows, scale, full):
    s_re, s_im = around(u, 0, x, row, rows, full), around(u, 1, x, row, rows, full)
    at = pl.ds(row, rows)
    for h in range(u.shape[2]):
        a, b = ga[x, h, at, :], gb[x, h, at, :]
        if scale != 1.0:
            a, b = a * (1.0 / scale), b * (1.0 / scale)
        d = divided(s_re[h], s_im[h], a, b)
        for k in (0, 1):
            e[k, x, h, at, :] = 0.4 * u[k, x, h, at, :] + d[k]


def is_even(place, shape):
    return jnp.full(shape, lax.rem(place[1], 2)) == 0


def rows_inside(shape, y0, ysize):
    row = lax.broadcasted_iota(jnp.int32, shape, 0) + y0
    return (row >= 0) & (row < ysize)


def restrict_rows(vals, t, out, to, row, rows, k, start):
    for h, val in enumerate(vals):
        t[k, h, pl.ds(start, val.shape[0]), :] = val
        part = [t[k, h, pl.ds(row + j, rows, 2), :] for j in range(4)]
        out[k, to, pl.ds(0, rows), pl.ds(LANES * h, LANES)] = (part[0] + part[3]) + 3.0 * (part[1] + part[2])


def restrict_xy(r, t, out, to, plane, row, rows, k, window):
    at = pl.ds(*window)
    vals = []
    for h in range(r.shape[2]):
        four = [r[k, plane + j, h, at, :] for j in range(4)]
        vals.append((four[0] + four[3]) + 3.0 * (four[1] + four[2]))
    restrict_rows(vals, t, out, to, row, rows, k, window[0])


def add_pairs(c0, c1, t, h, out, i, row, rows):
    t[0, h, pl.ds(0, c0.shape[0]), :] = c0 + c1
    val = t[0, h, pl.ds(row, rows, 2), :] + t[0, h, pl.ds(row + 1, rows, 2), :]
    out[i, pl.ds(0, rows), pl.ds(LANES * h, LANES)] = val


def weights(lanes, zsize, mean=False, shift=0):
    z = lax.broadcasted_iota(jnp.int32, (lanes, LANES), 0)
    i = lax.broadcasted_iota(jnp.int32, (lanes, LANES), 1) - shift
    d = z - 2 * i
    inner = (d == 0) | (d == 1)
    if mean:
        w = jnp.where(inner, 0.125, 0.0)
    else:
        w = jnp.where(inner, 3.0 / 512.0, jnp.where((d == -1) | (d == 2), 1.0 / 512.0, 0.0))
    return jnp.where((z < zsize) & (i >= 0) & (i < zsize // 2), w, 0.0).astype(jnp.bfloat16)


def exact_dot(part, w):
    planes, rows, lanes = part.shape
    x = part.reshape(planes * rows, lanes)
    hi = x.astype(jnp.bfloat16)
    rest = x - hi.astype(jnp.float32)
    mid = rest.astype(jnp.bfloat16)
    low = (rest - mid.astype(jnp.float32)).astype(jnp.bfloat16)
    dot = functools.partial(jnp.dot, preferred_element_type=jnp.float32)
    return (dot(hi, w) + (dot(mid, w) + dot(low, w))).reshape(planes, rows, w.shape[1])


PX, PY = 2, 8


def planes_kernel(f, c, x_first, x_last, planes, sems):
    n = c.shape[0]
    copies = []
    for side, x in enumerate((0, n - PX)):
        at = pl.ds(x, PX)
        copies += [(c.at[at], planes.at[side, 2]), (f.at[0, at], planes.at[side, 0]), (f.at[1, at], planes.at[side, 1])]
    copies = [pltpu.make_async_copy(src, dst, sems.at[i]) for i, (src, dst) in enumerate(copies)]
    for copy in copies:
        copy.start()
    for side, out in enumerate((x_first, x_last)):
        for copy in copies[3 * side : 3 * side + 3]:
            copy.wait()
        for j in range(PX):
            a, b = inverse(planes[side, 2, j], 1.0, None)
            out[j], out[PX + j] = divided(planes[side, 0, j], planes[side, 1, j], a, b)
        out[2 * PX] = planes[side, 2, (PX - 1) * side]


def first_kernel(place, f, c, u, ga, gb, y_chip, y_next):
    n, rows, lanes = c.shape
    cut = [pl.ds(LANES * h, LANES) for h in range(lanes // LANES)]
    row = lax.broadcasted_iota(jnp.int32, (8, LANES), 0)
    even = is_even(place, (8, LANES))

    def step(x, carry):
        for h, lane in enumerate(cut):
            point(f[0, x, :, lane], f[1, x, :, lane], c[x, :, lane], 1.0, None, u, ga, gb, x + PX, h, PY)
            made = []
            for start, shifts in ((0, (0, 3, 6)), (rows - 8, (3, 6, 0))):
                tiles = [u[k, x + PX, h, pl.ds(PY + start, 8), :] for k in (0, 1)] + [c[x, pl.ds(start, 8), lane]]
                re, im, cc = [pltpu.roll(v, shift, 0) if shift else v for v, shift in zip(tiles, shifts)]
                made.append(jnp.where(row < 3, re, jnp.where(row < 6, im, cc)))
            y_chip[x, :, lane], y_next[x, :, lane] = jnp.where(even, made[1], made[0]), jnp.where(even, made[0], made[1])
        return carry

    lax.fori_loop(0, n, step, 0, unroll=True)


def inner_kernel(f, c, u, ga, gb, e, r, fc_out, t, part):
    n, rows, lanes = c.shape
    halves = lanes // LANES
    at = pl.ds(PY, rows)
    cut = [pl.ds(LANES * h, LANES) for h in range(halves)]

    def middle(x, carry):
        second(u, ga, gb, e, x + PX, PY, rows, 1.0, True)
        return carry

    lax.fori_loop(1, n - 1, middle, 0, unroll=True)
    row = lax.broadcasted_iota(jnp.int32, (rows, LANES), 0)
    full = (row >= 2) & (row < rows - 2)

    def last(x, carry):
        for k in (0, 1):
            s = around(e, k, x + PX, PY, rows, True)
            for h in range(halves):
                r[k, x + PX, h, at, :] = 0.04 * f[k, x, :, cut[h]] + jnp.where(full, s[h], 0.0)
        return carry

    lax.fori_loop(2, n - 2, last, 0, unroll=True)
    for x in (0, 1, n - 2, n - 1):
        for k in (0, 1):
            for h in range(halves):
                r[k, x + PX, h, at, :] = 0.04 * f[k, x, :, cut[h]]
    for x in (PX - 1, n + PX):
        r[:, x] = jnp.zeros((2,) + r.shape[2:], jnp.float32)

    def pairs(i, carry):
        for h in range(halves):
            add_pairs(c[2 * i, :, cut[h]], c[2 * i + 1, :, cut[h]], t, h, part.at[2], i, 0, rows // 2)
        return carry

    lax.fori_loop(0, n // 2, pairs, 0, unroll=True)

    def coarse(i, carry):
        for k in (0, 1):
            restrict_xy(r, t, part, i, 2 * i + PX - 1, PY - 1, rows // 2, k, (PY, rows))
        return carry

    lax.fori_loop(2, n // 2 - 2, coarse, 0, unroll=True)
    w = weights(lanes, lanes)
    for k in (0, 1):
        fc_out[k, 2 : n // 2 - 2] = exact_dot(part[k, 2 : n // 2 - 2], w)
    fc_out[2] = exact_dot(part[2], weights(lanes, lanes, mean=True))


def inside(place, n, rows, xsize, ysize):
    x0, y0 = place[0] * n - PX, place[1] * rows - PY

    def ok(x, row, count):
        gx = x + x0
        return rows_inside((count, LANES), y0 + row, ysize) & ((gx >= 0) & (gx < xsize))

    return ok


def halo(re, im, cc, good, u, ga, gb, r, x, h, row, c_here, r_here):
    at = pl.ds(row, re.shape[0])
    re, im = jnp.where(good, re, 0.0), jnp.where(good, im, 0.0)
    u[0, x, h, at, :], u[1, x, h, at, :] = re, im
    if c_here:
        a, b = inverse(cc, 1.0, good)
        ga[x, h, at, :], gb[x, h, at, :] = a, b
    if r_here:
        a, b = 0.05 * (6.0 - cc), (0.05 * SHIFT_IMAG) * cc
        r[0, x, h, at, :], r[1, x, h, at, :] = re * a - im * b, im * a + re * b


def finish(e, r, x, row, count, good):
    for k in (0, 1):
        s = around(e, k, x, row, count, True)
        for h in range(e.shape[2]):
            at = pl.ds(row, count)
            r[k, x, h, at, :] = r[k, x, h, at, :] + jnp.where(good, s[h], 0.0)


def plane_cells(side, low, i, h):
    cut = pl.ds(LANES * h, LANES)
    c_here = i == (PX - 1 if low else 0)
    return side[i, :, cut], side[PX + i, :, cut], side[2 * PX, :, cut] if c_here else None, c_here


def faces_kernel(xsize, ysize, place, u_in, e_in, r_in, ga_in, gb_in, fc_in, xlo, xhi, y_chip, y_next, u, e, r, ga, gb, fc_out, part, q, sides, sems):
    n, (rows, lanes) = y_chip.shape[0], xlo.shape[1:]
    halves = lanes // LANES
    cut = [pl.ds(LANES * h, LANES) for h in range(halves)]
    ok = inside(place, n, rows, xsize, ysize)
    del u_in, e_in, r_in, ga_in, gb_in, fc_in
    copies = [pltpu.make_async_copy(src, sides.at[i], sems.at[i]) for i, src in enumerate((xlo, xhi))]
    for copy in copies:
        copy.start()
    low, high = PY - 4, PY + rows - 4
    good_lo, good_hi = ok(PX, 0, 8), ok(PX, PY + rows, 8)
    even = is_even(place, (8, LANES))

    def strips(x, carry):
        for h in range(halves):
            chip, other = y_chip[x, :, cut[h]], y_next[x, :, cut[h]]
            lo, hi = jnp.where(even, other, chip), jnp.where(even, chip, other)
            for tile, good, row, shifts in ((lo, good_lo, 0, (5, 2, 0)), (hi, good_hi, PY + rows, (0, 5, 2))):
                re, im, cc = [pltpu.roll(tile, shift, 0) if shift else tile for shift in shifts]
                halo(re, im, cc, good, u, ga, gb, r, x + PX, h, row, True, True)
        return carry

    lax.fori_loop(0, n, strips, 0, unroll=True)
    for copy in copies:
        copy.wait()
    for side, is_low, base in ((sides.at[0], True, 0), (sides.at[1], False, n + PX)):
        for i in range(PX):
            good = ok(base + i, PY, rows)
            for h in range(halves):
                re, im, cc, c_here = plane_cells(side, is_low, i, h)
                halo(re, im, cc, good, u, ga, gb, r, base + i, h, PY, c_here, False)
    for x in (PX - 1, PX, n + PX - 1, n + PX):
        second(u, ga, gb, e, x, PY, rows, 1.0, True)

    def middle(x, carry):
        for row in (low, high):
            second(u, ga, gb, e, x, row, 8, 1.0, True)
        return carry

    lax.fori_loop(PX + 1, n + PX - 1, middle, 0, unroll=True)
    for x in (PX, PX + 1, n + PX - 2, n + PX - 1):
        finish(e, r, x, PY + 4, rows - 8, ok(x, PY + 4, rows - 8))
    row = lax.broadcasted_iota(jnp.int32, (8, LANES), 0)
    good_low, good_high = ok(PX, low, 8) & (row < 6), ok(PX, high, 8) & (row >= 2)

    def last(x, carry):
        finish(e, r, x, low, 8, good_low)
        finish(e, r, x, high, 8, good_high)
        return carry

    lax.fori_loop(PX + 2, n + PX - 2, last, 0, unroll=True)
    m = n // 2 - 4

    def coarse(i, carry):
        x = 2 * i + PX + 3
        for k in (0, 1):
            for h in range(halves):
                for j, row in ((0, PY - 1), (8, PY + rows - 7)):
                    at = pl.ds(row, 8)
                    part[k, i, pl.ds(j, 8), cut[h]] = (r[k, x, h, at, :] + r[k, x + 3, h, at, :]) + 3.0 * (
                        r[k, x + 1, h, at, :] + r[k, x + 2, h, at, :]
                    )
        return carry

    lax.fori_loop(0, m, coarse, 0, unroll=True)
    w = weights(lanes, lanes)
    for k in (0, 1):
        q[k] = exact_dot(part[k], w)
        for row, start in ((0, 0), (rows // 2 - 2, 10)):
            four = [q[k, :, pl.ds(start + j, 2, 2), :] for j in range(4)]
            fc_out[k, pl.ds(2, m), pl.ds(row, 2), :] = (four[0] + four[3]) + 3.0 * (four[1] + four[2])


def pack_corners_kernel(place, xlo, xhi, chip, other, tiles, sems):
    count, rows = xlo.shape[:2]
    copies = []
    for i, side in enumerate((xlo, xhi)):
        for j, row in enumerate((0, rows - 8)):
            copies.append(pltpu.make_async_copy(side.at[:, pl.ds(row, 8)], tiles.at[j, pl.ds(count * i, count)], sems.at[2 * i + j]))
    for copy in copies:
        copy.start()
    even = is_even(place, (4, xlo.shape[2]))
    for copy in copies:
        copy.wait()
    for j in range(2 * count):
        first, last = tiles[0, j, pl.ds(0, 4), :], tiles[1, j, pl.ds(4, 4), :]
        chip[j], other[j] = jnp.where(even, last, first), jnp.where(even, first, last)


def corners_kernel(xsize, ysize, n, rows, place, u_in, e_in, r_in, ga_in, gb_in, fc_in, c_chip, c_next, u, e, r, ga, gb, fc_out, edge_out, t, part):
    halves = c_chip.shape[2] // LANES
    even = is_even(place, (4, LANES))
    ok = inside(place, n, rows, xsize, ysize)
    del u_in, e_in, r_in, ga_in, gb_in, fc_in
    low, high = PY - 4, PY + rows - 4
    held = 2 * PX + 1
    for first, low_planes, base in ((0, True, 0), (held, False, n + PX)):
        chip, other = c_chip.at[pl.ds(first, held)], c_next.at[pl.ds(first, held)]
        for i in range(PX):
            for h in range(halves):
                one, two = plane_cells(chip, low_planes, i, h), plane_cells(other, low_planes, i, h)
                for row, (p, q) in ((PY - 4, (two, one)), (PY + rows, (one, two))):
                    re, im, cc = [None if v is None else jnp.where(even, v, w) for v, w in zip(p[:3], q[:3])]
                    halo(re, im, cc, ok(base + i, row, 4), u, ga, gb, r, base + i, h, row, one[3], False)
    for x in (PX - 1, PX, n + PX - 1, n + PX):
        for row in (low, high):
            second(u, ga, gb, e, x, row, 8, 1.0, True)
    for x in (PX, PX + 1, n + PX - 2, n + PX - 1):
        for row in (low, high):
            finish(e, r, x, row, 8, ok(x, row, 8))
    planes = (0, 1, n // 2 - 2, n // 2 - 1)
    w = weights(part.shape[3], part.shape[3])
    for k in (0, 1):
        for j, i in enumerate(planes):
            restrict_xy(r, t, part, j, 2 * i + PX - 1, PY - 1, rows // 2, k, (low, rows + 8))
        for j, x in ((4, PX), (5, n + PX - 1)):
            restrict_rows([r[k, x, h, pl.ds(low, rows + 8), :] for h in range(halves)], t, part, j, PY - 1, rows // 2, k, low)
        val = exact_dot(part[k], w)
        for j, i in enumerate(planes):
            fc_out[k, i] = val[j]
        edge_out[0, k], edge_out[1, k] = val[4], val[5]


def iterate_kernel(u, e, out):
    n, rows = out.shape[1:3]
    at = pl.ds(PY, rows)

    def step(x, carry):
        for k in (0, 1):
            for h in range(u.shape[2]):
                out[k, x, :, pl.ds(LANES * h, LANES)] = e[k, x + PX, h, at, :] + 0.8 * u[k, x + PX, h, at, :]
        return carry

    lax.fori_loop(0, n, step, 0, unroll=2)


def whole_level(cells, u, e, r, ga, gb, planes, used, row, rows, scale, full, ok, u_put):
    first, count = used
    for x in range(planes):
        at = pl.ds(first, count)
        point(cells(0, x, at), cells(1, x, at), cells(2, x, at), scale, ok(x, first, count), u, ga, gb, x, 0, first)
    at = pl.ds(row, rows)
    for x in range(1, planes - 1):
        second(u, ga, gb, e, x, row, rows, scale, full)
        u_put(x)
    for x in range(2, planes - 2):
        good = ok(x, row, rows)
        for k in (0, 1):
            s = around(e, k, x, row, rows, full)[0] * (1.0 / scale)
            r[k, x, 0, at, :] = jnp.where(good, 0.04 * cells(k, x, at) + s, 0.0)


def rows_kernel(xdev, halo, place, xlo, fc, xhi, edges, chip, other, window):
    n, rows = fc.shape[1:3]
    row = lax.broadcasted_iota(jnp.int32, (8, LANES), 0)
    even = is_even(place, (8, LANES))
    here = jnp.full((rows, LANES), place[0])
    for k in range(3):
        window[k, pl.ds(0, halo)] = xlo[pl.ds(k * halo, halo)]
        window[k, pl.ds(halo, n)] = fc[k]
        window[k, pl.ds(n + halo, halo)] = xhi[pl.ds(k * halo, halo)]
    for k in (0, 1):
        window[k, halo - 1] += edges[0, k]
        window[k, halo] += jnp.where(here > 0, xlo[3 * halo + k], 0.0)
        window[k, n + halo - 1] += jnp.where(here < xdev - 1, xhi[3 * halo + k], 0.0)
        window[k, n + halo] += edges[1, k]
    for x in range(n + 2 * halo):
        made = []
        for start, own in ((0, row < 5), (rows - 8, row >= 3)):
            re, im, cc = [window[k, x, pl.ds(start, 8), :] for k in range(3)]
            made.append((jnp.where(own, re, pltpu.roll(cc, 5, 0)), jnp.where(own, im, pltpu.roll(cc, 2, 0))))
        for k, (first, last) in enumerate(zip(*made)):
            chip[k, x], other[k, x] = jnp.where(even, last, first), jnp.where(even, first, last)


def middle_kernel(halo, over, xsize, ysize, place, window, y_chip, y_next, u_out, fc_out, fc, ga, gb, u, e, r, t, part, part_c):
    planes, rows = window.shape[1:3]
    n = planes - 2 * halo
    for k in range(3):
        fc[k, :, 0, pl.ds(8, rows), :] = window[k]
    row = lax.broadcasted_iota(jnp.int32, (8, LANES), 0)
    even = is_even(place, (8, LANES))
    for x in range(planes):
        chip, other = [y_chip[k, x] for k in (0, 1)], [y_next[k, x] for k in (0, 1)]
        for start, split, p, q in ((0, 6, other, chip), (8 + rows, 3, chip, other)):
            at = pl.ds(start, 8)
            one, two = [jnp.where(even, v, w) for v, w in zip(p, q)]
            fc[0, x, 0, at, :], fc[1, x, 0, at, :] = one, two
            fc[2, x, 0, at, :] = jnp.where(row < split, pltpu.roll(one, 3, 0), pltpu.roll(two, 6, 0))
    x0, y0 = place[0] * n - halo, place[1] * rows - 8

    def ok(x, row, count):
        gx = x + x0
        return rows_inside((count, LANES), y0 + row, ysize) & ((gx >= 0) & (gx < xsize))

    def u_put(x):
        if halo <= x < n + halo:
            at = pl.ds(8, rows)
            for k in (0, 1):
                u_out[k, x - halo] = e[k, x, 0, at, :] + 0.8 * u[k, x, 0, at, :]

    def cells(k, x, at):
        return fc[k, x, 0, at, :]

    whole_level(cells, u, e, r, ga, gb, planes, (0, rows + 16), 4, rows + 8, 4.0, True, ok, u_put)
    width = n // 2 + 2 * over
    pairs = width // 2
    for i in range(width):
        x, row = 2 * i + halo - 1 - 2 * over, 7 - 2 * over
        for k in (0, 1):
            restrict_xy(r, t, part, i, x, row, width, k, (4, rows + 8))
        add_pairs(fc[2, x + 1, 0], fc[2, x + 2, 0], t, 0, part_c.at[i % 2], i // 2, row + 1, width)
    two = [(part.at[k], part_c.at[k], LANES // 2 * k) for k in (0, 1)]
    fc_out[pl.ds(0, width)] = sum(exact_dot(p[...], weights(LANES, LANES, shift=s)) for p, _, s in two)[:, :width]
    fc_out[pl.ds(width, pairs)] = sum(exact_dot(p[...], weights(LANES, LANES, True, s)) for _, p, s in two)[:, :width]


def coarse_kernel(n, sweeps, xsize, ysize, zsize, place, fc_own, xlo, xhi, y_chip, y_next, u_out, v_out, fc, ga, gb, u, e, r, t, part, part_c, gc, gd, v, w):
    m = n // 2
    planes = n + 18
    for src, x, first, count in ((xlo, 0, 0, 8), (fc_own, 8, 0, n + 2), (xhi, n + 10, 0, 8), (xlo, planes, 8, 4), (fc_own, planes + 4, n + 2, m + 1), (xhi, planes + m + 5, 8, 4)):
        fc[pl.ds(x, count), 0, pl.ds(15, n + 2), :] = src[pl.ds(first, count)]
    even = is_even(place, (8, LANES))
    for x in range(fc.shape[0]):
        chip, other = y_chip[x], y_next[x]
        fc[x, 0, pl.ds(7, 8), :], fc[x, 0, pl.ds(n + 17, 8), :] = jnp.where(even, other, chip), jnp.where(even, chip, other)
    lane = lax.broadcasted_iota(jnp.int32, (1, LANES), 1)

    def cells(k, x, at):
        val = fc[planes + x // 2 if k == 2 else x, 0, at, :]
        return pltpu.roll(val, LANES - zsize, 1) if k == 1 or (k == 2 and x % 2) else val

    def inside(x0, y0, xs, ys, zs):
        def ok(x, row, count):
            gx = x + x0
            here = rows_inside((count, LANES), y0 + row, ys) & (lane < zs)
            return here & ((gx >= 0) & (gx < xs))

        return ok

    def u_put(x):
        if 9 <= x < n + 9:
            at = pl.ds(16, n)
            for k in (0, 1):
                u_out[k, x - 9] = (e[k, x, 0, at, :] + 0.8 * u[k, x, 0, at, :])[:, :zsize]

    ok = inside(place[0] * n - 9, place[1] * n - 16, xsize, ysize, zsize)
    whole_level(cells, u, e, r, ga, gb, planes, (7, n + 18), 8, n + 16, 16.0, False, ok, u_put)
    width = m + 6
    every = pl.ds(8, n + 16)
    for i in range(width):
        for k in (0, 1):
            restrict_xy(r, t, part, i, 2 * i + 2, 9, width, k, (8, n + 16))
        t[0, 0, every, :] = cells(2, 2 * i + 3, every) + cells(2, 2 * i + 4, every)
        part_c[i, pl.ds(0, width), :] = t[0, 0, pl.ds(10, width, 2), :] + t[0, 0, pl.ds(11, width, 2), :]
    w_full = weights(LANES, zsize)
    f = [exact_dot(part[k], w_full) for k in (0, 1)] + [exact_dot(part_c[...], weights(LANES, zsize, True))]
    ok = inside(place[0] * m - 3, place[1] * m - 3, xsize // 2, ysize // 2, zsize // 2)
    for x in range(width):
        point(f[0][x], f[1][x], f[2][x], 64.0, ok(x, 0, 16), v, gc, gd, x, 0, 0)
    old = v
    for sweep in range(1, sweeps):
        new = w.at[sweep % 2]
        for x in range(sweep, width - sweep):
            at = pl.ds(1, m + 4)
            s = [around(old, k, x, 1, m + 4, False)[0] for k in (0, 1)]
            d = divided(*s, gc[x, 0, at, :] * (1.0 / 64.0), gd[x, 0, at, :] * (1.0 / 64.0))
            for k in (0, 1):
                val = 0.2 * old[k, x, 0, at, :] + v[k, x, 0, at, :] + d[k]
                if sweep < sweeps - 1:
                    new[k, x, 0, at, :] = val
                else:
                    v_out[k, x - 3] = val[2 : 2 + m, : zsize // 2]
        old = new


def body(source, wavenumber_sq):
    f32 = jnp.float32
    xdev, ydev = lax.axis_size("gx"), lax.axis_size("gy")
    place = jnp.stack([lax.axis_index("gx"), lax.axis_index("gy")]).astype(jnp.int32)

    def planes_step(first, last):
        before = lax.ppermute(last, "gx", [(i, (i + 1) % xdev) for i in range(xdev)])
        after = lax.ppermute(first, "gx", [((i + 1) % xdev, i) for i in range(xdev)])
        return before, after

    every = [(i, j) for i in range(xdev) for j in range(ydev)]
    number = lambda i, j: i * ydev + j
    on_chip = [(number(i, j), number(i, j ^ 1)) for i, j in every]
    next_chip = [(number(i, j), number(i ^ 1, j) if j in (0, ydev - 1) else number(i, ((j - 1) ^ 1) + 1)) for i, j in every]

    def rows_step(chip, other):
        return lax.ppermute(chip, ("gx", "gy"), on_chip), lax.ppermute(other, ("gx", "gy"), next_chip)

    _, n, rows, lanes = source.shape
    xsize, ysize = n * xdev, rows * ydev
    S = lambda *shape: jax.ShapeDtypeStruct(shape, f32)
    V = lambda *shape: pltpu.VMEM(shape, f32)

    halves = lanes // LANES
    state = (n + 2 * PX, halves, rows + 2 * PY, LANES)
    part = (n // 2, rows // 2, lanes)
    two, one, coarser = S(2, *state), S(*state), S(3, n // 2, rows // 2, lanes // 2)
    column = V(2, halves, rows + 2 * PY, LANES)
    held_planes = 2 * PX + 1
    x_first, x_last = pl.pallas_call(
        planes_kernel,
        in_specs=[pl.BlockSpec(memory_space=pltpu.HBM)] * 2,
        out_specs=[VMEM] * 2,
        out_shape=[S(held_planes, rows, lanes)] * 2,
        scratch_shapes=[V(2, 3, PX, rows, lanes), pltpu.SemaphoreType.DMA((6,))],
        compiler_params=params(24),
        name="pack_planes",
    )(*[pltpu.with_memory_space_constraint(x, pltpu.HBM) for x in (source, wavenumber_sq)])
    source, wavenumber_sq, x_first, x_last = lax.optimization_barrier((source, wavenumber_sq, x_first, x_last))
    xlo, xhi = planes_step(x_first, x_last)
    u, ga, gb, y_chip, y_next = pl.pallas_call(
        first_kernel,
        in_specs=[SMEM] + [VMEM] * 2,
        out_specs=[VMEM] * 5,
        out_shape=[two, one, one] + [S(n, 8, lanes)] * 2,
        compiler_params=params(24),
        cost_estimate=pl.CostEstimate(flops=30_000_000, bytes_accessed=8_000_000, transcendentals=0),
        name="first_iterate",
    )(place, source, wavenumber_sq)
    y_chip, y_next = rows_step(y_chip, y_next)
    e, r, fc = pl.pallas_call(
        inner_kernel,
        in_specs=[VMEM] * 5,
        out_specs=[VMEM] * 3,
        out_shape=[two, two, coarser],
        scratch_shapes=[column, V(3, *part)],
        compiler_params=params(24),
        cost_estimate=pl.CostEstimate(flops=70_000_000, bytes_accessed=16_000_000, transcendentals=0),
        name="inner_cells",
    )(source, wavenumber_sq, u, ga, gb)
    held = (u, e, r, ga, gb, fc)
    shapes = [two] * 3 + [one] * 2 + [coarser]
    xlo, xhi, held = lax.optimization_barrier((xlo, xhi, held))
    c_chip, c_next = rows_step(
        *pl.pallas_call(
            pack_corners_kernel,
            in_specs=[SMEM] + [ANY] * 2,
            out_specs=[VMEM] * 2,
            out_shape=[S(2 * held_planes, 4, lanes)] * 2,
            scratch_shapes=[V(2, 2 * held_planes, 8, lanes), pltpu.SemaphoreType.DMA((4,))],
            compiler_params=params(24),
            name="pack_corners",
        )(place, xlo, xhi)
    )
    in_place = {i + 1: i for i in range(6)}
    held = pl.pallas_call(
        functools.partial(faces_kernel, xsize, ysize),
        in_specs=[SMEM] + [VMEM] * 6 + [ANY] * 2 + [VMEM] * 2,
        out_specs=[VMEM] * 6,
        out_shape=shapes,
        input_output_aliases=in_place,
        scratch_shapes=[V(2, n // 2 - 4, 16, lanes), V(2, n // 2 - 4, 16, lanes // 2), V(2, held_planes, rows, lanes), pltpu.SemaphoreType.DMA((2,))],
        compiler_params=params(24),
        cost_estimate=pl.CostEstimate(flops=50_000_000, bytes_accessed=8_000_000, transcendentals=0),
        name="face_cells",
    )(place, *held, xlo, xhi, y_chip, y_next)
    u, e, _, _, _, fc, edges = pl.pallas_call(
        functools.partial(corners_kernel, xsize, ysize, n, rows),
        in_specs=[SMEM] + [VMEM] * 8,
        out_specs=[VMEM] * 7,
        out_shape=shapes + [S(2, 2, rows // 2, lanes // 2)],
        input_output_aliases=in_place,
        scratch_shapes=[column, V(2, 6, rows // 2, lanes)],
        compiler_params=params(24),
        name="corner_cells",
    )(place, *held, c_chip, c_next)
    fine_shape = S(2, n, rows, lanes)
    n, rows, lanes, xsize, ysize, zsize = n // 2, rows // 2, lanes // 2, xsize // 2, ysize // 2, lanes // 2
    h, over = 5, 1
    slab = lambda x, edge: jnp.concatenate([fc[:, x : x + h].reshape(3 * h, rows, lanes), edge], 0)
    xlo, xhi = planes_step(slab(0, edges[0]), slab(n - h, edges[1]))
    fine = pl.pallas_call(
        iterate_kernel,
        in_specs=[VMEM] * 2,
        out_specs=VMEM,
        out_shape=fine_shape,
        compiler_params=params(24),
        cost_estimate=pl.CostEstimate(flops=1_000_000, bytes_accessed=8_000_000, transcendentals=0),
        name="fine_iterate",
    )(u, e)
    xlo, xhi, fine = lax.optimization_barrier((xlo, xhi, fine))
    chip, other, window = pl.pallas_call(
        functools.partial(rows_kernel, xdev, h),
        in_specs=[SMEM] + [VMEM] * 4,
        out_specs=[VMEM] * 3,
        out_shape=[S(2, n + 2 * h, 8, lanes)] * 2 + [S(3, n + 2 * h, rows, lanes)],
        compiler_params=params(24),
        name="second_rows",
    )(place, xlo, fc, xhi, edges)
    chip, other = rows_step(chip, other)
    state = (n + 2 * h, 1, rows + 16, LANES)
    work = lambda s: [V(*s), V(*s), V(2, *s), V(2, *s), V(2, *s), V(2, 1, *s[2:])]
    width = n // 2 + 2 * over
    second_u, fc = pl.pallas_call(
        functools.partial(middle_kernel, h, over, xsize, ysize),
        in_specs=[SMEM] + [VMEM] * 3,
        out_specs=[VMEM] * 2,
        out_shape=[S(2, n, rows, lanes), S(width + width // 2, width, lanes)],
        scratch_shapes=[V(3, *state)] + work(state) + [V(2, width, 16, LANES), V(2, width // 2, 16, LANES)],
        compiler_params=params(24),
        name="second_level",
    )(place, window, chip, other)

    n, xsize, ysize, zsize = n // 2, xsize // 2, ysize // 2, zsize // 2
    m = n // 2

    def joined(lo, own, hi, cells):
        f = (lo[:n], own[: n + 2], hi[:n])
        c = (lo[n:], own[n + 2 :], hi[n:])
        return jnp.concatenate([a[:, cells] for a in f + c], 0)

    pick = lambda i, j: jnp.concatenate([fc[i : i + n], fc[n + 2 + j : n + 2 + j + m]], 0)
    xlo, xhi = planes_step(pick(2, 1), pick(0, 0))
    first, last = joined(xlo, fc, xhi, slice(2, n + 2)), joined(xlo, fc, xhi, slice(0, n))
    even = place[1] % 2 == 0
    chip, other = rows_step(jnp.where(even, last, first), jnp.where(even, first, last))
    state = (n + 18, 1, 40, LANES)
    small = (m + 6, 1, 16, LANES)
    third, coarse = pl.pallas_call(
        functools.partial(coarse_kernel, n, 4, xsize, ysize, zsize),
        in_specs=[SMEM] + [VMEM] * 5,
        out_specs=[VMEM] * 2,
        out_shape=[S(2, n, n, zsize), S(2, m, m, zsize // 2)],
        scratch_shapes=[V(n + 18 + m + 9, 1, 40, LANES)] + work(state) + [V(2, m + 6, 16, LANES), V(m + 6, 16, LANES)]
        + [V(*small), V(*small), V(2, *small), V(2, 2, *small)],
        compiler_params=params(24),
        name="coarse_levels",
    )(place, fc, xlo, xhi, chip, other)
    return fine, second_u, third, coarse


def solution(mesh):
    placed = (P(None, "gx", "gy", None), P("gx", "gy", None))
    return jax.shard_map(body, mesh=mesh, in_specs=placed, out_specs=(P(None, "gx", "gy", None),) * 4, check_vma=False)
```

```python
import functools
import jax
import jax.numpy as jnp
from jax import lax
from jax.experimental import pallas as pl
from jax.experimental.pallas import tpu as pltpu
from jax.sharding import PartitionSpec as P

DAMPING = 0.8
SHIFT_IMAG = 0.5
LANES = 128
VMEM = pl.BlockSpec(memory_space=pltpu.VMEM)
SMEM = pl.BlockSpec(memory_space=pltpu.SMEM)
ANY = pl.BlockSpec(memory_space=pl.ANY)


def params(mib):
    return pltpu.CompilerParams(vmem_limit_bytes=mib * 1024 * 1024)


def around(ref, k, x, row, rows, full):
    halves = ref.shape[2]
    mid = [ref[k, x, h, pl.ds(row, rows), :] for h in range(halves)]
    up = [pltpu.roll(m, 1, 1) for m in mid]
    down = [pltpu.roll(m, LANES - 1, 1) for m in mid]
    if full:
        lane = lax.broadcasted_iota(jnp.int32, mid[0].shape, 1)
        first, last = lane == 0, lane == LANES - 1
        up = [jnp.where(first, up[h - 1] if h else 0.0, up[h]) for h in range(halves)]
        down = [jnp.where(last, down[h + 1] if h < halves - 1 else 0.0, down[h]) for h in range(halves)]
    sums = []
    for h in range(halves):
        planes = ref[k, x - 1, h, pl.ds(row, rows), :] + ref[k, x + 1, h, pl.ds(row, rows), :]
        sides = ref[k, x, h, pl.ds(row - 1, rows), :] + ref[k, x, h, pl.ds(row + 1, rows), :]
        sums.append((planes + sides) + (up[h] + down[h]))
    return sums


def inverse(c, scale, ok):
    a = 6.0 / scale - c
    b = SHIFT_IMAG * c
    g = DAMPING / (a * a + b * b)
    if ok is not None:
        g = jnp.where(ok, g, 0.0)
    return g * a, g * b


def divided(re, im, a, b):
    return re * a + im * b, im * a - re * b


def point(re, im, c, scale, ok, u, ga, gb, x, h, row):
    a, b = inverse(c, scale, ok)
    at = pl.ds(row, c.shape[0])
    ga[x, h, at, :], gb[x, h, at, :] = a, b
    u[0, x, h, at, :], u[1, x, h, at, :] = divided(re, im, a, b)


def second(u, ga, gb, e, x, row, rows, scale, full):
    s_re, s_im = around(u, 0, x, row, rows, full), around(u, 1, x, row, rows, full)
    at = pl.ds(row, rows)
    for h in range(u.shape[2]):
        a, b = ga[x, h, at, :], gb[x, h, at, :]
        if scale != 1.0:
            a, b = a * (1.0 / scale), b * (1.0 / scale)
        d = divided(s_re[h], s_im[h], a, b)
        for k in (0, 1):
            e[k, x, h, at, :] = 0.4 * u[k, x, h, at, :] + d[k]


def is_even(place, shape):
    return jnp.full(shape, lax.rem(place[1], 2)) == 0


def rows_inside(shape, y0, ysize):
    row = lax.broadcasted_iota(jnp.int32, shape, 0) + y0
    return (row >= 0) & (row < ysize)


def restrict_rows(vals, t, out, to, row, rows, k, start):
    for h, val in enumerate(vals):
        t[k, h, pl.ds(start, val.shape[0]), :] = val
        part = [t[k, h, pl.ds(row + j, rows, 2), :] for j in range(4)]
        out[k, to, pl.ds(0, rows), pl.ds(LANES * h, LANES)] = (part[0] + part[3]) + 3.0 * (part[1] + part[2])


def restrict_xy(r, t, out, to, plane, row, rows, k, window):
    at = pl.ds(*window)
    vals = []
    for h in range(r.shape[2]):
        four = [r[k, plane + j, h, at, :] for j in range(4)]
        vals.append((four[0] + four[3]) + 3.0 * (four[1] + four[2]))
    restrict_rows(vals, t, out, to, row, rows, k, window[0])


def add_pairs(c0, c1, t, h, out, i, row, rows):
    t[0, h, pl.ds(0, c0.shape[0]), :] = c0 + c1
    val = t[0, h, pl.ds(row, rows, 2), :] + t[0, h, pl.ds(row + 1, rows, 2), :]
    out[i, pl.ds(0, rows), pl.ds(LANES * h, LANES)] = val


def weights(lanes, zsize, mean=False, shift=0):
    z = lax.broadcasted_iota(jnp.int32, (lanes, LANES), 0)
    i = lax.broadcasted_iota(jnp.int32, (lanes, LANES), 1) - shift
    d = z - 2 * i
    inner = (d == 0) | (d == 1)
    if mean:
        w = jnp.where(inner, 0.125, 0.0)
    else:
        w = jnp.where(inner, 3.0 / 512.0, jnp.where((d == -1) | (d == 2), 1.0 / 512.0, 0.0))
    return jnp.where((z < zsize) & (i >= 0) & (i < zsize // 2), w, 0.0).astype(jnp.bfloat16)


def exact_dot(part, w):
    planes, rows, lanes = part.shape
    x = part.reshape(planes * rows, lanes)
    hi = x.astype(jnp.bfloat16)
    rest = x - hi.astype(jnp.float32)
    mid = rest.astype(jnp.bfloat16)
    low = (rest - mid.astype(jnp.float32)).astype(jnp.bfloat16)
    dot = functools.partial(jnp.dot, preferred_element_type=jnp.float32)
    return (dot(hi, w) + (dot(mid, w) + dot(low, w))).reshape(planes, rows, w.shape[1])


PX, PY = 2, 8


def planes_kernel(f, c, x_first, x_last, planes, sems):
    n = c.shape[0]
    copies = []
    for side, x in enumerate((0, n - PX)):
        at = pl.ds(x, PX)
        copies += [(c.at[at], planes.at[side, 2]), (f.at[0, at], planes.at[side, 0]), (f.at[1, at], planes.at[side, 1])]
    copies = [pltpu.make_async_copy(src, dst, sems.at[i]) for i, (src, dst) in enumerate(copies)]
    for copy in copies:
        copy.start()
    for side, out in enumerate((x_first, x_last)):
        for copy in copies[3 * side : 3 * side + 3]:
            copy.wait()
        for j in range(PX):
            a, b = inverse(planes[side, 2, j], 1.0, None)
            out[j], out[PX + j] = divided(planes[side, 0, j], planes[side, 1, j], a, b)
        out[2 * PX] = planes[side, 2, (PX - 1) * side]


def first_kernel(place, f, c, u, ga, gb, y_chip, y_next):
    n, rows, lanes = c.shape
    cut = [pl.ds(LANES * h, LANES) for h in range(lanes // LANES)]
    row = lax.broadcasted_iota(jnp.int32, (8, LANES), 0)
    even = is_even(place, (8, LANES))

    def step(x, carry):
        for h, lane in enumerate(cut):
            point(f[0, x, :, lane], f[1, x, :, lane], c[x, :, lane], 1.0, None, u, ga, gb, x + PX, h, PY)
            made = []
            for start, shifts in ((0, (0, 3, 6)), (rows - 8, (3, 6, 0))):
                tiles = [u[k, x + PX, h, pl.ds(PY + start, 8), :] for k in (0, 1)] + [c[x, pl.ds(start, 8), lane]]
                re, im, cc = [pltpu.roll(v, shift, 0) if shift else v for v, shift in zip(tiles, shifts)]
                made.append(jnp.where(row < 3, re, jnp.where(row < 6, im, cc)))
            y_chip[x, :, lane], y_next[x, :, lane] = jnp.where(even, made[1], made[0]), jnp.where(even, made[0], made[1])
        return carry

    lax.fori_loop(0, n, step, 0, unroll=True)


def inner_kernel(f, c, u, ga, gb, e, r, fc_out, t, part):
    n, rows, lanes = c.shape
    halves = lanes // LANES
    at = pl.ds(PY, rows)
    cut = [pl.ds(LANES * h, LANES) for h in range(halves)]

    def middle(x, carry):
        second(u, ga, gb, e, x + PX, PY, rows, 1.0, True)
        return carry

    lax.fori_loop(1, n - 1, middle, 0, unroll=True)
    row = lax.broadcasted_iota(jnp.int32, (rows, LANES), 0)
    full = (row >= 2) & (row < rows - 2)

    def last(x, carry):
        for k in (0, 1):
            s = around(e, k, x + PX, PY, rows, True)
            for h in range(halves):
                r[k, x + PX, h, at, :] = 0.04 * f[k, x, :, cut[h]] + jnp.where(full, s[h], 0.0)
        return carry

    lax.fori_loop(2, n - 2, last, 0, unroll=True)
    for x in (0, 1, n - 2, n - 1):
        for k in (0, 1):
            for h in range(halves):
                r[k, x + PX, h, at, :] = 0.04 * f[k, x, :, cut[h]]
    for x in (PX - 1, n + PX):
        r[:, x] = jnp.zeros((2,) + r.shape[2:], jnp.float32)

    def pairs(i, carry):
        for h in range(halves):
            add_pairs(c[2 * i, :, cut[h]], c[2 * i + 1, :, cut[h]], t, h, part.at[2], i, 0, rows // 2)
        return carry

    lax.fori_loop(0, n // 2, pairs, 0, unroll=True)

    def coarse(i, carry):
        for k in (0, 1):
            restrict_xy(r, t, part, i, 2 * i + PX - 1, PY - 1, rows // 2, k, (PY, rows))
        return carry

    lax.fori_loop(2, n // 2 - 2, coarse, 0, unroll=True)
    w = weights(lanes, lanes)
    for k in (0, 1):
        fc_out[k, 2 : n // 2 - 2] = exact_dot(part[k, 2 : n // 2 - 2], w)
    fc_out[2] = exact_dot(part[2], weights(lanes, lanes, mean=True))


def inside(place, n, rows, xsize, ysize):
    x0, y0 = place[0] * n - PX, place[1] * rows - PY

    def ok(x, row, count):
        gx = x + x0
        return rows_inside((count, LANES), y0 + row, ysize) & ((gx >= 0) & (gx < xsize))

    return ok


def halo(re, im, cc, good, u, ga, gb, r, x, h, row, c_here, r_here):
    at = pl.ds(row, re.shape[0])
    re, im = jnp.where(good, re, 0.0), jnp.where(good, im, 0.0)
    u[0, x, h, at, :], u[1, x, h, at, :] = re, im
    if c_here:
        a, b = inverse(cc, 1.0, good)
        ga[x, h, at, :], gb[x, h, at, :] = a, b
    if r_here:
        a, b = 0.05 * (6.0 - cc), (0.05 * SHIFT_IMAG) * cc
        r[0, x, h, at, :], r[1, x, h, at, :] = re * a - im * b, im * a + re * b


def finish(e, r, x, row, count, good):
    for k in (0, 1):
        s = around(e, k, x, row, count, True)
        for h in range(e.shape[2]):
            at = pl.ds(row, count)
            r[k, x, h, at, :] = r[k, x, h, at, :] + jnp.where(good, s[h], 0.0)


def plane_cells(side, low, i, h):
    cut = pl.ds(LANES * h, LANES)
    c_here = i == (PX - 1 if low else 0)
    return side[i, :, cut], side[PX + i, :, cut], side[2 * PX, :, cut] if c_here else None, c_here


def faces_kernel(xsize, ysize, place, u_in, e_in, r_in, ga_in, gb_in, fc_in, xlo, xhi, y_chip, y_next, u, e, r, ga, gb, fc_out, part, q, sides, sems):
    n, (rows, lanes) = y_chip.shape[0], xlo.shape[1:]
    halves = lanes // LANES
    cut = [pl.ds(LANES * h, LANES) for h in range(halves)]
    ok = inside(place, n, rows, xsize, ysize)
    del u_in, e_in, r_in, ga_in, gb_in, fc_in
    copies = [pltpu.make_async_copy(src, sides.at[i], sems.at[i]) for i, src in enumerate((xlo, xhi))]
    for copy in copies:
        copy.start()
    low, high = PY - 4, PY + rows - 4
    good_lo, good_hi = ok(PX, 0, 8), ok(PX, PY + rows, 8)
    even = is_even(place, (8, LANES))

    def strips(x, carry):
        for h in range(halves):
            chip, other = y_chip[x, :, cut[h]], y_next[x, :, cut[h]]
            lo, hi = jnp.where(even, other, chip), jnp.where(even, chip, other)
            for tile, good, row, shifts in ((lo, good_lo, 0, (5, 2, 0)), (hi, good_hi, PY + rows, (0, 5, 2))):
                re, im, cc = [pltpu.roll(tile, shift, 0) if shift else tile for shift in shifts]
                halo(re, im, cc, good, u, ga, gb, r, x + PX, h, row, True, True)
        return carry

    lax.fori_loop(0, n, strips, 0, unroll=True)
    for copy in copies:
        copy.wait()
    for side, is_low, base in ((sides.at[0], True, 0), (sides.at[1], False, n + PX)):
        for i in range(PX):
            good = ok(base + i, PY, rows)
            for h in range(halves):
                re, im, cc, c_here = plane_cells(side, is_low, i, h)
                halo(re, im, cc, good, u, ga, gb, r, base + i, h, PY, c_here, False)
    for x in (PX - 1, PX, n + PX - 1, n + PX):
        second(u, ga, gb, e, x, PY, rows, 1.0, True)

    def middle(x, carry):
        for row in (low, high):
            second(u, ga, gb, e, x, row, 8, 1.0, True)
        return carry

    lax.fori_loop(PX + 1, n + PX - 1, middle, 0, unroll=True)
    for x in (PX, PX + 1, n + PX - 2, n + PX - 1):
        finish(e, r, x, PY + 4, rows - 8, ok(x, PY + 4, rows - 8))
    row = lax.broadcasted_iota(jnp.int32, (8, LANES), 0)
    good_low, good_high = ok(PX, low, 8) & (row < 6), ok(PX, high, 8) & (row >= 2)

    def last(x, carry):
        finish(e, r, x, low, 8, good_low)
        finish(e, r, x, high, 8, good_high)
        return carry

    lax.fori_loop(PX + 2, n + PX - 2, last, 0, unroll=True)
    m = n // 2 - 4

    def coarse(i, carry):
        x = 2 * i + PX + 3
        for k in (0, 1):
            for h in range(halves):
                for j, row in ((0, PY - 1), (8, PY + rows - 7)):
                    at = pl.ds(row, 8)
                    part[k, i, pl.ds(j, 8), cut[h]] = (r[k, x, h, at, :] + r[k, x + 3, h, at, :]) + 3.0 * (
                        r[k, x + 1, h, at, :] + r[k, x + 2, h, at, :]
                    )
        return carry

    lax.fori_loop(0, m, coarse, 0, unroll=True)
    w = weights(lanes, lanes)
    for k in (0, 1):
        q[k] = exact_dot(part[k], w)
        for row, start in ((0, 0), (rows // 2 - 2, 10)):
            four = [q[k, :, pl.ds(start + j, 2, 2), :] for j in range(4)]
            fc_out[k, pl.ds(2, m), pl.ds(row, 2), :] = (four[0] + four[3]) + 3.0 * (four[1] + four[2])


def pack_corners_kernel(place, xlo, xhi, chip, other, tiles, sems):
    count, rows = xlo.shape[:2]
    copies = []
    for i, side in enumerate((xlo, xhi)):
        for j, row in enumerate((0, rows - 8)):
            copies.append(pltpu.make_async_copy(side.at[:, pl.ds(row, 8)], tiles.at[j, pl.ds(count * i, count)], sems.at[2 * i + j]))
    for copy in copies:
        copy.start()
    even = is_even(place, (4, xlo.shape[2]))
    for copy in copies:
        copy.wait()
    for j in range(2 * count):
        first, last = tiles[0, j, pl.ds(0, 4), :], tiles[1, j, pl.ds(4, 4), :]
        chip[j], other[j] = jnp.where(even, last, first), jnp.where(even, first, last)


def corners_kernel(xsize, ysize, n, rows, place, u_in, e_in, r_in, ga_in, gb_in, fc_in, c_chip, c_next, u, e, r, ga, gb, fc_out, edge_out, t, part):
    halves = c_chip.shape[2] // LANES
    even = is_even(place, (4, LANES))
    ok = inside(place, n, rows, xsize, ysize)
    del u_in, e_in, r_in, ga_in, gb_in, fc_in
    low, high = PY - 4, PY + rows - 4
    held = 2 * PX + 1
    for first, low_planes, base in ((0, True, 0), (held, False, n + PX)):
        chip, other = c_chip.at[pl.ds(first, held)], c_next.at[pl.ds(first, held)]
        for i in range(PX):
            for h in range(halves):
                one, two = plane_cells(chip, low_planes, i, h), plane_cells(other, low_planes, i, h)
                for row, (p, q) in ((PY - 4, (two, one)), (PY + rows, (one, two))):
                    re, im, cc = [None if v is None else jnp.where(even, v, w) for v, w in zip(p[:3], q[:3])]
                    halo(re, im, cc, ok(base + i, row, 4), u, ga, gb, r, base + i, h, row, one[3], False)
    for x in (PX - 1, PX, n + PX - 1, n + PX):
        for row in (low, high):
            second(u, ga, gb, e, x, row, 8, 1.0, True)
    for x in (PX, PX + 1, n + PX - 2, n + PX - 1):
        for row in (low, high):
            finish(e, r, x, row, 8, ok(x, row, 8))
    planes = (0, 1, n // 2 - 2, n // 2 - 1)
    w = weights(part.shape[3], part.shape[3])
    for k in (0, 1):
        for j, i in enumerate(planes):
            restrict_xy(r, t, part, j, 2 * i + PX - 1, PY - 1, rows // 2, k, (low, rows + 8))
        for j, x in ((4, PX), (5, n + PX - 1)):
            restrict_rows([r[k, x, h, pl.ds(low, rows + 8), :] for h in range(halves)], t, part, j, PY - 1, rows // 2, k, low)
        val = exact_dot(part[k], w)
        for j, i in enumerate(planes):
            fc_out[k, i] = val[j]
        edge_out[0, k], edge_out[1, k] = val[4], val[5]


def iterate_kernel(u, e, out):
    n, rows = out.shape[1:3]
    at = pl.ds(PY, rows)

    def step(x, carry):
        for k in (0, 1):
            for h in range(u.shape[2]):
                out[k, x, :, pl.ds(LANES * h, LANES)] = e[k, x + PX, h, at, :] + 0.8 * u[k, x + PX, h, at, :]
        return carry

    lax.fori_loop(0, n, step, 0, unroll=2)


def whole_level(cells, u, e, r, ga, gb, planes, used, row, rows, scale, full, ok, u_put):
    first, count = used
    for x in range(planes):
        at = pl.ds(first, count)
        point(cells(0, x, at), cells(1, x, at), cells(2, x, at), scale, ok(x, first, count), u, ga, gb, x, 0, first)
    at = pl.ds(row, rows)
    for x in range(1, planes - 1):
        second(u, ga, gb, e, x, row, rows, scale, full)
        u_put(x)
    for x in range(2, planes - 2):
        good = ok(x, row, rows)
        for k in (0, 1):
            s = around(e, k, x, row, rows, full)[0] * (1.0 / scale)
            r[k, x, 0, at, :] = jnp.where(good, 0.04 * cells(k, x, at) + s, 0.0)


def rows_kernel(xdev, halo, place, xlo, fc, xhi, edges, chip, other, window):
    n, rows = fc.shape[1:3]
    row = lax.broadcasted_iota(jnp.int32, (8, LANES), 0)
    even = is_even(place, (8, LANES))
    here = jnp.full((rows, LANES), place[0])
    for k in range(3):
        window[k, pl.ds(0, halo)] = xlo[pl.ds(k * halo, halo)]
        window[k, pl.ds(halo, n)] = fc[k]
        window[k, pl.ds(n + halo, halo)] = xhi[pl.ds(k * halo, halo)]
    for k in (0, 1):
        window[k, halo - 1] += edges[0, k]
        window[k, halo] += jnp.where(here > 0, xlo[3 * halo + k], 0.0)
        window[k, n + halo - 1] += jnp.where(here < xdev - 1, xhi[3 * halo + k], 0.0)
        window[k, n + halo] += edges[1, k]
    for x in range(n + 2 * halo):
        made = []
        for start, own in ((0, row < 5), (rows - 8, row >= 3)):
            re, im, cc = [window[k, x, pl.ds(start, 8), :] for k in range(3)]
            made.append((jnp.where(own, re, pltpu.roll(cc, 5, 0)), jnp.where(own, im, pltpu.roll(cc, 2, 0))))
        for k, (first, last) in enumerate(zip(*made)):
            chip[k, x], other[k, x] = jnp.where(even, last, first), jnp.where(even, first, last)


def middle_kernel(halo, over, xsize, ysize, place, window, y_chip, y_next, u_out, fc_out, fc, ga, gb, u, e, r, t, part, part_c):
    planes, rows = window.shape[1:3]
    n = planes - 2 * halo
    for k in range(3):
        fc[k, :, 0, pl.ds(8, rows), :] = window[k]
    row = lax.broadcasted_iota(jnp.int32, (8, LANES), 0)
    even = is_even(place, (8, LANES))
    for x in range(planes):
        chip, other = [y_chip[k, x] for k in (0, 1)], [y_next[k, x] for k in (0, 1)]
        for start, split, p, q in ((0, 6, other, chip), (8 + rows, 3, chip, other)):
            at = pl.ds(start, 8)
            one, two = [jnp.where(even, v, w) for v, w in zip(p, q)]
            fc[0, x, 0, at, :], fc[1, x, 0, at, :] = one, two
            fc[2, x, 0, at, :] = jnp.where(row < split, pltpu.roll(one, 3, 0), pltpu.roll(two, 6, 0))
    x0, y0 = place[0] * n - halo, place[1] * rows - 8

    def ok(x, row, count):
        gx = x + x0
        return rows_inside((count, LANES), y0 + row, ysize) & ((gx >= 0) & (gx < xsize))

    def u_put(x):
        if halo <= x < n + halo:
            at = pl.ds(8, rows)
            for k in (0, 1):
                u_out[k, x - halo] = e[k, x, 0, at, :] + 0.8 * u[k, x, 0, at, :]

    def cells(k, x, at):
        return fc[k, x, 0, at, :]

    whole_level(cells, u, e, r, ga, gb, planes, (0, rows + 16), 4, rows + 8, 4.0, True, ok, u_put)
    width = n // 2 + 2 * over
    pairs = width // 2
    for i in range(width):
        x, row = 2 * i + halo - 1 - 2 * over, 7 - 2 * over
        for k in (0, 1):
            restrict_xy(r, t, part, i, x, row, width, k, (4, rows + 8))
        add_pairs(fc[2, x + 1, 0], fc[2, x + 2, 0], t, 0, part_c.at[i % 2], i // 2, row + 1, width)
    two = [(part.at[k], part_c.at[k], LANES // 2 * k) for k in (0, 1)]
    fc_out[pl.ds(0, width)] = sum(exact_dot(p[...], weights(LANES, LANES, shift=s)) for p, _, s in two)[:, :width]
    fc_out[pl.ds(width, pairs)] = sum(exact_dot(p[...], weights(LANES, LANES, True, s)) for _, p, s in two)[:, :width]


def coarse_kernel(n, sweeps, xsize, ysize, zsize, place, fc_own, xlo, xhi, y_chip, y_next, u_out, v_out, fc, ga, gb, u, e, r, t, part, part_c, gc, gd, v, w):
    m = n // 2
    planes = n + 18
    for src, x, first, count in ((xlo, 0, 0, 8), (fc_own, 8, 0, n + 2), (xhi, n + 10, 0, 8), (xlo, planes, 8, 4), (fc_own, planes + 4, n + 2, m + 1), (xhi, planes + m + 5, 8, 4)):
        fc[pl.ds(x, count), 0, pl.ds(15, n + 2), :] = src[pl.ds(first, count)]
    even = is_even(place, (8, LANES))
    for x in range(fc.shape[0]):
        chip, other = y_chip[x], y_next[x]
        fc[x, 0, pl.ds(7, 8), :], fc[x, 0, pl.ds(n + 17, 8), :] = jnp.where(even, other, chip), jnp.where(even, chip, other)
    lane = lax.broadcasted_iota(jnp.int32, (1, LANES), 1)

    def cells(k, x, at):
        val = fc[planes + x // 2 if k == 2 else x, 0, at, :]
        return pltpu.roll(val, LANES - zsize, 1) if k == 1 or (k == 2 and x % 2) else val

    def inside(x0, y0, xs, ys, zs):
        def ok(x, row, count):
            gx = x + x0
            here = rows_inside((count, LANES), y0 + row, ys) & (lane < zs)
            return here & ((gx >= 0) & (gx < xs))

        return ok

    def u_put(x):
        if 9 <= x < n + 9:
            at = pl.ds(16, n)
            for k in (0, 1):
                u_out[k, x - 9] = (e[k, x, 0, at, :] + 0.8 * u[k, x, 0, at, :])[:, :zsize]

    ok = inside(place[0] * n - 9, place[1] * n - 16, xsize, ysize, zsize)
    whole_level(cells, u, e, r, ga, gb, planes, (7, n + 18), 8, n + 16, 16.0, False, ok, u_put)
    width = m + 6
    every = pl.ds(8, n + 16)
    for i in range(width):
        for k in (0, 1):
            restrict_xy(r, t, part, i, 2 * i + 2, 9, width, k, (8, n + 16))
        t[0, 0, every, :] = cells(2, 2 * i + 3, every) + cells(2, 2 * i + 4, every)
        part_c[i, pl.ds(0, width), :] = t[0, 0, pl.ds(10, width, 2), :] + t[0, 0, pl.ds(11, width, 2), :]
    w_full = weights(LANES, zsize)
    f = [exact_dot(part[k], w_full) for k in (0, 1)] + [exact_dot(part_c[...], weights(LANES, zsize, True))]
    ok = inside(place[0] * m - 3, place[1] * m - 3, xsize // 2, ysize // 2, zsize // 2)
    for x in range(width):
        point(f[0][x], f[1][x], f[2][x], 64.0, ok(x, 0, 16), v, gc, gd, x, 0, 0)
    old = v
    for sweep in range(1, sweeps):
        new = w.at[sweep % 2]
        for x in range(sweep, width - sweep):
            at = pl.ds(1, m + 4)
            s = [around(old, k, x, 1, m + 4, False)[0] for k in (0, 1)]
            d = divided(*s, gc[x, 0, at, :] * (1.0 / 64.0), gd[x, 0, at, :] * (1.0 / 64.0))
            for k in (0, 1):
                val = 0.2 * old[k, x, 0, at, :] + v[k, x, 0, at, :] + d[k]
                if sweep < sweeps - 1:
                    new[k, x, 0, at, :] = val
                else:
                    v_out[k, x - 3] = val[2 : 2 + m, : zsize // 2]
        old = new


def body(source, wavenumber_sq):
    f32 = jnp.float32
    xdev, ydev = lax.axis_size("gx"), lax.axis_size("gy")
    place = jnp.stack([lax.axis_index("gx"), lax.axis_index("gy")]).astype(jnp.int32)

    def planes_step(first, last):
        before = lax.ppermute(last, "gx", [(i, (i + 1) % xdev) for i in range(xdev)])
        after = lax.ppermute(first, "gx", [((i + 1) % xdev, i) for i in range(xdev)])
        return before, after

    every = [(i, j) for i in range(xdev) for j in range(ydev)]
    number = lambda i, j: i * ydev + j
    on_chip = [(number(i, j), number(i, j ^ 1)) for i, j in every]
    next_chip = [(number(i, j), number(i ^ 1, j) if j in (0, ydev - 1) else number(i, ((j - 1) ^ 1) + 1)) for i, j in every]

    def rows_step(chip, other):
        return lax.ppermute(chip, ("gx", "gy"), on_chip), lax.ppermute(other, ("gx", "gy"), next_chip)

    _, n, rows, lanes = source.shape
    xsize, ysize = n * xdev, rows * ydev
    S = lambda *shape: jax.ShapeDtypeStruct(shape, f32)
    V = lambda *shape: pltpu.VMEM(shape, f32)

    halves = lanes // LANES
    state = (n + 2 * PX, halves, rows + 2 * PY, LANES)
    part = (n // 2, rows // 2, lanes)
    two, one, coarser = S(2, *state), S(*state), S(3, n // 2, rows // 2, lanes // 2)
    column = V(2, halves, rows + 2 * PY, LANES)
    held_planes = 2 * PX + 1
    x_first, x_last = pl.pallas_call(
        planes_kernel,
        in_specs=[pl.BlockSpec(memory_space=pltpu.HBM)] * 2,
        out_specs=[VMEM] * 2,
        out_shape=[S(held_planes + 2, rows, lanes)] * 2,
        scratch_shapes=[V(2, 3, PX, rows, lanes), pltpu.SemaphoreType.DMA((6,))],
        compiler_params=params(24),
        name="pack_planes",
    )(*[pltpu.with_memory_space_constraint(x, pltpu.HBM) for x in (source, wavenumber_sq)])
    source, wavenumber_sq, x_first, x_last = lax.optimization_barrier((source, wavenumber_sq, x_first, x_last))
    xlo, xhi = planes_step(x_first, x_last)
    u, ga, gb, y_chip, y_next = pl.pallas_call(
        first_kernel,
        in_specs=[SMEM] + [VMEM] * 2,
        out_specs=[VMEM] * 5,
        out_shape=[two, one, one] + [S(n, 8, lanes)] * 2,
        compiler_params=params(24),
        cost_estimate=pl.CostEstimate(flops=30_000_000, bytes_accessed=8_000_000, transcendentals=0),
        name="first_iterate",
    )(place, source, wavenumber_sq)
    y_chip, y_next = rows_step(y_chip, y_next)
    e, r, fc = pl.pallas_call(
        inner_kernel,
        in_specs=[VMEM] * 5,
        out_specs=[VMEM] * 3,
        out_shape=[two, two, coarser],
        scratch_shapes=[column, V(3, *part)],
        compiler_params=params(24),
        cost_estimate=pl.CostEstimate(flops=70_000_000, bytes_accessed=16_000_000, transcendentals=0),
        name="inner_cells",
    )(source, wavenumber_sq, u, ga, gb)
    held = (u, e, r, ga, gb, fc)
    shapes = [two] * 3 + [one] * 2 + [coarser]
    xlo, xhi, held = lax.optimization_barrier((xlo, xhi, held))
    xlo, xhi = xlo[:held_planes], xhi[:held_planes]
    c_chip, c_next = rows_step(
        *pl.pallas_call(
            pack_corners_kernel,
            in_specs=[SMEM] + [ANY] * 2,
            out_specs=[VMEM] * 2,
            out_shape=[S(2 * held_planes, 4, lanes)] * 2,
            scratch_shapes=[V(2, 2 * held_planes, 8, lanes), pltpu.SemaphoreType.DMA((4,))],
            compiler_params=params(24),
            name="pack_corners",
        )(place, xlo, xhi)
    )
    in_place = {i + 1: i for i in range(6)}
    held = pl.pallas_call(
        functools.partial(faces_kernel, xsize, ysize),
        in_specs=[SMEM] + [VMEM] * 6 + [ANY] * 2 + [VMEM] * 2,
        out_specs=[VMEM] * 6,
        out_shape=shapes,
        input_output_aliases=in_place,
        scratch_shapes=[V(2, n // 2 - 4, 16, lanes), V(2, n // 2 - 4, 16, lanes // 2), V(2, held_planes, rows, lanes), pltpu.SemaphoreType.DMA((2,))],
        compiler_params=params(24),
        cost_estimate=pl.CostEstimate(flops=50_000_000, bytes_accessed=8_000_000, transcendentals=0),
        name="face_cells",
    )(place, *held, xlo, xhi, y_chip, y_next)
    u, e, _, _, _, fc, edges = pl.pallas_call(
        functools.partial(corners_kernel, xsize, ysize, n, rows),
        in_specs=[SMEM] + [VMEM] * 8,
        out_specs=[VMEM] * 7,
        out_shape=shapes + [S(2, 2, rows // 2, lanes // 2)],
        input_output_aliases=in_place,
        scratch_shapes=[column, V(2, 6, rows // 2, lanes)],
        compiler_params=params(24),
        name="corner_cells",
    )(place, *held, c_chip, c_next)
    fine_shape = S(2, n, rows, lanes)
    n, rows, lanes, xsize, ysize, zsize = n // 2, rows // 2, lanes // 2, xsize // 2, ysize // 2, lanes // 2
    h, over = 5, 1
    slab = lambda x, edge: jnp.concatenate([fc[:, x : x + h].reshape(3 * h, rows, lanes), edge], 0)
    xlo, xhi = planes_step(slab(0, edges[0]), slab(n - h, edges[1]))
    fine = pl.pallas_call(
        iterate_kernel,
        in_specs=[VMEM] * 2,
        out_specs=VMEM,
        out_shape=fine_shape,
        compiler_params=params(24),
        cost_estimate=pl.CostEstimate(flops=1_000_000, bytes_accessed=8_000_000, transcendentals=0),
        name="fine_iterate",
    )(u, e)
    xlo, xhi, fine = lax.optimization_barrier((xlo, xhi, fine))
    chip, other, window = pl.pallas_call(
        functools.partial(rows_kernel, xdev, h),
        in_specs=[SMEM] + [VMEM] * 4,
        out_specs=[VMEM] * 3,
        out_shape=[S(2, n + 2 * h, 8, lanes)] * 2 + [S(3, n + 2 * h, rows, lanes)],
        compiler_params=params(24),
        name="second_rows",
    )(place, xlo, fc, xhi, edges)
    chip, other = rows_step(chip, other)
    state = (n + 2 * h, 1, rows + 16, LANES)
    work = lambda s: [V(*s), V(*s), V(2, *s), V(2, *s), V(2, *s), V(2, 1, *s[2:])]
    width = n // 2 + 2 * over
    second_u, fc = pl.pallas_call(
        functools.partial(middle_kernel, h, over, xsize, ysize),
        in_specs=[SMEM] + [VMEM] * 3,
        out_specs=[VMEM] * 2,
        out_shape=[S(2, n, rows, lanes), S(width + width // 2, width, lanes)],
        scratch_shapes=[V(3, *state)] + work(state) + [V(2, width, 16, LANES), V(2, width // 2, 16, LANES)],
        compiler_params=params(24),
        name="second_level",
    )(place, window, chip, other)

    n, xsize, ysize, zsize = n // 2, xsize // 2, ysize // 2, zsize // 2
    m = n // 2

    def joined(lo, own, hi, cells):
        f = (lo[:n], own[: n + 2], hi[:n])
        c = (lo[n:], own[n + 2 :], hi[n:])
        return jnp.concatenate([a[:, cells] for a in f + c], 0)

    pick = lambda i, j: jnp.concatenate([fc[i : i + n], fc[n + 2 + j : n + 2 + j + m]], 0)
    xlo, xhi = planes_step(pick(2, 1), pick(0, 0))
    first, last = joined(xlo, fc, xhi, slice(2, n + 2)), joined(xlo, fc, xhi, slice(0, n))
    even = place[1] % 2 == 0
    chip, other = rows_step(jnp.where(even, last, first), jnp.where(even, first, last))
    state = (n + 18, 1, 40, LANES)
    small = (m + 6, 1, 16, LANES)
    third, coarse = pl.pallas_call(
        functools.partial(coarse_kernel, n, 4, xsize, ysize, zsize),
        in_specs=[SMEM] + [VMEM] * 5,
        out_specs=[VMEM] * 2,
        out_shape=[S(2, n, n, zsize), S(2, m, m, zsize // 2)],
        scratch_shapes=[V(n + 18 + m + 9, 1, 40, LANES)] + work(state) + [V(2, m + 6, 16, LANES), V(m + 6, 16, LANES)]
        + [V(*small), V(*small), V(2, *small), V(2, 2, *small)],
        compiler_params=params(24),
        name="coarse_levels",
    )(place, fc, xlo, xhi, chip, other)
    return fine, second_u, third, coarse


def solution(mesh):
    placed = (P(None, "gx", "gy", None), P("gx", "gy", None))
    return jax.shard_map(body, mesh=mesh, in_specs=placed, out_specs=(P(None, "gx", "gy", None),) * 4, check_vma=False)
```

```python
import functools
import jax
import jax.numpy as jnp
from jax import lax
from jax.experimental import pallas as pl
from jax.experimental.pallas import tpu as pltpu
from jax.sharding import PartitionSpec as P

DAMPING = 0.8
SHIFT_IMAG = 0.5
LANES = 128
VMEM = pl.BlockSpec(memory_space=pltpu.VMEM)
SMEM = pl.BlockSpec(memory_space=pltpu.SMEM)
ANY = pl.BlockSpec(memory_space=pl.ANY)


def params(mib):
    return pltpu.CompilerParams(vmem_limit_bytes=mib * 1024 * 1024)


def around(ref, k, x, row, rows, full):
    halves = ref.shape[2]
    mid = [ref[k, x, h, pl.ds(row, rows), :] for h in range(halves)]
    up = [pltpu.roll(m, 1, 1) for m in mid]
    down = [pltpu.roll(m, LANES - 1, 1) for m in mid]
    if full:
        lane = lax.broadcasted_iota(jnp.int32, mid[0].shape, 1)
        first, last = lane == 0, lane == LANES - 1
        up = [jnp.where(first, up[h - 1] if h else 0.0, up[h]) for h in range(halves)]
        down = [jnp.where(last, down[h + 1] if h < halves - 1 else 0.0, down[h]) for h in range(halves)]
    sums = []
    for h in range(halves):
        planes = ref[k, x - 1, h, pl.ds(row, rows), :] + ref[k, x + 1, h, pl.ds(row, rows), :]
        sides = ref[k, x, h, pl.ds(row - 1, rows), :] + ref[k, x, h, pl.ds(row + 1, rows), :]
        sums.append((planes + sides) + (up[h] + down[h]))
    return sums


def inverse(c, scale, ok):
    a = 6.0 / scale - c
    b = SHIFT_IMAG * c
    g = DAMPING / (a * a + b * b)
    if ok is not None:
        g = jnp.where(ok, g, 0.0)
    return g * a, g * b


def divided(re, im, a, b):
    return re * a + im * b, im * a - re * b


def point(re, im, c, scale, ok, u, ga, gb, x, h, row):
    a, b = inverse(c, scale, ok)
    at = pl.ds(row, c.shape[0])
    ga[x, h, at, :], gb[x, h, at, :] = a, b
    u[0, x, h, at, :], u[1, x, h, at, :] = divided(re, im, a, b)


def second(u, ga, gb, e, x, row, rows, scale, full):
    s_re, s_im = around(u, 0, x, row, rows, full), around(u, 1, x, row, rows, full)
    at = pl.ds(row, rows)
    for h in range(u.shape[2]):
        a, b = ga[x, h, at, :], gb[x, h, at, :]
        if scale != 1.0:
            a, b = a * (1.0 / scale), b * (1.0 / scale)
        d = divided(s_re[h], s_im[h], a, b)
        for k in (0, 1):
            e[k, x, h, at, :] = 0.4 * u[k, x, h, at, :] + d[k]


def is_even(place, shape):
    return jnp.full(shape, lax.rem(place[1], 2)) == 0


def rows_inside(shape, y0, ysize):
    row = lax.broadcasted_iota(jnp.int32, shape, 0) + y0
    return (row >= 0) & (row < ysize)


def restrict_rows(vals, t, out, to, row, rows, k, start):
    for h, val in enumerate(vals):
        t[k, h, pl.ds(start, val.shape[0]), :] = val
        part = [t[k, h, pl.ds(row + j, rows, 2), :] for j in range(4)]
        out[k, to, pl.ds(0, rows), pl.ds(LANES * h, LANES)] = (part[0] + part[3]) + 3.0 * (part[1] + part[2])


def restrict_xy(r, t, out, to, plane, row, rows, k, window):
    at = pl.ds(*window)
    vals = []
    for h in range(r.shape[2]):
        four = [r[k, plane + j, h, at, :] for j in range(4)]
        vals.append((four[0] + four[3]) + 3.0 * (four[1] + four[2]))
    restrict_rows(vals, t, out, to, row, rows, k, window[0])


def add_pairs(c0, c1, t, h, out, i, row, rows):
    t[0, h, pl.ds(0, c0.shape[0]), :] = c0 + c1
    val = t[0, h, pl.ds(row, rows, 2), :] + t[0, h, pl.ds(row + 1, rows, 2), :]
    out[i, pl.ds(0, rows), pl.ds(LANES * h, LANES)] = val


def weights(lanes, zsize, mean=False, shift=0):
    z = lax.broadcasted_iota(jnp.int32, (lanes, LANES), 0)
    i = lax.broadcasted_iota(jnp.int32, (lanes, LANES), 1) - shift
    d = z - 2 * i
    inner = (d == 0) | (d == 1)
    if mean:
        w = jnp.where(inner, 0.125, 0.0)
    else:
        w = jnp.where(inner, 3.0 / 512.0, jnp.where((d == -1) | (d == 2), 1.0 / 512.0, 0.0))
    return jnp.where((z < zsize) & (i >= 0) & (i < zsize // 2), w, 0.0).astype(jnp.bfloat16)


def exact_dot(part, w):
    planes, rows, lanes = part.shape
    x = part.reshape(planes * rows, lanes)
    hi = x.astype(jnp.bfloat16)
    rest = x - hi.astype(jnp.float32)
    mid = rest.astype(jnp.bfloat16)
    low = (rest - mid.astype(jnp.float32)).astype(jnp.bfloat16)
    dot = functools.partial(jnp.dot, preferred_element_type=jnp.float32)
    return (dot(hi, w) + (dot(mid, w) + dot(low, w))).reshape(planes, rows, w.shape[1])


PX, PY = 2, 8


def planes_kernel(f, c, x_first, x_last, planes, sems):
    n = c.shape[0]
    copies = []
    for side, x in enumerate((0, n - PX)):
        at = pl.ds(x, PX)
        copies += [(c.at[at], planes.at[side, 2]), (f.at[0, at], planes.at[side, 0]), (f.at[1, at], planes.at[side, 1])]
    copies = [pltpu.make_async_copy(src, dst, sems.at[i]) for i, (src, dst) in enumerate(copies)]
    for copy in copies:
        copy.start()
    for side, out in enumerate((x_first, x_last)):
        for copy in copies[3 * side : 3 * side + 3]:
            copy.wait()
        for j in range(PX):
            a, b = inverse(planes[side, 2, j], 1.0, None)
            out[j], out[PX + j] = divided(planes[side, 0, j], planes[side, 1, j], a, b)
        out[2 * PX] = planes[side, 2, (PX - 1) * side]


def first_kernel(place, f, c, u, ga, gb, y_chip, y_next):
    n, rows, lanes = c.shape
    cut = [pl.ds(LANES * h, LANES) for h in range(lanes // LANES)]
    row = lax.broadcasted_iota(jnp.int32, (8, LANES), 0)
    even = is_even(place, (8, LANES))

    def step(x, carry):
        for h, lane in enumerate(cut):
            point(f[0, x, :, lane], f[1, x, :, lane], c[x, :, lane], 1.0, None, u, ga, gb, x + PX, h, PY)
            made = []
            for start, shifts in ((0, (0, 3, 6)), (rows - 8, (3, 6, 0))):
                tiles = [u[k, x + PX, h, pl.ds(PY + start, 8), :] for k in (0, 1)] + [c[x, pl.ds(start, 8), lane]]
                re, im, cc = [pltpu.roll(v, shift, 0) if shift else v for v, shift in zip(tiles, shifts)]
                made.append(jnp.where(row < 3, re, jnp.where(row < 6, im, cc)))
            y_chip[x, :, lane], y_next[x, :, lane] = jnp.where(even, made[1], made[0]), jnp.where(even, made[0], made[1])
        return carry

    lax.fori_loop(0, n, step, 0, unroll=True)


def inner_kernel(f, c, u, ga, gb, e, r, fc_out, t, part):
    n, rows, lanes = c.shape
    halves = lanes // LANES
    at = pl.ds(PY, rows)
    cut = [pl.ds(LANES * h, LANES) for h in range(halves)]

    def middle(x, carry):
        second(u, ga, gb, e, x + PX, PY, rows, 1.0, True)
        return carry

    lax.fori_loop(1, n - 1, middle, 0, unroll=True)
    row = lax.broadcasted_iota(jnp.int32, (rows, LANES), 0)
    full = (row >= 2) & (row < rows - 2)

    def last(x, carry):
        for k in (0, 1):
            s = around(e, k, x + PX, PY, rows, True)
            for h in range(halves):
                r[k, x + PX, h, at, :] = 0.04 * f[k, x, :, cut[h]] + jnp.where(full, s[h], 0.0)
        return carry

    lax.fori_loop(2, n - 2, last, 0, unroll=True)
    for x in (0, 1, n - 2, n - 1):
        for k in (0, 1):
            for h in range(halves):
                r[k, x + PX, h, at, :] = 0.04 * f[k, x, :, cut[h]]
    for x in (PX - 1, n + PX):
        r[:, x] = jnp.zeros((2,) + r.shape[2:], jnp.float32)

    def pairs(i, carry):
        for h in range(halves):
            add_pairs(c[2 * i, :, cut[h]], c[2 * i + 1, :, cut[h]], t, h, part.at[2], i, 0, rows // 2)
        return carry

    lax.fori_loop(0, n // 2, pairs, 0, unroll=True)

    def coarse(i, carry):
        for k in (0, 1):
            restrict_xy(r, t, part, i, 2 * i + PX - 1, PY - 1, rows // 2, k, (PY, rows))
        return carry

    lax.fori_loop(2, n // 2 - 2, coarse, 0, unroll=True)
    w = weights(lanes, lanes)
    for k in (0, 1):
        fc_out[k, 2 : n // 2 - 2] = exact_dot(part[k, 2 : n // 2 - 2], w)
    fc_out[2] = exact_dot(part[2], weights(lanes, lanes, mean=True))


def inside(place, n, rows, xsize, ysize):
    x0, y0 = place[0] * n - PX, place[1] * rows - PY

    def ok(x, row, count):
        gx = x + x0
        return rows_inside((count, LANES), y0 + row, ysize) & ((gx >= 0) & (gx < xsize))

    return ok


def halo(re, im, cc, good, u, ga, gb, r, x, h, row, c_here, r_here):
    at = pl.ds(row, re.shape[0])
    re, im = jnp.where(good, re, 0.0), jnp.where(good, im, 0.0)
    u[0, x, h, at, :], u[1, x, h, at, :] = re, im
    if c_here:
        a, b = inverse(cc, 1.0, good)
        ga[x, h, at, :], gb[x, h, at, :] = a, b
    if r_here:
        a, b = 0.05 * (6.0 - cc), (0.05 * SHIFT_IMAG) * cc
        r[0, x, h, at, :], r[1, x, h, at, :] = re * a - im * b, im * a + re * b


def finish(e, r, x, row, count, good):
    for k in (0, 1):
        s = around(e, k, x, row, count, True)
        for h in range(e.shape[2]):
            at = pl.ds(row, count)
            r[k, x, h, at, :] = r[k, x, h, at, :] + jnp.where(good, s[h], 0.0)


def plane_cells(side, low, i, h):
    cut = pl.ds(LANES * h, LANES)
    c_here = i == (PX - 1 if low else 0)
    return side[i, :, cut], side[PX + i, :, cut], side[2 * PX, :, cut] if c_here else None, c_here


def faces_kernel(xsize, ysize, place, u_in, e_in, r_in, ga_in, gb_in, fc_in, xlo, xhi, y_chip, y_next, u, e, r, ga, gb, fc_out, part, q, sides, sems):
    n, (rows, lanes) = y_chip.shape[0], xlo.shape[1:]
    halves = lanes // LANES
    cut = [pl.ds(LANES * h, LANES) for h in range(halves)]
    ok = inside(place, n, rows, xsize, ysize)
    del u_in, e_in, r_in, ga_in, gb_in, fc_in
    used = pl.ds(0, 2 * PX + 1)
    copies = [pltpu.make_async_copy(src.at[used], sides.at[i], sems.at[i]) for i, src in enumerate((xlo, xhi))]
    for copy in copies:
        copy.start()
    low, high = PY - 4, PY + rows - 4
    good_lo, good_hi = ok(PX, 0, 8), ok(PX, PY + rows, 8)
    even = is_even(place, (8, LANES))

    def strips(x, carry):
        for h in range(halves):
            chip, other = y_chip[x, :, cut[h]], y_next[x, :, cut[h]]
            lo, hi = jnp.where(even, other, chip), jnp.where(even, chip, other)
            for tile, good, row, shifts in ((lo, good_lo, 0, (5, 2, 0)), (hi, good_hi, PY + rows, (0, 5, 2))):
                re, im, cc = [pltpu.roll(tile, shift, 0) if shift else tile for shift in shifts]
                halo(re, im, cc, good, u, ga, gb, r, x + PX, h, row, True, True)
        return carry

    lax.fori_loop(0, n, strips, 0, unroll=True)
    for copy in copies:
        copy.wait()
    for side, is_low, base in ((sides.at[0], True, 0), (sides.at[1], False, n + PX)):
        for i in range(PX):
            good = ok(base + i, PY, rows)
            for h in range(halves):
                re, im, cc, c_here = plane_cells(side, is_low, i, h)
                halo(re, im, cc, good, u, ga, gb, r, base + i, h, PY, c_here, False)
    for x in (PX - 1, PX, n + PX - 1, n + PX):
        second(u, ga, gb, e, x, PY, rows, 1.0, True)

    def middle(x, carry):
        for row in (low, high):
            second(u, ga, gb, e, x, row, 8, 1.0, True)
        return carry

    lax.fori_loop(PX + 1, n + PX - 1, middle, 0, unroll=True)
    for x in (PX, PX + 1, n + PX - 2, n + PX - 1):
        finish(e, r, x, PY + 4, rows - 8, ok(x, PY + 4, rows - 8))
    row = lax.broadcasted_iota(jnp.int32, (8, LANES), 0)
    good_low, good_high = ok(PX, low, 8) & (row < 6), ok(PX, high, 8) & (row >= 2)

    def last(x, carry):
        finish(e, r, x, low, 8, good_low)
        finish(e, r, x, high, 8, good_high)
        return carry

    lax.fori_loop(PX + 2, n + PX - 2, last, 0, unroll=True)
    m = n // 2 - 4

    def coarse(i, carry):
        x = 2 * i + PX + 3
        for k in (0, 1):
            for h in range(halves):
                for j, row in ((0, PY - 1), (8, PY + rows - 7)):
                    at = pl.ds(row, 8)
                    part[k, i, pl.ds(j, 8), cut[h]] = (r[k, x, h, at, :] + r[k, x + 3, h, at, :]) + 3.0 * (
                        r[k, x + 1, h, at, :] + r[k, x + 2, h, at, :]
                    )
        return carry

    lax.fori_loop(0, m, coarse, 0, unroll=True)
    w = weights(lanes, lanes)
    for k in (0, 1):
        q[k] = exact_dot(part[k], w)
        for row, start in ((0, 0), (rows // 2 - 2, 10)):
            four = [q[k, :, pl.ds(start + j, 2, 2), :] for j in range(4)]
            fc_out[k, pl.ds(2, m), pl.ds(row, 2), :] = (four[0] + four[3]) + 3.0 * (four[1] + four[2])


def pack_corners_kernel(place, xlo, xhi, chip, other, tiles, sems):
    count, rows = 2 * PX + 1, xlo.shape[1]
    copies = []
    for i, side in enumerate((xlo, xhi)):
        for j, row in enumerate((0, rows - 8)):
            copies.append(pltpu.make_async_copy(side.at[pl.ds(0, count), pl.ds(row, 8)], tiles.at[j, pl.ds(count * i, count)], sems.at[2 * i + j]))
    for copy in copies:
        copy.start()
    even = is_even(place, (4, xlo.shape[2]))
    for copy in copies:
        copy.wait()
    for j in range(2 * count):
        first, last = tiles[0, j, pl.ds(0, 4), :], tiles[1, j, pl.ds(4, 4), :]
        chip[j], other[j] = jnp.where(even, last, first), jnp.where(even, first, last)


def corners_kernel(xsize, ysize, n, rows, place, u_in, e_in, r_in, ga_in, gb_in, fc_in, c_chip, c_next, u, e, r, ga, gb, fc_out, edge_out, t, part):
    halves = c_chip.shape[2] // LANES
    even = is_even(place, (4, LANES))
    ok = inside(place, n, rows, xsize, ysize)
    del u_in, e_in, r_in, ga_in, gb_in, fc_in
    low, high = PY - 4, PY + rows - 4
    held = 2 * PX + 1
    for first, low_planes, base in ((0, True, 0), (held, False, n + PX)):
        chip, other = c_chip.at[pl.ds(first, held)], c_next.at[pl.ds(first, held)]
        for i in range(PX):
            for h in range(halves):
                one, two = plane_cells(chip, low_planes, i, h), plane_cells(other, low_planes, i, h)
                for row, (p, q) in ((PY - 4, (two, one)), (PY + rows, (one, two))):
                    re, im, cc = [None if v is None else jnp.where(even, v, w) for v, w in zip(p[:3], q[:3])]
                    halo(re, im, cc, ok(base + i, row, 4), u, ga, gb, r, base + i, h, row, one[3], False)
    for x in (PX - 1, PX, n + PX - 1, n + PX):
        for row in (low, high):
            second(u, ga, gb, e, x, row, 8, 1.0, True)
    for x in (PX, PX + 1, n + PX - 2, n + PX - 1):
        for row in (low, high):
            finish(e, r, x, row, 8, ok(x, row, 8))
    planes = (0, 1, n // 2 - 2, n // 2 - 1)
    w = weights(part.shape[3], part.shape[3])
    for k in (0, 1):
        for j, i in enumerate(planes):
            restrict_xy(r, t, part, j, 2 * i + PX - 1, PY - 1, rows // 2, k, (low, rows + 8))
        for j, x in ((4, PX), (5, n + PX - 1)):
            restrict_rows([r[k, x, h, pl.ds(low, rows + 8), :] for h in range(halves)], t, part, j, PY - 1, rows // 2, k, low)
        val = exact_dot(part[k], w)
        for j, i in enumerate(planes):
            fc_out[k, i] = val[j]
        edge_out[0, k], edge_out[1, k] = val[4], val[5]


def iterate_kernel(u, e, out):
    n, rows = out.shape[1:3]
    at = pl.ds(PY, rows)

    def step(x, carry):
        for k in (0, 1):
            for h in range(u.shape[2]):
                out[k, x, :, pl.ds(LANES * h, LANES)] = e[k, x + PX, h, at, :] + 0.8 * u[k, x + PX, h, at, :]
        return carry

    lax.fori_loop(0, n, step, 0, unroll=2)


def whole_level(cells, u, e, r, ga, gb, planes, used, row, rows, scale, full, ok, u_put):
    first, count = used
    for x in range(planes):
        at = pl.ds(first, count)
        point(cells(0, x, at), cells(1, x, at), cells(2, x, at), scale, ok(x, first, count), u, ga, gb, x, 0, first)
    at = pl.ds(row, rows)
    for x in range(1, planes - 1):
        second(u, ga, gb, e, x, row, rows, scale, full)
        u_put(x)
    for x in range(2, planes - 2):
        good = ok(x, row, rows)
        for k in (0, 1):
            s = around(e, k, x, row, rows, full)[0] * (1.0 / scale)
            r[k, x, 0, at, :] = jnp.where(good, 0.04 * cells(k, x, at) + s, 0.0)


def rows_kernel(xdev, halo, place, xlo, fc, xhi, edges, chip, other, window):
    n, rows = fc.shape[1:3]
    row = lax.broadcasted_iota(jnp.int32, (8, LANES), 0)
    even = is_even(place, (8, LANES))
    here = jnp.full((rows, LANES), place[0])
    for k in range(3):
        window[k, pl.ds(0, halo)] = xlo[pl.ds(k * halo, halo)]
        window[k, pl.ds(halo, n)] = fc[k]
        window[k, pl.ds(n + halo, halo)] = xhi[pl.ds(k * halo, halo)]
    for k in (0, 1):
        window[k, halo - 1] += edges[0, k]
        window[k, halo] += jnp.where(here > 0, xlo[3 * halo + k], 0.0)
        window[k, n + halo - 1] += jnp.where(here < xdev - 1, xhi[3 * halo + k], 0.0)
        window[k, n + halo] += edges[1, k]
    for x in range(n + 2 * halo):
        made = []
        for start, own in ((0, row < 5), (rows - 8, row >= 3)):
            re, im, cc = [window[k, x, pl.ds(start, 8), :] for k in range(3)]
            made.append((jnp.where(own, re, pltpu.roll(cc, 5, 0)), jnp.where(own, im, pltpu.roll(cc, 2, 0))))
        for k, (first, last) in enumerate(zip(*made)):
            chip[k, x], other[k, x] = jnp.where(even, last, first), jnp.where(even, first, last)


def middle_kernel(halo, over, xsize, ysize, place, window, y_chip, y_next, u_out, fc_out, fc, ga, gb, u, e, r, t, part, part_c):
    planes, rows = window.shape[1:3]
    n = planes - 2 * halo
    for k in range(3):
        fc[k, :, 0, pl.ds(8, rows), :] = window[k]
    row = lax.broadcasted_iota(jnp.int32, (8, LANES), 0)
    even = is_even(place, (8, LANES))
    for x in range(planes):
        chip, other = [y_chip[k, x] for k in (0, 1)], [y_next[k, x] for k in (0, 1)]
        for start, split, p, q in ((0, 6, other, chip), (8 + rows, 3, chip, other)):
            at = pl.ds(start, 8)
            one, two = [jnp.where(even, v, w) for v, w in zip(p, q)]
            fc[0, x, 0, at, :], fc[1, x, 0, at, :] = one, two
            fc[2, x, 0, at, :] = jnp.where(row < split, pltpu.roll(one, 3, 0), pltpu.roll(two, 6, 0))
    x0, y0 = place[0] * n - halo, place[1] * rows - 8

    def ok(x, row, count):
        gx = x + x0
        return rows_inside((count, LANES), y0 + row, ysize) & ((gx >= 0) & (gx < xsize))

    def u_put(x):
        if halo <= x < n + halo:
            at = pl.ds(8, rows)
            for k in (0, 1):
                u_out[k, x - halo] = e[k, x, 0, at, :] + 0.8 * u[k, x, 0, at, :]

    def cells(k, x, at):
        return fc[k, x, 0, at, :]

    whole_level(cells, u, e, r, ga, gb, planes, (0, rows + 16), 4, rows + 8, 4.0, True, ok, u_put)
    width = n // 2 + 2 * over
    pairs = width // 2
    for i in range(width):
        x, row = 2 * i + halo - 1 - 2 * over, 7 - 2 * over
        for k in (0, 1):
            restrict_xy(r, t, part, i, x, row, width, k, (4, rows + 8))
        add_pairs(fc[2, x + 1, 0], fc[2, x + 2, 0], t, 0, part_c.at[i % 2], i // 2, row + 1, width)
    two = [(part.at[k], part_c.at[k], LANES // 2 * k) for k in (0, 1)]
    fc_out[pl.ds(0, width)] = sum(exact_dot(p[...], weights(LANES, LANES, shift=s)) for p, _, s in two)[:, :width]
    fc_out[pl.ds(width, pairs)] = sum(exact_dot(p[...], weights(LANES, LANES, True, s)) for _, p, s in two)[:, :width]


def coarse_kernel(n, sweeps, xsize, ysize, zsize, place, fc_own, xlo, xhi, y_chip, y_next, u_out, v_out, fc, ga, gb, u, e, r, t, part, part_c, gc, gd, v, w):
    m = n // 2
    planes = n + 18
    for src, x, first, count in ((xlo, 0, 0, 8), (fc_own, 8, 0, n + 2), (xhi, n + 10, 0, 8), (xlo, planes, 8, 4), (fc_own, planes + 4, n + 2, m + 1), (xhi, planes + m + 5, 8, 4)):
        fc[pl.ds(x, count), 0, pl.ds(15, n + 2), :] = src[pl.ds(first, count)]
    even = is_even(place, (8, LANES))
    for x in range(fc.shape[0]):
        chip, other = y_chip[x], y_next[x]
        fc[x, 0, pl.ds(7, 8), :], fc[x, 0, pl.ds(n + 17, 8), :] = jnp.where(even, other, chip), jnp.where(even, chip, other)
    lane = lax.broadcasted_iota(jnp.int32, (1, LANES), 1)

    def cells(k, x, at):
        val = fc[planes + x // 2 if k == 2 else x, 0, at, :]
        return pltpu.roll(val, LANES - zsize, 1) if k == 1 or (k == 2 and x % 2) else val

    def inside(x0, y0, xs, ys, zs):
        def ok(x, row, count):
            gx = x + x0
            here = rows_inside((count, LANES), y0 + row, ys) & (lane < zs)
            return here & ((gx >= 0) & (gx < xs))

        return ok

    def u_put(x):
        if 9 <= x < n + 9:
            at = pl.ds(16, n)
            for k in (0, 1):
                u_out[k, x - 9] = (e[k, x, 0, at, :] + 0.8 * u[k, x, 0, at, :])[:, :zsize]

    ok = inside(place[0] * n - 9, place[1] * n - 16, xsize, ysize, zsize)
    whole_level(cells, u, e, r, ga, gb, planes, (7, n + 18), 8, n + 16, 16.0, False, ok, u_put)
    width = m + 6
    every = pl.ds(8, n + 16)
    for i in range(width):
        for k in (0, 1):
            restrict_xy(r, t, part, i, 2 * i + 2, 9, width, k, (8, n + 16))
        t[0, 0, every, :] = cells(2, 2 * i + 3, every) + cells(2, 2 * i + 4, every)
        part_c[i, pl.ds(0, width), :] = t[0, 0, pl.ds(10, width, 2), :] + t[0, 0, pl.ds(11, width, 2), :]
    w_full = weights(LANES, zsize)
    f = [exact_dot(part[k], w_full) for k in (0, 1)] + [exact_dot(part_c[...], weights(LANES, zsize, True))]
    ok = inside(place[0] * m - 3, place[1] * m - 3, xsize // 2, ysize // 2, zsize // 2)
    for x in range(width):
        point(f[0][x], f[1][x], f[2][x], 64.0, ok(x, 0, 16), v, gc, gd, x, 0, 0)
    old = v
    for sweep in range(1, sweeps):
        new = w.at[sweep % 2]
        for x in range(sweep, width - sweep):
            at = pl.ds(1, m + 4)
            s = [around(old, k, x, 1, m + 4, False)[0] for k in (0, 1)]
            d = divided(*s, gc[x, 0, at, :] * (1.0 / 64.0), gd[x, 0, at, :] * (1.0 / 64.0))
            for k in (0, 1):
                val = 0.2 * old[k, x, 0, at, :] + v[k, x, 0, at, :] + d[k]
                if sweep < sweeps - 1:
                    new[k, x, 0, at, :] = val
                else:
                    v_out[k, x - 3] = val[2 : 2 + m, : zsize // 2]
        old = new


def body(source, wavenumber_sq):
    f32 = jnp.float32
    xdev, ydev = lax.axis_size("gx"), lax.axis_size("gy")
    place = jnp.stack([lax.axis_index("gx"), lax.axis_index("gy")]).astype(jnp.int32)

    def planes_step(first, last):
        before = lax.ppermute(last, "gx", [(i, (i + 1) % xdev) for i in range(xdev)])
        after = lax.ppermute(first, "gx", [((i + 1) % xdev, i) for i in range(xdev)])
        return before, after

    every = [(i, j) for i in range(xdev) for j in range(ydev)]
    number = lambda i, j: i * ydev + j
    on_chip = [(number(i, j), number(i, j ^ 1)) for i, j in every]
    next_chip = [(number(i, j), number(i ^ 1, j) if j in (0, ydev - 1) else number(i, ((j - 1) ^ 1) + 1)) for i, j in every]

    def rows_step(chip, other):
        return lax.ppermute(chip, ("gx", "gy"), on_chip), lax.ppermute(other, ("gx", "gy"), next_chip)

    _, n, rows, lanes = source.shape
    xsize, ysize = n * xdev, rows * ydev
    S = lambda *shape: jax.ShapeDtypeStruct(shape, f32)
    V = lambda *shape: pltpu.VMEM(shape, f32)

    halves = lanes // LANES
    state = (n + 2 * PX, halves, rows + 2 * PY, LANES)
    part = (n // 2, rows // 2, lanes)
    two, one, coarser = S(2, *state), S(*state), S(3, n // 2, rows // 2, lanes // 2)
    column = V(2, halves, rows + 2 * PY, LANES)
    held_planes = 2 * PX + 1
    x_first, x_last = pl.pallas_call(
        planes_kernel,
        in_specs=[pl.BlockSpec(memory_space=pltpu.HBM)] * 2,
        out_specs=[VMEM] * 2,
        out_shape=[S(held_planes + 2, rows, lanes)] * 2,
        scratch_shapes=[V(2, 3, PX, rows, lanes), pltpu.SemaphoreType.DMA((6,))],
        compiler_params=params(24),
        name="pack_planes",
    )(*[pltpu.with_memory_space_constraint(x, pltpu.HBM) for x in (source, wavenumber_sq)])
    source, wavenumber_sq, x_first, x_last = lax.optimization_barrier((source, wavenumber_sq, x_first, x_last))
    xlo, xhi = planes_step(x_first, x_last)
    u, ga, gb, y_chip, y_next = pl.pallas_call(
        first_kernel,
        in_specs=[SMEM] + [VMEM] * 2,
        out_specs=[VMEM] * 5,
        out_shape=[two, one, one] + [S(n, 8, lanes)] * 2,
        compiler_params=params(24),
        cost_estimate=pl.CostEstimate(flops=30_000_000, bytes_accessed=8_000_000, transcendentals=0),
        name="first_iterate",
    )(place, source, wavenumber_sq)
    y_chip, y_next = rows_step(y_chip, y_next)
    e, r, fc = pl.pallas_call(
        inner_kernel,
        in_specs=[VMEM] * 5,
        out_specs=[VMEM] * 3,
        out_shape=[two, two, coarser],
        scratch_shapes=[column, V(3, *part)],
        compiler_params=params(24),
        cost_estimate=pl.CostEstimate(flops=70_000_000, bytes_accessed=16_000_000, transcendentals=0),
        name="inner_cells",
    )(source, wavenumber_sq, u, ga, gb)
    held = (u, e, r, ga, gb, fc)
    shapes = [two] * 3 + [one] * 2 + [coarser]
    xlo, xhi, held = lax.optimization_barrier((xlo, xhi, held))
    c_chip, c_next = rows_step(
        *pl.pallas_call(
            pack_corners_kernel,
            in_specs=[SMEM] + [ANY] * 2,
            out_specs=[VMEM] * 2,
            out_shape=[S(2 * held_planes, 4, lanes)] * 2,
            scratch_shapes=[V(2, 2 * held_planes, 8, lanes), pltpu.SemaphoreType.DMA((4,))],
            compiler_params=params(24),
            name="pack_corners",
        )(place, xlo, xhi)
    )
    in_place = {i + 1: i for i in range(6)}
    held = pl.pallas_call(
        functools.partial(faces_kernel, xsize, ysize),
        in_specs=[SMEM] + [VMEM] * 6 + [ANY] * 2 + [VMEM] * 2,
        out_specs=[VMEM] * 6,
        out_shape=shapes,
        input_output_aliases=in_place,
        scratch_shapes=[V(2, n // 2 - 4, 16, lanes), V(2, n // 2 - 4, 16, lanes // 2), V(2, held_planes, rows, lanes), pltpu.SemaphoreType.DMA((2,))],
        compiler_params=params(24),
        cost_estimate=pl.CostEstimate(flops=50_000_000, bytes_accessed=8_000_000, transcendentals=0),
        name="face_cells",
    )(place, *held, xlo, xhi, y_chip, y_next)
    u, e, _, _, _, fc, edges = pl.pallas_call(
        functools.partial(corners_kernel, xsize, ysize, n, rows),
        in_specs=[SMEM] + [VMEM] * 8,
        out_specs=[VMEM] * 7,
        out_shape=shapes + [S(2, 2, rows // 2, lanes // 2)],
        input_output_aliases=in_place,
        scratch_shapes=[column, V(2, 6, rows // 2, lanes)],
        compiler_params=params(24),
        name="corner_cells",
    )(place, *held, c_chip, c_next)
    fine_shape = S(2, n, rows, lanes)
    n, rows, lanes, xsize, ysize, zsize = n // 2, rows // 2, lanes // 2, xsize // 2, ysize // 2, lanes // 2
    h, over = 5, 1
    slab = lambda x, edge: jnp.concatenate([fc[:, x : x + h].reshape(3 * h, rows, lanes), edge], 0)
    xlo, xhi = planes_step(slab(0, edges[0]), slab(n - h, edges[1]))
    fine = pl.pallas_call(
        iterate_kernel,
        in_specs=[VMEM] * 2,
        out_specs=VMEM,
        out_shape=fine_shape,
        compiler_params=params(24),
        cost_estimate=pl.CostEstimate(flops=1_000_000, bytes_accessed=8_000_000, transcendentals=0),
        name="fine_iterate",
    )(u, e)
    xlo, xhi, fine = lax.optimization_barrier((xlo, xhi, fine))
    chip, other, window = pl.pallas_call(
        functools.partial(rows_kernel, xdev, h),
        in_specs=[SMEM] + [VMEM] * 4,
        out_specs=[VMEM] * 3,
        out_shape=[S(2, n + 2 * h, 8, lanes)] * 2 + [S(3, n + 2 * h, rows, lanes)],
        compiler_params=params(24),
        name="second_rows",
    )(place, xlo, fc, xhi, edges)
    chip, other = rows_step(chip, other)
    state = (n + 2 * h, 1, rows + 16, LANES)
    work = lambda s: [V(*s), V(*s), V(2, *s), V(2, *s), V(2, *s), V(2, 1, *s[2:])]
    width = n // 2 + 2 * over
    second_u, fc = pl.pallas_call(
        functools.partial(middle_kernel, h, over, xsize, ysize),
        in_specs=[SMEM] + [VMEM] * 3,
        out_specs=[VMEM] * 2,
        out_shape=[S(2, n, rows, lanes), S(width + width // 2, width, lanes)],
        scratch_shapes=[V(3, *state)] + work(state) + [V(2, width, 16, LANES), V(2, width // 2, 16, LANES)],
        compiler_params=params(24),
        name="second_level",
    )(place, window, chip, other)

    n, xsize, ysize, zsize = n // 2, xsize // 2, ysize // 2, zsize // 2
    m = n // 2

    def joined(lo, own, hi, cells):
        f = (lo[:n], own[: n + 2], hi[:n])
        c = (lo[n:], own[n + 2 :], hi[n:])
        return jnp.concatenate([a[:, cells] for a in f + c], 0)

    pick = lambda i, j: jnp.concatenate([fc[i : i + n], fc[n + 2 + j : n + 2 + j + m]], 0)
    xlo, xhi = planes_step(pick(2, 1), pick(0, 0))
    first, last = joined(xlo, fc, xhi, slice(2, n + 2)), joined(xlo, fc, xhi, slice(0, n))
    even = place[1] % 2 == 0
    chip, other = rows_step(jnp.where(even, last, first), jnp.where(even, first, last))
    state = (n + 18, 1, 40, LANES)
    small = (m + 6, 1, 16, LANES)
    third, coarse = pl.pallas_call(
        functools.partial(coarse_kernel, n, 4, xsize, ysize, zsize),
        in_specs=[SMEM] + [VMEM] * 5,
        out_specs=[VMEM] * 2,
        out_shape=[S(2, n, n, zsize), S(2, m, m, zsize // 2)],
        scratch_shapes=[V(n + 18 + m + 9, 1, 40, LANES)] + work(state) + [V(2, m + 6, 16, LANES), V(m + 6, 16, LANES)]
        + [V(*small), V(*small), V(2, *small), V(2, 2, *small)],
        compiler_params=params(24),
        name="coarse_levels",
    )(place, fc, xlo, xhi, chip, other)
    return fine, second_u, third, coarse


def solution(mesh):
    placed = (P(None, "gx", "gy", None), P("gx", "gy", None))
    return jax.shard_map(body, mesh=mesh, in_specs=placed, out_specs=(P(None, "gx", "gy", None),) * 4, check_vma=False)
```

```python
import functools
import jax
import jax.numpy as jnp
from jax import lax
from jax.experimental import pallas as pl
from jax.experimental.pallas import tpu as pltpu
from jax.sharding import PartitionSpec as P

DAMPING = 0.8
SHIFT_IMAG = 0.5
LANES = 128
VMEM = pl.BlockSpec(memory_space=pltpu.VMEM)
SMEM = pl.BlockSpec(memory_space=pltpu.SMEM)
ANY = pl.BlockSpec(memory_space=pl.ANY)


def params(mib):
    return pltpu.CompilerParams(vmem_limit_bytes=mib * 1024 * 1024)


def around(ref, k, x, row, rows, full):
    halves = ref.shape[2]
    mid = [ref[k, x, h, pl.ds(row, rows), :] for h in range(halves)]
    up = [pltpu.roll(m, 1, 1) for m in mid]
    down = [pltpu.roll(m, LANES - 1, 1) for m in mid]
    if full:
        lane = lax.broadcasted_iota(jnp.int32, mid[0].shape, 1)
        first, last = lane == 0, lane == LANES - 1
        up = [jnp.where(first, up[h - 1] if h else 0.0, up[h]) for h in range(halves)]
        down = [jnp.where(last, down[h + 1] if h < halves - 1 else 0.0, down[h]) for h in range(halves)]
    sums = []
    for h in range(halves):
        planes = ref[k, x - 1, h, pl.ds(row, rows), :] + ref[k, x + 1, h, pl.ds(row, rows), :]
        sides = ref[k, x, h, pl.ds(row - 1, rows), :] + ref[k, x, h, pl.ds(row + 1, rows), :]
        sums.append((planes + sides) + (up[h] + down[h]))
    return sums


def inverse(c, scale, ok):
    a = 6.0 / scale - c
    b = SHIFT_IMAG * c
    g = DAMPING / (a * a + b * b)
    if ok is not None:
        g = jnp.where(ok, g, 0.0)
    return g * a, g * b


def divided(re, im, a, b):
    return re * a + im * b, im * a - re * b


def point(re, im, c, scale, ok, u, ga, gb, x, h, row):
    a, b = inverse(c, scale, ok)
    at = pl.ds(row, c.shape[0])
    ga[x, h, at, :], gb[x, h, at, :] = a, b
    u[0, x, h, at, :], u[1, x, h, at, :] = divided(re, im, a, b)


def second(u, ga, gb, e, x, row, rows, scale, full):
    s_re, s_im = around(u, 0, x, row, rows, full), around(u, 1, x, row, rows, full)
    at = pl.ds(row, rows)
    for h in range(u.shape[2]):
        a, b = ga[x, h, at, :], gb[x, h, at, :]
        if scale != 1.0:
            a, b = a * (1.0 / scale), b * (1.0 / scale)
        d = divided(s_re[h], s_im[h], a, b)
        for k in (0, 1):
            e[k, x, h, at, :] = 0.4 * u[k, x, h, at, :] + d[k]


def is_even(place, shape):
    return jnp.full(shape, lax.rem(place[1], 2)) == 0


def rows_inside(shape, y0, ysize):
    row = lax.broadcasted_iota(jnp.int32, shape, 0) + y0
    return (row >= 0) & (row < ysize)


def restrict_rows(vals, t, out, to, row, rows, k, start):
    for h, val in enumerate(vals):
        t[k, h, pl.ds(start, val.shape[0]), :] = val
        part = [t[k, h, pl.ds(row + j, rows, 2), :] for j in range(4)]
        out[k, to, pl.ds(0, rows), pl.ds(LANES * h, LANES)] = (part[0] + part[3]) + 3.0 * (part[1] + part[2])


def restrict_xy(r, t, out, to, plane, row, rows, k, window):
    at = pl.ds(*window)
    vals = []
    for h in range(r.shape[2]):
        four = [r[k, plane + j, h, at, :] for j in range(4)]
        vals.append((four[0] + four[3]) + 3.0 * (four[1] + four[2]))
    restrict_rows(vals, t, out, to, row, rows, k, window[0])


def add_pairs(c0, c1, t, h, out, i, row, rows):
    t[0, h, pl.ds(0, c0.shape[0]), :] = c0 + c1
    val = t[0, h, pl.ds(row, rows, 2), :] + t[0, h, pl.ds(row + 1, rows, 2), :]
    out[i, pl.ds(0, rows), pl.ds(LANES * h, LANES)] = val


def weights(lanes, zsize, mean=False, shift=0):
    z = lax.broadcasted_iota(jnp.int32, (lanes, LANES), 0)
    i = lax.broadcasted_iota(jnp.int32, (lanes, LANES), 1) - shift
    d = z - 2 * i
    inner = (d == 0) | (d == 1)
    if mean:
        w = jnp.where(inner, 0.125, 0.0)
    else:
        w = jnp.where(inner, 3.0 / 512.0, jnp.where((d == -1) | (d == 2), 1.0 / 512.0, 0.0))
    return jnp.where((z < zsize) & (i >= 0) & (i < zsize // 2), w, 0.0).astype(jnp.bfloat16)


def split_dot(part, w):
    planes, rows, lanes = part.shape
    x = part.reshape(planes * rows, lanes)
    hi = x.astype(jnp.bfloat16)
    low = (x - hi.astype(jnp.float32)).astype(jnp.bfloat16)
    dot = functools.partial(jnp.dot, preferred_element_type=jnp.float32)
    return (dot(hi, w) + dot(low, w)).reshape(planes, rows, w.shape[1])


PX, PY = 2, 8


def planes_kernel(f, c, x_first, x_last, planes, sems):
    n = c.shape[0]
    copies = []
    for side, x in enumerate((0, n - PX)):
        at = pl.ds(x, PX)
        copies += [(c.at[at], planes.at[side, 2]), (f.at[0, at], planes.at[side, 0]), (f.at[1, at], planes.at[side, 1])]
    copies = [pltpu.make_async_copy(src, dst, sems.at[i]) for i, (src, dst) in enumerate(copies)]
    for copy in copies:
        copy.start()
    for side, out in enumerate((x_first, x_last)):
        for copy in copies[3 * side : 3 * side + 3]:
            copy.wait()
        for j in range(PX):
            a, b = inverse(planes[side, 2, j], 1.0, None)
            out[j], out[PX + j] = divided(planes[side, 0, j], planes[side, 1, j], a, b)
        out[2 * PX] = planes[side, 2, (PX - 1) * side]


def first_kernel(place, f, c, u, ga, gb, y_chip, y_next):
    n, rows, lanes = c.shape
    cut = [pl.ds(LANES * h, LANES) for h in range(lanes // LANES)]
    row = lax.broadcasted_iota(jnp.int32, (8, LANES), 0)
    even = is_even(place, (8, LANES))

    def step(x, carry):
        for h, lane in enumerate(cut):
            point(f[0, x, :, lane], f[1, x, :, lane], c[x, :, lane], 1.0, None, u, ga, gb, x + PX, h, PY)
            made = []
            for start, shifts in ((0, (0, 3, 6)), (rows - 8, (3, 6, 0))):
                tiles = [u[k, x + PX, h, pl.ds(PY + start, 8), :] for k in (0, 1)] + [c[x, pl.ds(start, 8), lane]]
                re, im, cc = [pltpu.roll(v, shift, 0) if shift else v for v, shift in zip(tiles, shifts)]
                made.append(jnp.where(row < 3, re, jnp.where(row < 6, im, cc)))
            y_chip[x, :, lane], y_next[x, :, lane] = jnp.where(even, made[1], made[0]), jnp.where(even, made[0], made[1])
        return carry

    lax.fori_loop(0, n, step, 0, unroll=True)


def inner_kernel(f, c, u, ga, gb, e, r, fc_out, t, part):
    n, rows, lanes = c.shape
    halves = lanes // LANES
    at = pl.ds(PY, rows)
    cut = [pl.ds(LANES * h, LANES) for h in range(halves)]

    def middle(x, carry):
        second(u, ga, gb, e, x + PX, PY, rows, 1.0, True)
        return carry

    lax.fori_loop(1, n - 1, middle, 0, unroll=True)
    row = lax.broadcasted_iota(jnp.int32, (rows, LANES), 0)
    full = (row >= 2) & (row < rows - 2)

    def last(x, carry):
        for k in (0, 1):
            s = around(e, k, x + PX, PY, rows, True)
            for h in range(halves):
                r[k, x + PX, h, at, :] = 0.04 * f[k, x, :, cut[h]] + jnp.where(full, s[h], 0.0)
        return carry

    lax.fori_loop(2, n - 2, last, 0, unroll=True)
    for x in (0, 1, n - 2, n - 1):
        for k in (0, 1):
            for h in range(halves):
                r[k, x + PX, h, at, :] = 0.04 * f[k, x, :, cut[h]]
    for x in (PX - 1, n + PX):
        r[:, x] = jnp.zeros((2,) + r.shape[2:], jnp.float32)

    def pairs(i, carry):
        for h in range(halves):
            add_pairs(c[2 * i, :, cut[h]], c[2 * i + 1, :, cut[h]], t, h, part.at[2], i, 0, rows // 2)
        return carry

    lax.fori_loop(0, n // 2, pairs, 0, unroll=True)

    def coarse(i, carry):
        for k in (0, 1):
            restrict_xy(r, t, part, i, 2 * i + PX - 1, PY - 1, rows // 2, k, (PY, rows))
        return carry

    lax.fori_loop(2, n // 2 - 2, coarse, 0, unroll=True)
    w = weights(lanes, lanes)
    for k in (0, 1):
        fc_out[k, 2 : n // 2 - 2] = split_dot(part[k, 2 : n // 2 - 2], w)
    fc_out[2] = split_dot(part[2], weights(lanes, lanes, mean=True))


def inside(place, n, rows, xsize, ysize):
    x0, y0 = place[0] * n - PX, place[1] * rows - PY

    def ok(x, row, count):
        gx = x + x0
        return rows_inside((count, LANES), y0 + row, ysize) & ((gx >= 0) & (gx < xsize))

    return ok


def halo(re, im, cc, good, u, ga, gb, r, x, h, row, c_here, r_here):
    at = pl.ds(row, re.shape[0])
    re, im = jnp.where(good, re, 0.0), jnp.where(good, im, 0.0)
    u[0, x, h, at, :], u[1, x, h, at, :] = re, im
    if c_here:
        a, b = inverse(cc, 1.0, good)
        ga[x, h, at, :], gb[x, h, at, :] = a, b
    if r_here:
        a, b = 0.05 * (6.0 - cc), (0.05 * SHIFT_IMAG) * cc
        r[0, x, h, at, :], r[1, x, h, at, :] = re * a - im * b, im * a + re * b


def finish(e, r, x, row, count, good):
    for k in (0, 1):
        s = around(e, k, x, row, count, True)
        for h in range(e.shape[2]):
            at = pl.ds(row, count)
            r[k, x, h, at, :] = r[k, x, h, at, :] + jnp.where(good, s[h], 0.0)


def plane_cells(side, low, i, h):
    cut = pl.ds(LANES * h, LANES)
    c_here = i == (PX - 1 if low else 0)
    return side[i, :, cut], side[PX + i, :, cut], side[2 * PX, :, cut] if c_here else None, c_here


def faces_kernel(xsize, ysize, place, u_in, e_in, r_in, ga_in, gb_in, fc_in, xlo, xhi, y_chip, y_next, u, e, r, ga, gb, fc_out, part, q, sides, sems):
    n, (rows, lanes) = y_chip.shape[0], xlo.shape[1:]
    halves = lanes // LANES
    cut = [pl.ds(LANES * h, LANES) for h in range(halves)]
    ok = inside(place, n, rows, xsize, ysize)
    del u_in, e_in, r_in, ga_in, gb_in, fc_in
    used = pl.ds(0, 2 * PX + 1)
    copies = [pltpu.make_async_copy(src.at[used], sides.at[i], sems.at[i]) for i, src in enumerate((xlo, xhi))]
    for copy in copies:
        copy.start()
    low, high = PY - 4, PY + rows - 4
    good_lo, good_hi = ok(PX, 0, 8), ok(PX, PY + rows, 8)
    even = is_even(place, (8, LANES))

    def strips(x, carry):
        for h in range(halves):
            chip, other = y_chip[x, :, cut[h]], y_next[x, :, cut[h]]
            lo, hi = jnp.where(even, other, chip), jnp.where(even, chip, other)
            for tile, good, row, shifts in ((lo, good_lo, 0, (5, 2, 0)), (hi, good_hi, PY + rows, (0, 5, 2))):
                re, im, cc = [pltpu.roll(tile, shift, 0) if shift else tile for shift in shifts]
                halo(re, im, cc, good, u, ga, gb, r, x + PX, h, row, True, True)
        return carry

    lax.fori_loop(0, n, strips, 0, unroll=True)
    for copy in copies:
        copy.wait()
    for side, is_low, base in ((sides.at[0], True, 0), (sides.at[1], False, n + PX)):
        for i in range(PX):
            good = ok(base + i, PY, rows)
            for h in range(halves):
                re, im, cc, c_here = plane_cells(side, is_low, i, h)
                halo(re, im, cc, good, u, ga, gb, r, base + i, h, PY, c_here, False)
    for x in (PX - 1, PX, n + PX - 1, n + PX):
        second(u, ga, gb, e, x, PY, rows, 1.0, True)

    def middle(x, carry):
        for row in (low, high):
            second(u, ga, gb, e, x, row, 8, 1.0, True)
        return carry

    lax.fori_loop(PX + 1, n + PX - 1, middle, 0, unroll=True)
    for x in (PX, PX + 1, n + PX - 2, n + PX - 1):
        finish(e, r, x, PY + 4, rows - 8, ok(x, PY + 4, rows - 8))
    row = lax.broadcasted_iota(jnp.int32, (8, LANES), 0)
    good_low, good_high = ok(PX, low, 8) & (row < 6), ok(PX, high, 8) & (row >= 2)

    def last(x, carry):
        finish(e, r, x, low, 8, good_low)
        finish(e, r, x, high, 8, good_high)
        return carry

    lax.fori_loop(PX + 2, n + PX - 2, last, 0, unroll=True)
    m = n // 2 - 4

    def coarse(i, carry):
        x = 2 * i + PX + 3
        for k in (0, 1):
            for h in range(halves):
                for j, row in ((0, PY - 1), (8, PY + rows - 7)):
                    at = pl.ds(row, 8)
                    part[k, i, pl.ds(j, 8), cut[h]] = (r[k, x, h, at, :] + r[k, x + 3, h, at, :]) + 3.0 * (
                        r[k, x + 1, h, at, :] + r[k, x + 2, h, at, :]
                    )
        return carry

    lax.fori_loop(0, m, coarse, 0, unroll=True)
    w = weights(lanes, lanes)
    for k in (0, 1):
        q[k] = split_dot(part[k], w)
        for row, start in ((0, 0), (rows // 2 - 2, 10)):
            four = [q[k, :, pl.ds(start + j, 2, 2), :] for j in range(4)]
            fc_out[k, pl.ds(2, m), pl.ds(row, 2), :] = (four[0] + four[3]) + 3.0 * (four[1] + four[2])


def pack_corners_kernel(place, xlo, xhi, chip, other, tiles, sems):
    count, rows = 2 * PX + 1, xlo.shape[1]
    copies = []
    for i, side in enumerate((xlo, xhi)):
        for j, row in enumerate((0, rows - 8)):
            copies.append(pltpu.make_async_copy(side.at[pl.ds(0, count), pl.ds(row, 8)], tiles.at[j, pl.ds(count * i, count)], sems.at[2 * i + j]))
    for copy in copies:
        copy.start()
    even = is_even(place, (4, xlo.shape[2]))
    for copy in copies:
        copy.wait()
    for j in range(2 * count):
        first, last = tiles[0, j, pl.ds(0, 4), :], tiles[1, j, pl.ds(4, 4), :]
        chip[j], other[j] = jnp.where(even, last, first), jnp.where(even, first, last)


def corners_kernel(xsize, ysize, n, rows, place, u_in, e_in, r_in, ga_in, gb_in, fc_in, c_chip, c_next, u, e, r, ga, gb, fc_out, edge_out, t, part):
    halves = c_chip.shape[2] // LANES
    even = is_even(place, (4, LANES))
    ok = inside(place, n, rows, xsize, ysize)
    del u_in, e_in, r_in, ga_in, gb_in, fc_in
    low, high = PY - 4, PY + rows - 4
    held = 2 * PX + 1
    for first, low_planes, base in ((0, True, 0), (held, False, n + PX)):
        chip, other = c_chip.at[pl.ds(first, held)], c_next.at[pl.ds(first, held)]
        for i in range(PX):
            for h in range(halves):
                one, two = plane_cells(chip, low_planes, i, h), plane_cells(other, low_planes, i, h)
                for row, (p, q) in ((PY - 4, (two, one)), (PY + rows, (one, two))):
                    re, im, cc = [None if v is None else jnp.where(even, v, w) for v, w in zip(p[:3], q[:3])]
                    halo(re, im, cc, ok(base + i, row, 4), u, ga, gb, r, base + i, h, row, one[3], False)
    for x in (PX - 1, PX, n + PX - 1, n + PX):
        for row in (low, high):
            second(u, ga, gb, e, x, row, 8, 1.0, True)
    for x in (PX, PX + 1, n + PX - 2, n + PX - 1):
        for row in (low, high):
            finish(e, r, x, row, 8, ok(x, row, 8))
    planes = (0, 1, n // 2 - 2, n // 2 - 1)
    w = weights(part.shape[3], part.shape[3])
    for k in (0, 1):
        for j, i in enumerate(planes):
            restrict_xy(r, t, part, j, 2 * i + PX - 1, PY - 1, rows // 2, k, (low, rows + 8))
        for j, x in ((4, PX), (5, n + PX - 1)):
            restrict_rows([r[k, x, h, pl.ds(low, rows + 8), :] for h in range(halves)], t, part, j, PY - 1, rows // 2, k, low)
        val = split_dot(part[k], w)
        for j, i in enumerate(planes):
            fc_out[k, i] = val[j]
        edge_out[0, k], edge_out[1, k] = val[4], val[5]


def iterate_kernel(u, e, out):
    n, rows = out.shape[1:3]
    at = pl.ds(PY, rows)

    def step(x, carry):
        for k in (0, 1):
            for h in range(u.shape[2]):
                out[k, x, :, pl.ds(LANES * h, LANES)] = e[k, x + PX, h, at, :] + 0.8 * u[k, x + PX, h, at, :]
        return carry

    lax.fori_loop(0, n, step, 0, unroll=2)


def whole_level(cells, u, e, r, ga, gb, planes, used, row, rows, scale, full, ok, u_put):
    first, count = used
    for x in range(planes):
        at = pl.ds(first, count)
        point(cells(0, x, at), cells(1, x, at), cells(2, x, at), scale, ok(x, first, count), u, ga, gb, x, 0, first)
    at = pl.ds(row, rows)
    for x in range(1, planes - 1):
        second(u, ga, gb, e, x, row, rows, scale, full)
        u_put(x)
    for x in range(2, planes - 2):
        good = ok(x, row, rows)
        for k in (0, 1):
            s = around(e, k, x, row, rows, full)[0] * (1.0 / scale)
            r[k, x, 0, at, :] = jnp.where(good, 0.04 * cells(k, x, at) + s, 0.0)


def rows_kernel(xdev, halo, place, xlo, fc, xhi, edges, chip, other, window):
    n, rows = fc.shape[1:3]
    row = lax.broadcasted_iota(jnp.int32, (8, LANES), 0)
    even = is_even(place, (8, LANES))
    here = jnp.full((rows, LANES), place[0])
    for k in range(3):
        window[k, pl.ds(0, halo)] = xlo[pl.ds(k * halo, halo)]
        window[k, pl.ds(halo, n)] = fc[k]
        window[k, pl.ds(n + halo, halo)] = xhi[pl.ds(k * halo, halo)]
    for k in (0, 1):
        window[k, halo - 1] += edges[0, k]
        window[k, halo] += jnp.where(here > 0, xlo[3 * halo + k], 0.0)
        window[k, n + halo - 1] += jnp.where(here < xdev - 1, xhi[3 * halo + k], 0.0)
        window[k, n + halo] += edges[1, k]
    for x in range(n + 2 * halo):
        made = []
        for start, own in ((0, row < 5), (rows - 8, row >= 3)):
            re, im, cc = [window[k, x, pl.ds(start, 8), :] for k in range(3)]
            made.append((jnp.where(own, re, pltpu.roll(cc, 5, 0)), jnp.where(own, im, pltpu.roll(cc, 2, 0))))
        for k, (first, last) in enumerate(zip(*made)):
            chip[k, x], other[k, x] = jnp.where(even, last, first), jnp.where(even, first, last)


def middle_kernel(halo, over, xsize, ysize, place, window, y_chip, y_next, u_out, fc_out, fc, ga, gb, u, e, r, t, part, part_c):
    planes, rows = window.shape[1:3]
    n = planes - 2 * halo
    for k in range(3):
        fc[k, :, 0, pl.ds(8, rows), :] = window[k]
    row = lax.broadcasted_iota(jnp.int32, (8, LANES), 0)
    even = is_even(place, (8, LANES))
    for x in range(planes):
        chip, other = [y_chip[k, x] for k in (0, 1)], [y_next[k, x] for k in (0, 1)]
        for start, split, p, q in ((0, 6, other, chip), (8 + rows, 3, chip, other)):
            at = pl.ds(start, 8)
            one, two = [jnp.where(even, v, w) for v, w in zip(p, q)]
            fc[0, x, 0, at, :], fc[1, x, 0, at, :] = one, two
            fc[2, x, 0, at, :] = jnp.where(row < split, pltpu.roll(one, 3, 0), pltpu.roll(two, 6, 0))
    x0, y0 = place[0] * n - halo, place[1] * rows - 8

    def ok(x, row, count):
        gx = x + x0
        return rows_inside((count, LANES), y0 + row, ysize) & ((gx >= 0) & (gx < xsize))

    def u_put(x):
        if halo <= x < n + halo:
            at = pl.ds(8, rows)
            for k in (0, 1):
                u_out[k, x - halo] = e[k, x, 0, at, :] + 0.8 * u[k, x, 0, at, :]

    def cells(k, x, at):
        return fc[k, x, 0, at, :]

    whole_level(cells, u, e, r, ga, gb, planes, (0, rows + 16), 4, rows + 8, 4.0, True, ok, u_put)
    width = n // 2 + 2 * over
    pairs = width // 2
    for i in range(width):
        x, row = 2 * i + halo - 1 - 2 * over, 7 - 2 * over
        for k in (0, 1):
            restrict_xy(r, t, part, i, x, row, width, k, (4, rows + 8))
        add_pairs(fc[2, x + 1, 0], fc[2, x + 2, 0], t, 0, part_c.at[i % 2], i // 2, row + 1, width)
    two = [(part.at[k], part_c.at[k], LANES // 2 * k) for k in (0, 1)]
    fc_out[pl.ds(0, width)] = sum(split_dot(p[...], weights(LANES, LANES, shift=s)) for p, _, s in two)[:, :width]
    fc_out[pl.ds(width, pairs)] = sum(split_dot(p[...], weights(LANES, LANES, True, s)) for _, p, s in two)[:, :width]


def coarse_kernel(n, sweeps, xsize, ysize, zsize, place, fc_own, xlo, xhi, y_chip, y_next, u_out, v_out, fc, ga, gb, u, e, r, t, part, part_c, gc, gd, v, w):
    m = n // 2
    planes = n + 18
    own, own_c = range(8, n + 10), range(planes + 4, planes + m + 5)
    for src, x, first, count in ((xlo, 0, 0, 8), (xhi, n + 10, 0, 8), (xlo, planes, 8, 4), (xhi, planes + m + 5, 8, 4)):
        fc[pl.ds(x, count), 0, pl.ds(16, n), :] = src[pl.ds(first, count)]
    fc[pl.ds(8, n + 2), 0, pl.ds(15, n + 2), :] = fc_own[pl.ds(0, n + 2)]
    fc[pl.ds(planes + 4, m + 1), 0, pl.ds(15, n + 2), :] = fc_own[pl.ds(n + 2, m + 1)]
    even = is_even(place, (8, LANES))
    for x in range(fc.shape[0]):
        out = 1 if x in own or x in own_c else 0
        chip, other = y_chip[x], y_next[x]
        fc[x, 0, pl.ds(8 - out, 8), :] = jnp.where(even, other, chip)
        fc[x, 0, pl.ds(n + 16 + out, 8), :] = jnp.where(even, chip, other)
    lane = lax.broadcasted_iota(jnp.int32, (1, LANES), 1)

    def cells(k, x, at):
        val = fc[planes + x // 2 if k == 2 else x, 0, at, :]
        return pltpu.roll(val, LANES - zsize, 1) if k == 1 or (k == 2 and x % 2) else val

    def inside(x0, y0, xs, ys, zs):
        def ok(x, row, count):
            gx = x + x0
            here = rows_inside((count, LANES), y0 + row, ys) & (lane < zs)
            return here & ((gx >= 0) & (gx < xs))

        return ok

    def u_put(x):
        if 9 <= x < n + 9:
            at = pl.ds(16, n)
            for k in (0, 1):
                u_out[k, x - 9] = (e[k, x, 0, at, :] + 0.8 * u[k, x, 0, at, :])[:, :zsize]

    ok = inside(place[0] * n - 9, place[1] * n - 16, xsize, ysize, zsize)
    whole_level(cells, u, e, r, ga, gb, planes, (7, n + 18), 8, n + 16, 16.0, False, ok, u_put)
    width = m + 6
    every = pl.ds(8, n + 16)
    for i in range(width):
        for k in (0, 1):
            restrict_xy(r, t, part, i, 2 * i + 2, 9, width, k, (8, n + 16))
        t[0, 0, every, :] = cells(2, 2 * i + 3, every) + cells(2, 2 * i + 4, every)
        part_c[i, pl.ds(0, width), :] = t[0, 0, pl.ds(10, width, 2), :] + t[0, 0, pl.ds(11, width, 2), :]
    w_full = weights(LANES, zsize)
    f = [split_dot(part[k], w_full) for k in (0, 1)] + [split_dot(part_c[...], weights(LANES, zsize, True))]
    ok = inside(place[0] * m - 3, place[1] * m - 3, xsize // 2, ysize // 2, zsize // 2)
    for x in range(width):
        point(f[0][x], f[1][x], f[2][x], 64.0, ok(x, 0, 16), v, gc, gd, x, 0, 0)
    old = v
    for sweep in range(1, sweeps):
        new = w.at[sweep % 2]
        for x in range(sweep, width - sweep):
            at = pl.ds(1, m + 4)
            s = [around(old, k, x, 1, m + 4, False)[0] for k in (0, 1)]
            d = divided(*s, gc[x, 0, at, :] * (1.0 / 64.0), gd[x, 0, at, :] * (1.0 / 64.0))
            for k in (0, 1):
                val = 0.2 * old[k, x, 0, at, :] + v[k, x, 0, at, :] + d[k]
                if sweep < sweeps - 1:
                    new[k, x, 0, at, :] = val
                else:
                    v_out[k, x - 3] = val[2 : 2 + m, : zsize // 2]
        old = new


def body(source, wavenumber_sq):
    f32 = jnp.float32
    xdev, ydev = lax.axis_size("gx"), lax.axis_size("gy")
    place = jnp.stack([lax.axis_index("gx"), lax.axis_index("gy")]).astype(jnp.int32)

    def planes_step(first, last):
        before = lax.ppermute(last, "gx", [(i, (i + 1) % xdev) for i in range(xdev)])
        after = lax.ppermute(first, "gx", [((i + 1) % xdev, i) for i in range(xdev)])
        return before, after

    every = [(i, j) for i in range(xdev) for j in range(ydev)]
    number = lambda i, j: i * ydev + j
    on_chip = [(number(i, j), number(i, j ^ 1)) for i, j in every]
    next_chip = [(number(i, j), number(i ^ 1, j) if j in (0, ydev - 1) else number(i, ((j - 1) ^ 1) + 1)) for i, j in every]

    def rows_step(chip, other):
        return lax.ppermute(chip, ("gx", "gy"), on_chip), lax.ppermute(other, ("gx", "gy"), next_chip)

    _, n, rows, lanes = source.shape
    xsize, ysize = n * xdev, rows * ydev
    S = lambda *shape: jax.ShapeDtypeStruct(shape, f32)
    V = lambda *shape: pltpu.VMEM(shape, f32)

    halves = lanes // LANES
    state = (n + 2 * PX, halves, rows + 2 * PY, LANES)
    part = (n // 2, rows // 2, lanes)
    two, one, coarser = S(2, *state), S(*state), S(3, n // 2, rows // 2, lanes // 2)
    column = V(2, halves, rows + 2 * PY, LANES)
    held_planes = 2 * PX + 1
    x_first, x_last = pl.pallas_call(
        planes_kernel,
        in_specs=[pl.BlockSpec(memory_space=pltpu.HBM)] * 2,
        out_specs=[VMEM] * 2,
        out_shape=[S(held_planes + 2, rows, lanes)] * 2,
        scratch_shapes=[V(2, 3, PX, rows, lanes), pltpu.SemaphoreType.DMA((6,))],
        compiler_params=params(24),
        name="pack_planes",
    )(*[pltpu.with_memory_space_constraint(x, pltpu.HBM) for x in (source, wavenumber_sq)])
    source, wavenumber_sq, x_first, x_last = lax.optimization_barrier((source, wavenumber_sq, x_first, x_last))
    xlo, xhi = planes_step(x_first, x_last)
    u, ga, gb, y_chip, y_next = pl.pallas_call(
        first_kernel,
        in_specs=[SMEM] + [VMEM] * 2,
        out_specs=[VMEM] * 5,
        out_shape=[two, one, one] + [S(n, 8, lanes)] * 2,
        compiler_params=params(24),
        cost_estimate=pl.CostEstimate(flops=30_000_000, bytes_accessed=8_000_000, transcendentals=0),
        name="first_iterate",
    )(place, source, wavenumber_sq)
    y_chip, y_next = rows_step(y_chip, y_next)
    e, r, fc = pl.pallas_call(
        inner_kernel,
        in_specs=[VMEM] * 5,
        out_specs=[VMEM] * 3,
        out_shape=[two, two, coarser],
        scratch_shapes=[column, V(3, *part)],
        compiler_params=params(24),
        cost_estimate=pl.CostEstimate(flops=70_000_000, bytes_accessed=16_000_000, transcendentals=0),
        name="inner_cells",
    )(source, wavenumber_sq, u, ga, gb)
    held = (u, e, r, ga, gb, fc)
    shapes = [two] * 3 + [one] * 2 + [coarser]
    xlo, xhi, held = lax.optimization_barrier((xlo, xhi, held))
    c_chip, c_next = rows_step(
        *pl.pallas_call(
            pack_corners_kernel,
            in_specs=[SMEM] + [ANY] * 2,
            out_specs=[VMEM] * 2,
            out_shape=[S(2 * held_planes, 4, lanes)] * 2,
            scratch_shapes=[V(2, 2 * held_planes, 8, lanes), pltpu.SemaphoreType.DMA((4,))],
            compiler_params=params(24),
            name="pack_corners",
        )(place, xlo, xhi)
    )
    in_place = {i + 1: i for i in range(6)}
    held = pl.pallas_call(
        functools.partial(faces_kernel, xsize, ysize),
        in_specs=[SMEM] + [VMEM] * 6 + [ANY] * 2 + [VMEM] * 2,
        out_specs=[VMEM] * 6,
        out_shape=shapes,
        input_output_aliases=in_place,
        scratch_shapes=[V(2, n // 2 - 4, 16, lanes), V(2, n // 2 - 4, 16, lanes // 2), V(2, held_planes, rows, lanes), pltpu.SemaphoreType.DMA((2,))],
        compiler_params=params(24),
        cost_estimate=pl.CostEstimate(flops=50_000_000, bytes_accessed=8_000_000, transcendentals=0),
        name="face_cells",
    )(place, *held, xlo, xhi, y_chip, y_next)
    u, e, _, _, _, fc, edges = pl.pallas_call(
        functools.partial(corners_kernel, xsize, ysize, n, rows),
        in_specs=[SMEM] + [VMEM] * 8,
        out_specs=[VMEM] * 7,
        out_shape=shapes + [S(2, 2, rows // 2, lanes // 2)],
        input_output_aliases=in_place,
        scratch_shapes=[column, V(2, 6, rows // 2, lanes)],
        compiler_params=params(24),
        name="corner_cells",
    )(place, *held, c_chip, c_next)
    fine_shape = S(2, n, rows, lanes)
    n, rows, lanes, xsize, ysize, zsize = n // 2, rows // 2, lanes // 2, xsize // 2, ysize // 2, lanes // 2
    h, over = 5, 1
    slab = lambda x, edge: jnp.concatenate([fc[:, x : x + h].reshape(3 * h, rows, lanes), edge], 0)
    xlo, xhi = planes_step(slab(0, edges[0]), slab(n - h, edges[1]))
    fine = pl.pallas_call(
        iterate_kernel,
        in_specs=[VMEM] * 2,
        out_specs=VMEM,
        out_shape=fine_shape,
        compiler_params=params(24),
        cost_estimate=pl.CostEstimate(flops=1_000_000, bytes_accessed=8_000_000, transcendentals=0),
        name="fine_iterate",
    )(u, e)
    xlo, xhi, fine = lax.optimization_barrier((xlo, xhi, fine))
    chip, other, window = pl.pallas_call(
        functools.partial(rows_kernel, xdev, h),
        in_specs=[SMEM] + [VMEM] * 4,
        out_specs=[VMEM] * 3,
        out_shape=[S(2, n + 2 * h, 8, lanes)] * 2 + [S(3, n + 2 * h, rows, lanes)],
        compiler_params=params(24),
        name="second_rows",
    )(place, xlo, fc, xhi, edges)
    chip, other = rows_step(chip, other)
    state = (n + 2 * h, 1, rows + 16, LANES)
    work = lambda s: [V(*s), V(*s), V(2, *s), V(2, *s), V(2, *s), V(2, 1, *s[2:])]
    width = n // 2 + 2 * over
    second_u, fc = pl.pallas_call(
        functools.partial(middle_kernel, h, over, xsize, ysize),
        in_specs=[SMEM] + [VMEM] * 3,
        out_specs=[VMEM] * 2,
        out_shape=[S(2, n, rows, lanes), S(width + width // 2, width, lanes)],
        scratch_shapes=[V(3, *state)] + work(state) + [V(2, width, 16, LANES), V(2, width // 2, 16, LANES)],
        compiler_params=params(24),
        name="second_level",
    )(place, window, chip, other)

    n, xsize, ysize, zsize = n // 2, xsize // 2, ysize // 2, zsize // 2
    m = n // 2

    def joined(start):
        own = fc[:, start : start + n]
        return jnp.concatenate([xlo[:n], own[: n + 2], xhi[:n], xlo[n:], own[n + 2 :], xhi[n:]], 0)

    pick = lambda i, j: jnp.concatenate([fc[i : i + n, 1 : n + 1], fc[n + 2 + j : n + 2 + j + m, 1 : n + 1]], 0)
    xlo, xhi = planes_step(pick(2, 1), pick(0, 0))
    first, last = joined(2), joined(0)
    even = place[1] % 2 == 0
    chip, other = rows_step(jnp.where(even, last, first), jnp.where(even, first, last))
    state = (n + 18, 1, 40, LANES)
    small = (m + 6, 1, 16, LANES)
    third, coarse = pl.pallas_call(
        functools.partial(coarse_kernel, n, 4, xsize, ysize, zsize),
        in_specs=[SMEM] + [VMEM] * 5,
        out_specs=[VMEM] * 2,
        out_shape=[S(2, n, n, zsize), S(2, m, m, zsize // 2)],
        scratch_shapes=[V(n + 18 + m + 9, 1, 40, LANES)] + work(state) + [V(2, m + 6, 16, LANES), V(m + 6, 16, LANES)]
        + [V(*small), V(*small), V(2, *small), V(2, 2, *small)],
        compiler_params=params(24),
        name="coarse_levels",
    )(place, fc, xlo, xhi, chip, other)
    return fine, second_u, third, coarse


def solution(mesh):
    placed = (P(None, "gx", "gy", None), P("gx", "gy", None))
    return jax.shard_map(body, mesh=mesh, in_specs=placed, out_specs=(P(None, "gx", "gy", None),) * 4, check_vma=False)
```

```python
import functools
import jax
import jax.numpy as jnp
from jax import lax
from jax.experimental import pallas as pl
from jax.experimental.pallas import tpu as pltpu
from jax.sharding import PartitionSpec as P

DAMPING = 0.8
SHIFT_IMAG = 0.5
LANES = 128
VMEM = pl.BlockSpec(memory_space=pltpu.VMEM)
SMEM = pl.BlockSpec(memory_space=pltpu.SMEM)
ANY = pl.BlockSpec(memory_space=pl.ANY)


def params(mib):
    return pltpu.CompilerParams(vmem_limit_bytes=mib * 1024 * 1024)


def around(ref, k, x, row, rows, full):
    halves = ref.shape[2]
    mid = [ref[k, x, h, pl.ds(row, rows), :] for h in range(halves)]
    up = [pltpu.roll(m, 1, 1) for m in mid]
    down = [pltpu.roll(m, LANES - 1, 1) for m in mid]
    if full:
        lane = lax.broadcasted_iota(jnp.int32, mid[0].shape, 1)
        first, last = lane == 0, lane == LANES - 1
        up = [jnp.where(first, up[h - 1] if h else 0.0, up[h]) for h in range(halves)]
        down = [jnp.where(last, down[h + 1] if h < halves - 1 else 0.0, down[h]) for h in range(halves)]
    sums = []
    for h in range(halves):
        planes = ref[k, x - 1, h, pl.ds(row, rows), :] + ref[k, x + 1, h, pl.ds(row, rows), :]
        sides = ref[k, x, h, pl.ds(row - 1, rows), :] + ref[k, x, h, pl.ds(row + 1, rows), :]
        sums.append((planes + sides) + (up[h] + down[h]))
    return sums


def inverse(c, scale, ok):
    a = 6.0 / scale - c
    b = SHIFT_IMAG * c
    g = DAMPING / (a * a + b * b)
    if ok is not None:
        g = jnp.where(ok, g, 0.0)
    return g * a, g * b


def divided(re, im, a, b):
    return re * a + im * b, im * a - re * b


def point(re, im, c, scale, ok, u, ga, gb, x, h, row):
    a, b = inverse(c, scale, ok)
    at = pl.ds(row, c.shape[0])
    ga[x, h, at, :], gb[x, h, at, :] = a, b
    u[0, x, h, at, :], u[1, x, h, at, :] = divided(re, im, a, b)


def second(u, ga, gb, e, x, row, rows, scale, full):
    s_re, s_im = around(u, 0, x, row, rows, full), around(u, 1, x, row, rows, full)
    at = pl.ds(row, rows)
    for h in range(u.shape[2]):
        a, b = ga[x, h, at, :], gb[x, h, at, :]
        if scale != 1.0:
            a, b = a * (1.0 / scale), b * (1.0 / scale)
        d = divided(s_re[h], s_im[h], a, b)
        for k in (0, 1):
            e[k, x, h, at, :] = 0.4 * u[k, x, h, at, :] + d[k]


def is_even(place, shape):
    return jnp.full(shape, lax.rem(place[1], 2)) == 0


def rows_inside(shape, y0, ysize):
    row = lax.broadcasted_iota(jnp.int32, shape, 0) + y0
    return (row >= 0) & (row < ysize)


def restrict_rows(vals, t, out, to, row, rows, k, start):
    for h, val in enumerate(vals):
        t[k, h, pl.ds(start, val.shape[0]), :] = val
        part = [t[k, h, pl.ds(row + j, rows, 2), :] for j in range(4)]
        out[k, to, pl.ds(0, rows), pl.ds(LANES * h, LANES)] = (part[0] + part[3]) + 3.0 * (part[1] + part[2])


def restrict_xy(r, t, out, to, plane, row, rows, k, window):
    at = pl.ds(*window)
    vals = []
    for h in range(r.shape[2]):
        four = [r[k, plane + j, h, at, :] for j in range(4)]
        vals.append((four[0] + four[3]) + 3.0 * (four[1] + four[2]))
    restrict_rows(vals, t, out, to, row, rows, k, window[0])


def add_pairs(c0, c1, t, h, out, i, row, rows):
    t[0, h, pl.ds(0, c0.shape[0]), :] = c0 + c1
    val = t[0, h, pl.ds(row, rows, 2), :] + t[0, h, pl.ds(row + 1, rows, 2), :]
    out[i, pl.ds(0, rows), pl.ds(LANES * h, LANES)] = val


def weights(lanes, zsize, mean=False, shift=0):
    z = lax.broadcasted_iota(jnp.int32, (lanes, LANES), 0)
    i = lax.broadcasted_iota(jnp.int32, (lanes, LANES), 1) - shift
    d = z - 2 * i
    inner = (d == 0) | (d == 1)
    if mean:
        w = jnp.where(inner, 0.125, 0.0)
    else:
        w = jnp.where(inner, 3.0 / 512.0, jnp.where((d == -1) | (d == 2), 1.0 / 512.0, 0.0))
    return jnp.where((z < zsize) & (i >= 0) & (i < zsize // 2), w, 0.0).astype(jnp.bfloat16)


def split_dot(part, w):
    planes, rows, lanes = part.shape
    x = part.reshape(planes * rows, lanes)
    hi = x.astype(jnp.bfloat16)
    low = (x - hi.astype(jnp.float32)).astype(jnp.bfloat16)
    dot = functools.partial(jnp.dot, preferred_element_type=jnp.float32)
    return (dot(hi, w) + dot(low, w)).reshape(planes, rows, w.shape[1])


PX, PY = 2, 8


def planes_kernel(f, c, x_first, x_last, planes, sems):
    n = c.shape[0]
    copies = []
    for side, x in enumerate((0, n - PX)):
        at = pl.ds(x, PX)
        copies += [(c.at[at], planes.at[side, 2]), (f.at[0, at], planes.at[side, 0]), (f.at[1, at], planes.at[side, 1])]
    copies = [pltpu.make_async_copy(src, dst, sems.at[i]) for i, (src, dst) in enumerate(copies)]
    for copy in copies:
        copy.start()
    for side, out in enumerate((x_first, x_last)):
        for copy in copies[3 * side : 3 * side + 3]:
            copy.wait()
        for j in range(PX):
            a, b = inverse(planes[side, 2, j], 1.0, None)
            out[j], out[PX + j] = divided(planes[side, 0, j], planes[side, 1, j], a, b)
        out[2 * PX] = planes[side, 2, (PX - 1) * side]


def first_kernel(place, f, c, u, ga, gb, y_chip, y_next):
    n, rows, lanes = c.shape
    cut = [pl.ds(LANES * h, LANES) for h in range(lanes // LANES)]
    row = lax.broadcasted_iota(jnp.int32, (8, LANES), 0)
    even = is_even(place, (8, LANES))

    def step(x, carry):
        for h, lane in enumerate(cut):
            point(f[0, x, :, lane], f[1, x, :, lane], c[x, :, lane], 1.0, None, u, ga, gb, x + PX, h, PY)
            made = []
            for start, shifts in ((0, (0, 3, 6)), (rows - 8, (3, 6, 0))):
                tiles = [u[k, x + PX, h, pl.ds(PY + start, 8), :] for k in (0, 1)] + [c[x, pl.ds(start, 8), lane]]
                re, im, cc = [pltpu.roll(v, shift, 0) if shift else v for v, shift in zip(tiles, shifts)]
                made.append(jnp.where(row < 3, re, jnp.where(row < 6, im, cc)))
            y_chip[x, :, lane], y_next[x, :, lane] = jnp.where(even, made[1], made[0]), jnp.where(even, made[0], made[1])
        return carry

    lax.fori_loop(0, n, step, 0, unroll=True)


def both_ends(ranges, step):
    for first, last in ranges:
        lax.fori_loop(first, last, step, 0, unroll=True)


def inner_kernel(late, f, c, u, ga, gb, e, r, fc_out, t, part):
    n, rows, lanes = c.shape
    halves = lanes // LANES
    at = pl.ds(PY, rows)
    cut = [pl.ds(LANES * h, LANES) for h in range(halves)]

    def middle(x, carry):
        second(u, ga, gb, e, x + PX, PY, rows, 1.0, True)
        return carry

    lo, hi = late
    both_ends(((1, 2 * lo + 2), (2 * hi - 2, n - 1)), middle)
    row = lax.broadcasted_iota(jnp.int32, (rows, LANES), 0)
    full = (row >= 2) & (row < rows - 2)

    def last(x, carry):
        for k in (0, 1):
            s = around(e, k, x + PX, PY, rows, True)
            for h in range(halves):
                r[k, x + PX, h, at, :] = 0.04 * f[k, x, :, cut[h]] + jnp.where(full, s[h], 0.0)
        return carry

    both_ends(((2, 2 * lo + 1), (2 * hi - 1, n - 2)), last)
    for x in (0, 1, *range(2 * lo + 1, 2 * hi - 1), n - 2, n - 1):
        for k in (0, 1):
            for h in range(halves):
                r[k, x + PX, h, at, :] = 0.04 * f[k, x, :, cut[h]]
    for x in (PX - 1, n + PX):
        r[:, x] = jnp.zeros((2,) + r.shape[2:], jnp.float32)

    def pairs(i, carry):
        for h in range(halves):
            add_pairs(c[2 * i, :, cut[h]], c[2 * i + 1, :, cut[h]], t, h, part.at[2], i, 0, rows // 2)
        return carry

    lax.fori_loop(0, n // 2, pairs, 0, unroll=True)

    def coarse(i, carry):
        for k in (0, 1):
            restrict_xy(r, t, part, i, 2 * i + PX - 1, PY - 1, rows // 2, k, (PY, rows))
        return carry

    early = ((2, lo), (hi, n // 2 - 2))
    both_ends(early, coarse)
    w = weights(lanes, lanes)
    for k in (0, 1):
        for i, j in early:
            fc_out[k, i:j] = split_dot(part[k, i:j], w)
    fc_out[2] = split_dot(part[2], weights(lanes, lanes, mean=True))


def inside(place, n, rows, xsize, ysize):
    x0, y0 = place[0] * n - PX, place[1] * rows - PY

    def ok(x, row, count):
        gx = x + x0
        return rows_inside((count, LANES), y0 + row, ysize) & ((gx >= 0) & (gx < xsize))

    return ok


def halo(re, im, cc, good, u, ga, gb, r, x, h, row, c_here, r_here):
    at = pl.ds(row, re.shape[0])
    re, im = jnp.where(good, re, 0.0), jnp.where(good, im, 0.0)
    u[0, x, h, at, :], u[1, x, h, at, :] = re, im
    if c_here:
        a, b = inverse(cc, 1.0, good)
        ga[x, h, at, :], gb[x, h, at, :] = a, b
    if r_here:
        a, b = 0.05 * (6.0 - cc), (0.05 * SHIFT_IMAG) * cc
        r[0, x, h, at, :], r[1, x, h, at, :] = re * a - im * b, im * a + re * b


def finish(e, r, x, row, count, good):
    for k in (0, 1):
        s = around(e, k, x, row, count, True)
        for h in range(e.shape[2]):
            at = pl.ds(row, count)
            r[k, x, h, at, :] = r[k, x, h, at, :] + jnp.where(good, s[h], 0.0)


def plane_cells(side, low, i, h):
    cut = pl.ds(LANES * h, LANES)
    c_here = i == (PX - 1 if low else 0)
    return side[i, :, cut], side[PX + i, :, cut], side[2 * PX, :, cut] if c_here else None, c_here


def faces_kernel(late, xsize, ysize, place, u_in, e_in, r_in, ga_in, gb_in, fc_in, xlo, xhi, y_chip, y_next, u, e, r, ga, gb, fc_out, part, q, sides, sems):
    n, (rows, lanes) = y_chip.shape[0], xlo.shape[1:]
    halves = lanes // LANES
    cut = [pl.ds(LANES * h, LANES) for h in range(halves)]
    ok = inside(place, n, rows, xsize, ysize)
    del u_in, e_in, r_in, ga_in, gb_in, fc_in
    used = pl.ds(0, 2 * PX + 1)
    copies = [pltpu.make_async_copy(src.at[used], sides.at[i], sems.at[i]) for i, src in enumerate((xlo, xhi))]
    for copy in copies:
        copy.start()
    low, high = PY - 4, PY + rows - 4
    good_lo, good_hi = ok(PX, 0, 8), ok(PX, PY + rows, 8)
    even = is_even(place, (8, LANES))

    def strips(x, carry):
        for h in range(halves):
            chip, other = y_chip[x, :, cut[h]], y_next[x, :, cut[h]]
            lo, hi = jnp.where(even, other, chip), jnp.where(even, chip, other)
            for tile, good, row, shifts in ((lo, good_lo, 0, (5, 2, 0)), (hi, good_hi, PY + rows, (0, 5, 2))):
                re, im, cc = [pltpu.roll(tile, shift, 0) if shift else tile for shift in shifts]
                halo(re, im, cc, good, u, ga, gb, r, x + PX, h, row, True, True)
        return carry

    lax.fori_loop(0, n, strips, 0, unroll=True)
    for copy in copies:
        copy.wait()
    for side, is_low, base in ((sides.at[0], True, 0), (sides.at[1], False, n + PX)):
        for i in range(PX):
            good = ok(base + i, PY, rows)
            for h in range(halves):
                re, im, cc, c_here = plane_cells(side, is_low, i, h)
                halo(re, im, cc, good, u, ga, gb, r, base + i, h, PY, c_here, False)
    for x in (PX - 1, PX, n + PX - 1, n + PX):
        second(u, ga, gb, e, x, PY, rows, 1.0, True)

    def middle(x, carry):
        for row in (low, high):
            second(u, ga, gb, e, x, row, 8, 1.0, True)
        return carry

    lo, hi = late
    both_ends(((PX + 1, PX + 2 * lo + 2), (PX + 2 * hi - 2, n + PX - 1)), middle)
    for x in (PX, PX + 1, n + PX - 2, n + PX - 1):
        finish(e, r, x, PY + 4, rows - 8, ok(x, PY + 4, rows - 8))
    row = lax.broadcasted_iota(jnp.int32, (8, LANES), 0)
    good_low, good_high = ok(PX, low, 8) & (row < 6), ok(PX, high, 8) & (row >= 2)

    def last(x, carry):
        finish(e, r, x, low, 8, good_low)
        finish(e, r, x, high, 8, good_high)
        return carry

    both_ends(((PX + 2, PX + 2 * lo + 1), (PX + 2 * hi - 1, n + PX - 2)), last)
    m = n // 2 - 4

    def coarse(i, carry):
        x = 2 * i + PX + 3
        for k in (0, 1):
            for h in range(halves):
                for j, row in ((0, PY - 1), (8, PY + rows - 7)):
                    at = pl.ds(row, 8)
                    part[k, i, pl.ds(j, 8), cut[h]] = (r[k, x, h, at, :] + r[k, x + 3, h, at, :]) + 3.0 * (
                        r[k, x + 1, h, at, :] + r[k, x + 2, h, at, :]
                    )
        return carry

    both_ends(((0, lo - 2), (hi - 2, m)), coarse)
    w = weights(lanes, lanes)
    for k in (0, 1):
        q[k] = split_dot(part[k], w)
        for row, start in ((0, 0), (rows // 2 - 2, 10)):
            four = [q[k, :, pl.ds(start + j, 2, 2), :] for j in range(4)]
            fc_out[k, pl.ds(2, m), pl.ds(row, 2), :] = (four[0] + four[3]) + 3.0 * (four[1] + four[2])


def pack_corners_kernel(place, xlo, xhi, chip, other, tiles, sems):
    count, rows = 2 * PX + 1, xlo.shape[1]
    copies = []
    for i, side in enumerate((xlo, xhi)):
        for j, row in enumerate((0, rows - 8)):
            copies.append(pltpu.make_async_copy(side.at[pl.ds(0, count), pl.ds(row, 8)], tiles.at[j, pl.ds(count * i, count)], sems.at[2 * i + j]))
    for copy in copies:
        copy.start()
    even = is_even(place, (4, xlo.shape[2]))
    for copy in copies:
        copy.wait()
    for j in range(2 * count):
        first, last = tiles[0, j, pl.ds(0, 4), :], tiles[1, j, pl.ds(4, 4), :]
        chip[j], other[j] = jnp.where(even, last, first), jnp.where(even, first, last)


def corners_kernel(xsize, ysize, n, rows, place, u_in, e_in, r_in, ga_in, gb_in, fc_in, c_chip, c_next, u, e, r, ga, gb, fc_out, edge_out, t, part):
    halves = c_chip.shape[2] // LANES
    even = is_even(place, (4, LANES))
    ok = inside(place, n, rows, xsize, ysize)
    del u_in, e_in, r_in, ga_in, gb_in, fc_in
    low, high = PY - 4, PY + rows - 4
    held = 2 * PX + 1
    for first, low_planes, base in ((0, True, 0), (held, False, n + PX)):
        chip, other = c_chip.at[pl.ds(first, held)], c_next.at[pl.ds(first, held)]
        for i in range(PX):
            for h in range(halves):
                one, two = plane_cells(chip, low_planes, i, h), plane_cells(other, low_planes, i, h)
                for row, (p, q) in ((PY - 4, (two, one)), (PY + rows, (one, two))):
                    re, im, cc = [None if v is None else jnp.where(even, v, w) for v, w in zip(p[:3], q[:3])]
                    halo(re, im, cc, ok(base + i, row, 4), u, ga, gb, r, base + i, h, row, one[3], False)
    for x in (PX - 1, PX, n + PX - 1, n + PX):
        for row in (low, high):
            second(u, ga, gb, e, x, row, 8, 1.0, True)
    for x in (PX, PX + 1, n + PX - 2, n + PX - 1):
        for row in (low, high):
            finish(e, r, x, row, 8, ok(x, row, 8))
    planes = (0, 1, n // 2 - 2, n // 2 - 1)
    w = weights(part.shape[3], part.shape[3])
    for k in (0, 1):
        for j, i in enumerate(planes):
            restrict_xy(r, t, part, j, 2 * i + PX - 1, PY - 1, rows // 2, k, (low, rows + 8))
        for j, x in ((4, PX), (5, n + PX - 1)):
            restrict_rows([r[k, x, h, pl.ds(low, rows + 8), :] for h in range(halves)], t, part, j, PY - 1, rows // 2, k, low)
        val = split_dot(part[k], w)
        for j, i in enumerate(planes):
            fc_out[k, i] = val[j]
        edge_out[0, k], edge_out[1, k] = val[4], val[5]


def late_kernel(late, xsize, ysize, n, rows, place, u, e_in, r_in, ga, gb, e, r, out, t, part):
    halves = u.shape[2]
    ok = inside(place, n, rows, xsize, ysize)
    del e_in, r_in
    lo, hi = late
    low = PY - 4
    for x in range(PX + 2 * lo + 2, PX + 2 * hi - 2):
        second(u, ga, gb, e, x, low, rows + 8, 1.0, True)
    good = ok(PX, low, rows + 8)
    for x in range(PX + 2 * lo + 1, PX + 2 * hi - 1):
        finish(e, r, x, low, rows + 8, good)
    w = weights(LANES * halves, LANES * halves)
    for k in (0, 1):
        for i in range(lo, hi):
            restrict_xy(r, t, part, i - lo, 2 * i + PX - 1, PY - 1, rows // 2, k, (low, rows + 8))
        out[k] = split_dot(part[k], w)


def iterate_kernel(u, e, out):
    n, rows = out.shape[1:3]
    at = pl.ds(PY, rows)

    def step(x, carry):
        for k in (0, 1):
            for h in range(u.shape[2]):
                out[k, x, :, pl.ds(LANES * h, LANES)] = e[k, x + PX, h, at, :] + 0.8 * u[k, x + PX, h, at, :]
        return carry

    lax.fori_loop(0, n, step, 0, unroll=8)


def whole_level(cells, u, e, r, ga, gb, planes, used, row, rows, scale, full, ok, u_put):
    first, count = used
    for x in range(planes):
        at = pl.ds(first, count)
        point(cells(0, x, at), cells(1, x, at), cells(2, x, at), scale, ok(x, first, count), u, ga, gb, x, 0, first)
    at = pl.ds(row, rows)
    for x in range(1, planes - 1):
        second(u, ga, gb, e, x, row, rows, scale, full)
        u_put(x)
    for x in range(2, planes - 2):
        good = ok(x, row, rows)
        for k in (0, 1):
            s = around(e, k, x, row, rows, full)[0] * (1.0 / scale)
            r[k, x, 0, at, :] = jnp.where(good, 0.04 * cells(k, x, at) + s, 0.0)


def rows_kernel(xdev, halo, place, xlo, fc, fc_late, xhi, edges, chip, other, window):
    n, rows = fc.shape[1:3]
    row = lax.broadcasted_iota(jnp.int32, (8, LANES), 0)
    even = is_even(place, (8, LANES))
    here = jnp.full((rows, LANES), place[0])
    for k in range(3):
        window[k, pl.ds(0, halo)] = xlo[pl.ds(k * halo, halo)]
        window[k, pl.ds(halo, n)] = fc[k]
        if k < 2:
            window[k, pl.ds(2 * halo, n - 2 * halo)] = fc_late[k]
        window[k, pl.ds(n + halo, halo)] = xhi[pl.ds(k * halo, halo)]
    for k in (0, 1):
        window[k, halo - 1] += edges[0, k]
        window[k, halo] += jnp.where(here > 0, xlo[3 * halo + k], 0.0)
        window[k, n + halo - 1] += jnp.where(here < xdev - 1, xhi[3 * halo + k], 0.0)
        window[k, n + halo] += edges[1, k]
    for x in range(n + 2 * halo):
        made = []
        for start, own in ((0, row < 5), (rows - 8, row >= 3)):
            re, im, cc = [window[k, x, pl.ds(start, 8), :] for k in range(3)]
            made.append((jnp.where(own, re, pltpu.roll(cc, 5, 0)), jnp.where(own, im, pltpu.roll(cc, 2, 0))))
        for k, (first, last) in enumerate(zip(*made)):
            chip[k, x], other[k, x] = jnp.where(even, last, first), jnp.where(even, first, last)


def middle_kernel(halo, over, xsize, ysize, place, window, y_chip, y_next, u_out, fc_out, fc, ga, gb, u, e, r, t, part, part_c):
    planes, rows = window.shape[1:3]
    n = planes - 2 * halo
    for k in range(3):
        fc[k, :, 0, pl.ds(8, rows), :] = window[k]
    row = lax.broadcasted_iota(jnp.int32, (8, LANES), 0)
    even = is_even(place, (8, LANES))
    for x in range(planes):
        chip, other = [y_chip[k, x] for k in (0, 1)], [y_next[k, x] for k in (0, 1)]
        for start, split, p, q in ((0, 6, other, chip), (8 + rows, 3, chip, other)):
            at = pl.ds(start, 8)
            one, two = [jnp.where(even, v, w) for v, w in zip(p, q)]
            fc[0, x, 0, at, :], fc[1, x, 0, at, :] = one, two
            fc[2, x, 0, at, :] = jnp.where(row < split, pltpu.roll(one, 3, 0), pltpu.roll(two, 6, 0))
    x0, y0 = place[0] * n - halo, place[1] * rows - 8

    def ok(x, row, count):
        gx = x + x0
        return rows_inside((count, LANES), y0 + row, ysize) & ((gx >= 0) & (gx < xsize))

    def u_put(x):
        if halo <= x < n + halo:
            at = pl.ds(8, rows)
            for k in (0, 1):
                u_out[k, x - halo] = e[k, x, 0, at, :] + 0.8 * u[k, x, 0, at, :]

    def cells(k, x, at):
        return fc[k, x, 0, at, :]

    whole_level(cells, u, e, r, ga, gb, planes, (0, rows + 16), 4, rows + 8, 4.0, True, ok, u_put)
    width = n // 2 + 2 * over
    pairs = width // 2
    for i in range(width):
        x, row = 2 * i + halo - 1 - 2 * over, 7 - 2 * over
        for k in (0, 1):
            restrict_xy(r, t, part, i, x, row, width, k, (4, rows + 8))
        add_pairs(fc[2, x + 1, 0], fc[2, x + 2, 0], t, 0, part_c.at[i % 2], i // 2, row + 1, width)
    two = [(part.at[k], part_c.at[k], LANES // 2 * k) for k in (0, 1)]
    fc_out[pl.ds(0, width)] = sum(split_dot(p[...], weights(LANES, LANES, shift=s)) for p, _, s in two)[:, :width]
    fc_out[pl.ds(width, pairs)] = sum(split_dot(p[...], weights(LANES, LANES, True, s)) for _, p, s in two)[:, :width]


def coarse_kernel(n, sweeps, xsize, ysize, zsize, place, fc_own, xlo, xhi, y_chip, y_next, u_out, v_out, fc, ga, gb, u, e, r, t, part, part_c, gc, gd, v, w):
    m = n // 2
    planes = n + 18
    own, own_c = range(8, n + 10), range(planes + 4, planes + m + 5)
    for src, x, first, count in ((xlo, 0, 0, 8), (xhi, n + 10, 0, 8), (xlo, planes, 8, 4), (xhi, planes + m + 5, 8, 4)):
        fc[pl.ds(x, count), 0, pl.ds(16, n), :] = src[pl.ds(first, count)]
    fc[pl.ds(8, n + 2), 0, pl.ds(15, n + 2), :] = fc_own[pl.ds(0, n + 2)]
    fc[pl.ds(planes + 4, m + 1), 0, pl.ds(15, n + 2), :] = fc_own[pl.ds(n + 2, m + 1)]
    even = is_even(place, (8, LANES))
    for x in range(fc.shape[0]):
        out = 1 if x in own or x in own_c else 0
        chip, other = y_chip[x], y_next[x]
        fc[x, 0, pl.ds(8 - out, 8), :] = jnp.where(even, other, chip)
        fc[x, 0, pl.ds(n + 16 + out, 8), :] = jnp.where(even, chip, other)
    lane = lax.broadcasted_iota(jnp.int32, (1, LANES), 1)

    def cells(k, x, at):
        val = fc[planes + x // 2 if k == 2 else x, 0, at, :]
        return pltpu.roll(val, LANES - zsize, 1) if k == 1 or (k == 2 and x % 2) else val

    def inside(x0, y0, xs, ys, zs):
        def ok(x, row, count):
            gx = x + x0
            here = rows_inside((count, LANES), y0 + row, ys) & (lane < zs)
            return here & ((gx >= 0) & (gx < xs))

        return ok

    def u_put(x):
        if 9 <= x < n + 9:
            at = pl.ds(16, n)
            for k in (0, 1):
                u_out[k, x - 9] = (e[k, x, 0, at, :] + 0.8 * u[k, x, 0, at, :])[:, :zsize]

    ok = inside(place[0] * n - 9, place[1] * n - 16, xsize, ysize, zsize)
    whole_level(cells, u, e, r, ga, gb, planes, (7, n + 18), 8, n + 16, 16.0, False, ok, u_put)
    width = m + 6
    every = pl.ds(8, n + 16)
    for i in range(width):
        for k in (0, 1):
            restrict_xy(r, t, part, i, 2 * i + 2, 9, width, k, (8, n + 16))
        t[0, 0, every, :] = cells(2, 2 * i + 3, every) + cells(2, 2 * i + 4, every)
        part_c[i, pl.ds(0, width), :] = t[0, 0, pl.ds(10, width, 2), :] + t[0, 0, pl.ds(11, width, 2), :]
    w_full = weights(LANES, zsize)
    f = [split_dot(part[k], w_full) for k in (0, 1)] + [split_dot(part_c[...], weights(LANES, zsize, True))]
    ok = inside(place[0] * m - 3, place[1] * m - 3, xsize // 2, ysize // 2, zsize // 2)
    for x in range(width):
        point(f[0][x], f[1][x], f[2][x], 64.0, ok(x, 0, 16), v, gc, gd, x, 0, 0)
    old = v
    for sweep in range(1, sweeps):
        new = w.at[sweep % 2]
        for x in range(sweep, width - sweep):
            at = pl.ds(1, m + 4)
            s = [around(old, k, x, 1, m + 4, False)[0] for k in (0, 1)]
            d = divided(*s, gc[x, 0, at, :] * (1.0 / 64.0), gd[x, 0, at, :] * (1.0 / 64.0))
            for k in (0, 1):
                val = 0.2 * old[k, x, 0, at, :] + v[k, x, 0, at, :] + d[k]
                if sweep < sweeps - 1:
                    new[k, x, 0, at, :] = val
                else:
                    v_out[k, x - 3] = val[2 : 2 + m, : zsize // 2]
        old = new


def body(source, wavenumber_sq):
    f32 = jnp.float32
    xdev, ydev = lax.axis_size("gx"), lax.axis_size("gy")
    place = jnp.stack([lax.axis_index("gx"), lax.axis_index("gy")]).astype(jnp.int32)

    def planes_step(first, last):
        before = lax.ppermute(last, "gx", [(i, (i + 1) % xdev) for i in range(xdev)])
        after = lax.ppermute(first, "gx", [((i + 1) % xdev, i) for i in range(xdev)])
        return before, after

    every = [(i, j) for i in range(xdev) for j in range(ydev)]
    number = lambda i, j: i * ydev + j
    on_chip = [(number(i, j), number(i, j ^ 1)) for i, j in every]
    next_chip = [(number(i, j), number(i ^ 1, j) if j in (0, ydev - 1) else number(i, ((j - 1) ^ 1) + 1)) for i, j in every]

    def rows_step(chip, other):
        return lax.ppermute(chip, ("gx", "gy"), on_chip), lax.ppermute(other, ("gx", "gy"), next_chip)

    _, n, rows, lanes = source.shape
    xsize, ysize = n * xdev, rows * ydev
    S = lambda *shape: jax.ShapeDtypeStruct(shape, f32)
    V = lambda *shape: pltpu.VMEM(shape, f32)

    halo_next = 5
    late = (halo_next, n // 2 - halo_next)
    halves = lanes // LANES
    state = (n + 2 * PX, halves, rows + 2 * PY, LANES)
    part = (n // 2, rows // 2, lanes)
    two, one, coarser = S(2, *state), S(*state), S(3, n // 2, rows // 2, lanes // 2)
    column = V(2, halves, rows + 2 * PY, LANES)
    held_planes = 2 * PX + 1
    x_first, x_last = pl.pallas_call(
        planes_kernel,
        in_specs=[pl.BlockSpec(memory_space=pltpu.HBM)] * 2,
        out_specs=[VMEM] * 2,
        out_shape=[S(held_planes + 2, rows, lanes)] * 2,
        scratch_shapes=[V(2, 3, PX, rows, lanes), pltpu.SemaphoreType.DMA((6,))],
        compiler_params=params(24),
        name="pack_planes",
    )(*[pltpu.with_memory_space_constraint(x, pltpu.HBM) for x in (source, wavenumber_sq)])
    source, wavenumber_sq, x_first, x_last = lax.optimization_barrier((source, wavenumber_sq, x_first, x_last))
    xlo, xhi = planes_step(x_first, x_last)
    u, ga, gb, y_chip, y_next = pl.pallas_call(
        first_kernel,
        in_specs=[SMEM] + [VMEM] * 2,
        out_specs=[VMEM] * 5,
        out_shape=[two, one, one] + [S(n, 8, lanes)] * 2,
        compiler_params=params(24),
        cost_estimate=pl.CostEstimate(flops=30_000_000, bytes_accessed=8_000_000, transcendentals=0),
        name="first_iterate",
    )(place, source, wavenumber_sq)
    y_chip, y_next = rows_step(y_chip, y_next)
    e, r, fc = pl.pallas_call(
        functools.partial(inner_kernel, late),
        in_specs=[VMEM] * 5,
        out_specs=[VMEM] * 3,
        out_shape=[two, two, coarser],
        scratch_shapes=[column, V(3, *part)],
        compiler_params=params(24),
        cost_estimate=pl.CostEstimate(flops=70_000_000, bytes_accessed=16_000_000, transcendentals=0),
        name="inner_cells",
    )(source, wavenumber_sq, u, ga, gb)
    held = (u, e, r, ga, gb, fc)
    shapes = [two] * 3 + [one] * 2 + [coarser]
    xlo, xhi, held = lax.optimization_barrier((xlo, xhi, held))
    c_chip, c_next = rows_step(
        *pl.pallas_call(
            pack_corners_kernel,
            in_specs=[SMEM] + [ANY] * 2,
            out_specs=[VMEM] * 2,
            out_shape=[S(2 * held_planes, 4, lanes)] * 2,
            scratch_shapes=[V(2, 2 * held_planes, 8, lanes), pltpu.SemaphoreType.DMA((4,))],
            compiler_params=params(24),
            name="pack_corners",
        )(place, xlo, xhi)
    )
    in_place = {i + 1: i for i in range(6)}
    held = pl.pallas_call(
        functools.partial(faces_kernel, late, xsize, ysize),
        in_specs=[SMEM] + [VMEM] * 6 + [ANY] * 2 + [VMEM] * 2,
        out_specs=[VMEM] * 6,
        out_shape=shapes,
        input_output_aliases=in_place,
        scratch_shapes=[V(2, n // 2 - 4, 16, lanes), V(2, n // 2 - 4, 16, lanes // 2), V(2, held_planes, rows, lanes), pltpu.SemaphoreType.DMA((2,))],
        compiler_params=params(24),
        cost_estimate=pl.CostEstimate(flops=50_000_000, bytes_accessed=8_000_000, transcendentals=0),
        name="face_cells",
    )(place, *held, xlo, xhi, y_chip, y_next)
    u, e, r, ga, gb, fc, edges = pl.pallas_call(
        functools.partial(corners_kernel, xsize, ysize, n, rows),
        in_specs=[SMEM] + [VMEM] * 8,
        out_specs=[VMEM] * 7,
        out_shape=shapes + [S(2, 2, rows // 2, lanes // 2)],
        input_output_aliases=in_place,
        scratch_shapes=[column, V(2, 6, rows // 2, lanes)],
        compiler_params=params(24),
        name="corner_cells",
    )(place, *held, c_chip, c_next)
    fine_shape = S(2, n, rows, lanes)
    n, rows, lanes, xsize, ysize, zsize = n // 2, rows // 2, lanes // 2, xsize // 2, ysize // 2, lanes // 2
    h, over = halo_next, 1
    slab = lambda x, edge: jnp.concatenate([fc[:, x : x + h].reshape(3 * h, rows, lanes), edge], 0)
    xlo, xhi = planes_step(slab(0, edges[0]), slab(n - h, edges[1]))
    e, _, fc_late = pl.pallas_call(
        functools.partial(late_kernel, late, 2 * xsize, 2 * ysize, 2 * n, 2 * rows),
        in_specs=[SMEM] + [VMEM] * 5,
        out_specs=[VMEM] * 3,
        out_shape=[two, two, S(2, late[1] - late[0], rows, lanes)],
        input_output_aliases={2: 0, 3: 1},
        scratch_shapes=[column, V(2, late[1] - late[0], rows, 2 * lanes)],
        compiler_params=params(24),
        cost_estimate=pl.CostEstimate(flops=30_000_000, bytes_accessed=8_000_000, transcendentals=0),
        name="late_cells",
    )(place, u, e, r, ga, gb)
    fine = pl.pallas_call(
        iterate_kernel,
        in_specs=[VMEM] * 2,
        out_specs=VMEM,
        out_shape=fine_shape,
        compiler_params=params(24),
        cost_estimate=pl.CostEstimate(flops=1_000_000, bytes_accessed=8_000_000, transcendentals=0),
        name="fine_iterate",
    )(u, e)
    xlo, xhi, fine, fc_late = lax.optimization_barrier((xlo, xhi, fine, fc_late))
    chip, other, window = pl.pallas_call(
        functools.partial(rows_kernel, xdev, h),
        in_specs=[SMEM] + [VMEM] * 5,
        out_specs=[VMEM] * 3,
        out_shape=[S(2, n + 2 * h, 8, lanes)] * 2 + [S(3, n + 2 * h, rows, lanes)],
        compiler_params=params(24),
        name="second_rows",
    )(place, xlo, fc, fc_late, xhi, edges)
    chip, other = rows_step(chip, other)
    state = (n + 2 * h, 1, rows + 16, LANES)
    work = lambda s: [V(*s), V(*s), V(2, *s), V(2, *s), V(2, *s), V(2, 1, *s[2:])]
    width = n // 2 + 2 * over
    second_u, fc = pl.pallas_call(
        functools.partial(middle_kernel, h, over, xsize, ysize),
        in_specs=[SMEM] + [VMEM] * 3,
        out_specs=[VMEM] * 2,
        out_shape=[S(2, n, rows, lanes), S(width + width // 2, width, lanes)],
        scratch_shapes=[V(3, *state)] + work(state) + [V(2, width, 16, LANES), V(2, width // 2, 16, LANES)],
        compiler_params=params(24),
        name="second_level",
    )(place, window, chip, other)

    n, xsize, ysize, zsize = n // 2, xsize // 2, ysize // 2, zsize // 2
    m = n // 2

    def joined(start):
        own = fc[:, start : start + n]
        return jnp.concatenate([xlo[:n], own[: n + 2], xhi[:n], xlo[n:], own[n + 2 :], xhi[n:]], 0)

    pick = lambda i, j: jnp.concatenate([fc[i : i + n, 1 : n + 1], fc[n + 2 + j : n + 2 + j + m, 1 : n + 1]], 0)
    xlo, xhi = planes_step(pick(2, 1), pick(0, 0))
    first, last = joined(2), joined(0)
    even = place[1] % 2 == 0
    chip, other = rows_step(jnp.where(even, last, first), jnp.where(even, first, last))
    state = (n + 18, 1, 40, LANES)
    small = (m + 6, 1, 16, LANES)
    third, coarse = pl.pallas_call(
        functools.partial(coarse_kernel, n, 4, xsize, ysize, zsize),
        in_specs=[SMEM] + [VMEM] * 5,
        out_specs=[VMEM] * 2,
        out_shape=[S(2, n, n, zsize), S(2, m, m, zsize // 2)],
        scratch_shapes=[V(n + 18 + m + 9, 1, 40, LANES)] + work(state) + [V(2, m + 6, 16, LANES), V(m + 6, 16, LANES)]
        + [V(*small), V(*small), V(2, *small), V(2, 2, *small)],
        compiler_params=params(24),
        name="coarse_levels",
    )(place, fc, xlo, xhi, chip, other)
    return fine, second_u, third, coarse


def solution(mesh):
    placed = (P(None, "gx", "gy", None), P("gx", "gy", None))
    return jax.shard_map(body, mesh=mesh, in_specs=placed, out_specs=(P(None, "gx", "gy", None),) * 4, check_vma=False)
```

```python
import functools
import jax
import jax.numpy as jnp
from jax import lax
from jax.experimental import pallas as pl
from jax.experimental.pallas import tpu as pltpu
from jax.sharding import PartitionSpec as P

DAMPING = 0.8
SHIFT_IMAG = 0.5
LANES = 128
VMEM = pl.BlockSpec(memory_space=pltpu.VMEM)
SMEM = pl.BlockSpec(memory_space=pltpu.SMEM)
ANY = pl.BlockSpec(memory_space=pl.ANY)


def params(mib):
    return pltpu.CompilerParams(vmem_limit_bytes=mib * 1024 * 1024)


def around(ref, k, x, row, rows, full):
    halves = ref.shape[2]
    mid = [ref[k, x, h, pl.ds(row, rows), :] for h in range(halves)]
    up = [pltpu.roll(m, 1, 1) for m in mid]
    down = [pltpu.roll(m, LANES - 1, 1) for m in mid]
    if full:
        lane = lax.broadcasted_iota(jnp.int32, mid[0].shape, 1)
        first, last = lane == 0, lane == LANES - 1
        up = [jnp.where(first, up[h - 1] if h else 0.0, up[h]) for h in range(halves)]
        down = [jnp.where(last, down[h + 1] if h < halves - 1 else 0.0, down[h]) for h in range(halves)]
    sums = []
    for h in range(halves):
        planes = ref[k, x - 1, h, pl.ds(row, rows), :] + ref[k, x + 1, h, pl.ds(row, rows), :]
        sides = ref[k, x, h, pl.ds(row - 1, rows), :] + ref[k, x, h, pl.ds(row + 1, rows), :]
        sums.append((planes + sides) + (up[h] + down[h]))
    return sums


def inverse(c, scale, ok):
    a = 6.0 / scale - c
    b = SHIFT_IMAG * c
    g = DAMPING / (a * a + b * b)
    if ok is not None:
        g = jnp.where(ok, g, 0.0)
    return g * a, g * b


def divided(re, im, a, b):
    return re * a + im * b, im * a - re * b


def point(re, im, c, scale, ok, u, ga, gb, x, h, row):
    a, b = inverse(c, scale, ok)
    at = pl.ds(row, c.shape[0])
    ga[x, h, at, :], gb[x, h, at, :] = a, b
    u[0, x, h, at, :], u[1, x, h, at, :] = divided(re, im, a, b)


def second(u, ga, gb, e, x, row, rows, scale, full):
    s_re, s_im = around(u, 0, x, row, rows, full), around(u, 1, x, row, rows, full)
    at = pl.ds(row, rows)
    for h in range(u.shape[2]):
        a, b = ga[x, h, at, :], gb[x, h, at, :]
        if scale != 1.0:
            a, b = a * (1.0 / scale), b * (1.0 / scale)
        d = divided(s_re[h], s_im[h], a, b)
        for k in (0, 1):
            e[k, x, h, at, :] = 0.4 * u[k, x, h, at, :] + d[k]


def is_even(place, shape):
    return jnp.full(shape, lax.rem(place[1], 2)) == 0


def rows_inside(shape, y0, ysize):
    row = lax.broadcasted_iota(jnp.int32, shape, 0) + y0
    return (row >= 0) & (row < ysize)


def restrict_rows(vals, t, out, to, row, rows, k, start):
    for h, val in enumerate(vals):
        t[k, h, pl.ds(start, val.shape[0]), :] = val
        part = [t[k, h, pl.ds(row + j, rows, 2), :] for j in range(4)]
        out[k, to, pl.ds(0, rows), pl.ds(LANES * h, LANES)] = (part[0] + part[3]) + 3.0 * (part[1] + part[2])


def restrict_xy(r, t, out, to, plane, row, rows, k, window):
    at = pl.ds(*window)
    vals = []
    for h in range(r.shape[2]):
        four = [r[k, plane + j, h, at, :] for j in range(4)]
        vals.append((four[0] + four[3]) + 3.0 * (four[1] + four[2]))
    restrict_rows(vals, t, out, to, row, rows, k, window[0])


def add_pairs(c0, c1, t, h, out, i, row, rows):
    t[0, h, pl.ds(0, c0.shape[0]), :] = c0 + c1
    val = t[0, h, pl.ds(row, rows, 2), :] + t[0, h, pl.ds(row + 1, rows, 2), :]
    out[i, pl.ds(0, rows), pl.ds(LANES * h, LANES)] = val


def weights(lanes, zsize, mean=False, shift=0):
    z = lax.broadcasted_iota(jnp.int32, (lanes, LANES), 0)
    i = lax.broadcasted_iota(jnp.int32, (lanes, LANES), 1) - shift
    d = z - 2 * i
    inner = (d == 0) | (d == 1)
    if mean:
        w = jnp.where(inner, 0.125, 0.0)
    else:
        w = jnp.where(inner, 3.0 / 512.0, jnp.where((d == -1) | (d == 2), 1.0 / 512.0, 0.0))
    return jnp.where((z < zsize) & (i >= 0) & (i < zsize // 2), w, 0.0).astype(jnp.bfloat16)


def split_dot(part, w):
    planes, rows, lanes = part.shape
    x = part.reshape(planes * rows, lanes)
    hi = x.astype(jnp.bfloat16)
    low = (x - hi.astype(jnp.float32)).astype(jnp.bfloat16)
    dot = functools.partial(jnp.dot, preferred_element_type=jnp.float32)
    return (dot(hi, w) + dot(low, w)).reshape(planes, rows, w.shape[1])


PX, PY = 2, 8


def planes_kernel(f, c, x_first, x_last, planes, sems):
    n = c.shape[0]
    copies = []
    for side, x in enumerate((0, n - PX)):
        at = pl.ds(x, PX)
        copies += [(c.at[at], planes.at[side, 2]), (f.at[0, at], planes.at[side, 0]), (f.at[1, at], planes.at[side, 1])]
    copies = [pltpu.make_async_copy(src, dst, sems.at[i]) for i, (src, dst) in enumerate(copies)]
    for copy in copies:
        copy.start()
    for side, out in enumerate((x_first, x_last)):
        for copy in copies[3 * side : 3 * side + 3]:
            copy.wait()
        for j in range(PX):
            a, b = inverse(planes[side, 2, j], 1.0, None)
            out[j], out[PX + j] = divided(planes[side, 0, j], planes[side, 1, j], a, b)
        out[2 * PX] = planes[side, 2, (PX - 1) * side]


def first_kernel(place, f, c, u, ga, gb, y_chip, y_next):
    n, rows, lanes = c.shape
    cut = [pl.ds(LANES * h, LANES) for h in range(lanes // LANES)]
    row = lax.broadcasted_iota(jnp.int32, (8, LANES), 0)
    even = is_even(place, (8, LANES))

    def step(x, carry):
        for h, lane in enumerate(cut):
            point(f[0, x, :, lane], f[1, x, :, lane], c[x, :, lane], 1.0, None, u, ga, gb, x + PX, h, PY)
            made = []
            for start, shifts in ((0, (0, 3, 6)), (rows - 8, (3, 6, 0))):
                tiles = [u[k, x + PX, h, pl.ds(PY + start, 8), :] for k in (0, 1)] + [c[x, pl.ds(start, 8), lane]]
                re, im, cc = [pltpu.roll(v, shift, 0) if shift else v for v, shift in zip(tiles, shifts)]
                made.append(jnp.where(row < 3, re, jnp.where(row < 6, im, cc)))
            y_chip[x, :, lane], y_next[x, :, lane] = jnp.where(even, made[1], made[0]), jnp.where(even, made[0], made[1])
        return carry

    lax.fori_loop(0, n, step, 0, unroll=True)


def both_ends(ranges, step):
    for first, last in ranges:
        lax.fori_loop(first, last, step, 0, unroll=True)


def inner_kernel(late, f, c, u, ga, gb, e, r, fc_out, t, part):
    n, rows, lanes = c.shape
    halves = lanes // LANES
    at = pl.ds(PY, rows)
    cut = [pl.ds(LANES * h, LANES) for h in range(halves)]

    def middle(x, carry):
        second(u, ga, gb, e, x + PX, PY, rows, 1.0, True)
        return carry

    lo, hi = late
    both_ends(((1, 2 * lo + 2), (2 * hi - 2, n - 1)), middle)
    row = lax.broadcasted_iota(jnp.int32, (rows, LANES), 0)
    full = (row >= 2) & (row < rows - 2)

    def last(x, carry):
        for k in (0, 1):
            s = around(e, k, x + PX, PY, rows, True)
            for h in range(halves):
                r[k, x + PX, h, at, :] = 0.04 * f[k, x, :, cut[h]] + jnp.where(full, s[h], 0.0)
        return carry

    both_ends(((2, 2 * lo + 1), (2 * hi - 1, n - 2)), last)
    for x in (0, 1, *range(2 * lo + 1, 2 * hi - 1), n - 2, n - 1):
        for k in (0, 1):
            for h in range(halves):
                r[k, x + PX, h, at, :] = 0.04 * f[k, x, :, cut[h]]
    for x in (PX - 1, n + PX):
        r[:, x] = jnp.zeros((2,) + r.shape[2:], jnp.float32)

    def pairs(i, carry):
        for h in range(halves):
            add_pairs(c[2 * i, :, cut[h]], c[2 * i + 1, :, cut[h]], t, h, part.at[2], i, 0, rows // 2)
        return carry

    lax.fori_loop(0, n // 2, pairs, 0, unroll=True)

    def coarse(i, carry):
        for k in (0, 1):
            restrict_xy(r, t, part, i, 2 * i + PX - 1, PY - 1, rows // 2, k, (PY, rows))
        return carry

    early = ((2, lo), (hi, n // 2 - 2))
    both_ends(early, coarse)
    w = weights(lanes, lanes)
    for k in (0, 1):
        for i, j in early:
            fc_out[k, i:j] = split_dot(part[k, i:j], w)
    fc_out[2] = split_dot(part[2], weights(lanes, lanes, mean=True))


def inside(place, n, rows, xsize, ysize):
    x0, y0 = place[0] * n - PX, place[1] * rows - PY

    def ok(x, row, count):
        gx = x + x0
        return rows_inside((count, LANES), y0 + row, ysize) & ((gx >= 0) & (gx < xsize))

    return ok


def halo(re, im, cc, good, u, ga, gb, r, x, h, row, c_here, r_here):
    at = pl.ds(row, re.shape[0])
    re, im = jnp.where(good, re, 0.0), jnp.where(good, im, 0.0)
    u[0, x, h, at, :], u[1, x, h, at, :] = re, im
    if c_here:
        a, b = inverse(cc, 1.0, good)
        ga[x, h, at, :], gb[x, h, at, :] = a, b
    if r_here:
        a, b = 0.05 * (6.0 - cc), (0.05 * SHIFT_IMAG) * cc
        r[0, x, h, at, :], r[1, x, h, at, :] = re * a - im * b, im * a + re * b


def finish(e, r, x, row, count, good):
    for k in (0, 1):
        s = around(e, k, x, row, count, True)
        for h in range(e.shape[2]):
            at = pl.ds(row, count)
            r[k, x, h, at, :] = r[k, x, h, at, :] + jnp.where(good, s[h], 0.0)


def plane_cells(side, low, i, h):
    cut = pl.ds(LANES * h, LANES)
    c_here = i == (PX - 1 if low else 0)
    return side[i, :, cut], side[PX + i, :, cut], side[2 * PX, :, cut] if c_here else None, c_here


def faces_kernel(late, xsize, ysize, place, u_in, e_in, r_in, ga_in, gb_in, fc_in, xlo, xhi, y_chip, y_next, u, e, r, ga, gb, fc_out, part, q, sides, sems):
    n, (rows, lanes) = y_chip.shape[0], xlo.shape[1:]
    halves = lanes // LANES
    cut = [pl.ds(LANES * h, LANES) for h in range(halves)]
    ok = inside(place, n, rows, xsize, ysize)
    del u_in, e_in, r_in, ga_in, gb_in, fc_in
    used = pl.ds(0, 2 * PX + 1)
    copies = [pltpu.make_async_copy(src.at[used], sides.at[i], sems.at[i]) for i, src in enumerate((xlo, xhi))]
    for copy in copies:
        copy.start()
    low, high = PY - 4, PY + rows - 4
    good_lo, good_hi = ok(PX, 0, 8), ok(PX, PY + rows, 8)
    even = is_even(place, (8, LANES))

    def strips(x, carry):
        for h in range(halves):
            chip, other = y_chip[x, :, cut[h]], y_next[x, :, cut[h]]
            lo, hi = jnp.where(even, other, chip), jnp.where(even, chip, other)
            for tile, good, row, shifts in ((lo, good_lo, 0, (5, 2, 0)), (hi, good_hi, PY + rows, (0, 5, 2))):
                re, im, cc = [pltpu.roll(tile, shift, 0) if shift else tile for shift in shifts]
                halo(re, im, cc, good, u, ga, gb, r, x + PX, h, row, True, True)
        return carry

    lax.fori_loop(0, n, strips, 0, unroll=True)
    for copy in copies:
        copy.wait()
    for side, is_low, base in ((sides.at[0], True, 0), (sides.at[1], False, n + PX)):
        for i in range(PX):
            good = ok(base + i, PY, rows)
            for h in range(halves):
                re, im, cc, c_here = plane_cells(side, is_low, i, h)
                halo(re, im, cc, good, u, ga, gb, r, base + i, h, PY, c_here, False)
    for x in (PX - 1, PX, n + PX - 1, n + PX):
        second(u, ga, gb, e, x, PY, rows, 1.0, True)

    def middle(x, carry):
        for row in (low, high):
            second(u, ga, gb, e, x, row, 8, 1.0, True)
        return carry

    lo, hi = late
    both_ends(((PX + 1, PX + 2 * lo + 2), (PX + 2 * hi - 2, n + PX - 1)), middle)
    for x in (PX, PX + 1, n + PX - 2, n + PX - 1):
        finish(e, r, x, PY + 4, rows - 8, ok(x, PY + 4, rows - 8))
    row = lax.broadcasted_iota(jnp.int32, (8, LANES), 0)
    good_low, good_high = ok(PX, low, 8) & (row < 6), ok(PX, high, 8) & (row >= 2)

    def last(x, carry):
        finish(e, r, x, low, 8, good_low)
        finish(e, r, x, high, 8, good_high)
        return carry

    both_ends(((PX + 2, PX + 2 * lo + 1), (PX + 2 * hi - 1, n + PX - 2)), last)
    m = n // 2 - 4

    def coarse(i, carry):
        x = 2 * i + PX + 3
        for k in (0, 1):
            for h in range(halves):
                for j, row in ((0, PY - 1), (8, PY + rows - 7)):
                    at = pl.ds(row, 8)
                    part[k, i, pl.ds(j, 8), cut[h]] = (r[k, x, h, at, :] + r[k, x + 3, h, at, :]) + 3.0 * (
                        r[k, x + 1, h, at, :] + r[k, x + 2, h, at, :]
                    )
        return carry

    both_ends(((0, lo - 2), (hi - 2, m)), coarse)
    w = weights(lanes, lanes)
    for k in (0, 1):
        q[k] = split_dot(part[k], w)
        for row, start in ((0, 0), (rows // 2 - 2, 10)):
            four = [q[k, :, pl.ds(start + j, 2, 2), :] for j in range(4)]
            fc_out[k, pl.ds(2, m), pl.ds(row, 2), :] = (four[0] + four[3]) + 3.0 * (four[1] + four[2])


def pack_corners_kernel(place, xlo, xhi, chip, other, tiles, sems):
    count, rows = 2 * PX + 1, xlo.shape[1]
    copies = []
    for i, side in enumerate((xlo, xhi)):
        for j, row in enumerate((0, rows - 8)):
            copies.append(pltpu.make_async_copy(side.at[pl.ds(0, count), pl.ds(row, 8)], tiles.at[j, pl.ds(count * i, count)], sems.at[2 * i + j]))
    for copy in copies:
        copy.start()
    even = is_even(place, (4, xlo.shape[2]))
    for copy in copies:
        copy.wait()
    for j in range(2 * count):
        first, last = tiles[0, j, pl.ds(0, 4), :], tiles[1, j, pl.ds(4, 4), :]
        chip[j], other[j] = jnp.where(even, last, first), jnp.where(even, first, last)


def corners_kernel(xsize, ysize, n, rows, place, u_in, e_in, r_in, ga_in, gb_in, fc_in, c_chip, c_next, u, e, r, ga, gb, fc_out, edge_out, t, part):
    halves = c_chip.shape[2] // LANES
    even = is_even(place, (4, LANES))
    ok = inside(place, n, rows, xsize, ysize)
    del u_in, e_in, r_in, ga_in, gb_in, fc_in
    low, high = PY - 4, PY + rows - 4
    held = 2 * PX + 1
    for first, low_planes, base in ((0, True, 0), (held, False, n + PX)):
        chip, other = c_chip.at[pl.ds(first, held)], c_next.at[pl.ds(first, held)]
        for i in range(PX):
            for h in range(halves):
                one, two = plane_cells(chip, low_planes, i, h), plane_cells(other, low_planes, i, h)
                for row, (p, q) in ((PY - 4, (two, one)), (PY + rows, (one, two))):
                    re, im, cc = [None if v is None else jnp.where(even, v, w) for v, w in zip(p[:3], q[:3])]
                    halo(re, im, cc, ok(base + i, row, 4), u, ga, gb, r, base + i, h, row, one[3], False)
    for x in (PX - 1, PX, n + PX - 1, n + PX):
        for row in (low, high):
            second(u, ga, gb, e, x, row, 8, 1.0, True)
    for x in (PX, PX + 1, n + PX - 2, n + PX - 1):
        for row in (low, high):
            finish(e, r, x, row, 8, ok(x, row, 8))
    planes = (0, 1, n // 2 - 2, n // 2 - 1)
    w = weights(part.shape[3], part.shape[3])
    for k in (0, 1):
        for j, i in enumerate(planes):
            restrict_xy(r, t, part, j, 2 * i + PX - 1, PY - 1, rows // 2, k, (low, rows + 8))
        for j, x in ((4, PX), (5, n + PX - 1)):
            restrict_rows([r[k, x, h, pl.ds(low, rows + 8), :] for h in range(halves)], t, part, j, PY - 1, rows // 2, k, low)
        val = split_dot(part[k], w)
        for j, i in enumerate(planes):
            fc_out[k, i] = val[j]
        edge_out[0, k], edge_out[1, k] = val[4], val[5]


def late_kernel(late, xsize, ysize, n, rows, place, u, e_in, r_in, ga, gb, e, r, out, fine, t, part, made, sems):
    halves = u.shape[2]
    ok = inside(place, n, rows, xsize, ysize)
    del e_in, r_in
    lo, hi = late
    low = PY - 4
    own = pl.ds(PY, rows)
    copies = []

    def iterate(first, last):
        for x in range(first, last):
            for k in (0, 1):
                for h in range(halves):
                    made[k, x, :, pl.ds(LANES * h, LANES)] = e[k, x + PX, h, own, :] + 0.8 * u[k, x + PX, h, own, :]
        at = pl.ds(first, last - first)
        for k in (0, 1):
            copies.append(pltpu.make_async_copy(made.at[k, at], fine.at[k, at], sems.at[len(copies)]))
            copies[-1].start()

    iterate(0, 2 * lo + 2)
    iterate(2 * hi - 2, n)
    for x in range(PX + 2 * lo + 2, PX + 2 * hi - 2):
        second(u, ga, gb, e, x, low, rows + 8, 1.0, True)
    good = ok(PX, low, rows + 8)
    for x in range(PX + 2 * lo + 1, PX + 2 * hi - 1):
        finish(e, r, x, low, rows + 8, good)
    iterate(2 * lo + 2, 2 * hi - 2)
    w = weights(LANES * halves, LANES * halves)
    for k in (0, 1):
        for i in range(lo, hi):
            restrict_xy(r, t, part, i - lo, 2 * i + PX - 1, PY - 1, rows // 2, k, (low, rows + 8))
        out[k] = split_dot(part[k], w)
    for copy in copies:
        copy.wait()


def whole_level(cells, u, e, r, ga, gb, planes, used, row, rows, scale, full, ok, u_put):
    first, count = used
    for x in range(planes):
        at = pl.ds(first, count)
        point(cells(0, x, at), cells(1, x, at), cells(2, x, at), scale, ok(x, first, count), u, ga, gb, x, 0, first)
    at = pl.ds(row, rows)
    for x in range(1, planes - 1):
        second(u, ga, gb, e, x, row, rows, scale, full)
        u_put(x)
    for x in range(2, planes - 2):
        good = ok(x, row, rows)
        for k in (0, 1):
            s = around(e, k, x, row, rows, full)[0] * (1.0 / scale)
            r[k, x, 0, at, :] = jnp.where(good, 0.04 * cells(k, x, at) + s, 0.0)


def rows_kernel(xdev, halo, place, xlo, fc, fc_late, xhi, edges, chip, other, window):
    n, rows = fc.shape[1:3]
    row = lax.broadcasted_iota(jnp.int32, (8, LANES), 0)
    even = is_even(place, (8, LANES))
    here = jnp.full((rows, LANES), place[0])
    for k in range(3):
        window[k, pl.ds(0, halo)] = xlo[pl.ds(k * halo, halo)]
        window[k, pl.ds(halo, n)] = fc[k]
        if k < 2:
            window[k, pl.ds(2 * halo, n - 2 * halo)] = fc_late[k]
        window[k, pl.ds(n + halo, halo)] = xhi[pl.ds(k * halo, halo)]
    for k in (0, 1):
        window[k, halo - 1] += edges[0, k]
        window[k, halo] += jnp.where(here > 0, xlo[3 * halo + k], 0.0)
        window[k, n + halo - 1] += jnp.where(here < xdev - 1, xhi[3 * halo + k], 0.0)
        window[k, n + halo] += edges[1, k]
    for x in range(n + 2 * halo):
        made = []
        for start, own in ((0, row < 5), (rows - 8, row >= 3)):
            re, im, cc = [window[k, x, pl.ds(start, 8), :] for k in range(3)]
            made.append((jnp.where(own, re, pltpu.roll(cc, 5, 0)), jnp.where(own, im, pltpu.roll(cc, 2, 0))))
        for k, (first, last) in enumerate(zip(*made)):
            chip[k, x], other[k, x] = jnp.where(even, last, first), jnp.where(even, first, last)


def middle_kernel(halo, over, xsize, ysize, place, window, y_chip, y_next, u_out, fc_out, fc, ga, gb, u, e, r, t, part, part_c):
    planes, rows = window.shape[1:3]
    n = planes - 2 * halo
    for k in range(3):
        fc[k, :, 0, pl.ds(8, rows), :] = window[k]
    row = lax.broadcasted_iota(jnp.int32, (8, LANES), 0)
    even = is_even(place, (8, LANES))
    for x in range(planes):
        chip, other = [y_chip[k, x] for k in (0, 1)], [y_next[k, x] for k in (0, 1)]
        for start, split, p, q in ((0, 6, other, chip), (8 + rows, 3, chip, other)):
            at = pl.ds(start, 8)
            one, two = [jnp.where(even, v, w) for v, w in zip(p, q)]
            fc[0, x, 0, at, :], fc[1, x, 0, at, :] = one, two
            fc[2, x, 0, at, :] = jnp.where(row < split, pltpu.roll(one, 3, 0), pltpu.roll(two, 6, 0))
    x0, y0 = place[0] * n - halo, place[1] * rows - 8

    def ok(x, row, count):
        gx = x + x0
        return rows_inside((count, LANES), y0 + row, ysize) & ((gx >= 0) & (gx < xsize))

    def u_put(x):
        if halo <= x < n + halo:
            at = pl.ds(8, rows)
            for k in (0, 1):
                u_out[k, x - halo] = e[k, x, 0, at, :] + 0.8 * u[k, x, 0, at, :]

    def cells(k, x, at):
        return fc[k, x, 0, at, :]

    whole_level(cells, u, e, r, ga, gb, planes, (0, rows + 16), 4, rows + 8, 4.0, True, ok, u_put)
    width = n // 2 + 2 * over
    pairs = width // 2
    for i in range(width):
        x, row = 2 * i + halo - 1 - 2 * over, 7 - 2 * over
        for k in (0, 1):
            restrict_xy(r, t, part, i, x, row, width, k, (4, rows + 8))
        add_pairs(fc[2, x + 1, 0], fc[2, x + 2, 0], t, 0, part_c.at[i % 2], i // 2, row + 1, width)
    two = [(part.at[k], part_c.at[k], LANES // 2 * k) for k in (0, 1)]
    fc_out[pl.ds(0, width)] = sum(split_dot(p[...], weights(LANES, LANES, shift=s)) for p, _, s in two)[:, :width]
    fc_out[pl.ds(width, pairs)] = sum(split_dot(p[...], weights(LANES, LANES, True, s)) for _, p, s in two)[:, :width]


def coarse_kernel(n, sweeps, xsize, ysize, zsize, place, fc_own, xlo, xhi, y_chip, y_next, u_out, v_out, fc, ga, gb, u, e, r, t, part, part_c, gc, gd, v, w):
    m = n // 2
    planes = n + 18
    own, own_c = range(8, n + 10), range(planes + 4, planes + m + 5)
    for src, x, first, count in ((xlo, 0, 0, 8), (xhi, n + 10, 0, 8), (xlo, planes, 8, 4), (xhi, planes + m + 5, 8, 4)):
        fc[pl.ds(x, count), 0, pl.ds(16, n), :] = src[pl.ds(first, count)]
    fc[pl.ds(8, n + 2), 0, pl.ds(15, n + 2), :] = fc_own[pl.ds(0, n + 2)]
    fc[pl.ds(planes + 4, m + 1), 0, pl.ds(15, n + 2), :] = fc_own[pl.ds(n + 2, m + 1)]
    even = is_even(place, (8, LANES))
    for x in range(fc.shape[0]):
        out = 1 if x in own or x in own_c else 0
        chip, other = y_chip[x], y_next[x]
        fc[x, 0, pl.ds(8 - out, 8), :] = jnp.where(even, other, chip)
        fc[x, 0, pl.ds(n + 16 + out, 8), :] = jnp.where(even, chip, other)
    lane = lax.broadcasted_iota(jnp.int32, (1, LANES), 1)

    def cells(k, x, at):
        val = fc[planes + x // 2 if k == 2 else x, 0, at, :]
        return pltpu.roll(val, LANES - zsize, 1) if k == 1 or (k == 2 and x % 2) else val

    def inside(x0, y0, xs, ys, zs):
        def ok(x, row, count):
            gx = x + x0
            here = rows_inside((count, LANES), y0 + row, ys) & (lane < zs)
            return here & ((gx >= 0) & (gx < xs))

        return ok

    def u_put(x):
        if 9 <= x < n + 9:
            at = pl.ds(16, n)
            for k in (0, 1):
                u_out[k, x - 9] = (e[k, x, 0, at, :] + 0.8 * u[k, x, 0, at, :])[:, :zsize]

    ok = inside(place[0] * n - 9, place[1] * n - 16, xsize, ysize, zsize)
    whole_level(cells, u, e, r, ga, gb, planes, (7, n + 18), 8, n + 16, 16.0, False, ok, u_put)
    width = m + 6
    every = pl.ds(8, n + 16)
    for i in range(width):
        for k in (0, 1):
            restrict_xy(r, t, part, i, 2 * i + 2, 9, width, k, (8, n + 16))
        t[0, 0, every, :] = cells(2, 2 * i + 3, every) + cells(2, 2 * i + 4, every)
        part_c[i, pl.ds(0, width), :] = t[0, 0, pl.ds(10, width, 2), :] + t[0, 0, pl.ds(11, width, 2), :]
    w_full = weights(LANES, zsize)
    f = [split_dot(part[k], w_full) for k in (0, 1)] + [split_dot(part_c[...], weights(LANES, zsize, True))]
    ok = inside(place[0] * m - 3, place[1] * m - 3, xsize // 2, ysize // 2, zsize // 2)
    for x in range(width):
        point(f[0][x], f[1][x], f[2][x], 64.0, ok(x, 0, 16), v, gc, gd, x, 0, 0)
    old = v
    for sweep in range(1, sweeps):
        new = w.at[sweep % 2]
        for x in range(sweep, width - sweep):
            at = pl.ds(1, m + 4)
            s = [around(old, k, x, 1, m + 4, False)[0] for k in (0, 1)]
            d = divided(*s, gc[x, 0, at, :] * (1.0 / 64.0), gd[x, 0, at, :] * (1.0 / 64.0))
            for k in (0, 1):
                val = 0.2 * old[k, x, 0, at, :] + v[k, x, 0, at, :] + d[k]
                if sweep < sweeps - 1:
                    new[k, x, 0, at, :] = val
                else:
                    v_out[k, x - 3] = val[2 : 2 + m, : zsize // 2]
        old = new


def body(source, wavenumber_sq):
    f32 = jnp.float32
    xdev, ydev = lax.axis_size("gx"), lax.axis_size("gy")
    place = jnp.stack([lax.axis_index("gx"), lax.axis_index("gy")]).astype(jnp.int32)

    def planes_step(first, last):
        before = lax.ppermute(last, "gx", [(i, (i + 1) % xdev) for i in range(xdev)])
        after = lax.ppermute(first, "gx", [((i + 1) % xdev, i) for i in range(xdev)])
        return before, after

    every = [(i, j) for i in range(xdev) for j in range(ydev)]
    number = lambda i, j: i * ydev + j
    on_chip = [(number(i, j), number(i, j ^ 1)) for i, j in every]
    next_chip = [(number(i, j), number(i ^ 1, j) if j in (0, ydev - 1) else number(i, ((j - 1) ^ 1) + 1)) for i, j in every]

    def rows_step(chip, other):
        return lax.ppermute(chip, ("gx", "gy"), on_chip), lax.ppermute(other, ("gx", "gy"), next_chip)

    _, n, rows, lanes = source.shape
    xsize, ysize = n * xdev, rows * ydev
    S = lambda *shape: jax.ShapeDtypeStruct(shape, f32)
    V = lambda *shape: pltpu.VMEM(shape, f32)

    halo_next = 5
    late = (halo_next, n // 2 - halo_next)
    halves = lanes // LANES
    state = (n + 2 * PX, halves, rows + 2 * PY, LANES)
    part = (n // 2, rows // 2, lanes)
    two, one, coarser = S(2, *state), S(*state), S(3, n // 2, rows // 2, lanes // 2)
    column = V(2, halves, rows + 2 * PY, LANES)
    held_planes = 2 * PX + 1
    x_first, x_last = pl.pallas_call(
        planes_kernel,
        in_specs=[pl.BlockSpec(memory_space=pltpu.HBM)] * 2,
        out_specs=[VMEM] * 2,
        out_shape=[S(held_planes + 2, rows, lanes)] * 2,
        scratch_shapes=[V(2, 3, PX, rows, lanes), pltpu.SemaphoreType.DMA((6,))],
        compiler_params=params(24),
        name="pack_planes",
    )(*[pltpu.with_memory_space_constraint(x, pltpu.HBM) for x in (source, wavenumber_sq)])
    source, wavenumber_sq, x_first, x_last = lax.optimization_barrier((source, wavenumber_sq, x_first, x_last))
    xlo, xhi = planes_step(x_first, x_last)
    u, ga, gb, y_chip, y_next = pl.pallas_call(
        first_kernel,
        in_specs=[SMEM] + [VMEM] * 2,
        out_specs=[VMEM] * 5,
        out_shape=[two, one, one] + [S(n, 8, lanes)] * 2,
        compiler_params=params(24),
        cost_estimate=pl.CostEstimate(flops=30_000_000, bytes_accessed=8_000_000, transcendentals=0),
        name="first_iterate",
    )(place, source, wavenumber_sq)
    y_chip, y_next = rows_step(y_chip, y_next)
    e, r, fc = pl.pallas_call(
        functools.partial(inner_kernel, late),
        in_specs=[VMEM] * 5,
        out_specs=[VMEM] * 3,
        out_shape=[two, two, coarser],
        scratch_shapes=[column, V(3, *part)],
        compiler_params=params(24),
        cost_estimate=pl.CostEstimate(flops=70_000_000, bytes_accessed=16_000_000, transcendentals=0),
        name="inner_cells",
    )(source, wavenumber_sq, u, ga, gb)
    held = (u, e, r, ga, gb, fc)
    shapes = [two] * 3 + [one] * 2 + [coarser]
    xlo, xhi, held = lax.optimization_barrier((xlo, xhi, held))
    c_chip, c_next = rows_step(
        *pl.pallas_call(
            pack_corners_kernel,
            in_specs=[SMEM] + [ANY] * 2,
            out_specs=[VMEM] * 2,
            out_shape=[S(2 * held_planes, 4, lanes)] * 2,
            scratch_shapes=[V(2, 2 * held_planes, 8, lanes), pltpu.SemaphoreType.DMA((4,))],
            compiler_params=params(24),
            name="pack_corners",
        )(place, xlo, xhi)
    )
    in_place = {i + 1: i for i in range(6)}
    held = pl.pallas_call(
        functools.partial(faces_kernel, late, xsize, ysize),
        in_specs=[SMEM] + [VMEM] * 6 + [ANY] * 2 + [VMEM] * 2,
        out_specs=[VMEM] * 6,
        out_shape=shapes,
        input_output_aliases=in_place,
        scratch_shapes=[V(2, n // 2 - 4, 16, lanes), V(2, n // 2 - 4, 16, lanes // 2), V(2, held_planes, rows, lanes), pltpu.SemaphoreType.DMA((2,))],
        compiler_params=params(24),
        cost_estimate=pl.CostEstimate(flops=50_000_000, bytes_accessed=8_000_000, transcendentals=0),
        name="face_cells",
    )(place, *held, xlo, xhi, y_chip, y_next)
    u, e, r, ga, gb, fc, edges = pl.pallas_call(
        functools.partial(corners_kernel, xsize, ysize, n, rows),
        in_specs=[SMEM] + [VMEM] * 8,
        out_specs=[VMEM] * 7,
        out_shape=shapes + [S(2, 2, rows // 2, lanes // 2)],
        input_output_aliases=in_place,
        scratch_shapes=[column, V(2, 6, rows // 2, lanes)],
        compiler_params=params(24),
        name="corner_cells",
    )(place, *held, c_chip, c_next)
    fine_shape = S(2, n, rows, lanes)
    n, rows, lanes, xsize, ysize, zsize = n // 2, rows // 2, lanes // 2, xsize // 2, ysize // 2, lanes // 2
    h, over = halo_next, 1
    slab = lambda x, edge: jnp.concatenate([fc[:, x : x + h].reshape(3 * h, rows, lanes), edge], 0)
    xlo, xhi = planes_step(slab(0, edges[0]), slab(n - h, edges[1]))
    _, _, fc_late, fine = pl.pallas_call(
        functools.partial(late_kernel, late, 2 * xsize, 2 * ysize, 2 * n, 2 * rows),
        in_specs=[SMEM] + [VMEM] * 5,
        out_specs=[VMEM] * 3 + [ANY],
        out_shape=[two, two, S(2, late[1] - late[0], rows, lanes), fine_shape],
        input_output_aliases={2: 0, 3: 1},
        scratch_shapes=[column, V(2, late[1] - late[0], rows, 2 * lanes), V(*fine_shape.shape), pltpu.SemaphoreType.DMA((6,))],
        compiler_params=params(24),
        cost_estimate=pl.CostEstimate(flops=30_000_000, bytes_accessed=8_000_000, transcendentals=0),
        name="late_cells",
    )(place, u, e, r, ga, gb)
    xlo, xhi, fine, fc_late = lax.optimization_barrier((xlo, xhi, fine, fc_late))
    chip, other, window = pl.pallas_call(
        functools.partial(rows_kernel, xdev, h),
        in_specs=[SMEM] + [VMEM] * 5,
        out_specs=[VMEM] * 3,
        out_shape=[S(2, n + 2 * h, 8, lanes)] * 2 + [S(3, n + 2 * h, rows, lanes)],
        compiler_params=params(24),
        name="second_rows",
    )(place, xlo, fc, fc_late, xhi, edges)
    chip, other = rows_step(chip, other)
    state = (n + 2 * h, 1, rows + 16, LANES)
    work = lambda s: [V(*s), V(*s), V(2, *s), V(2, *s), V(2, *s), V(2, 1, *s[2:])]
    width = n // 2 + 2 * over
    second_u, fc = pl.pallas_call(
        functools.partial(middle_kernel, h, over, xsize, ysize),
        in_specs=[SMEM] + [VMEM] * 3,
        out_specs=[VMEM] * 2,
        out_shape=[S(2, n, rows, lanes), S(width + width // 2, width, lanes)],
        scratch_shapes=[V(3, *state)] + work(state) + [V(2, width, 16, LANES), V(2, width // 2, 16, LANES)],
        compiler_params=params(24),
        name="second_level",
    )(place, window, chip, other)

    n, xsize, ysize, zsize = n // 2, xsize // 2, ysize // 2, zsize // 2
    m = n // 2

    def joined(start):
        own = fc[:, start : start + n]
        return jnp.concatenate([xlo[:n], own[: n + 2], xhi[:n], xlo[n:], own[n + 2 :], xhi[n:]], 0)

    pick = lambda i, j: jnp.concatenate([fc[i : i + n, 1 : n + 1], fc[n + 2 + j : n + 2 + j + m, 1 : n + 1]], 0)
    xlo, xhi = planes_step(pick(2, 1), pick(0, 0))
    first, last = joined(2), joined(0)
    even = place[1] % 2 == 0
    chip, other = rows_step(jnp.where(even, last, first), jnp.where(even, first, last))
    state = (n + 18, 1, 40, LANES)
    small = (m + 6, 1, 16, LANES)
    third, coarse = pl.pallas_call(
        functools.partial(coarse_kernel, n, 4, xsize, ysize, zsize),
        in_specs=[SMEM] + [VMEM] * 5,
        out_specs=[VMEM] * 2,
        out_shape=[S(2, n, n, zsize), S(2, m, m, zsize // 2)],
        scratch_shapes=[V(n + 18 + m + 9, 1, 40, LANES)] + work(state) + [V(2, m + 6, 16, LANES), V(m + 6, 16, LANES)]
        + [V(*small), V(*small), V(2, *small), V(2, 2, *small)],
        compiler_params=params(24),
        name="coarse_levels",
    )(place, fc, xlo, xhi, chip, other)
    return fine, second_u, third, coarse


def solution(mesh):
    placed = (P(None, "gx", "gy", None), P("gx", "gy", None))
    return jax.shard_map(body, mesh=mesh, in_specs=placed, out_specs=(P(None, "gx", "gy", None),) * 4, check_vma=False)
```
